32 devices in a mesh: dp: 32 (over z, y, x, core), refl: 1.
Axes of the slice: x: 2, y: 2, z: 4, core: 2. Of those that a mesh axis runs over, the one named last changes fastest.
Arguments:
- intensities: bfloat16 [1024, 16384], P('dp', 'refl'), may hold values from -12 to 12
- observed: int32 [1024, 16384], P('dp', 'refl'), may hold values 0 or 1
- qweights: bfloat16 [1024, 16384], P('dp', 'refl'), may hold values from 0.25 to 4
- ops: int32 [4, 16384], P(None, 'refl'), may hold values from 0 to 16383, as said below
- pick: int32 [32, 32], P(None, 'dp'), may hold values from 0 to 7
Outputs:
- corr: float32 [4, 1024, 128], P(None, ('dp', 'refl'))
- returned: float32 [4, 32, 32, 4, 32], P(None, 'dp', None, None, 'refl')
The draws below stay inside these ranges and needn't reach their ends.
Inputs may be any that keep to these rules, and one draw needn't show every extreme that they name: Each row of ops is a permutation of the reflections that maps every aligned block of 16384 reflections onto itself.
All inputs are finite; a program needn't handle non-finite values. No bound on the sum of `observed` on one device may be relied on, other than what follows from the above.
Results may differ from the reference program's by a relative error of at most 0.0084.
Values may be sent and summed in bfloat16 or wider, within the bound.
No kernel may reach another device: no remote copies, remote signals or barrier semaphores. Data moves between devices by JAX's collectives and lax.ppermute only.
A program may use at most 128 MiB of HBM per device.

```python
import math
import jax
import jax.numpy as jnp
from jax import lax

BLK = 32
SUB = 4
REFL = 16384
NOPS = 4
REFL_DEV = 16384
BLOCKS = 32
DATASETS = 1024


def draw_intensities(key, part):
    first, second, third = jax.random.split(jax.random.fold_in(key, 11), 3)
    common = jax.random.normal(first, (1, REFL), jnp.float32)
    amplitude = jax.random.uniform(second, (DATASETS, 1), jnp.float32, -1.5, 1.5)
    noise = 0.8 * jax.random.normal(third, (DATASETS, REFL), jnp.float32)
    values = amplitude * common + noise
    return jnp.clip(values, -12.0, 12.0).astype(jnp.bfloat16)


def draw_ops(key, part):
    parts_count = REFL // REFL_DEV
    keys = jax.random.split(jax.random.fold_in(key, 23), NOPS * parts_count)
    perms = jax.vmap(lambda single: jax.random.permutation(single, REFL_DEV))(keys)
    perms = perms.reshape(NOPS, parts_count, REFL_DEV).astype(jnp.int32)
    offsets = (jnp.arange(parts_count, dtype=jnp.int32) * REFL_DEV)[None, :, None]
    return (perms + offsets).reshape(NOPS, REFL)


def place_ends(result, own_key, least, high):
    longest = result.shape.index(max(result.shape))
    spots = []
    for shift in (0, 1):
        where = [jax.random.randint(jax.random.fold_in(own_key, axis), (), 0, length) for axis, length in enumerate(result.shape)]
        where[longest] = (where[longest] + shift) % result.shape[longest]
        spots.append(tuple(where))
    return result.at[spots[0]].set(least).at[spots[1]].set(high)


def levels(own_key, extent, shards, low, largest):
    level, own = 1.0, jax.random.fold_in(own_key, 6)
    for position, shards_of in shards:
        steps = jnp.exp(jax.random.uniform(jax.random.fold_in(own, position), (shards_of,), jnp.float32, low / len(shards), largest / len(shards)))
        level = level * jnp.repeat(steps, extent[position] // shards_of).reshape([-1 if axis == position else 1 for axis in range(len(extent))])
    return level


def setup_inputs(seed: int = 0) -> dict:
    arg_keys = jax.random.split(jax.random.key(seed), 6)
    return {
        "intensities": draw_intensities(jax.random.fold_in(arg_keys[5], 71), 0),
        "observed": place_ends((jax.random.randint(arg_keys[1], (DATASETS, REFL), 0, 2) < 1).astype(jnp.int32), jax.random.fold_in(arg_keys[1], 1), 0, 1),
        "qweights": jnp.clip(jnp.exp(math.log(4.0) - 2.7725887 * jax.random.uniform(arg_keys[2], (DATASETS, REFL), jnp.float32) ** levels(arg_keys[2], (DATASETS, REFL), ((0, 32),), -0.2, 0.2)), 0.25, 4.0).astype(jnp.bfloat16),
        "ops": draw_ops(jax.random.fold_in(arg_keys[5], 71), 0),
        "pick": place_ends(jax.random.randint(arg_keys[4], (BLOCKS, BLOCKS), 0, BLK // SUB), jax.random.fold_in(arg_keys[4], 1), 0, (BLK // SUB) - 1).astype(jnp.int32),
    }


def gram(left, right):
    return jnp.dot(left.astype(jnp.float32), right.astype(jnp.float32).T, precision=lax.Precision.HIGHEST, preferred_element_type=jnp.float32)

def reference(intensities, observed, qweights, ops, pick):
    weights = observed.astype(jnp.float32) * qweights.astype(jnp.float32)
    values = intensities.astype(jnp.float32)
    own_w = weights.astype(jnp.bfloat16)
    own_wx = (weights * values).astype(jnp.bfloat16)
    own_wxx = (weights * values * values).astype(jnp.bfloat16)
    blocks = DATASETS // BLK
    source = (jnp.arange(blocks, dtype=jnp.int32) * BLK)[None, :, None] + pick[:, :, None] * SUB + jnp.arange(SUB, dtype=jnp.int32)[None, None, :]
    source = source.reshape(blocks, blocks * SUB)

    def per_block(index):
        rows = source[index]
        part_w = own_w[rows]
        part_x = intensities[rows]
        start = (index * BLK).astype(jnp.int32)
        left_w = lax.dynamic_slice_in_dim(own_w, start, BLK, 0)
        left_wx = lax.dynamic_slice_in_dim(own_wx, start, BLK, 0)
        left_wxx = lax.dynamic_slice_in_dim(own_wxx, start, BLK, 0)
        results = []
        for k in range(NOPS):
            perm = ops[k]
            moved_w = part_w[:, perm]
            wide_w = moved_w.astype(jnp.float32)
            wide_x = part_x[:, perm].astype(jnp.float32)
            moved_wy = (wide_w * wide_x).astype(jnp.bfloat16)
            moved_wyy = (wide_w * wide_x * wide_x).astype(jnp.bfloat16)
            total_w = gram(left_w, moved_w)
            sum_x = gram(left_wx, moved_w)
            sum_xx = gram(left_wxx, moved_w)
            sum_y = gram(left_w, moved_wy)
            sum_xy = gram(left_wx, moved_wy)
            sum_yy = gram(left_w, moved_wyy)
            numer = total_w * sum_xy - sum_x * sum_y
            var_x = jnp.maximum(total_w * sum_xx - sum_x * sum_x, 0.05 * total_w * sum_xx)
            var_y = jnp.maximum(total_w * sum_yy - sum_y * sum_y, 0.05 * total_w * sum_yy)
            results.append(numer / jnp.sqrt(var_x * var_y))
        return jnp.stack(results, 0)
    out = lax.map(per_block, jnp.arange(blocks, dtype=jnp.int32))
    corr = jnp.transpose(out, (1, 0, 2, 3)).reshape(NOPS, DATASETS, blocks * SUB)
    returned = jnp.transpose(corr.reshape(NOPS, blocks, BLK, blocks, SUB), (0, 3, 1, 4, 2))
    return (corr, returned)
```

```python
import functools

import jax
import jax.numpy as jnp
from jax import lax
from jax.experimental import pallas as pl
from jax.experimental.pallas import tpu as pltpu
from jax.sharding import PartitionSpec as P

SUB = 4
NOPS = 4
LANES = 128
SLAB = 2 * SUB
VMEM_LIMIT = 56 * 1024 * 1024


def params():
    return pltpu.CompilerParams(vmem_limit_bytes=VMEM_LIMIT)


def pack_kernel(pick_ref, x_ref, obs_ref, qw_ref, send_ref, w_ref, slabs, sems):
    blk, width = x_ref.shape
    step = min(512, width)

    @pl.loop(0, width // step)
    def _(i):
        cols = pl.ds(pl.multiple_of(i * step, step), step)
        wide_w = obs_ref[:, cols].astype(jnp.float32) * qw_ref[:, cols].astype(jnp.float32)
        wide_x = x_ref[:, cols].astype(jnp.float32)
        w_ref[:, cols] = wide_w.astype(jnp.bfloat16)
        for g in range(blk // SUB):
            rows = slice(g * SUB, (g + 1) * SUB)
            slab = jnp.concatenate([wide_x[rows], wide_w[rows]], 0)
            slabs[g, :, cols] = slab.astype(jnp.bfloat16)

    groups = send_ref.shape[0]

    def copy(d):
        return pltpu.make_async_copy(slabs.at[pick_ref[d]], send_ref.at[d], sems.at[d])

    @pl.loop(0, groups)
    def _(d):
        copy(d).start()

    @pl.loop(0, groups)
    def _(d):
        copy(d).wait()


def pack(pick, intensities, observed, qweights):
    blk, width = intensities.shape
    groups = pick.shape[0]
    whole = pl.BlockSpec(memory_space=pltpu.VMEM)
    return pl.pallas_call(
        pack_kernel,
        out_shape=(
            jax.ShapeDtypeStruct((groups, SLAB, width), jnp.bfloat16),
            jax.ShapeDtypeStruct((blk, width), jnp.bfloat16),
        ),
        in_specs=[pl.BlockSpec(memory_space=pltpu.SMEM), whole, whole, whole],
        out_specs=(pl.BlockSpec(memory_space=pl.ANY), whole),
        scratch_shapes=[
            pltpu.VMEM((blk // SUB, SLAB, width), jnp.bfloat16),
            pltpu.SemaphoreType.DMA((groups,)),
        ],
        compiler_params=params(),
        cost_estimate=pl.CostEstimate(
            flops=blk * width * 4, bytes_accessed=(groups * SLAB * 2 + blk * 10) * width, transcendentals=0
        ),
        name="pack",
    )(pick, intensities, observed, qweights)


def move_kernel(ops_ref, x_ref, w_ref, moved_ref, table, target):
    blk, width = x_ref.shape

    @pl.when(pl.program_id(0) == 0)
    def _():
        @pl.loop(0, width // LANES)
        def _(i):
            cols = pl.ds(pl.multiple_of(i * LANES, LANES), LANES)
            wide_x = x_ref[:, cols].astype(jnp.float32)
            wide_w = w_ref[:, cols].astype(jnp.float32)
            wx = (wide_w * wide_x).astype(jnp.bfloat16).astype(jnp.float32)
            wxx = (wide_w * wide_x * wide_x).astype(jnp.bfloat16).astype(jnp.float32)
            stacked = jnp.concatenate([wide_w, wx, wxx, jnp.zeros((LANES - 3 * blk, LANES), jnp.float32)], 0)
            table[cols, :] = stacked.T

    unroll = 16

    @pl.loop(0, width // unroll)
    def _(i):
        base = pl.multiple_of(i * unroll, unroll)
        for j in range(unroll):
            to = ops_ref[0, 0, base + j]
            target[pl.ds(to, 1), :] = table[pl.ds(base + j, 1), :]

    step = min(512, width)

    @pl.loop(0, width // step)
    def _(i):
        rows = pl.ds(pl.multiple_of(i * step, step), step)
        moved_ref[rows, :] = target[rows, :].astype(jnp.bfloat16)


def move(local_ops, intensities, own_w):
    blk, width = intensities.shape
    whole = pl.BlockSpec(memory_space=pltpu.VMEM)
    return pl.pallas_call(
        move_kernel,
        grid=(NOPS,),
        out_shape=jax.ShapeDtypeStruct((width, NOPS * LANES), jnp.bfloat16),
        in_specs=[
            pl.BlockSpec((1, 1, width), lambda k: (k, 0, 0), memory_space=pltpu.SMEM),
            whole,
            whole,
        ],
        out_specs=pl.BlockSpec((width, LANES), lambda k: (0, k)),
        scratch_shapes=[
            pltpu.VMEM((width, LANES), jnp.float32),
            pltpu.VMEM((width, LANES), jnp.float32),
        ],
        compiler_params=params(),
        cost_estimate=pl.CostEstimate(
            flops=0, bytes_accessed=NOPS * width * LANES * 100, transcendentals=0
        ),
        name="move",
    )(local_ops[:, None, :], intensities, own_w)


def sums_kernel(got_ref, moved_ref, out_ref):
    rows, depth = got_ref.shape
    step = min(512, depth)

    @pl.when(pl.program_id(0) == 0)
    def _():
        out_ref[...] = jnp.zeros_like(out_ref)

    is_x = lax.broadcasted_iota(jnp.int32, (rows // SLAB, SLAB, step), 1) < SUB

    @pl.loop(0, depth // step)
    def _(i):
        cols = pl.ds(pl.multiple_of(i * step, step), step)
        raw = got_ref[:, cols]
        wide = raw.astype(jnp.float32).reshape(rows // SLAB, SLAB, step)
        product = wide * pltpu.roll(wide, SUB, 1)
        second = jnp.where(is_x, product * wide, product)
        second = second.reshape(rows, step).astype(jnp.bfloat16)
        right = moved_ref[cols, :]
        out_ref[0] += jnp.dot(raw, right, preferred_element_type=jnp.float32)
        out_ref[1] += jnp.dot(second, right, preferred_element_type=jnp.float32)


def sums(got, moved):
    rows, width = got.shape
    depth = min(2048, width)
    return pl.pallas_call(
        sums_kernel,
        grid=(width // depth,),
        out_shape=jax.ShapeDtypeStruct((2, rows, moved.shape[1]), jnp.float32),
        in_specs=[
            pl.BlockSpec((rows, depth), lambda i: (0, i)),
            pl.BlockSpec((depth, moved.shape[1]), lambda i: (i, 0)),
        ],
        out_specs=pl.BlockSpec((2, rows, moved.shape[1]), lambda i: (0, 0, 0)),
        compiler_params=params(),
        cost_estimate=pl.CostEstimate(
            flops=4 * rows * width * moved.shape[1],
            bytes_accessed=2 * width * (rows + moved.shape[1]),
            transcendentals=0,
        ),
        name="sums",
    )(got, moved)


def pearson(share, blk):
    first, second = share[0], share[1]
    total_w = first[:, SUB:, :, :blk]
    sum_x = first[:, SUB:, :, blk : 2 * blk]
    sum_xx = first[:, SUB:, :, 2 * blk : 3 * blk]
    sum_y = second[:, SUB:, :, :blk]
    sum_xy = second[:, SUB:, :, blk : 2 * blk]
    sum_yy = second[:, :SUB, :, :blk]
    numer = total_w * sum_xy - sum_x * sum_y
    var_x = jnp.maximum(total_w * sum_xx - sum_x * sum_x, 0.05 * total_w * sum_xx)
    var_y = jnp.maximum(total_w * sum_yy - sum_y * sum_y, 0.05 * total_w * sum_yy)
    return numer / jnp.sqrt(var_x * var_y)


def shards(intensities, observed, qweights, ops, pick):
    blk, width = intensities.shape
    groups = lax.axis_size("dp")
    shares = lax.axis_size("refl")
    local_ops = ops - lax.axis_index("refl") * width
    send, own_w = pack(pick[:, 0], intensities, observed, qweights)
    got = lax.all_to_all(send, "dp", split_axis=0, concat_axis=0, tiled=True)
    moved = move(local_ops, intensities, own_w)
    stats = sums(got.reshape(groups * SLAB, width), moved)
    if shares > 1:
        stats = lax.psum(stats, "refl")
    stats = stats.reshape(2, groups, SLAB, NOPS, LANES)
    full = pearson(stats, blk)
    rows = blk // shares
    if shares > 1:
        full = lax.dynamic_slice_in_dim(full, lax.axis_index("refl") * rows, rows, 3)
    corr = jnp.transpose(full, (2, 3, 0, 1)).reshape(NOPS, rows, groups * SUB)
    back = lax.all_to_all(full, "dp", split_axis=0, concat_axis=0, tiled=True)
    returned = jnp.transpose(back, (2, 0, 1, 3))[:, None]
    return (corr, returned)


def solution(mesh):
    return jax.shard_map(
        shards,
        mesh=mesh,
        in_specs=(
            P("dp", "refl"),
            P("dp", "refl"),
            P("dp", "refl"),
            P(None, "refl"),
            P(None, "dp"),
        ),
        out_specs=(P(None, ("dp", "refl"), None), P(None, "dp", None, None, "refl")),
        check_vma=False,
    )
```

```python
import functools

import jax
import jax.numpy as jnp
from jax import lax
from jax.experimental import pallas as pl
from jax.experimental.pallas import tpu as pltpu
from jax.sharding import PartitionSpec as P

SUB = 4
NOPS = 4
LANES = 128
SLAB = 2 * SUB
VMEM_LIMIT = 56 * 1024 * 1024
PLANES = 4
PLANE = 8
UNROLL = 64


def params():
    return pltpu.CompilerParams(vmem_limit_bytes=VMEM_LIMIT)


def pack_kernel(pick_ref, x_ref, obs_ref, qw_ref, send_ref, w_ref, slabs, sems):
    blk, width = x_ref.shape
    step = min(512, width)

    @pl.loop(0, width // step)
    def _(i):
        cols = pl.ds(pl.multiple_of(i * step, step), step)
        wide_w = obs_ref[:, cols].astype(jnp.float32) * qw_ref[:, cols].astype(jnp.float32)
        wide_x = x_ref[:, cols].astype(jnp.float32)
        w_ref[:, cols] = wide_w.astype(jnp.bfloat16)
        for g in range(blk // SUB):
            rows = slice(g * SUB, (g + 1) * SUB)
            slab = jnp.concatenate([wide_x[rows], wide_w[rows]], 0)
            slabs[g, :, cols] = slab.astype(jnp.bfloat16)

    groups = send_ref.shape[0]

    def copy(d):
        return pltpu.make_async_copy(slabs.at[pick_ref[d]], send_ref.at[d], sems.at[d])

    @pl.loop(0, groups)
    def _(d):
        copy(d).start()

    @pl.loop(0, groups)
    def _(d):
        copy(d).wait()


def pack(pick, intensities, observed, qweights):
    blk, width = intensities.shape
    groups = pick.shape[0]
    whole = pl.BlockSpec(memory_space=pltpu.VMEM)
    return pl.pallas_call(
        pack_kernel,
        out_shape=(
            jax.ShapeDtypeStruct((groups, SLAB, width), jnp.bfloat16),
            jax.ShapeDtypeStruct((blk, width), jnp.bfloat16),
        ),
        in_specs=[pl.BlockSpec(memory_space=pltpu.SMEM), whole, whole, whole],
        out_specs=(pl.BlockSpec(memory_space=pl.ANY), whole),
        scratch_shapes=[
            pltpu.VMEM((blk // SUB, SLAB, width), jnp.bfloat16),
            pltpu.SemaphoreType.DMA((groups,)),
        ],
        compiler_params=params(),
        cost_estimate=pl.CostEstimate(
            flops=blk * width * 4, bytes_accessed=(groups * SLAB * 2 + blk * 10) * width, transcendentals=0
        ),
        name="pack",
    )(pick, intensities, observed, qweights)


def move_kernel(ops_ref, x_ref, w_ref, moved_ref, table, target):
    blk, width = x_ref.shape

    @pl.when(pl.program_id(0) == 0)
    def _():
        @pl.loop(0, width // LANES)
        def _(i):
            cols = pl.ds(pl.multiple_of(i * LANES, LANES), LANES)
            wide_x = x_ref[:, cols].astype(jnp.float32)
            wide_w = w_ref[:, cols].astype(jnp.float32)
            wx = (wide_w * wide_x).astype(jnp.bfloat16).astype(jnp.float32)
            wxx = (wide_w * wide_x * wide_x).astype(jnp.bfloat16).astype(jnp.float32)
            stacked = jnp.concatenate([wide_w, wx, wxx, jnp.zeros((LANES - 3 * blk, LANES), jnp.float32)], 0)
            table[cols, :] = stacked.T

    unroll = 16

    @pl.loop(0, width // unroll)
    def _(i):
        base = pl.multiple_of(i * unroll, unroll)
        for j in range(unroll):
            to = ops_ref[0, 0, base + j]
            target[pl.ds(to, 1), :] = table[pl.ds(base + j, 1), :]

    step = min(512, width)

    @pl.loop(0, width // step)
    def _(i):
        rows = pl.ds(pl.multiple_of(i * step, step), step)
        moved_ref[rows, :] = target[rows, :].astype(jnp.bfloat16)


def move(local_ops, intensities, own_w):
    blk, width = intensities.shape
    whole = pl.BlockSpec(memory_space=pltpu.VMEM)
    return pl.pallas_call(
        move_kernel,
        grid=(NOPS,),
        out_shape=jax.ShapeDtypeStruct((width, NOPS * LANES), jnp.bfloat16),
        in_specs=[
            pl.BlockSpec((1, 1, width), lambda k: (k, 0, 0), memory_space=pltpu.SMEM),
            whole,
            whole,
        ],
        out_specs=pl.BlockSpec((width, LANES), lambda k: (0, k)),
        scratch_shapes=[
            pltpu.VMEM((width, LANES), jnp.float32),
            pltpu.VMEM((width, LANES), jnp.float32),
        ],
        compiler_params=params(),
        cost_estimate=pl.CostEstimate(
            flops=0, bytes_accessed=NOPS * width * LANES * 100, transcendentals=0
        ),
        name="move",
    )(local_ops[:, None, :], intensities, own_w)


def sums_kernel(got_ref, moved_ref, out_ref):
    rows, depth = got_ref.shape
    step = min(512, depth)

    @pl.when(pl.program_id(0) == 0)
    def _():
        out_ref[...] = jnp.zeros_like(out_ref)

    is_x = lax.broadcasted_iota(jnp.int32, (rows // SLAB, SLAB, step), 1) < SUB

    @pl.loop(0, depth // step)
    def _(i):
        cols = pl.ds(pl.multiple_of(i * step, step), step)
        raw = got_ref[:, cols]
        wide = raw.astype(jnp.float32).reshape(rows // SLAB, SLAB, step)
        product = wide * pltpu.roll(wide, SUB, 1)
        second = jnp.where(is_x, product * wide, product)
        second = second.reshape(rows, step).astype(jnp.bfloat16)
        right = moved_ref[cols, :]
        out_ref[0] += jnp.dot(raw, right, preferred_element_type=jnp.float32)
        out_ref[1] += jnp.dot(second, right, preferred_element_type=jnp.float32)


def sums(got, moved):
    rows, width = got.shape
    depth = min(2048, width)
    return pl.pallas_call(
        sums_kernel,
        grid=(width // depth,),
        out_shape=jax.ShapeDtypeStruct((2, rows, moved.shape[1]), jnp.float32),
        in_specs=[
            pl.BlockSpec((rows, depth), lambda i: (0, i)),
            pl.BlockSpec((depth, moved.shape[1]), lambda i: (i, 0)),
        ],
        out_specs=pl.BlockSpec((2, rows, moved.shape[1]), lambda i: (0, 0, 0)),
        compiler_params=params(),
        cost_estimate=pl.CostEstimate(
            flops=4 * rows * width * moved.shape[1],
            bytes_accessed=2 * width * (rows + moved.shape[1]),
            transcendentals=0,
        ),
        name="sums",
    )(got, moved)


def pearson(share, blk):
    first, second = share[0], share[1]
    total_w = first[:, SUB:, :, :blk]
    sum_x = first[:, SUB:, :, blk : 2 * blk]
    sum_xx = first[:, SUB:, :, 2 * blk : 3 * blk]
    sum_y = second[:, SUB:, :, :blk]
    sum_xy = second[:, SUB:, :, blk : 2 * blk]
    sum_yy = second[:, :SUB, :, :blk]
    numer = total_w * sum_xy - sum_x * sum_y
    var_x = jnp.maximum(total_w * sum_xx - sum_x * sum_x, 0.05 * total_w * sum_xx)
    var_y = jnp.maximum(total_w * sum_yy - sum_y * sum_y, 0.05 * total_w * sum_yy)
    return numer / jnp.sqrt(var_x * var_y)


def plane_pack_kernel(pick_ref, x_ref, w_ref, send_ref, slabs, sems):
    blk, width = x_ref.shape
    step = min(512, width)

    @pl.loop(0, width // step)
    def _(i):
        cols = pl.ds(pl.multiple_of(i * step, step), step)
        wide_x = x_ref[:, cols].astype(jnp.float32)
        wide_w = w_ref[:, cols].astype(jnp.float32)
        for g in range(blk // SUB):
            rows = slice(g * SUB, (g + 1) * SUB)
            slab = jnp.concatenate([wide_x[rows], wide_w[rows]], 0)
            slabs[g, :, cols] = slab.astype(jnp.bfloat16)

    me = lax.axis_index("dp")
    mine = lax.div(me, PLANE)
    partner = mine + 1 - 2 * lax.rem(mine, 2)

    def copies(c):
        first = pick_ref[mine * PLANE + c]
        second = pick_ref[partner * PLANE + c]
        return (
            pltpu.make_async_copy(slabs.at[first], send_ref.at[c, 0], sems.at[c, 0]),
            pltpu.make_async_copy(slabs.at[second], send_ref.at[c, 1], sems.at[c, 1]),
        )

    for c in range(PLANE):
        for copy in copies(c):
            copy.start()
    for c in range(PLANE):
        for copy in copies(c):
            copy.wait()


def plane_pack(pick, x, w):
    blk, width = x.shape
    whole = pl.BlockSpec(memory_space=pltpu.VMEM)
    return pl.pallas_call(
        plane_pack_kernel,
        out_shape=jax.ShapeDtypeStruct((PLANE, 2, SLAB, width), jnp.bfloat16),
        in_specs=[pl.BlockSpec(memory_space=pltpu.SMEM), whole, whole],
        out_specs=pl.BlockSpec(memory_space=pl.ANY),
        scratch_shapes=[
            pltpu.VMEM((blk // SUB, SLAB, width), jnp.bfloat16),
            pltpu.SemaphoreType.DMA((PLANE, 2)),
        ],
        compiler_params=params(),
        cost_estimate=pl.CostEstimate(
            flops=blk * width * 4, bytes_accessed=(PLANE * 2 * SLAB * 2 + blk * 4) * width, transcendentals=0
        ),
        name="plane_pack",
    )(pick, x, w)


def table_kernel(x_ref, x1_ref, w_ref, w1_ref, table_ref):
    width = x_ref.shape[1]

    @pl.loop(0, width // LANES)
    def _(i):
        cols = pl.ds(pl.multiple_of(i * LANES, LANES), LANES)
        parts = [ref[:, cols].astype(jnp.float32) for ref in (x_ref, x1_ref, w_ref, w1_ref)]
        table_ref[cols, :] = jnp.concatenate(parts, 0).T


def make_table(x, x1, w, w1):
    blk, width = x.shape
    step = min(2048, width)
    spec = pl.BlockSpec((blk, step), lambda i: (0, i))
    return pl.pallas_call(
        table_kernel,
        grid=(width // step,),
        out_shape=jax.ShapeDtypeStruct((width, LANES), jnp.float32),
        in_specs=[spec] * 4,
        out_specs=pl.BlockSpec((step, LANES), lambda i: (i, 0)),
        compiler_params=params(),
        cost_estimate=pl.CostEstimate(flops=0, bytes_accessed=width * LANES * 8, transcendentals=0),
        name="table",
    )(x, x1, w, w1)


def place_kernel(ops_ref, table_ref, after_ref, moved_ref, target):
    depth = table_ref.shape[0]
    width = target.shape[0]

    @pl.loop(0, depth // UNROLL)
    def _(i):
        base = pl.multiple_of(i * UNROLL, UNROLL)
        for j in range(UNROLL):
            to = ops_ref[0, 0, base + j]
            target[pl.ds(to, 1), :] = table_ref[pl.ds(base + j, 1), :]

    @pl.when(pl.program_id(1) == pl.num_programs(1) - 1)
    def _():
        step = min(512, width)

        @pl.loop(0, width // step)
        def _(i):
            rows = pl.ds(pl.multiple_of(i * step, step), step)
            moved_ref[rows, :] = target[rows, :].astype(jnp.bfloat16)


def place(ops, table, after):
    count = ops.shape[0]
    width = table.shape[0]
    depth = min(2048, width)
    return pl.pallas_call(
        place_kernel,
        grid=(count, width // depth),
        out_shape=jax.ShapeDtypeStruct((width, count * LANES), jnp.bfloat16),
        in_specs=[
            pl.BlockSpec((1, 1, depth), lambda k, i: (k, 0, i), memory_space=pltpu.SMEM),
            pl.BlockSpec((depth, LANES), lambda k, i: (i, 0)),
            pl.BlockSpec(memory_space=pl.ANY),
        ],
        out_specs=pl.BlockSpec((width, LANES), lambda k, i: (0, k)),
        scratch_shapes=[pltpu.VMEM((width, LANES), jnp.float32)],
        compiler_params=params(),
        cost_estimate=pl.CostEstimate(
            flops=0, bytes_accessed=count * width * LANES * 64, transcendentals=0
        ),
        name="place",
    )(ops[:, None, :], table, after)


def plane_sums_kernel(own_ref, far_ref, first_ref, second_ref, out_ref):
    rows, depth = own_ref.shape
    step = min(512, depth)
    half = LANES // 2

    @pl.when(pl.program_id(0) == 0)
    def _():
        out_ref[...] = jnp.zeros_like(out_ref)

    is_x = lax.broadcasted_iota(jnp.int32, (rows // SLAB, SLAB, step), 1) < SUB
    low = lax.broadcasted_iota(jnp.int32, (step, LANES), 1) < half

    @pl.loop(0, depth // step)
    def _(i):
        cols = pl.ds(pl.multiple_of(i * step, step), step)
        raws, products = [], []
        for ref in (own_ref, far_ref):
            raw = ref[:, cols]
            wide = raw.astype(jnp.float32).reshape(rows // SLAB, SLAB, step)
            product = wide * pltpu.roll(wide, SUB, 1)
            both = jnp.where(is_x, product * wide, product)
            raws.append(raw)
            products.append(both.reshape(rows, step).astype(jnp.bfloat16))
        linear, square = [], []
        for ref in (first_ref, second_ref):
            even, odd = None, None
            for k in range(2):
                values = ref[cols, k * LANES : (k + 1) * LANES].astype(jnp.float32)
                swapped = pltpu.roll(values, half, 1)
                product = values * swapped
                linear.append(jnp.where(low, product, values).astype(jnp.bfloat16))
                if k == 0:
                    even = product * values
                else:
                    odd = product * swapped
            square.append(jnp.where(low, even, odd).astype(jnp.bfloat16))
        right = jnp.concatenate(linear + square, 1)
        out_ref[0] += jnp.dot(jnp.concatenate(raws, 0), right, preferred_element_type=jnp.float32)
        out_ref[1] += jnp.dot(jnp.concatenate(products, 0), right, preferred_element_type=jnp.float32)


def plane_sums(own, far, first, second):
    rows, width = own.shape
    depth = min(2048, width)
    lanes = (NOPS + NOPS // 2) * LANES
    part = pl.BlockSpec((rows, depth), lambda i: (0, i))
    moved = pl.BlockSpec((depth, 2 * LANES), lambda i: (i, 0))
    return pl.pallas_call(
        plane_sums_kernel,
        grid=(width // depth,),
        out_shape=jax.ShapeDtypeStruct((2, 2 * rows, lanes), jnp.float32),
        in_specs=[part, part, moved, moved],
        out_specs=pl.BlockSpec((2, 2 * rows, lanes), lambda i: (0, 0, 0)),
        compiler_params=params(),
        cost_estimate=pl.CostEstimate(
            flops=8 * rows * width * lanes,
            bytes_accessed=width * (4 * rows + 8 * LANES),
            transcendentals=0,
        ),
        name="plane_sums",
    )(own, far, first, second)


def ratio(total_w, sum_x, sum_xx, sum_y, sum_xy, sum_yy):
    numer = total_w * sum_xy - sum_x * sum_y
    var_x = jnp.maximum(total_w * sum_xx - sum_x * sum_x, 0.05 * total_w * sum_xx)
    var_y = jnp.maximum(total_w * sum_yy - sum_y * sum_y, 0.05 * total_w * sum_yy)
    return numer / jnp.sqrt(var_x * var_y)


def plane_pearson(stats, blk, which):
    stats = stats.reshape(2, 2, PLANE, 2, SLAB, -1)[:, :, :, which]
    lead = (2, PLANE, SUB)
    straight = NOPS * LANES

    def linear(part, rows, offset):
        picked = part[:, :, rows, :straight].reshape(*lead, NOPS, 4, blk)
        return picked[:, :, :, :, offset + which]

    total_w = linear(stats[0], slice(SUB, None), 2)
    sum_x = linear(stats[0], slice(SUB, None), 0)
    sum_y = linear(stats[1], slice(SUB, None), 2)
    sum_xy = linear(stats[1], slice(SUB, None), 0)
    sum_yy = linear(stats[1], slice(None, SUB), 2)
    sum_xx = stats[0][:, :, SUB:, straight:].reshape(*lead, NOPS, 2, blk)[:, :, :, :, which]
    return ratio(total_w, sum_x, sum_xx, sum_y, sum_xy, sum_yy)


def shards_by_plane(intensities, observed, qweights, ops, pick):
    blk, width = intensities.shape
    groups = PLANES * PLANE
    near = [(i, i ^ PLANE) for i in range(groups)]
    far = [(i, i ^ (2 * PLANE)) for i in range(groups)]
    rings = [[z * PLANE + c for c in range(PLANE)] for z in range(PLANES)]
    plane = lax.axis_index("dp") // PLANE
    odd, upper = plane % 2 == 1, plane >= 2

    def spread(send):
        got = lax.all_to_all(send, "dp", split_axis=0, concat_axis=0, axis_index_groups=rings, tiled=True)
        return got.reshape(PLANE * 2 * SLAB, width)

    own_pick = pick[:, 0]
    own_w = (observed.astype(jnp.float32) * qweights.astype(jnp.float32)).astype(jnp.bfloat16)
    near_x = lax.ppermute(intensities, "dp", near)
    near_w = lax.ppermute(own_w, "dp", near)
    far_pick = lax.ppermute(own_pick, "dp", far)
    own_got = spread(plane_pack(own_pick, intensities, own_w))
    later_x, later_w, near_x, near_w = lax.optimization_barrier((intensities, own_w, near_x, near_w))
    far_x = lax.ppermute(later_x, "dp", far)
    far_w = lax.ppermute(later_w, "dp", far)
    table = make_table(intensities, near_x, own_w, near_w)
    first = place(ops[:2], table, own_pick)
    far_send = plane_pack(far_pick, far_x, far_w)
    far_got = spread(far_send)
    second = place(ops[2:], table, far_send)
    stats = plane_sums(own_got, far_got, first, second)
    mine = plane_pearson(stats, blk, 0)
    other = plane_pearson(stats, blk, 1)

    from_near = lax.ppermute(other, "dp", near)
    pair = jnp.stack([mine, from_near], 1)
    pair = jnp.where(odd, pair[:, ::-1], pair)
    pair = jnp.where(upper, pair[::-1], pair)
    corr = jnp.transpose(pair.reshape(groups, SUB, NOPS, blk), (2, 3, 0, 1)).reshape(NOPS, blk, groups * SUB)

    both = jnp.stack([mine, other], 2)
    both = jnp.where(upper, both[::-1], both)
    back = jnp.repeat(both, 2, 0).reshape(groups, 2, SUB, NOPS, blk)
    back = lax.all_to_all(back, "dp", split_axis=0, concat_axis=0, tiled=True)
    back = back.reshape(2, 2, PLANE, 2, SUB, NOPS, blk)
    back = jnp.where(odd, back[:, 1, :, ::-1], back[:, 0])
    returned = jnp.transpose(back, (4, 0, 2, 1, 3, 5)).reshape(NOPS, 1, groups, SUB, blk)
    return (corr, returned)


def shards(intensities, observed, qweights, ops, pick):
    if lax.axis_size("dp") == PLANES * PLANE and lax.axis_size("refl") == 1:
        return shards_by_plane(intensities, observed, qweights, ops, pick)
    return shards_direct(intensities, observed, qweights, ops, pick)


def shards_direct(intensities, observed, qweights, ops, pick):
    blk, width = intensities.shape
    groups = lax.axis_size("dp")
    shares = lax.axis_size("refl")
    local_ops = ops - lax.axis_index("refl") * width
    send, own_w = pack(pick[:, 0], intensities, observed, qweights)
    got = lax.all_to_all(send, "dp", split_axis=0, concat_axis=0, tiled=True)
    moved = move(local_ops, intensities, own_w)
    stats = sums(got.reshape(groups * SLAB, width), moved)
    if shares > 1:
        stats = lax.psum(stats, "refl")
    stats = stats.reshape(2, groups, SLAB, NOPS, LANES)
    full = pearson(stats, blk)
    rows = blk // shares
    if shares > 1:
        full = lax.dynamic_slice_in_dim(full, lax.axis_index("refl") * rows, rows, 3)
    corr = jnp.transpose(full, (2, 3, 0, 1)).reshape(NOPS, rows, groups * SUB)
    back = lax.all_to_all(full, "dp", split_axis=0, concat_axis=0, tiled=True)
    returned = jnp.transpose(back, (2, 0, 1, 3))[:, None]
    return (corr, returned)


def solution(mesh):
    return jax.shard_map(
        shards,
        mesh=mesh,
        in_specs=(
            P("dp", "refl"),
            P("dp", "refl"),
            P("dp", "refl"),
            P(None, "refl"),
            P(None, "dp"),
        ),
        out_specs=(P(None, ("dp", "refl"), None), P(None, "dp", None, None, "refl")),
        check_vma=False,
    )
```

```python
import functools

import jax
import jax.numpy as jnp
from jax import lax
from jax.experimental import pallas as pl
from jax.experimental.pallas import tpu as pltpu
from jax.sharding import PartitionSpec as P

SUB = 4
NOPS = 4
LANES = 128
SLAB = 2 * SUB
VMEM_LIMIT = 56 * 1024 * 1024
PLANES = 4
PLANE = 8
UNROLL = 64


def params():
    return pltpu.CompilerParams(vmem_limit_bytes=VMEM_LIMIT)


def pack_kernel(pick_ref, x_ref, obs_ref, qw_ref, send_ref, w_ref, slabs, sems):
    blk, width = x_ref.shape
    step = min(512, width)

    @pl.loop(0, width // step)
    def _(i):
        cols = pl.ds(pl.multiple_of(i * step, step), step)
        wide_w = obs_ref[:, cols].astype(jnp.float32) * qw_ref[:, cols].astype(jnp.float32)
        wide_x = x_ref[:, cols].astype(jnp.float32)
        w_ref[:, cols] = wide_w.astype(jnp.bfloat16)
        for g in range(blk // SUB):
            rows = slice(g * SUB, (g + 1) * SUB)
            slab = jnp.concatenate([wide_x[rows], wide_w[rows]], 0)
            slabs[g, :, cols] = slab.astype(jnp.bfloat16)

    groups = send_ref.shape[0]

    def copy(d):
        return pltpu.make_async_copy(slabs.at[pick_ref[d]], send_ref.at[d], sems.at[d])

    @pl.loop(0, groups)
    def _(d):
        copy(d).start()

    @pl.loop(0, groups)
    def _(d):
        copy(d).wait()


def pack(pick, intensities, observed, qweights):
    blk, width = intensities.shape
    groups = pick.shape[0]
    whole = pl.BlockSpec(memory_space=pltpu.VMEM)
    return pl.pallas_call(
        pack_kernel,
        out_shape=(
            jax.ShapeDtypeStruct((groups, SLAB, width), jnp.bfloat16),
            jax.ShapeDtypeStruct((blk, width), jnp.bfloat16),
        ),
        in_specs=[pl.BlockSpec(memory_space=pltpu.SMEM), whole, whole, whole],
        out_specs=(pl.BlockSpec(memory_space=pl.ANY), whole),
        scratch_shapes=[
            pltpu.VMEM((blk // SUB, SLAB, width), jnp.bfloat16),
            pltpu.SemaphoreType.DMA((groups,)),
        ],
        compiler_params=params(),
        cost_estimate=pl.CostEstimate(
            flops=blk * width * 4, bytes_accessed=(groups * SLAB * 2 + blk * 10) * width, transcendentals=0
        ),
        name="pack",
    )(pick, intensities, observed, qweights)


def move_kernel(ops_ref, x_ref, w_ref, moved_ref, table, target):
    blk, width = x_ref.shape

    @pl.when(pl.program_id(0) == 0)
    def _():
        @pl.loop(0, width // LANES)
        def _(i):
            cols = pl.ds(pl.multiple_of(i * LANES, LANES), LANES)
            wide_x = x_ref[:, cols].astype(jnp.float32)
            wide_w = w_ref[:, cols].astype(jnp.float32)
            wx = (wide_w * wide_x).astype(jnp.bfloat16).astype(jnp.float32)
            wxx = (wide_w * wide_x * wide_x).astype(jnp.bfloat16).astype(jnp.float32)
            stacked = jnp.concatenate([wide_w, wx, wxx, jnp.zeros((LANES - 3 * blk, LANES), jnp.float32)], 0)
            table[cols, :] = stacked.T

    unroll = 16

    @pl.loop(0, width // unroll)
    def _(i):
        base = pl.multiple_of(i * unroll, unroll)
        for j in range(unroll):
            to = ops_ref[0, 0, base + j]
            target[pl.ds(to, 1), :] = table[pl.ds(base + j, 1), :]

    step = min(512, width)

    @pl.loop(0, width // step)
    def _(i):
        rows = pl.ds(pl.multiple_of(i * step, step), step)
        moved_ref[rows, :] = target[rows, :].astype(jnp.bfloat16)


def move(local_ops, intensities, own_w):
    blk, width = intensities.shape
    whole = pl.BlockSpec(memory_space=pltpu.VMEM)
    return pl.pallas_call(
        move_kernel,
        grid=(NOPS,),
        out_shape=jax.ShapeDtypeStruct((width, NOPS * LANES), jnp.bfloat16),
        in_specs=[
            pl.BlockSpec((1, 1, width), lambda k: (k, 0, 0), memory_space=pltpu.SMEM),
            whole,
            whole,
        ],
        out_specs=pl.BlockSpec((width, LANES), lambda k: (0, k)),
        scratch_shapes=[
            pltpu.VMEM((width, LANES), jnp.float32),
            pltpu.VMEM((width, LANES), jnp.float32),
        ],
        compiler_params=params(),
        cost_estimate=pl.CostEstimate(
            flops=0, bytes_accessed=NOPS * width * LANES * 100, transcendentals=0
        ),
        name="move",
    )(local_ops[:, None, :], intensities, own_w)


def sums_kernel(got_ref, moved_ref, out_ref):
    rows, depth = got_ref.shape
    step = min(512, depth)

    @pl.when(pl.program_id(0) == 0)
    def _():
        out_ref[...] = jnp.zeros_like(out_ref)

    is_x = lax.broadcasted_iota(jnp.int32, (rows // SLAB, SLAB, step), 1) < SUB

    @pl.loop(0, depth // step)
    def _(i):
        cols = pl.ds(pl.multiple_of(i * step, step), step)
        raw = got_ref[:, cols]
        wide = raw.astype(jnp.float32).reshape(rows // SLAB, SLAB, step)
        product = wide * pltpu.roll(wide, SUB, 1)
        second = jnp.where(is_x, product * wide, product)
        second = second.reshape(rows, step).astype(jnp.bfloat16)
        right = moved_ref[cols, :]
        out_ref[0] += jnp.dot(raw, right, preferred_element_type=jnp.float32)
        out_ref[1] += jnp.dot(second, right, preferred_element_type=jnp.float32)


def sums(got, moved):
    rows, width = got.shape
    depth = min(2048, width)
    return pl.pallas_call(
        sums_kernel,
        grid=(width // depth,),
        out_shape=jax.ShapeDtypeStruct((2, rows, moved.shape[1]), jnp.float32),
        in_specs=[
            pl.BlockSpec((rows, depth), lambda i: (0, i)),
            pl.BlockSpec((depth, moved.shape[1]), lambda i: (i, 0)),
        ],
        out_specs=pl.BlockSpec((2, rows, moved.shape[1]), lambda i: (0, 0, 0)),
        compiler_params=params(),
        cost_estimate=pl.CostEstimate(
            flops=4 * rows * width * moved.shape[1],
            bytes_accessed=2 * width * (rows + moved.shape[1]),
            transcendentals=0,
        ),
        name="sums",
    )(got, moved)


def pearson(share, blk):
    first, second = share[0], share[1]
    total_w = first[:, SUB:, :, :blk]
    sum_x = first[:, SUB:, :, blk : 2 * blk]
    sum_xx = first[:, SUB:, :, 2 * blk : 3 * blk]
    sum_y = second[:, SUB:, :, :blk]
    sum_xy = second[:, SUB:, :, blk : 2 * blk]
    sum_yy = second[:, :SUB, :, :blk]
    numer = total_w * sum_xy - sum_x * sum_y
    var_x = jnp.maximum(total_w * sum_xx - sum_x * sum_x, 0.05 * total_w * sum_xx)
    var_y = jnp.maximum(total_w * sum_yy - sum_y * sum_y, 0.05 * total_w * sum_yy)
    return numer / jnp.sqrt(var_x * var_y)


def fill_slabs(slabs, x_ref, w_ref):
    blk, width = x_ref.shape
    step = min(512, width)

    @pl.loop(0, width // step)
    def _(i):
        cols = pl.ds(pl.multiple_of(i * step, step), step)
        wide_x = x_ref[:, cols].astype(jnp.float32)
        wide_w = w_ref[:, cols].astype(jnp.float32)
        for g in range(blk // SUB):
            rows = slice(g * SUB, (g + 1) * SUB)
            slab = jnp.concatenate([wide_x[rows], wide_w[rows]], 0)
            slabs[g, :, cols] = slab.astype(jnp.bfloat16)


def send_slabs(slabs, pick_ref, send_ref, sems):
    mine = lax.div(lax.axis_index("dp"), PLANE)
    partner = mine + 1 - 2 * lax.rem(mine, 2)
    copies = []
    for c in range(PLANE):
        for t, plane in enumerate((mine, partner)):
            group = pick_ref[plane * PLANE + c]
            copies.append(pltpu.make_async_copy(slabs.at[group], send_ref.at[c, t], sems.at[c, t]))
    for copy in copies:
        copy.start()
    for copy in copies:
        copy.wait()


def own_pack_kernel(pick_ref, x_ref, w_ref, send_ref, slabs, sems):
    fill_slabs(slabs, x_ref, w_ref)
    send_slabs(slabs, pick_ref, send_ref, sems)


def far_pack_kernel(pick_ref, xo_ref, wo_ref, xi_ref, wi_ref, after_ref, send_ref, x_buf, w_buf, slabs, sems, in_sems):
    plane = lax.div(lax.axis_index("dp"), PLANE)
    inner = (plane == 1) | (plane == 2)

    def fetch(x_ref, w_ref):
        copies = (
            pltpu.make_async_copy(x_ref, x_buf, in_sems.at[0]),
            pltpu.make_async_copy(w_ref, w_buf, in_sems.at[1]),
        )
        for copy in copies:
            copy.start()
        for copy in copies:
            copy.wait()

    @pl.when(inner)
    def _():
        fetch(xi_ref, wi_ref)

    @pl.when(jnp.logical_not(inner))
    def _():
        fetch(xo_ref, wo_ref)

    fill_slabs(slabs, x_buf, w_buf)
    send_slabs(slabs, pick_ref, send_ref, sems)


def pack_call(kernel, name, specs, scratch, blk, width, *operands):
    return pl.pallas_call(
        kernel,
        out_shape=jax.ShapeDtypeStruct((PLANE, 2, SLAB, width), jnp.bfloat16),
        in_specs=[pl.BlockSpec(memory_space=pltpu.SMEM)] + specs,
        out_specs=pl.BlockSpec(memory_space=pl.ANY),
        scratch_shapes=scratch
        + [pltpu.VMEM((blk // SUB, SLAB, width), jnp.bfloat16), pltpu.SemaphoreType.DMA((PLANE, 2))],
        compiler_params=params(),
        cost_estimate=pl.CostEstimate(
            flops=blk * width * 4, bytes_accessed=(PLANE * 2 * SLAB * 2 + blk * 4) * width, transcendentals=0
        ),
        name=name,
    )(*operands)


def own_pack(pick, x, w):
    specs = [pl.BlockSpec(memory_space=pltpu.VMEM)] * 2
    return pack_call(own_pack_kernel, "own_pack", specs, [], *x.shape, pick, x, w)


def far_pack(pick, x_outer, w_outer, x_inner, w_inner, after):
    blk, width = x_outer.shape
    buf = pltpu.VMEM((blk, width), jnp.bfloat16)

    def kernel(pick_ref, xo, wo, xi, wi, after_ref, send_ref, x_buf, w_buf, in_sems, slabs, sems):
        far_pack_kernel(pick_ref, xo, wo, xi, wi, after_ref, send_ref, x_buf, w_buf, slabs, sems, in_sems)

    return pack_call(
        kernel, "far_pack", [pl.BlockSpec(memory_space=pl.ANY)] * 5,
        [buf, buf, pltpu.SemaphoreType.DMA((2,))], blk, width,
        pick, x_outer, w_outer, x_inner, w_inner, after,
    )


def place_kernel(ops_ref, x_ref, x1_ref, w_ref, w1_ref, after_ref, moved_ref, table, target):
    depth = x_ref.shape[1]
    width = target.shape[0]
    part = pl.multiple_of(pl.program_id(1) * depth, depth)

    @pl.when(pl.program_id(0) == 0)
    def _():
        step = min(256, depth)
        diagonal = lax.broadcasted_iota(jnp.int32, (step, step), 0) == lax.broadcasted_iota(
            jnp.int32, (step, step), 1
        )
        identity = jnp.where(diagonal, 1.0, 0.0).astype(jnp.bfloat16)
        for i in range(depth // step):
            cols = slice(i * step, (i + 1) * step)
            rows = jnp.concatenate([x_ref[:, cols], x1_ref[:, cols], w_ref[:, cols], w1_ref[:, cols]], 0)
            table[pl.ds(part + i * step, step), :] = lax.dot_general(
                identity, rows, (((1,), (1,)), ((), ())), preferred_element_type=jnp.float32
            )

    @pl.loop(0, depth // UNROLL)
    def _(i):
        base = pl.multiple_of(i * UNROLL, UNROLL)
        row = pl.multiple_of(part + base, UNROLL)
        for j in range(UNROLL):
            to = ops_ref[0, 0, base + j]
            target[pl.ds(to, 1), :] = table[pl.ds(row + j, 1), :]

    @pl.when(pl.program_id(1) == pl.num_programs(1) - 1)
    def _():
        step = min(512, width)

        @pl.loop(0, width // step)
        def _(i):
            rows = pl.ds(pl.multiple_of(i * step, step), step)
            moved_ref[rows, :] = target[rows, :].astype(jnp.bfloat16)


def place(ops, x, x1, w, w1, after):
    count = ops.shape[0]
    blk, width = x.shape
    depth = min(2048, width)
    last = width // depth - 1
    part = pl.BlockSpec((blk, depth), lambda k, i: (0, jnp.where(k == 0, i, last)))
    return pl.pallas_call(
        place_kernel,
        grid=(count, width // depth),
        out_shape=jax.ShapeDtypeStruct((width, count * LANES), jnp.bfloat16),
        in_specs=[
            pl.BlockSpec((1, 1, depth), lambda k, i: (k, 0, i), memory_space=pltpu.SMEM),
            part,
            part,
            part,
            part,
            pl.BlockSpec(memory_space=pl.ANY),
        ],
        out_specs=pl.BlockSpec((width, LANES), lambda k, i: (0, k)),
        scratch_shapes=[pltpu.VMEM((width, LANES), jnp.float32)] * 2,
        compiler_params=params(),
        cost_estimate=pl.CostEstimate(
            flops=0, bytes_accessed=count * width * LANES * 64, transcendentals=0
        ),
        name="place",
    )(ops[:, None, :], x, x1, w, w1, after)


def ratio(total_w, sum_x, sum_xx, sum_y, sum_xy, sum_yy):
    numer = total_w * sum_xy - sum_x * sum_y
    var_x = jnp.maximum(total_w * sum_xx - sum_x * sum_x, 0.05 * total_w * sum_xx)
    var_y = jnp.maximum(total_w * sum_yy - sum_y * sum_y, 0.05 * total_w * sum_yy)
    return numer / jnp.sqrt(var_x * var_y)


def plane_sums_kernel(own_ref, far_ref, first_ref, second_ref, out_ref, acc):
    rows, depth = own_ref.shape
    step = min(1024, depth)
    half = LANES // 2
    slabs = rows // SLAB
    blk = half // 2

    @pl.when(pl.program_id(0) == 0)
    def _():
        acc[...] = jnp.zeros_like(acc)

    @pl.loop(0, depth // step)
    def _(i):
        cols = pl.ds(pl.multiple_of(i * step, step), step)
        is_x = lax.broadcasted_iota(jnp.int32, (slabs, SLAB, step), 1) < SUB
        weights, products = [], []
        for ref in (own_ref, far_ref):
            wide = ref[:, cols].astype(jnp.float32).reshape(slabs, SLAB, step)
            rolled = pltpu.roll(wide, SUB, 1)
            product = wide * rolled
            both = jnp.where(is_x, product * wide, product)
            products.append(both.reshape(rows, step).astype(jnp.bfloat16))
            mine = rolled.reshape(slabs // 2, 2, SLAB, step)[:, 0]
            partner = wide.reshape(slabs // 2, 2, SLAB, step)[:, 1]
            pair = jnp.where(is_x[: slabs // 2], mine, partner)
            weights.append(pair.reshape(rows // 2, step).astype(jnp.bfloat16))
        low = lax.broadcasted_iota(jnp.int32, (step, LANES), 1) < half
        linear, square = [], []
        for ref in (first_ref, second_ref):
            even, odd = None, None
            for k in range(2):
                values = ref[cols, k * LANES : (k + 1) * LANES].astype(jnp.float32)
                swapped = pltpu.roll(values, half, 1)
                product = values * swapped
                linear.append(jnp.where(low, product, values).astype(jnp.bfloat16))
                if k == 0:
                    even = product * values
                else:
                    odd = product * swapped
            square.append(jnp.where(low, even, odd).astype(jnp.bfloat16))
        left = jnp.concatenate(weights + products, 0)
        right = jnp.concatenate(linear + square, 1)
        acc[...] += jnp.dot(left, right, preferred_element_type=jnp.float32)

    @pl.when(pl.program_id(0) == pl.num_programs(0) - 1)
    def _():
        tiles = slabs
        top = lax.broadcasted_iota(jnp.int32, (tiles, SLAB, LANES), 1) < SUB
        lane = lax.broadcasted_iota(jnp.int32, (tiles * SLAB, LANES), 1)
        result = jnp.zeros((tiles * SLAB, LANES), jnp.float32)
        for k in range(NOPS):
            lanes = slice(k * LANES, (k + 1) * LANES)
            squares = slice((NOPS + k // 2) * LANES, (NOPS + k // 2 + 1) * LANES)
            with_w = acc[:rows, lanes]
            with_y = acc[rows:, lanes].reshape(tiles, 2, SLAB, LANES)
            mine, partner = with_y[:, 0], with_y[:, 1]
            y = jnp.where(top, pltpu.roll(mine, SUB, 1), partner).reshape(tiles * SLAB, LANES)
            yy = jnp.where(top, mine, pltpu.roll(partner, SUB, 1)).reshape(tiles * SLAB, LANES)
            sum_xx = acc[:rows, squares]
            if k % 2 == 1:
                sum_xx = pltpu.roll(sum_xx, half, 1)
            both = ratio(
                pltpu.roll(with_w, half, 1), with_w, sum_xx, pltpu.roll(y, half, 1), y, pltpu.roll(yy, half, 1)
            )
            both = jnp.where(
                top.reshape(tiles * SLAB, LANES), both, pltpu.roll(both, LANES - blk, 1)
            )
            moved = both if k == 0 else pltpu.roll(both, k * blk, 1)
            result = jnp.where((lane >= k * blk) & (lane < (k + 1) * blk), moved, result)
        out_ref[...] = result


def plane_sums(own, far, first, second):
    rows, width = own.shape
    depth = min(2048, width)
    lanes = (NOPS + NOPS // 2) * LANES
    part = pl.BlockSpec((rows, depth), lambda i: (0, i))
    moved = pl.BlockSpec((depth, 2 * LANES), lambda i: (i, 0))
    return pl.pallas_call(
        plane_sums_kernel,
        grid=(width // depth,),
        out_shape=jax.ShapeDtypeStruct((rows, LANES), jnp.float32),
        in_specs=[part, part, moved, moved],
        out_specs=pl.BlockSpec((rows, LANES), lambda i: (0, 0)),
        scratch_shapes=[pltpu.VMEM((3 * rows, lanes), jnp.float32)],
        compiler_params=params(),
        cost_estimate=pl.CostEstimate(
            flops=6 * rows * width * lanes,
            bytes_accessed=width * (4 * rows + 8 * LANES),
            transcendentals=0,
        ),
        name="plane_sums",
    )(own, far, first, second)


def shards_by_plane(intensities, observed, qweights, ops, pick):
    blk, width = intensities.shape
    groups = PLANES * PLANE
    near = [(i, i ^ PLANE) for i in range(groups)]
    far = [(i, i ^ (2 * PLANE)) for i in range(groups)]
    middle = [(i, 3 * PLANE + 2 * (i % PLANE) - i) for i in range(PLANE, 3 * PLANE)]
    outward = [(i, i - PLANE if i < 2 * PLANE else i + PLANE) for i in range(PLANE, 3 * PLANE)]
    rings = [[z * PLANE + c for c in range(PLANE)] for z in range(PLANES)]
    plane = lax.axis_index("dp") // PLANE
    odd, upper = plane % 2 == 1, plane >= 2

    def spread(send):
        got = lax.all_to_all(send, "dp", split_axis=0, concat_axis=0, axis_index_groups=rings, tiled=True)
        return got.reshape(PLANE * 2 * SLAB, width)

    own_pick = pick[:, 0]
    near_x = lax.ppermute(intensities, "dp", near)
    mid_x = lax.ppermute(intensities, "dp", middle)
    far_pick = lax.ppermute(own_pick, "dp", far)
    own_w = (observed.astype(jnp.float32) * qweights.astype(jnp.float32)).astype(jnp.bfloat16)
    near_w = lax.ppermute(own_w, "dp", near)
    mid_w = lax.ppermute(own_w, "dp", middle)
    own_got = spread(own_pack(own_pick, intensities, own_w))
    near_x, mid_x, near_w, mid_w, far_pick = lax.optimization_barrier((near_x, mid_x, near_w, mid_w, far_pick))
    outer_x = lax.ppermute(mid_x, "dp", outward)
    inner_x = lax.ppermute(near_x, "dp", middle)
    outer_w = lax.ppermute(mid_w, "dp", outward)
    inner_w = lax.ppermute(near_w, "dp", middle)
    first = place(ops[:2], intensities, near_x, own_w, near_w, own_pick)
    far_send = far_pack(far_pick, outer_x, outer_w, inner_x, inner_w, first)
    far_got = spread(far_send)
    second = place(ops[2:], intensities, near_x, own_w, near_w, far_send)
    stats = plane_sums(own_got, far_got, first, second)
    stats = stats.reshape(2, PLANE, 2, SUB, NOPS * blk)
    mine, other = stats[:, :, 0], stats[:, :, 1]

    from_near = lax.ppermute(other, "dp", near)
    pair = jnp.stack([mine, from_near], 1)
    pair = jnp.where(odd, pair[:, ::-1], pair)
    pair = jnp.where(upper, pair[::-1], pair)
    corr = pair.reshape(groups * SUB, NOPS * blk).T.reshape(NOPS, blk, groups * SUB)

    both = jnp.where(upper, stats[::-1], stats).reshape(2, 1, PLANE, 2 * SUB, NOPS * blk)
    back = jnp.broadcast_to(both, (2, 2, PLANE, 2 * SUB, NOPS * blk)).reshape(groups, 2 * SUB, NOPS * blk)
    back = lax.all_to_all(back, "dp", split_axis=0, concat_axis=0, tiled=True)
    back = back.reshape(2, 2, PLANE, 2, SUB, NOPS, blk)
    back = jnp.where(odd, back[:, 1, :, ::-1], back[:, 0])
    returned = jnp.transpose(back, (4, 0, 2, 1, 3, 5)).reshape(NOPS, 1, groups, SUB, blk)
    return (corr, returned)


def shards(intensities, observed, qweights, ops, pick):
    if lax.axis_size("dp") == PLANES * PLANE and lax.axis_size("refl") == 1:
        return shards_by_plane(intensities, observed, qweights, ops, pick)
    return shards_direct(intensities, observed, qweights, ops, pick)


def shards_direct(intensities, observed, qweights, ops, pick):
    blk, width = intensities.shape
    groups = lax.axis_size("dp")
    shares = lax.axis_size("refl")
    local_ops = ops - lax.axis_index("refl") * width
    send, own_w = pack(pick[:, 0], intensities, observed, qweights)
    got = lax.all_to_all(send, "dp", split_axis=0, concat_axis=0, tiled=True)
    moved = move(local_ops, intensities, own_w)
    stats = sums(got.reshape(groups * SLAB, width), moved)
    if shares > 1:
        stats = lax.psum(stats, "refl")
    stats = stats.reshape(2, groups, SLAB, NOPS, LANES)
    full = pearson(stats, blk)
    rows = blk // shares
    if shares > 1:
        full = lax.dynamic_slice_in_dim(full, lax.axis_index("refl") * rows, rows, 3)
    corr = jnp.transpose(full, (2, 3, 0, 1)).reshape(NOPS, rows, groups * SUB)
    back = lax.all_to_all(full, "dp", split_axis=0, concat_axis=0, tiled=True)
    returned = jnp.transpose(back, (2, 0, 1, 3))[:, None]
    return (corr, returned)


def solution(mesh):
    return jax.shard_map(
        shards,
        mesh=mesh,
        in_specs=(
            P("dp", "refl"),
            P("dp", "refl"),
            P("dp", "refl"),
            P(None, "refl"),
            P(None, "dp"),
        ),
        out_specs=(P(None, ("dp", "refl"), None), P(None, "dp", None, None, "refl")),
        check_vma=False,
    )
```

```python
import functools

import jax
import jax.numpy as jnp
from jax import lax
from jax.experimental import pallas as pl
from jax.experimental.pallas import tpu as pltpu
from jax.sharding import PartitionSpec as P

SUB = 4
NOPS = 4
LANES = 128
SLAB = 2 * SUB
VMEM_LIMIT = 56 * 1024 * 1024
PLANES = 4
PLANE = 8
UNROLL = 64
HALVES = 2


def params():
    return pltpu.CompilerParams(vmem_limit_bytes=VMEM_LIMIT)


def pack_kernel(pick_ref, x_ref, obs_ref, qw_ref, send_ref, w_ref, slabs, sems):
    blk, width = x_ref.shape
    step = min(512, width)

    @pl.loop(0, width // step)
    def _(i):
        cols = pl.ds(pl.multiple_of(i * step, step), step)
        wide_w = obs_ref[:, cols].astype(jnp.float32) * qw_ref[:, cols].astype(jnp.float32)
        wide_x = x_ref[:, cols].astype(jnp.float32)
        w_ref[:, cols] = wide_w.astype(jnp.bfloat16)
        for g in range(blk // SUB):
            rows = slice(g * SUB, (g + 1) * SUB)
            slab = jnp.concatenate([wide_x[rows], wide_w[rows]], 0)
            slabs[g, :, cols] = slab.astype(jnp.bfloat16)

    groups = send_ref.shape[0]

    def copy(d):
        return pltpu.make_async_copy(slabs.at[pick_ref[d]], send_ref.at[d], sems.at[d])

    @pl.loop(0, groups)
    def _(d):
        copy(d).start()

    @pl.loop(0, groups)
    def _(d):
        copy(d).wait()


def pack(pick, intensities, observed, qweights):
    blk, width = intensities.shape
    groups = pick.shape[0]
    whole = pl.BlockSpec(memory_space=pltpu.VMEM)
    return pl.pallas_call(
        pack_kernel,
        out_shape=(
            jax.ShapeDtypeStruct((groups, SLAB, width), jnp.bfloat16),
            jax.ShapeDtypeStruct((blk, width), jnp.bfloat16),
        ),
        in_specs=[pl.BlockSpec(memory_space=pltpu.SMEM), whole, whole, whole],
        out_specs=(pl.BlockSpec(memory_space=pl.ANY), whole),
        scratch_shapes=[
            pltpu.VMEM((blk // SUB, SLAB, width), jnp.bfloat16),
            pltpu.SemaphoreType.DMA((groups,)),
        ],
        compiler_params=params(),
        cost_estimate=pl.CostEstimate(
            flops=blk * width * 4, bytes_accessed=(groups * SLAB * 2 + blk * 10) * width, transcendentals=0
        ),
        name="pack",
    )(pick, intensities, observed, qweights)


def move_kernel(ops_ref, x_ref, w_ref, moved_ref, table, target):
    blk, width = x_ref.shape

    @pl.when(pl.program_id(0) == 0)
    def _():
        @pl.loop(0, width // LANES)
        def _(i):
            cols = pl.ds(pl.multiple_of(i * LANES, LANES), LANES)
            wide_x = x_ref[:, cols].astype(jnp.float32)
            wide_w = w_ref[:, cols].astype(jnp.float32)
            wx = (wide_w * wide_x).astype(jnp.bfloat16).astype(jnp.float32)
            wxx = (wide_w * wide_x * wide_x).astype(jnp.bfloat16).astype(jnp.float32)
            stacked = jnp.concatenate([wide_w, wx, wxx, jnp.zeros((LANES - 3 * blk, LANES), jnp.float32)], 0)
            table[cols, :] = stacked.T

    unroll = 16

    @pl.loop(0, width // unroll)
    def _(i):
        base = pl.multiple_of(i * unroll, unroll)
        for j in range(unroll):
            to = ops_ref[0, 0, base + j]
            target[pl.ds(to, 1), :] = table[pl.ds(base + j, 1), :]

    step = min(512, width)

    @pl.loop(0, width // step)
    def _(i):
        rows = pl.ds(pl.multiple_of(i * step, step), step)
        moved_ref[rows, :] = target[rows, :].astype(jnp.bfloat16)


def move(local_ops, intensities, own_w):
    blk, width = intensities.shape
    whole = pl.BlockSpec(memory_space=pltpu.VMEM)
    return pl.pallas_call(
        move_kernel,
        grid=(NOPS,),
        out_shape=jax.ShapeDtypeStruct((width, NOPS * LANES), jnp.bfloat16),
        in_specs=[
            pl.BlockSpec((1, 1, width), lambda k: (k, 0, 0), memory_space=pltpu.SMEM),
            whole,
            whole,
        ],
        out_specs=pl.BlockSpec((width, LANES), lambda k: (0, k)),
        scratch_shapes=[
            pltpu.VMEM((width, LANES), jnp.float32),
            pltpu.VMEM((width, LANES), jnp.float32),
        ],
        compiler_params=params(),
        cost_estimate=pl.CostEstimate(
            flops=0, bytes_accessed=NOPS * width * LANES * 100, transcendentals=0
        ),
        name="move",
    )(local_ops[:, None, :], intensities, own_w)


def sums_kernel(got_ref, moved_ref, out_ref):
    rows, depth = got_ref.shape
    step = min(512, depth)

    @pl.when(pl.program_id(0) == 0)
    def _():
        out_ref[...] = jnp.zeros_like(out_ref)

    is_x = lax.broadcasted_iota(jnp.int32, (rows // SLAB, SLAB, step), 1) < SUB

    @pl.loop(0, depth // step)
    def _(i):
        cols = pl.ds(pl.multiple_of(i * step, step), step)
        raw = got_ref[:, cols]
        wide = raw.astype(jnp.float32).reshape(rows // SLAB, SLAB, step)
        product = wide * pltpu.roll(wide, SUB, 1)
        second = jnp.where(is_x, product * wide, product)
        second = second.reshape(rows, step).astype(jnp.bfloat16)
        right = moved_ref[cols, :]
        out_ref[0] += jnp.dot(raw, right, preferred_element_type=jnp.float32)
        out_ref[1] += jnp.dot(second, right, preferred_element_type=jnp.float32)


def sums(got, moved):
    rows, width = got.shape
    depth = min(2048, width)
    return pl.pallas_call(
        sums_kernel,
        grid=(width // depth,),
        out_shape=jax.ShapeDtypeStruct((2, rows, moved.shape[1]), jnp.float32),
        in_specs=[
            pl.BlockSpec((rows, depth), lambda i: (0, i)),
            pl.BlockSpec((depth, moved.shape[1]), lambda i: (i, 0)),
        ],
        out_specs=pl.BlockSpec((2, rows, moved.shape[1]), lambda i: (0, 0, 0)),
        compiler_params=params(),
        cost_estimate=pl.CostEstimate(
            flops=4 * rows * width * moved.shape[1],
            bytes_accessed=2 * width * (rows + moved.shape[1]),
            transcendentals=0,
        ),
        name="sums",
    )(got, moved)


def pearson(share, blk):
    first, second = share[0], share[1]
    total_w = first[:, SUB:, :, :blk]
    sum_x = first[:, SUB:, :, blk : 2 * blk]
    sum_xx = first[:, SUB:, :, 2 * blk : 3 * blk]
    sum_y = second[:, SUB:, :, :blk]
    sum_xy = second[:, SUB:, :, blk : 2 * blk]
    sum_yy = second[:, :SUB, :, :blk]
    numer = total_w * sum_xy - sum_x * sum_y
    var_x = jnp.maximum(total_w * sum_xx - sum_x * sum_x, 0.05 * total_w * sum_xx)
    var_y = jnp.maximum(total_w * sum_yy - sum_y * sum_y, 0.05 * total_w * sum_yy)
    return numer / jnp.sqrt(var_x * var_y)


def weigh_kernel(x_ref, obs_ref, qw_ref, out_ref):
    blk = x_ref.shape[0]
    weights = obs_ref[...].astype(jnp.float32) * qw_ref[...].astype(jnp.float32)
    out_ref[:blk, :] = x_ref[...]
    out_ref[blk:, :] = weights.astype(jnp.bfloat16)


def weigh(x, observed, qweights, part):
    blk, width = x.shape
    depth = min(2048, width // HALVES)
    count = width // HALVES // depth
    spec = pl.BlockSpec((blk, depth), lambda i: (0, part * count + i))
    return pl.pallas_call(
        weigh_kernel,
        grid=(count,),
        out_shape=jax.ShapeDtypeStruct((2 * blk, width // HALVES), jnp.bfloat16),
        in_specs=[spec] * 3,
        out_specs=pl.BlockSpec((2 * blk, depth), lambda i: (0, i)),
        compiler_params=params(),
        cost_estimate=pl.CostEstimate(
            flops=blk * width, bytes_accessed=blk * width * 12 // HALVES, transcendentals=0
        ),
        name="weigh",
    )(x, observed, qweights)


def fill_slabs(slabs, xw_ref, offset):
    blk, width = xw_ref.shape[0] // 2, xw_ref.shape[1]
    step = min(512, width)

    @pl.loop(0, width // step)
    def _(i):
        start = pl.multiple_of(i * step, step)
        wide = xw_ref[:, pl.ds(start, step)].astype(jnp.float32)
        for g in range(blk // SUB):
            rows = slice(g * SUB, (g + 1) * SUB)
            slab = jnp.concatenate([wide[:blk][rows], wide[blk:][rows]], 0)
            slabs[g, :, pl.ds(offset + start, step)] = slab.astype(jnp.bfloat16)


def send_slabs(slabs, pick_ref, send_ref, sems):
    mine = lax.div(lax.axis_index("dp"), PLANE)
    partner = mine + 1 - 2 * lax.rem(mine, 2)
    copies = []
    for c in range(PLANE):
        for t, plane in enumerate((mine, partner)):
            group = pick_ref[plane * PLANE + c]
            copies.append(pltpu.make_async_copy(slabs.at[group], send_ref.at[c, t], sems.at[c, t]))
    for copy in copies:
        copy.start()
    for copy in copies:
        copy.wait()


def own_pack_kernel(pick_ref, *refs):
    halves, (send_ref, slabs, sems) = refs[:HALVES], refs[HALVES:]
    for part, ref in enumerate(halves):
        fill_slabs(slabs, ref, part * ref.shape[1])
    send_slabs(slabs, pick_ref, send_ref, sems)


def far_pack_kernel(pick_ref, outer_ref, inner_ref, after_ref, send_ref, buf, in_sem, slabs, sems):
    plane = lax.div(lax.axis_index("dp"), PLANE)
    inner = (plane == 1) | (plane == 2)

    def fetch(ref):
        copy = pltpu.make_async_copy(ref, buf, in_sem)
        copy.start()
        copy.wait()

    @pl.when(inner)
    def _():
        fetch(inner_ref)

    @pl.when(jnp.logical_not(inner))
    def _():
        fetch(outer_ref)

    fill_slabs(slabs, buf, 0)
    send_slabs(slabs, pick_ref, send_ref, sems)


def pack_call(kernel, name, specs, scratch, blk, width, *operands):
    return pl.pallas_call(
        kernel,
        out_shape=jax.ShapeDtypeStruct((PLANE, 2, SLAB, width), jnp.bfloat16),
        in_specs=[pl.BlockSpec(memory_space=pltpu.SMEM)] + specs,
        out_specs=pl.BlockSpec(memory_space=pl.ANY),
        scratch_shapes=scratch
        + [pltpu.VMEM((blk // SUB, SLAB, width), jnp.bfloat16), pltpu.SemaphoreType.DMA((PLANE, 2))],
        compiler_params=params(),
        cost_estimate=pl.CostEstimate(
            flops=blk * width * 4, bytes_accessed=(PLANE * 2 * SLAB * 2 + blk * 4) * width, transcendentals=0
        ),
        name=name,
    )(*operands)


def own_pack(pick, halves):
    rows, width = halves[0].shape
    specs = [pl.BlockSpec(memory_space=pltpu.VMEM)] * HALVES
    return pack_call(own_pack_kernel, "own_pack", specs, [], rows // 2, HALVES * width, pick, *halves)


def far_pack(pick, outer, inner, after):
    rows, width = outer.shape
    scratch = [pltpu.VMEM((rows, width), jnp.bfloat16), pltpu.SemaphoreType.DMA]
    specs = [pl.BlockSpec(memory_space=pl.ANY)] * 3
    return pack_call(far_pack_kernel, "far_pack", specs, scratch, rows // 2, width, pick, outer, inner, after)


def place_kernel(begun, ops_ref, mine_ref, near_ref, before_ref, after_ref, moved_ref, table, target):
    rows, depth = mine_ref.shape
    blk = rows // 2
    width = target.shape[0]
    step = min(512, width)
    part = pl.multiple_of(pl.program_id(1) * depth, depth)

    @pl.when(pl.program_id(0) == 0)
    def _():
        size = min(256, depth)
        diagonal = lax.broadcasted_iota(jnp.int32, (size, size), 0) == lax.broadcasted_iota(
            jnp.int32, (size, size), 1
        )
        identity = jnp.where(diagonal, 1.0, 0.0).astype(jnp.bfloat16)
        for i in range(depth // size):
            cols = slice(i * size, (i + 1) * size)
            both = [mine_ref[:blk, cols], near_ref[:blk, cols], mine_ref[blk:, cols], near_ref[blk:, cols]]
            table[pl.ds(part + i * size, size), :] = lax.dot_general(
                identity,
                jnp.concatenate(both, 0),
                (((1,), (1,)), ((), ())),
                preferred_element_type=jnp.float32,
            )

    if begun:

        @pl.when(pl.program_id(1) == 0)
        def _():
            @pl.loop(0, width // step)
            def _(i):
                here = pl.ds(pl.multiple_of(i * step, step), step)
                target[here, :] = before_ref[here, :].astype(jnp.float32)

    @pl.loop(0, depth // UNROLL)
    def _(i):
        base = pl.multiple_of(i * UNROLL, UNROLL)
        row = pl.multiple_of(part + base, UNROLL)
        for j in range(UNROLL):
            to = ops_ref[0, 0, base + j]
            target[pl.ds(to, 1), :] = table[pl.ds(row + j, 1), :]

    @pl.when(pl.program_id(1) == pl.num_programs(1) - 1)
    def _():
        @pl.loop(0, width // step)
        def _(i):
            here = pl.ds(pl.multiple_of(i * step, step), step)
            moved_ref[here, :] = target[here, :].astype(jnp.bfloat16)


def place(ops, first, count, part, mine, near, before, after):
    width = ops.shape[2]
    rows, span = mine.shape
    depth = min(2048, span)
    chunks = span // depth
    some = pl.BlockSpec((rows, depth), lambda k, i: (0, jnp.where(k == 0, i, chunks - 1)))
    anywhere = pl.BlockSpec(memory_space=pl.ANY)
    begun = before is not None
    return pl.pallas_call(
        functools.partial(place_kernel, begun),
        grid=(count, chunks),
        out_shape=jax.ShapeDtypeStruct((width, count * LANES), jnp.bfloat16),
        in_specs=[
            pl.BlockSpec((1, 1, depth), lambda k, i: (first + k, 0, part * chunks + i), memory_space=pltpu.SMEM),
            some,
            some,
            pl.BlockSpec((width, LANES), lambda k, i: (0, first + k)) if begun else anywhere,
            anywhere,
        ],
        out_specs=pl.BlockSpec((width, LANES), lambda k, i: (0, k)),
        scratch_shapes=[pltpu.VMEM((span, LANES), jnp.float32), pltpu.VMEM((width, LANES), jnp.float32)],
        compiler_params=params(),
        cost_estimate=pl.CostEstimate(
            flops=0, bytes_accessed=count * span * LANES * 64, transcendentals=0
        ),
        name="place",
    )(ops, mine, near, before if begun else after, after)


def ratio(total_w, sum_x, sum_xx, sum_y, sum_xy, sum_yy):
    numer = total_w * sum_xy - sum_x * sum_y
    var_x = jnp.maximum(total_w * sum_xx - sum_x * sum_x, 0.05 * total_w * sum_xx)
    var_y = jnp.maximum(total_w * sum_yy - sum_y * sum_y, 0.05 * total_w * sum_yy)
    return numer / jnp.sqrt(var_x * var_y)


def plane_sums_kernel(begun, ended, own_ref, far_ref, first_ref, second_ref, before_ref, out_ref, *scratch):
    rows, depth = own_ref.shape
    step = min(1024, depth)
    half = LANES // 2
    slabs = rows // SLAB
    blk = half // 2

    acc = scratch[0] if ended else out_ref

    @pl.when(pl.program_id(0) == 0)
    def _():
        if begun:
            acc[...] = before_ref[...]
        else:
            acc[...] = jnp.zeros_like(acc)

    @pl.loop(0, depth // step)
    def _(i):
        cols = pl.ds(pl.multiple_of(i * step, step), step)
        is_x = lax.broadcasted_iota(jnp.int32, (slabs, SLAB, step), 1) < SUB
        weights, products = [], []
        for ref in (own_ref, far_ref):
            wide = ref[:, cols].astype(jnp.float32).reshape(slabs, SLAB, step)
            rolled = pltpu.roll(wide, SUB, 1)
            product = wide * rolled
            both = jnp.where(is_x, product * wide, product)
            products.append(both.reshape(rows, step).astype(jnp.bfloat16))
            mine = rolled.reshape(slabs // 2, 2, SLAB, step)[:, 0]
            partner = wide.reshape(slabs // 2, 2, SLAB, step)[:, 1]
            pair = jnp.where(is_x[: slabs // 2], mine, partner)
            weights.append(pair.reshape(rows // 2, step).astype(jnp.bfloat16))
        low = lax.broadcasted_iota(jnp.int32, (step, LANES), 1) < half
        linear, square = [], []
        for ref in (first_ref, second_ref):
            even, odd = None, None
            for k in range(2):
                values = ref[cols, k * LANES : (k + 1) * LANES].astype(jnp.float32)
                swapped = pltpu.roll(values, half, 1)
                product = values * swapped
                linear.append(jnp.where(low, product, values).astype(jnp.bfloat16))
                if k == 0:
                    even = product * values
                else:
                    odd = product * swapped
            square.append(jnp.where(low, even, odd).astype(jnp.bfloat16))
        left = jnp.concatenate(weights + products, 0)
        right = jnp.concatenate(linear + square, 1)
        acc[...] += jnp.dot(left, right, preferred_element_type=jnp.float32)

    if not ended:
        return

    @pl.when(pl.program_id(0) == pl.num_programs(0) - 1)
    def _():
        tiles = slabs
        top = lax.broadcasted_iota(jnp.int32, (tiles, SLAB, LANES), 1) < SUB
        lane = lax.broadcasted_iota(jnp.int32, (tiles * SLAB, LANES), 1)
        result = jnp.zeros((tiles * SLAB, LANES), jnp.float32)
        for k in range(NOPS):
            lanes = slice(k * LANES, (k + 1) * LANES)
            squares = slice((NOPS + k // 2) * LANES, (NOPS + k // 2 + 1) * LANES)
            with_w = acc[:rows, lanes]
            with_y = acc[rows:, lanes].reshape(tiles, 2, SLAB, LANES)
            mine, partner = with_y[:, 0], with_y[:, 1]
            y = jnp.where(top, pltpu.roll(mine, SUB, 1), partner).reshape(tiles * SLAB, LANES)
            yy = jnp.where(top, mine, pltpu.roll(partner, SUB, 1)).reshape(tiles * SLAB, LANES)
            sum_xx = acc[:rows, squares]
            if k % 2 == 1:
                sum_xx = pltpu.roll(sum_xx, half, 1)
            both = ratio(
                pltpu.roll(with_w, half, 1), with_w, sum_xx, pltpu.roll(y, half, 1), y, pltpu.roll(yy, half, 1)
            )
            both = jnp.where(
                top.reshape(tiles * SLAB, LANES), both, pltpu.roll(both, LANES - blk, 1)
            )
            moved = both if k == 0 else pltpu.roll(both, k * blk, 1)
            result = jnp.where((lane >= k * blk) & (lane < (k + 1) * blk), moved, result)
        out_ref[...] = result


def plane_sums(part, own, far, first, second, before):
    rows, width = far.shape
    depth = min(2048, width)
    chunks = width // depth
    lanes = (NOPS + NOPS // 2) * LANES
    moved = pl.BlockSpec((depth, 2 * LANES), lambda i: (part * chunks + i, 0))
    begun, ended = before is not None, part == HALVES - 1
    total = (3 * rows, lanes)
    shape = (rows, LANES) if ended else total
    return pl.pallas_call(
        functools.partial(plane_sums_kernel, begun, ended),
        grid=(chunks,),
        out_shape=jax.ShapeDtypeStruct(shape, jnp.float32),
        in_specs=[
            pl.BlockSpec((rows, depth), lambda i: (0, part * chunks + i)),
            pl.BlockSpec((rows, depth), lambda i: (0, i)),
            moved,
            moved,
            pl.BlockSpec(total, lambda i: (0, 0)) if begun else pl.BlockSpec(memory_space=pl.ANY),
        ],
        out_specs=pl.BlockSpec(shape, lambda i: (0, 0)),
        scratch_shapes=[pltpu.VMEM(total, jnp.float32)] if ended else [],
        compiler_params=params(),
        cost_estimate=pl.CostEstimate(
            flops=6 * rows * width * lanes,
            bytes_accessed=width * (4 * rows + 8 * LANES),
            transcendentals=0,
        ),
        name="plane_sums",
    )(own, far, first, second, before if begun else far)


def shards_by_plane(intensities, observed, qweights, ops, pick):
    blk = intensities.shape[0]
    groups = PLANES * PLANE
    near = [(i, i ^ PLANE) for i in range(groups)]
    far = [(i, i ^ (2 * PLANE)) for i in range(groups)]
    middle = [(i, 3 * PLANE + 2 * (i % PLANE) - i) for i in range(PLANE, 3 * PLANE)]
    outward = [(i, i - PLANE if i < 2 * PLANE else i + PLANE) for i in range(PLANE, 3 * PLANE)]
    rings = [[z * PLANE + c for c in range(PLANE)] for z in range(PLANES)]
    plane = lax.axis_index("dp") // PLANE
    odd, upper = plane % 2 == 1, plane >= 2

    def spread(send):
        got = lax.all_to_all(send, "dp", split_axis=0, concat_axis=0, axis_index_groups=rings, tiled=True)
        return got.reshape(PLANE * 2 * SLAB, send.shape[-1])

    own_pick = pick[:, 0]
    ops = ops[:, None, :]
    mine_0 = weigh(intensities, observed, qweights, 0)
    near_0 = lax.ppermute(mine_0, "dp", near)
    mid_0 = lax.ppermute(mine_0, "dp", middle)
    far_pick = lax.ppermute(own_pick, "dp", far)
    mine_1 = weigh(intensities, observed, qweights, 1)
    own_got = spread(own_pack(own_pick, (mine_0, mine_1)))
    near_0, mid_0, far_pick, later_1 = lax.optimization_barrier((near_0, mid_0, far_pick, mine_1))
    near_1 = lax.ppermute(later_1, "dp", near)
    mid_1 = lax.ppermute(later_1, "dp", middle)
    outer_0 = lax.ppermute(mid_0, "dp", outward)
    inner_0 = lax.ppermute(near_0, "dp", middle)
    moved_0 = place(ops, 0, NOPS, 0, mine_0, near_0, None, own_pick)
    near_1, mid_1, outer_0, inner_0 = lax.optimization_barrier((near_1, mid_1, outer_0, inner_0))
    outer_1 = lax.ppermute(mid_1, "dp", outward)
    inner_1 = lax.ppermute(near_1, "dp", middle)
    far_send_0 = far_pack(far_pick, outer_0, inner_0, moved_0)
    far_got_0 = spread(far_send_0)
    first = place(ops, 0, NOPS // 2, 1, mine_1, near_1, moved_0, far_send_0)
    far_send_1 = far_pack(far_pick, outer_1, inner_1, first)
    far_got_1 = spread(far_send_1)
    second = place(ops, NOPS // 2, NOPS // 2, 1, mine_1, near_1, moved_0, far_send_1)
    sums_0 = plane_sums(0, own_got, far_got_0, first, second, None)
    stats = plane_sums(1, own_got, far_got_1, first, second, sums_0)
    stats = stats.reshape(2, PLANE, 2, SUB, NOPS * blk)
    mine, other = stats[:, :, 0], stats[:, :, 1]

    from_near = lax.ppermute(other, "dp", near)
    pair = jnp.stack([mine, from_near], 1)
    pair = jnp.where(odd, pair[:, ::-1], pair)
    pair = jnp.where(upper, pair[::-1], pair)
    corr = pair.reshape(groups * SUB, NOPS * blk).T.reshape(NOPS, blk, groups * SUB)

    both = jnp.where(upper, stats[::-1], stats).reshape(2, 1, PLANE, 2 * SUB, NOPS * blk)
    back = jnp.broadcast_to(both, (2, 2, PLANE, 2 * SUB, NOPS * blk)).reshape(groups, 2 * SUB, NOPS * blk)
    back = lax.all_to_all(back, "dp", split_axis=0, concat_axis=0, tiled=True)
    back = back.reshape(2, 2, PLANE, 2, SUB, NOPS, blk)
    back = jnp.where(odd, back[:, 1, :, ::-1], back[:, 0])
    returned = jnp.transpose(back, (4, 0, 2, 1, 3, 5)).reshape(NOPS, 1, groups, SUB, blk)
    return (corr, returned)


def shards(intensities, observed, qweights, ops, pick):
    if lax.axis_size("dp") == PLANES * PLANE and lax.axis_size("refl") == 1:
        return shards_by_plane(intensities, observed, qweights, ops, pick)
    return shards_direct(intensities, observed, qweights, ops, pick)


def shards_direct(intensities, observed, qweights, ops, pick):
    blk, width = intensities.shape
    groups = lax.axis_size("dp")
    shares = lax.axis_size("refl")
    local_ops = ops - lax.axis_index("refl") * width
    send, own_w = pack(pick[:, 0], intensities, observed, qweights)
    got = lax.all_to_all(send, "dp", split_axis=0, concat_axis=0, tiled=True)
    moved = move(local_ops, intensities, own_w)
    stats = sums(got.reshape(groups * SLAB, width), moved)
    if shares > 1:
        stats = lax.psum(stats, "refl")
    stats = stats.reshape(2, groups, SLAB, NOPS, LANES)
    full = pearson(stats, blk)
    rows = blk // shares
    if shares > 1:
        full = lax.dynamic_slice_in_dim(full, lax.axis_index("refl") * rows, rows, 3)
    corr = jnp.transpose(full, (2, 3, 0, 1)).reshape(NOPS, rows, groups * SUB)
    back = lax.all_to_all(full, "dp", split_axis=0, concat_axis=0, tiled=True)
    returned = jnp.transpose(back, (2, 0, 1, 3))[:, None]
    return (corr, returned)


def solution(mesh):
    return jax.shard_map(
        shards,
        mesh=mesh,
        in_specs=(
            P("dp", "refl"),
            P("dp", "refl"),
            P("dp", "refl"),
            P(None, "refl"),
            P(None, "dp"),
        ),
        out_specs=(P(None, ("dp", "refl"), None), P(None, "dp", None, None, "refl")),
        check_vma=False,
    )
```

```python
import functools

import jax
import jax.numpy as jnp
from jax import lax
from jax.experimental import pallas as pl
from jax.experimental.pallas import tpu as pltpu
from jax.sharding import PartitionSpec as P

SUB = 4
NOPS = 4
LANES = 128
SLAB = 2 * SUB
VMEM_LIMIT = 56 * 1024 * 1024
PLANES = 4
PLANE = 8
UNROLL = 64
HALVES = 2


def params():
    return pltpu.CompilerParams(vmem_limit_bytes=VMEM_LIMIT)


def pack_kernel(pick_ref, x_ref, obs_ref, qw_ref, send_ref, w_ref, slabs, sems):
    blk, width = x_ref.shape
    step = min(512, width)

    @pl.loop(0, width // step)
    def _(i):
        cols = pl.ds(pl.multiple_of(i * step, step), step)
        wide_w = obs_ref[:, cols].astype(jnp.float32) * qw_ref[:, cols].astype(jnp.float32)
        wide_x = x_ref[:, cols].astype(jnp.float32)
        w_ref[:, cols] = wide_w.astype(jnp.bfloat16)
        for g in range(blk // SUB):
            rows = slice(g * SUB, (g + 1) * SUB)
            slab = jnp.concatenate([wide_x[rows], wide_w[rows]], 0)
            slabs[g, :, cols] = slab.astype(jnp.bfloat16)

    groups = send_ref.shape[0]

    def copy(d):
        return pltpu.make_async_copy(slabs.at[pick_ref[d]], send_ref.at[d], sems.at[d])

    @pl.loop(0, groups)
    def _(d):
        copy(d).start()

    @pl.loop(0, groups)
    def _(d):
        copy(d).wait()


def pack(pick, intensities, observed, qweights):
    blk, width = intensities.shape
    groups = pick.shape[0]
    whole = pl.BlockSpec(memory_space=pltpu.VMEM)
    return pl.pallas_call(
        pack_kernel,
        out_shape=(
            jax.ShapeDtypeStruct((groups, SLAB, width), jnp.bfloat16),
            jax.ShapeDtypeStruct((blk, width), jnp.bfloat16),
        ),
        in_specs=[pl.BlockSpec(memory_space=pltpu.SMEM), whole, whole, whole],
        out_specs=(pl.BlockSpec(memory_space=pl.ANY), whole),
        scratch_shapes=[
            pltpu.VMEM((blk // SUB, SLAB, width), jnp.bfloat16),
            pltpu.SemaphoreType.DMA((groups,)),
        ],
        compiler_params=params(),
        cost_estimate=pl.CostEstimate(
            flops=blk * width * 4, bytes_accessed=(groups * SLAB * 2 + blk * 10) * width, transcendentals=0
        ),
        name="pack",
    )(pick, intensities, observed, qweights)


def move_kernel(ops_ref, x_ref, w_ref, moved_ref, table, target):
    blk, width = x_ref.shape

    @pl.when(pl.program_id(0) == 0)
    def _():
        @pl.loop(0, width // LANES)
        def _(i):
            cols = pl.ds(pl.multiple_of(i * LANES, LANES), LANES)
            wide_x = x_ref[:, cols].astype(jnp.float32)
            wide_w = w_ref[:, cols].astype(jnp.float32)
            wx = (wide_w * wide_x).astype(jnp.bfloat16).astype(jnp.float32)
            wxx = (wide_w * wide_x * wide_x).astype(jnp.bfloat16).astype(jnp.float32)
            stacked = jnp.concatenate([wide_w, wx, wxx, jnp.zeros((LANES - 3 * blk, LANES), jnp.float32)], 0)
            table[cols, :] = stacked.T

    unroll = 16

    @pl.loop(0, width // unroll)
    def _(i):
        base = pl.multiple_of(i * unroll, unroll)
        for j in range(unroll):
            to = ops_ref[0, 0, base + j]
            target[pl.ds(to, 1), :] = table[pl.ds(base + j, 1), :]

    step = min(512, width)

    @pl.loop(0, width // step)
    def _(i):
        rows = pl.ds(pl.multiple_of(i * step, step), step)
        moved_ref[rows, :] = target[rows, :].astype(jnp.bfloat16)


def move(local_ops, intensities, own_w):
    blk, width = intensities.shape
    whole = pl.BlockSpec(memory_space=pltpu.VMEM)
    return pl.pallas_call(
        move_kernel,
        grid=(NOPS,),
        out_shape=jax.ShapeDtypeStruct((width, NOPS * LANES), jnp.bfloat16),
        in_specs=[
            pl.BlockSpec((1, 1, width), lambda k: (k, 0, 0), memory_space=pltpu.SMEM),
            whole,
            whole,
        ],
        out_specs=pl.BlockSpec((width, LANES), lambda k: (0, k)),
        scratch_shapes=[
            pltpu.VMEM((width, LANES), jnp.float32),
            pltpu.VMEM((width, LANES), jnp.float32),
        ],
        compiler_params=params(),
        cost_estimate=pl.CostEstimate(
            flops=0, bytes_accessed=NOPS * width * LANES * 100, transcendentals=0
        ),
        name="move",
    )(local_ops[:, None, :], intensities, own_w)


def sums_kernel(got_ref, moved_ref, out_ref):
    rows, depth = got_ref.shape
    step = min(512, depth)

    @pl.when(pl.program_id(0) == 0)
    def _():
        out_ref[...] = jnp.zeros_like(out_ref)

    is_x = lax.broadcasted_iota(jnp.int32, (rows // SLAB, SLAB, step), 1) < SUB

    @pl.loop(0, depth // step)
    def _(i):
        cols = pl.ds(pl.multiple_of(i * step, step), step)
        raw = got_ref[:, cols]
        wide = raw.astype(jnp.float32).reshape(rows // SLAB, SLAB, step)
        product = wide * pltpu.roll(wide, SUB, 1)
        second = jnp.where(is_x, product * wide, product)
        second = second.reshape(rows, step).astype(jnp.bfloat16)
        right = moved_ref[cols, :]
        out_ref[0] += jnp.dot(raw, right, preferred_element_type=jnp.float32)
        out_ref[1] += jnp.dot(second, right, preferred_element_type=jnp.float32)


def sums(got, moved):
    rows, width = got.shape
    depth = min(2048, width)
    return pl.pallas_call(
        sums_kernel,
        grid=(width // depth,),
        out_shape=jax.ShapeDtypeStruct((2, rows, moved.shape[1]), jnp.float32),
        in_specs=[
            pl.BlockSpec((rows, depth), lambda i: (0, i)),
            pl.BlockSpec((depth, moved.shape[1]), lambda i: (i, 0)),
        ],
        out_specs=pl.BlockSpec((2, rows, moved.shape[1]), lambda i: (0, 0, 0)),
        compiler_params=params(),
        cost_estimate=pl.CostEstimate(
            flops=4 * rows * width * moved.shape[1],
            bytes_accessed=2 * width * (rows + moved.shape[1]),
            transcendentals=0,
        ),
        name="sums",
    )(got, moved)


def pearson(share, blk):
    first, second = share[0], share[1]
    total_w = first[:, SUB:, :, :blk]
    sum_x = first[:, SUB:, :, blk : 2 * blk]
    sum_xx = first[:, SUB:, :, 2 * blk : 3 * blk]
    sum_y = second[:, SUB:, :, :blk]
    sum_xy = second[:, SUB:, :, blk : 2 * blk]
    sum_yy = second[:, :SUB, :, :blk]
    numer = total_w * sum_xy - sum_x * sum_y
    var_x = jnp.maximum(total_w * sum_xx - sum_x * sum_x, 0.05 * total_w * sum_xx)
    var_y = jnp.maximum(total_w * sum_yy - sum_y * sum_y, 0.05 * total_w * sum_yy)
    return numer / jnp.sqrt(var_x * var_y)


def weigh_kernel(x_ref, obs_ref, qw_ref, out_ref):
    blk = x_ref.shape[0]
    weights = obs_ref[...].astype(jnp.float32) * qw_ref[...].astype(jnp.float32)
    out_ref[:blk, :] = x_ref[...]
    out_ref[blk:, :] = weights.astype(jnp.bfloat16)


def weigh(x, observed, qweights, part):
    blk, width = x.shape
    depth = min(2048, width // HALVES)
    count = width // HALVES // depth
    spec = pl.BlockSpec((blk, depth), lambda i: (0, part * count + i))
    return pl.pallas_call(
        weigh_kernel,
        grid=(count,),
        out_shape=jax.ShapeDtypeStruct((2 * blk, width // HALVES), jnp.bfloat16),
        in_specs=[spec] * 3,
        out_specs=pl.BlockSpec((2 * blk, depth), lambda i: (0, i)),
        compiler_params=params(),
        cost_estimate=pl.CostEstimate(
            flops=blk * width, bytes_accessed=blk * width * 12 // HALVES, transcendentals=0
        ),
        name="weigh",
    )(x, observed, qweights)


def fill_slabs(slabs, xw_ref, offset):
    blk, width = xw_ref.shape[0] // 2, xw_ref.shape[1]
    step = min(512, width)

    @pl.loop(0, width // step)
    def _(i):
        start = pl.multiple_of(i * step, step)
        wide = xw_ref[:, pl.ds(start, step)].astype(jnp.float32)
        for g in range(blk // SUB):
            rows = slice(g * SUB, (g + 1) * SUB)
            slab = jnp.concatenate([wide[:blk][rows], wide[blk:][rows]], 0)
            slabs[g, :, pl.ds(offset + start, step)] = slab.astype(jnp.bfloat16)


def send_slabs(slabs, pick_ref, send_ref, sems):
    mine = lax.div(lax.axis_index("dp"), PLANE)
    partner = mine + 1 - 2 * lax.rem(mine, 2)
    copies = []
    for c in range(PLANE):
        for t, plane in enumerate((mine, partner)):
            group = pick_ref[plane * PLANE + c]
            copies.append(pltpu.make_async_copy(slabs.at[group], send_ref.at[c, t], sems.at[c, t]))
    for copy in copies:
        copy.start()
    for copy in copies:
        copy.wait()


def own_pack_kernel(pick_ref, *refs):
    halves, (send_ref, slabs, sems) = refs[:HALVES], refs[HALVES:]
    for part, ref in enumerate(halves):
        fill_slabs(slabs, ref, part * ref.shape[1])
    send_slabs(slabs, pick_ref, send_ref, sems)


def far_pack_kernel(pick_ref, outer_ref, inner_ref, after_ref, send_ref, slabs, sems):
    plane = lax.div(lax.axis_index("dp"), PLANE)
    inner = (plane == 1) | (plane == 2)

    @pl.when(inner)
    def _():
        fill_slabs(slabs, inner_ref, 0)

    @pl.when(jnp.logical_not(inner))
    def _():
        fill_slabs(slabs, outer_ref, 0)

    send_slabs(slabs, pick_ref, send_ref, sems)


def pack_call(kernel, name, specs, blk, width, *operands):
    return pl.pallas_call(
        kernel,
        out_shape=jax.ShapeDtypeStruct((PLANE, 2, SLAB, width), jnp.bfloat16),
        in_specs=[pl.BlockSpec(memory_space=pltpu.SMEM)] + specs,
        out_specs=pl.BlockSpec(memory_space=pl.ANY),
        scratch_shapes=[pltpu.VMEM((blk // SUB, SLAB, width), jnp.bfloat16), pltpu.SemaphoreType.DMA((PLANE, 2))],
        compiler_params=params(),
        cost_estimate=pl.CostEstimate(
            flops=blk * width * 4, bytes_accessed=(PLANE * 2 * SLAB * 2 + blk * 4) * width, transcendentals=0
        ),
        name=name,
    )(*operands)


def own_pack(pick, halves):
    rows, width = halves[0].shape
    specs = [pl.BlockSpec(memory_space=pltpu.VMEM)] * HALVES
    return pack_call(own_pack_kernel, "own_pack", specs, rows // 2, HALVES * width, pick, *halves)


def far_pack(pick, outer, inner, after):
    rows, width = outer.shape
    specs = [pl.BlockSpec(memory_space=pltpu.VMEM)] * 2 + [pl.BlockSpec(memory_space=pl.ANY)]
    return pack_call(far_pack_kernel, "far_pack", specs, rows // 2, width, pick, outer, inner, after)


def place_kernel(begun, ops_ref, mine_ref, near_ref, before_ref, after_ref, moved_ref, table, target):
    rows, depth = mine_ref.shape
    blk = rows // 2
    width = target.shape[0]
    step = min(512, width)
    part = pl.multiple_of(pl.program_id(1) * depth, depth)
    table_rows = table.reshape(table.shape[0], 1, LANES)
    target_rows = target.reshape(width, 1, LANES)

    @pl.when(pl.program_id(0) == 0)
    def _():
        size = min(256, depth)
        diagonal = lax.broadcasted_iota(jnp.int32, (size, size), 0) == lax.broadcasted_iota(
            jnp.int32, (size, size), 1
        )
        identity = jnp.where(diagonal, 1.0, 0.0).astype(jnp.bfloat16)
        for i in range(depth // size):
            cols = slice(i * size, (i + 1) * size)
            both = [mine_ref[:blk, cols], near_ref[:blk, cols], mine_ref[blk:, cols], near_ref[blk:, cols]]
            table[pl.ds(part + i * size, size), :] = lax.dot_general(
                identity,
                jnp.concatenate(both, 0),
                (((1,), (1,)), ((), ())),
                preferred_element_type=jnp.float32,
            )

    if begun:

        @pl.when(pl.program_id(1) == 0)
        def _():
            @pl.loop(0, width // step)
            def _(i):
                here = pl.ds(pl.multiple_of(i * step, step), step)
                target[here, :] = before_ref[here, :].astype(jnp.float32)

    @pl.loop(0, depth // UNROLL)
    def _(i):
        base = pl.multiple_of(i * UNROLL, UNROLL)
        row = pl.multiple_of(part + base, UNROLL)
        for j in range(UNROLL):
            target_rows[ops_ref[0, 0, base + j]] = table_rows[row + j]

    @pl.when(pl.program_id(1) == pl.num_programs(1) - 1)
    def _():
        @pl.loop(0, width // step)
        def _(i):
            here = pl.ds(pl.multiple_of(i * step, step), step)
            moved_ref[here, :] = target[here, :].astype(jnp.bfloat16)


def place(ops, first, count, part, mine, near, before, after):
    width = ops.shape[2]
    rows, span = mine.shape
    depth = min(2048, span)
    chunks = span // depth
    some = pl.BlockSpec((rows, depth), lambda k, i: (0, jnp.where(k == 0, i, chunks - 1)))
    anywhere = pl.BlockSpec(memory_space=pl.ANY)
    begun = before is not None
    return pl.pallas_call(
        functools.partial(place_kernel, begun),
        grid=(count, chunks),
        out_shape=jax.ShapeDtypeStruct((width, count * LANES), jnp.bfloat16),
        in_specs=[
            pl.BlockSpec((1, 1, depth), lambda k, i: (first + k, 0, part * chunks + i), memory_space=pltpu.SMEM),
            some,
            some,
            pl.BlockSpec((width, LANES), lambda k, i: (0, first + k)) if begun else anywhere,
            anywhere,
        ],
        out_specs=pl.BlockSpec((width, LANES), lambda k, i: (0, k)),
        scratch_shapes=[pltpu.VMEM((span, LANES), jnp.float32), pltpu.VMEM((width, LANES), jnp.float32)],
        compiler_params=params(),
        cost_estimate=pl.CostEstimate(
            flops=0, bytes_accessed=count * span * LANES * 64, transcendentals=0
        ),
        name="place",
    )(ops, mine, near, before if begun else after, after)


def ratio(total_w, sum_x, sum_xx, sum_y, sum_xy, sum_yy):
    numer = total_w * sum_xy - sum_x * sum_y
    var_x = jnp.maximum(total_w * sum_xx - sum_x * sum_x, 0.05 * total_w * sum_xx)
    var_y = jnp.maximum(total_w * sum_yy - sum_y * sum_y, 0.05 * total_w * sum_yy)
    return numer / jnp.sqrt(var_x * var_y)


def plane_sums_kernel(begun, ended, own_ref, far_ref, first_ref, second_ref, before_ref, out_ref, *scratch):
    rows, depth = own_ref.shape
    step = min(1024, depth)
    half = LANES // 2
    slabs = rows // SLAB
    blk = half // 2

    acc = scratch[0] if ended else out_ref

    @pl.when(pl.program_id(0) == 0)
    def _():
        if begun:
            acc[...] = before_ref[...]
        else:
            acc[...] = jnp.zeros_like(acc)

    for i in range(depth // step):
        cols = slice(i * step, (i + 1) * step)
        is_x = lax.broadcasted_iota(jnp.int32, (slabs, SLAB, step), 1) < SUB
        weights, products = [], []
        for ref in (own_ref, far_ref):
            wide = ref[:, cols].astype(jnp.float32).reshape(slabs, SLAB, step)
            rolled = pltpu.roll(wide, SUB, 1)
            product = wide * rolled
            both = jnp.where(is_x, product * wide, product)
            products.append(both.reshape(rows, step).astype(jnp.bfloat16))
            mine = rolled.reshape(slabs // 2, 2, SLAB, step)[:, 0]
            partner = wide.reshape(slabs // 2, 2, SLAB, step)[:, 1]
            pair = jnp.where(is_x[: slabs // 2], mine, partner)
            weights.append(pair.reshape(rows // 2, step).astype(jnp.bfloat16))
        low = lax.broadcasted_iota(jnp.int32, (step, LANES), 1) < half
        linear, square = [], []
        for ref in (first_ref, second_ref):
            even, odd = None, None
            for k in range(2):
                values = ref[cols, k * LANES : (k + 1) * LANES].astype(jnp.float32)
                swapped = pltpu.roll(values, half, 1)
                product = values * swapped
                linear.append(jnp.where(low, product, values).astype(jnp.bfloat16))
                if k == 0:
                    even = product * values
                else:
                    odd = product * swapped
            square.append(jnp.where(low, even, odd).astype(jnp.bfloat16))
        left = jnp.concatenate(weights + products, 0)
        right = jnp.concatenate(linear + square, 1)
        acc[...] += jnp.dot(left, right, preferred_element_type=jnp.float32)

    if not ended:
        return

    @pl.when(pl.program_id(0) == pl.num_programs(0) - 1)
    def _():
        tiles = slabs
        top = lax.broadcasted_iota(jnp.int32, (tiles, SLAB, LANES), 1) < SUB
        lane = lax.broadcasted_iota(jnp.int32, (tiles * SLAB, LANES), 1)
        result = jnp.zeros((tiles * SLAB, LANES), jnp.float32)
        for k in range(NOPS):
            lanes = slice(k * LANES, (k + 1) * LANES)
            squares = slice((NOPS + k // 2) * LANES, (NOPS + k // 2 + 1) * LANES)
            with_w = acc[:rows, lanes]
            with_y = acc[rows:, lanes].reshape(tiles, 2, SLAB, LANES)
            mine, partner = with_y[:, 0], with_y[:, 1]
            y = jnp.where(top, pltpu.roll(mine, SUB, 1), partner).reshape(tiles * SLAB, LANES)
            yy = jnp.where(top, mine, pltpu.roll(partner, SUB, 1)).reshape(tiles * SLAB, LANES)
            sum_xx = acc[:rows, squares]
            if k % 2 == 1:
                sum_xx = pltpu.roll(sum_xx, half, 1)
            both = ratio(
                pltpu.roll(with_w, half, 1), with_w, sum_xx, pltpu.roll(y, half, 1), y, pltpu.roll(yy, half, 1)
            )
            both = jnp.where(
                top.reshape(tiles * SLAB, LANES), both, pltpu.roll(both, LANES - blk, 1)
            )
            moved = both if k == 0 else pltpu.roll(both, k * blk, 1)
            result = jnp.where((lane >= k * blk) & (lane < (k + 1) * blk), moved, result)
        out_ref[...] = result


def plane_sums(part, own, far, first, second, before):
    rows, width = far.shape
    depth = min(4096, width)
    chunks = width // depth
    lanes = (NOPS + NOPS // 2) * LANES
    moved = pl.BlockSpec((depth, 2 * LANES), lambda i: (part * chunks + i, 0))
    begun, ended = before is not None, part == HALVES - 1
    total = (3 * rows, lanes)
    shape = (rows, LANES) if ended else total
    return pl.pallas_call(
        functools.partial(plane_sums_kernel, begun, ended),
        grid=(chunks,),
        out_shape=jax.ShapeDtypeStruct(shape, jnp.float32),
        in_specs=[
            pl.BlockSpec((rows, depth), lambda i: (0, part * chunks + i)),
            pl.BlockSpec((rows, depth), lambda i: (0, i)),
            moved,
            moved,
            pl.BlockSpec(total, lambda i: (0, 0)) if begun else pl.BlockSpec(memory_space=pl.ANY),
        ],
        out_specs=pl.BlockSpec(shape, lambda i: (0, 0)),
        scratch_shapes=[pltpu.VMEM(total, jnp.float32)] if ended else [],
        compiler_params=params(),
        cost_estimate=pl.CostEstimate(
            flops=6 * rows * width * lanes,
            bytes_accessed=width * (4 * rows + 8 * LANES),
            transcendentals=0,
        ),
        name="plane_sums",
    )(own, far, first, second, before if begun else far)


def shards_by_plane(intensities, observed, qweights, ops, pick):
    blk = intensities.shape[0]
    groups = PLANES * PLANE
    near = [(i, i ^ PLANE) for i in range(groups)]
    far = [(i, i ^ (2 * PLANE)) for i in range(groups)]
    middle = [(i, 3 * PLANE + 2 * (i % PLANE) - i) for i in range(PLANE, 3 * PLANE)]
    outward = [(i, i - PLANE if i < 2 * PLANE else i + PLANE) for i in range(PLANE, 3 * PLANE)]
    rings = [[z * PLANE + c for c in range(PLANE)] for z in range(PLANES)]
    plane = lax.axis_index("dp") // PLANE
    odd, upper = plane % 2 == 1, plane >= 2

    def spread(send):
        got = lax.all_to_all(send, "dp", split_axis=0, concat_axis=0, axis_index_groups=rings, tiled=True)
        return got.reshape(PLANE * 2 * SLAB, send.shape[-1])

    own_pick = pick[:, 0]
    ops = ops[:, None, :]
    mine_0 = weigh(intensities, observed, qweights, 0)
    near_0 = lax.ppermute(mine_0, "dp", near)
    mid_0 = lax.ppermute(mine_0, "dp", middle)
    far_pick = lax.ppermute(own_pick, "dp", far)
    mine_1 = weigh(intensities, observed, qweights, 1)
    own_send = own_pack(own_pick, (mine_0, mine_1))
    near_0, mid_0, far_pick, later_1, own_send = lax.optimization_barrier((near_0, mid_0, far_pick, mine_1, own_send))
    own_got = spread(own_send)
    near_1 = lax.ppermute(later_1, "dp", near)
    mid_1 = lax.ppermute(later_1, "dp", middle)
    outer_0 = lax.ppermute(mid_0, "dp", outward)
    inner_0 = lax.ppermute(near_0, "dp", middle)
    moved_0 = place(ops, 0, NOPS, 0, mine_0, near_0, None, own_pick)
    near_1, mid_1, outer_0, inner_0 = lax.optimization_barrier((near_1, mid_1, outer_0, inner_0))
    outer_1 = lax.ppermute(mid_1, "dp", outward)
    inner_1 = lax.ppermute(near_1, "dp", middle)
    far_send_0 = far_pack(far_pick, outer_0, inner_0, moved_0)
    far_got_0 = spread(far_send_0)
    first = place(ops, 0, NOPS // 2, 1, mine_1, near_1, moved_0, far_send_0)
    far_send_1 = far_pack(far_pick, outer_1, inner_1, first)
    far_got_1 = spread(far_send_1)
    second = place(ops, NOPS // 2, NOPS // 2, 1, mine_1, near_1, moved_0, far_send_1)
    sums_0 = plane_sums(0, own_got, far_got_0, first, second, None)
    stats = plane_sums(1, own_got, far_got_1, first, second, sums_0)
    stats = stats.reshape(2, PLANE, 2, SUB, NOPS * blk)
    mine, other = stats[:, :, 0], stats[:, :, 1]

    from_near = lax.ppermute(other, "dp", near)
    pair = jnp.stack([mine, from_near], 1)
    pair = jnp.where(odd, pair[:, ::-1], pair)
    pair = jnp.where(upper, pair[::-1], pair)
    corr = pair.reshape(groups * SUB, NOPS * blk).T.reshape(NOPS, blk, groups * SUB)

    both = jnp.where(upper, stats[::-1], stats).reshape(2, 1, PLANE, 2 * SUB, NOPS * blk)
    back = jnp.broadcast_to(both, (2, 2, PLANE, 2 * SUB, NOPS * blk)).reshape(groups, 2 * SUB, NOPS * blk)
    back = lax.all_to_all(back, "dp", split_axis=0, concat_axis=0, tiled=True)
    back = back.reshape(2, 2, PLANE, 2, SUB, NOPS, blk)
    back = jnp.where(odd, back[:, 1, :, ::-1], back[:, 0])
    returned = jnp.transpose(back, (4, 0, 2, 1, 3, 5)).reshape(NOPS, 1, groups, SUB, blk)
    return (corr, returned)


def shards(intensities, observed, qweights, ops, pick):
    if lax.axis_size("dp") == PLANES * PLANE and lax.axis_size("refl") == 1:
        return shards_by_plane(intensities, observed, qweights, ops, pick)
    return shards_direct(intensities, observed, qweights, ops, pick)


def shards_direct(intensities, observed, qweights, ops, pick):
    blk, width = intensities.shape
    groups = lax.axis_size("dp")
    shares = lax.axis_size("refl")
    local_ops = ops - lax.axis_index("refl") * width
    send, own_w = pack(pick[:, 0], intensities, observed, qweights)
    got = lax.all_to_all(send, "dp", split_axis=0, concat_axis=0, tiled=True)
    moved = move(local_ops, intensities, own_w)
    stats = sums(got.reshape(groups * SLAB, width), moved)
    if shares > 1:
        stats = lax.psum(stats, "refl")
    stats = stats.reshape(2, groups, SLAB, NOPS, LANES)
    full = pearson(stats, blk)
    rows = blk // shares
    if shares > 1:
        full = lax.dynamic_slice_in_dim(full, lax.axis_index("refl") * rows, rows, 3)
    corr = jnp.transpose(full, (2, 3, 0, 1)).reshape(NOPS, rows, groups * SUB)
    back = lax.all_to_all(full, "dp", split_axis=0, concat_axis=0, tiled=True)
    returned = jnp.transpose(back, (2, 0, 1, 3))[:, None]
    return (corr, returned)


def solution(mesh):
    return jax.shard_map(
        shards,
        mesh=mesh,
        in_specs=(
            P("dp", "refl"),
            P("dp", "refl"),
            P("dp", "refl"),
            P(None, "refl"),
            P(None, "dp"),
        ),
        out_specs=(P(None, ("dp", "refl"), None), P(None, "dp", None, None, "refl")),
        check_vma=False,
    )
```

```python
import functools

import jax
import jax.numpy as jnp
from jax import lax
from jax.experimental import pallas as pl
from jax.experimental.pallas import tpu as pltpu
from jax.sharding import PartitionSpec as P

SUB = 4
NOPS = 4
LANES = 128
SLAB = 2 * SUB
VMEM_LIMIT = 56 * 1024 * 1024
PLANES = 4
PLANE = 8
UNROLL = 64
HALVES = 2


def params():
    return pltpu.CompilerParams(vmem_limit_bytes=VMEM_LIMIT)


def pack_kernel(pick_ref, x_ref, obs_ref, qw_ref, send_ref, w_ref, slabs, sems):
    blk, width = x_ref.shape
    step = min(512, width)

    @pl.loop(0, width // step)
    def _(i):
        cols = pl.ds(pl.multiple_of(i * step, step), step)
        wide_w = obs_ref[:, cols].astype(jnp.float32) * qw_ref[:, cols].astype(jnp.float32)
        wide_x = x_ref[:, cols].astype(jnp.float32)
        w_ref[:, cols] = wide_w.astype(jnp.bfloat16)
        for g in range(blk // SUB):
            rows = slice(g * SUB, (g + 1) * SUB)
            slab = jnp.concatenate([wide_x[rows], wide_w[rows]], 0)
            slabs[g, :, cols] = slab.astype(jnp.bfloat16)

    groups = send_ref.shape[0]

    def copy(d):
        return pltpu.make_async_copy(slabs.at[pick_ref[d]], send_ref.at[d], sems.at[d])

    @pl.loop(0, groups)
    def _(d):
        copy(d).start()

    @pl.loop(0, groups)
    def _(d):
        copy(d).wait()


def pack(pick, intensities, observed, qweights):
    blk, width = intensities.shape
    groups = pick.shape[0]
    whole = pl.BlockSpec(memory_space=pltpu.VMEM)
    return pl.pallas_call(
        pack_kernel,
        out_shape=(
            jax.ShapeDtypeStruct((groups, SLAB, width), jnp.bfloat16),
            jax.ShapeDtypeStruct((blk, width), jnp.bfloat16),
        ),
        in_specs=[pl.BlockSpec(memory_space=pltpu.SMEM), whole, whole, whole],
        out_specs=(pl.BlockSpec(memory_space=pl.ANY), whole),
        scratch_shapes=[
            pltpu.VMEM((blk // SUB, SLAB, width), jnp.bfloat16),
            pltpu.SemaphoreType.DMA((groups,)),
        ],
        compiler_params=params(),
        cost_estimate=pl.CostEstimate(
            flops=blk * width * 4, bytes_accessed=(groups * SLAB * 2 + blk * 10) * width, transcendentals=0
        ),
        name="pack",
    )(pick, intensities, observed, qweights)


def move_kernel(ops_ref, x_ref, w_ref, moved_ref, table, target):
    blk, width = x_ref.shape

    @pl.when(pl.program_id(0) == 0)
    def _():
        @pl.loop(0, width // LANES)
        def _(i):
            cols = pl.ds(pl.multiple_of(i * LANES, LANES), LANES)
            wide_x = x_ref[:, cols].astype(jnp.float32)
            wide_w = w_ref[:, cols].astype(jnp.float32)
            wx = (wide_w * wide_x).astype(jnp.bfloat16).astype(jnp.float32)
            wxx = (wide_w * wide_x * wide_x).astype(jnp.bfloat16).astype(jnp.float32)
            stacked = jnp.concatenate([wide_w, wx, wxx, jnp.zeros((LANES - 3 * blk, LANES), jnp.float32)], 0)
            table[cols, :] = stacked.T

    unroll = 16

    @pl.loop(0, width // unroll)
    def _(i):
        base = pl.multiple_of(i * unroll, unroll)
        for j in range(unroll):
            to = ops_ref[0, 0, base + j]
            target[pl.ds(to, 1), :] = table[pl.ds(base + j, 1), :]

    step = min(512, width)

    @pl.loop(0, width // step)
    def _(i):
        rows = pl.ds(pl.multiple_of(i * step, step), step)
        moved_ref[rows, :] = target[rows, :].astype(jnp.bfloat16)


def move(local_ops, intensities, own_w):
    blk, width = intensities.shape
    whole = pl.BlockSpec(memory_space=pltpu.VMEM)
    return pl.pallas_call(
        move_kernel,
        grid=(NOPS,),
        out_shape=jax.ShapeDtypeStruct((width, NOPS * LANES), jnp.bfloat16),
        in_specs=[
            pl.BlockSpec((1, 1, width), lambda k: (k, 0, 0), memory_space=pltpu.SMEM),
            whole,
            whole,
        ],
        out_specs=pl.BlockSpec((width, LANES), lambda k: (0, k)),
        scratch_shapes=[
            pltpu.VMEM((width, LANES), jnp.float32),
            pltpu.VMEM((width, LANES), jnp.float32),
        ],
        compiler_params=params(),
        cost_estimate=pl.CostEstimate(
            flops=0, bytes_accessed=NOPS * width * LANES * 100, transcendentals=0
        ),
        name="move",
    )(local_ops[:, None, :], intensities, own_w)


def sums_kernel(got_ref, moved_ref, out_ref):
    rows, depth = got_ref.shape
    step = min(512, depth)

    @pl.when(pl.program_id(0) == 0)
    def _():
        out_ref[...] = jnp.zeros_like(out_ref)

    is_x = lax.broadcasted_iota(jnp.int32, (rows // SLAB, SLAB, step), 1) < SUB

    @pl.loop(0, depth // step)
    def _(i):
        cols = pl.ds(pl.multiple_of(i * step, step), step)
        raw = got_ref[:, cols]
        wide = raw.astype(jnp.float32).reshape(rows // SLAB, SLAB, step)
        product = wide * pltpu.roll(wide, SUB, 1)
        second = jnp.where(is_x, product * wide, product)
        second = second.reshape(rows, step).astype(jnp.bfloat16)
        right = moved_ref[cols, :]
        out_ref[0] += jnp.dot(raw, right, preferred_element_type=jnp.float32)
        out_ref[1] += jnp.dot(second, right, preferred_element_type=jnp.float32)


def sums(got, moved):
    rows, width = got.shape
    depth = min(2048, width)
    return pl.pallas_call(
        sums_kernel,
        grid=(width // depth,),
        out_shape=jax.ShapeDtypeStruct((2, rows, moved.shape[1]), jnp.float32),
        in_specs=[
            pl.BlockSpec((rows, depth), lambda i: (0, i)),
            pl.BlockSpec((depth, moved.shape[1]), lambda i: (i, 0)),
        ],
        out_specs=pl.BlockSpec((2, rows, moved.shape[1]), lambda i: (0, 0, 0)),
        compiler_params=params(),
        cost_estimate=pl.CostEstimate(
            flops=4 * rows * width * moved.shape[1],
            bytes_accessed=2 * width * (rows + moved.shape[1]),
            transcendentals=0,
        ),
        name="sums",
    )(got, moved)


def pearson(share, blk):
    first, second = share[0], share[1]
    total_w = first[:, SUB:, :, :blk]
    sum_x = first[:, SUB:, :, blk : 2 * blk]
    sum_xx = first[:, SUB:, :, 2 * blk : 3 * blk]
    sum_y = second[:, SUB:, :, :blk]
    sum_xy = second[:, SUB:, :, blk : 2 * blk]
    sum_yy = second[:, :SUB, :, :blk]
    numer = total_w * sum_xy - sum_x * sum_y
    var_x = jnp.maximum(total_w * sum_xx - sum_x * sum_x, 0.05 * total_w * sum_xx)
    var_y = jnp.maximum(total_w * sum_yy - sum_y * sum_y, 0.05 * total_w * sum_yy)
    return numer / jnp.sqrt(var_x * var_y)


def weigh_kernel(x_ref, obs_ref, qw_ref, out_ref):
    blk = x_ref.shape[0]
    weights = obs_ref[...].astype(jnp.float32) * qw_ref[...].astype(jnp.float32)
    out_ref[:blk, :] = x_ref[...]
    out_ref[blk:, :] = weights.astype(jnp.bfloat16)


def weigh(x, observed, qweights, part):
    blk, width = x.shape
    depth = min(2048, width // HALVES)
    count = width // HALVES // depth
    spec = pl.BlockSpec((blk, depth), lambda i: (0, part * count + i))
    return pl.pallas_call(
        weigh_kernel,
        grid=(count,),
        out_shape=jax.ShapeDtypeStruct((2 * blk, width // HALVES), jnp.bfloat16),
        in_specs=[spec] * 3,
        out_specs=pl.BlockSpec((2 * blk, depth), lambda i: (0, i)),
        compiler_params=params(),
        cost_estimate=pl.CostEstimate(
            flops=blk * width, bytes_accessed=blk * width * 12 // HALVES, transcendentals=0
        ),
        name="weigh",
    )(x, observed, qweights)


def fill_slabs(slabs, xw_ref, offset):
    blk, width = xw_ref.shape[0] // 2, xw_ref.shape[1]
    step = min(512, width)

    @pl.loop(0, width // step)
    def _(i):
        start = pl.multiple_of(i * step, step)
        wide = xw_ref[:, pl.ds(start, step)].astype(jnp.float32)
        for g in range(blk // SUB):
            rows = slice(g * SUB, (g + 1) * SUB)
            slab = jnp.concatenate([wide[:blk][rows], wide[blk:][rows]], 0)
            slabs[g, :, pl.ds(offset + start, step)] = slab.astype(jnp.bfloat16)


def send_slabs(slabs, pick_ref, send_ref, sems):
    mine = lax.div(lax.axis_index("dp"), PLANE)
    partner = mine + 1 - 2 * lax.rem(mine, 2)
    copies = []
    for c in range(PLANE):
        for t, plane in enumerate((mine, partner)):
            group = pick_ref[plane * PLANE + c]
            copies.append(pltpu.make_async_copy(slabs.at[group], send_ref.at[c, t], sems.at[c, t]))
    for copy in copies:
        copy.start()
    for copy in copies:
        copy.wait()


def own_pack_kernel(pick_ref, *refs):
    halves, (send_ref, slabs, sems) = refs[:HALVES], refs[HALVES:]
    for part, ref in enumerate(halves):
        fill_slabs(slabs, ref, part * ref.shape[1])
    send_slabs(slabs, pick_ref, send_ref, sems)


def far_pack_kernel(pick_ref, outer_ref, inner_ref, after_ref, send_ref, slabs, sems):
    plane = lax.div(lax.axis_index("dp"), PLANE)
    inner = (plane == 1) | (plane == 2)

    @pl.when(inner)
    def _():
        fill_slabs(slabs, inner_ref, 0)

    @pl.when(jnp.logical_not(inner))
    def _():
        fill_slabs(slabs, outer_ref, 0)

    send_slabs(slabs, pick_ref, send_ref, sems)


def pack_call(kernel, name, specs, blk, width, *operands):
    return pl.pallas_call(
        kernel,
        out_shape=jax.ShapeDtypeStruct((PLANE, 2, SLAB, width), jnp.bfloat16),
        in_specs=[pl.BlockSpec(memory_space=pltpu.SMEM)] + specs,
        out_specs=pl.BlockSpec(memory_space=pl.ANY),
        scratch_shapes=[pltpu.VMEM((blk // SUB, SLAB, width), jnp.bfloat16), pltpu.SemaphoreType.DMA((PLANE, 2))],
        compiler_params=params(),
        cost_estimate=pl.CostEstimate(
            flops=blk * width * 4, bytes_accessed=(PLANE * 2 * SLAB * 2 + blk * 4) * width, transcendentals=0
        ),
        name=name,
    )(*operands)


def own_pack(pick, halves):
    rows, width = halves[0].shape
    specs = [pl.BlockSpec(memory_space=pltpu.VMEM)] * HALVES
    return pack_call(own_pack_kernel, "own_pack", specs, rows // 2, HALVES * width, pick, *halves)


def far_pack(pick, outer, inner, after):
    rows, width = outer.shape
    specs = [pl.BlockSpec(memory_space=pltpu.VMEM)] * 2 + [pl.BlockSpec(memory_space=pl.ANY)]
    return pack_call(far_pack_kernel, "far_pack", specs, rows // 2, width, pick, outer, inner, after)


def place_kernel(joined, ops_ref, *refs):
    blocks, refs = refs[: 2 * HALVES], refs[2 * HALVES :]
    other_ref, outs, (table, target) = refs[0], refs[2 if joined else 1 : -2], refs[-2:]
    rows, depth = blocks[0].shape
    blk = rows // 2
    width = target.shape[0]
    chunks = width // HALVES // depth
    step = min(512, width)
    size = min(256, depth)

    def fill(mine_ref, near_ref):
        diagonal = lax.broadcasted_iota(jnp.int32, (size, size), 0) == lax.broadcasted_iota(
            jnp.int32, (size, size), 1
        )
        identity = jnp.where(diagonal, 1.0, 0.0).astype(jnp.bfloat16)
        for i in range(depth // size):
            cols = slice(i * size, (i + 1) * size)
            both = [mine_ref[:blk, cols], near_ref[:blk, cols], mine_ref[blk:, cols], near_ref[blk:, cols]]
            table[cols, :] = lax.dot_general(
                identity,
                jnp.concatenate(both, 0),
                (((1,), (1,)), ((), ())),
                preferred_element_type=jnp.float32,
            )

    for part in range(HALVES):

        @pl.when(lax.div(pl.program_id(0), chunks) == part)
        def _():
            fill(blocks[part], blocks[HALVES + part])

    @pl.loop(0, depth // UNROLL)
    def _(i):
        base = pl.multiple_of(i * UNROLL, UNROLL)
        for j in range(UNROLL):
            target[pl.ds(ops_ref[0, 0, base + j], 1), :] = table[pl.ds(base + j, 1), :]

    @pl.when(pl.program_id(0) == pl.num_programs(0) - 1)
    def _():
        lane = lax.broadcasted_iota(jnp.int32, (step, LANES), 1)
        first = lax.rem(lane, 2 * blk) < blk

        @pl.loop(0, width // step)
        def _(i):
            here = pl.ds(pl.multiple_of(i * step, step), step)
            values = target[here, :]
            if joined:
                earlier = other_ref[here, :].astype(jnp.float32)
                keep = jnp.where(first, earlier, pltpu.roll(values, blk, 1))
                give = jnp.where(first, pltpu.roll(earlier, LANES - blk, 1), values)
                outs[0][here, :] = keep.astype(jnp.bfloat16)
                outs[1][here, :] = give.astype(jnp.bfloat16)
            else:
                outs[0][here, :] = values.astype(jnp.bfloat16)


def place(ops, which, mine, near, earlier, after, weight):
    width = ops.shape[2]
    rows, span = mine[0].shape
    depth = min(2048, span)
    chunks = span // depth
    some = [
        pl.BlockSpec((rows, depth), lambda i, part=part: (0, jnp.clip(i - part * chunks, 0, chunks - 1)))
        for part in range(HALVES)
    ]
    anywhere = pl.BlockSpec(memory_space=pl.ANY)
    whole = pl.BlockSpec((width, LANES), lambda i: (0, 0))
    joined = earlier is not None
    count = 2 if joined else 1
    outs = pl.pallas_call(
        functools.partial(place_kernel, joined),
        grid=(HALVES * chunks,),
        out_shape=(jax.ShapeDtypeStruct((width, LANES), jnp.bfloat16),) * count,
        in_specs=[
            pl.BlockSpec((1, 1, depth), lambda i: (which, 0, i), memory_space=pltpu.SMEM),
            *some,
            *some,
            whole if joined else anywhere,
            *([anywhere] if joined else []),
        ],
        out_specs=(whole,) * count,
        scratch_shapes=[pltpu.VMEM((depth, LANES), jnp.float32), pltpu.VMEM((width, LANES), jnp.float32)],
        compiler_params=params(),
        cost_estimate=pl.CostEstimate(flops=0, bytes_accessed=weight * width * LANES, transcendentals=0),
        name="place",
    )(ops, *mine, *near, *((earlier, after) if joined else (after,)))
    return outs if joined else outs[0]


def ratio(total_w, sum_x, sum_xx, sum_y, sum_xy, sum_yy):
    numer = total_w * sum_xy - sum_x * sum_y
    var_x = jnp.maximum(total_w * sum_xx - sum_x * sum_x, 0.05 * total_w * sum_xx)
    var_y = jnp.maximum(total_w * sum_yy - sum_y * sum_y, 0.05 * total_w * sum_yy)
    return numer / jnp.sqrt(var_x * var_y)


def plane_sums_kernel(begun, ended, own_ref, far_ref, *refs):
    moved_refs, (before_ref, *outs) = refs[:4], refs[4:]
    acc = outs[-1]
    rows, depth = own_ref.shape
    step = min(1024, depth)
    half = LANES // 2
    slabs = rows // SLAB // 2

    @pl.when(pl.program_id(0) == 0)
    def _():
        if begun:
            acc[...] = before_ref[...]
        else:
            acc[...] = jnp.zeros_like(acc)

    for i in range(depth // step):
        cols = slice(i * step, (i + 1) * step)
        is_x = lax.broadcasted_iota(jnp.int32, (slabs, SLAB, step), 1) < SUB
        weights, products = ([], []), ([], [])
        for ref in (own_ref, far_ref):
            full = ref[:, cols].astype(jnp.float32).reshape(slabs, 2, SLAB, step)
            for t in range(2):
                wide = full[:, t]
                rolled = pltpu.roll(wide, SUB, 1)
                product = wide * rolled
                both = jnp.where(is_x, product * wide, product)
                products[t].append(both.reshape(slabs * SLAB, step))
                even = rolled.reshape(slabs // 2, 2, SLAB, step)[:, 0]
                odd = wide.reshape(slabs // 2, 2, SLAB, step)[:, 1]
                pair = jnp.where(is_x[: slabs // 2], even, odd)
                weights[t].append(pair.reshape(slabs // 2 * SLAB, step))
        low = lax.broadcasted_iota(jnp.int32, (step, LANES), 1) < half
        for t in range(2):
            linear, square = [], []
            for a in range(2):
                values = moved_refs[2 * t + a][cols, :].astype(jnp.float32)
                swapped = pltpu.roll(values, half, 1)
                product = values * swapped
                linear.append(jnp.where(low, product, values).astype(jnp.bfloat16))
                square.append(product * (values if a == 0 else swapped))
            right = jnp.concatenate(linear + [jnp.where(low, *square).astype(jnp.bfloat16)], 1)
            left = jnp.concatenate(weights[t] + products[t], 0).astype(jnp.bfloat16)
            acc[t] += jnp.dot(left, right, preferred_element_type=jnp.float32)

    if not ended:
        return

    @pl.when(pl.program_id(0) == pl.num_programs(0) - 1)
    def _():
        near_ref, back_ref = outs[0], outs[1]
        count = 2 * slabs * SUB
        tiles = count // SLAB
        top = lax.broadcasted_iota(jnp.int32, (tiles, SLAB, LANES), 1) < SUB
        low = lax.broadcasted_iota(jnp.int32, (count, LANES), 1) < half
        me = lax.axis_index("dp")
        results = []
        for t in range(2):
            ratios = []
            for a in range(2):
                lanes = slice(a * LANES, (a + 1) * LANES)
                with_w = acc[t, :count, lanes]
                with_y = acc[t, count:, lanes].reshape(tiles, 2, SLAB, LANES)
                even, odd = with_y[:, 0], with_y[:, 1]
                y = jnp.where(top, pltpu.roll(even, SUB, 1), odd).reshape(count, LANES)
                yy = jnp.where(top, even, pltpu.roll(odd, SUB, 1)).reshape(count, LANES)
                sum_xx = acc[t, :count, 2 * LANES :]
                if a == 1:
                    sum_xx = pltpu.roll(sum_xx, half, 1)
                ratios.append(
                    ratio(
                        pltpu.roll(with_w, half, 1), with_w, sum_xx, pltpu.roll(y, half, 1), y, pltpu.roll(yy, half, 1)
                    )
                )
            kept, got = ratios
            straight = jnp.where(low, kept, pltpu.roll(got, half, 1))
            crossed = jnp.where(low, got, pltpu.roll(kept, half, 1))
            results.append(jnp.where(lax.rem(me, 2) == 0, straight, crossed))
        mine, near = results
        near_ref[...] = near
        back_ref[0] = mine
        back_ref[1] = near


def plane_sums(part, own, far, moved, before):
    rows, width = far.shape
    depth = min(2048, width)
    chunks = width // depth
    begun, ended = before is not None, part == HALVES - 1
    total = (2, 2 * rows * 3 // 4, 3 * LANES)
    count = rows // 2
    placed = pl.BlockSpec((depth, LANES), lambda i: (part * chunks + i, 0))
    entire = pl.BlockSpec(total, lambda i: (0, 0, 0))
    if ended:
        shapes = ((count, LANES), (2, count, LANES))
        out_specs = (pl.BlockSpec(shapes[0], lambda i: (0, 0)), pl.BlockSpec(shapes[1], lambda i: (0, 0, 0)))
    else:
        shapes, out_specs = (total,), (entire,)
    outs = pl.pallas_call(
        functools.partial(plane_sums_kernel, begun, ended),
        grid=(chunks,),
        out_shape=tuple(jax.ShapeDtypeStruct(shape, jnp.float32) for shape in shapes),
        in_specs=[
            pl.BlockSpec((rows, depth), lambda i: (0, part * chunks + i)),
            pl.BlockSpec((rows, depth), lambda i: (0, i)),
            placed,
            placed,
            placed,
            placed,
            entire if begun else pl.BlockSpec(memory_space=pl.ANY),
        ],
        out_specs=out_specs,
        scratch_shapes=[pltpu.VMEM(total, jnp.float32)] if ended else [],
        compiler_params=params(),
        cost_estimate=pl.CostEstimate(
            flops=18 * rows * width * LANES,
            bytes_accessed=width * (4 * rows + 8 * LANES),
            transcendentals=0,
        ),
        name="plane_sums",
    )(own, far, *moved, before if begun else far)
    return outs if ended else outs[0]


def shards_by_plane(intensities, observed, qweights, ops, pick):
    blk = intensities.shape[0]
    groups = PLANES * PLANE
    swap = [(i, i ^ 1) for i in range(groups)]
    beside = [(i, i ^ PLANE) for i in range(groups)]
    across = [(i, i ^ (2 * PLANE)) for i in range(groups)]
    middle = [(i, 3 * PLANE + 2 * (i % PLANE) - i) for i in range(PLANE, 3 * PLANE)]
    outward = [(i, i - PLANE if i < 2 * PLANE else i + PLANE) for i in range(PLANE, 3 * PLANE)]
    rings = [[z * PLANE + c for c in range(PLANE)] for z in range(PLANES)]
    plane = lax.axis_index("dp") // PLANE
    odd, upper = plane % 2 == 1, plane >= 2

    def spread(send):
        got = lax.all_to_all(send, "dp", split_axis=0, concat_axis=0, axis_index_groups=rings, tiled=True)
        return got.reshape(PLANE * 2 * SLAB, send.shape[-1])

    own_pick = pick[:, 0]
    core = lax.axis_index("dp") % 2
    ops = lax.dynamic_slice_in_dim(ops, core * (NOPS // 2), NOPS // 2, 0)[:, None, :]
    mine = [weigh(intensities, observed, qweights, part) for part in range(HALVES)]
    near = [lax.ppermute(rows, "dp", beside) for rows in mine]
    mid = [lax.ppermute(rows, "dp", middle) for rows in mine]
    other = [lax.ppermute(rows, "dp", swap) for rows in mine]
    far_pick = lax.ppermute(own_pick, "dp", across)

    own_send = own_pack(own_pick, mine)
    own_send, other = lax.optimization_barrier((own_send, other))
    own_got = spread(own_send)
    placed = place(ops, 0, mine, other, None, own_pick, 4)
    keep, give = place(ops, 1, mine, other, placed, own_pick, 4)
    own_moved = [keep, lax.ppermute(give, "dp", swap)]

    near, mid, far_pick, keep = lax.optimization_barrier((near, mid, far_pick, keep))
    own_moved[0] = keep
    near_other = [lax.ppermute(rows, "dp", swap) for rows in near]
    outer_0 = lax.ppermute(mid[0], "dp", outward)
    inner_0 = lax.ppermute(near[0], "dp", middle)
    placed = place(ops, 0, near, near_other, None, own_got, 32)
    outer_0, inner_0, mid_1, near_1 = lax.optimization_barrier((outer_0, inner_0, mid[1], near[1]))
    outer_1 = lax.ppermute(mid_1, "dp", outward)
    inner_1 = lax.ppermute(near_1, "dp", middle)
    far_send_0 = far_pack(far_pick, outer_0, inner_0, placed)
    far_got_0 = spread(far_send_0)
    keep, give = place(ops, 1, near, near_other, placed, far_send_0, 32)
    far_send_1 = far_pack(far_pick, outer_1, inner_1, keep)
    moved = own_moved + [keep, lax.ppermute(give, "dp", swap)]
    far_got_1 = spread(far_send_1)
    sums = plane_sums(0, own_got, far_got_0, moved, None)
    theirs, both = plane_sums(1, own_got, far_got_1, moved, sums)
    both = both.reshape(2, 2, PLANE, SUB, NOPS * blk)

    from_near = lax.ppermute(theirs, "dp", beside).reshape(2, PLANE, SUB, NOPS * blk)
    pair = jnp.stack([both[0], from_near], 1)
    pair = jnp.where(odd, pair[:, ::-1], pair)
    pair = jnp.where(upper, pair[::-1], pair)
    corr = pair.reshape(groups * SUB, NOPS * blk).T.reshape(NOPS, blk, groups * SUB)

    both = jnp.transpose(both, (1, 2, 0, 3, 4))
    both = jnp.where(upper, both[::-1], both).reshape(2, 1, PLANE, 2 * SUB, NOPS * blk)
    back = jnp.broadcast_to(both, (2, 2, PLANE, 2 * SUB, NOPS * blk)).reshape(groups, 2 * SUB, NOPS * blk)
    back = lax.all_to_all(back, "dp", split_axis=0, concat_axis=0, tiled=True)
    back = back.reshape(2, 2, PLANE, 2, SUB, NOPS, blk)
    back = jnp.where(odd, back[:, 1, :, ::-1], back[:, 0])
    returned = jnp.transpose(back, (4, 0, 2, 1, 3, 5)).reshape(NOPS, 1, groups, SUB, blk)
    return (corr, returned)


def shards(intensities, observed, qweights, ops, pick):
    if lax.axis_size("dp") == PLANES * PLANE and lax.axis_size("refl") == 1:
        return shards_by_plane(intensities, observed, qweights, ops, pick)
    return shards_direct(intensities, observed, qweights, ops, pick)


def shards_direct(intensities, observed, qweights, ops, pick):
    blk, width = intensities.shape
    groups = lax.axis_size("dp")
    shares = lax.axis_size("refl")
    local_ops = ops - lax.axis_index("refl") * width
    send, own_w = pack(pick[:, 0], intensities, observed, qweights)
    got = lax.all_to_all(send, "dp", split_axis=0, concat_axis=0, tiled=True)
    moved = move(local_ops, intensities, own_w)
    stats = sums(got.reshape(groups * SLAB, width), moved)
    if shares > 1:
        stats = lax.psum(stats, "refl")
    stats = stats.reshape(2, groups, SLAB, NOPS, LANES)
    full = pearson(stats, blk)
    rows = blk // shares
    if shares > 1:
        full = lax.dynamic_slice_in_dim(full, lax.axis_index("refl") * rows, rows, 3)
    corr = jnp.transpose(full, (2, 3, 0, 1)).reshape(NOPS, rows, groups * SUB)
    back = lax.all_to_all(full, "dp", split_axis=0, concat_axis=0, tiled=True)
    returned = jnp.transpose(back, (2, 0, 1, 3))[:, None]
    return (corr, returned)


def solution(mesh):
    return jax.shard_map(
        shards,
        mesh=mesh,
        in_specs=(
            P("dp", "refl"),
            P("dp", "refl"),
            P("dp", "refl"),
            P(None, "refl"),
            P(None, "dp"),
        ),
        out_specs=(P(None, ("dp", "refl"), None), P(None, "dp", None, None, "refl")),
        check_vma=False,
    )
```

```python
import functools

import jax
import jax.numpy as jnp
from jax import lax
from jax.experimental import pallas as pl
from jax.experimental.pallas import tpu as pltpu
from jax.sharding import PartitionSpec as P

SUB = 4
NOPS = 4
LANES = 128
SLAB = 2 * SUB
MIB = 1024 * 1024
PLANES = 4
PLANE = 8
UNROLL = 64
HALVES = 2


def params(mib=56):
    return pltpu.CompilerParams(vmem_limit_bytes=mib * MIB)


def pack_kernel(pick_ref, x_ref, obs_ref, qw_ref, send_ref, w_ref, slabs, sems):
    blk, width = x_ref.shape
    step = min(512, width)

    @pl.loop(0, width // step)
    def _(i):
        cols = pl.ds(pl.multiple_of(i * step, step), step)
        wide_w = obs_ref[:, cols].astype(jnp.float32) * qw_ref[:, cols].astype(jnp.float32)
        wide_x = x_ref[:, cols].astype(jnp.float32)
        w_ref[:, cols] = wide_w.astype(jnp.bfloat16)
        for g in range(blk // SUB):
            rows = slice(g * SUB, (g + 1) * SUB)
            slab = jnp.concatenate([wide_x[rows], wide_w[rows]], 0)
            slabs[g, :, cols] = slab.astype(jnp.bfloat16)

    groups = send_ref.shape[0]

    def copy(d):
        return pltpu.make_async_copy(slabs.at[pick_ref[d]], send_ref.at[d], sems.at[d])

    @pl.loop(0, groups)
    def _(d):
        copy(d).start()

    @pl.loop(0, groups)
    def _(d):
        copy(d).wait()


def pack(pick, intensities, observed, qweights):
    blk, width = intensities.shape
    groups = pick.shape[0]
    whole = pl.BlockSpec(memory_space=pltpu.VMEM)
    return pl.pallas_call(
        pack_kernel,
        out_shape=(
            jax.ShapeDtypeStruct((groups, SLAB, width), jnp.bfloat16),
            jax.ShapeDtypeStruct((blk, width), jnp.bfloat16),
        ),
        in_specs=[pl.BlockSpec(memory_space=pltpu.SMEM), whole, whole, whole],
        out_specs=(pl.BlockSpec(memory_space=pl.ANY), whole),
        scratch_shapes=[
            pltpu.VMEM((blk // SUB, SLAB, width), jnp.bfloat16),
            pltpu.SemaphoreType.DMA((groups,)),
        ],
        compiler_params=params(),
        cost_estimate=pl.CostEstimate(
            flops=blk * width * 4, bytes_accessed=(groups * SLAB * 2 + blk * 10) * width, transcendentals=0
        ),
        name="pack",
    )(pick, intensities, observed, qweights)


def move_kernel(ops_ref, x_ref, w_ref, moved_ref, table, target):
    blk, width = x_ref.shape

    @pl.when(pl.program_id(0) == 0)
    def _():
        @pl.loop(0, width // LANES)
        def _(i):
            cols = pl.ds(pl.multiple_of(i * LANES, LANES), LANES)
            wide_x = x_ref[:, cols].astype(jnp.float32)
            wide_w = w_ref[:, cols].astype(jnp.float32)
            wx = (wide_w * wide_x).astype(jnp.bfloat16).astype(jnp.float32)
            wxx = (wide_w * wide_x * wide_x).astype(jnp.bfloat16).astype(jnp.float32)
            stacked = jnp.concatenate([wide_w, wx, wxx, jnp.zeros((LANES - 3 * blk, LANES), jnp.float32)], 0)
            table[cols, :] = stacked.T

    unroll = 16

    @pl.loop(0, width // unroll)
    def _(i):
        base = pl.multiple_of(i * unroll, unroll)
        for j in range(unroll):
            to = ops_ref[0, 0, base + j]
            target[pl.ds(to, 1), :] = table[pl.ds(base + j, 1), :]

    step = min(512, width)

    @pl.loop(0, width // step)
    def _(i):
        rows = pl.ds(pl.multiple_of(i * step, step), step)
        moved_ref[rows, :] = target[rows, :].astype(jnp.bfloat16)


def move(local_ops, intensities, own_w):
    blk, width = intensities.shape
    whole = pl.BlockSpec(memory_space=pltpu.VMEM)
    return pl.pallas_call(
        move_kernel,
        grid=(NOPS,),
        out_shape=jax.ShapeDtypeStruct((width, NOPS * LANES), jnp.bfloat16),
        in_specs=[
            pl.BlockSpec((1, 1, width), lambda k: (k, 0, 0), memory_space=pltpu.SMEM),
            whole,
            whole,
        ],
        out_specs=pl.BlockSpec((width, LANES), lambda k: (0, k)),
        scratch_shapes=[
            pltpu.VMEM((width, LANES), jnp.float32),
            pltpu.VMEM((width, LANES), jnp.float32),
        ],
        compiler_params=params(),
        cost_estimate=pl.CostEstimate(
            flops=0, bytes_accessed=NOPS * width * LANES * 100, transcendentals=0
        ),
        name="move",
    )(local_ops[:, None, :], intensities, own_w)


def sums_kernel(got_ref, moved_ref, out_ref):
    rows, depth = got_ref.shape
    step = min(512, depth)

    @pl.when(pl.program_id(0) == 0)
    def _():
        out_ref[...] = jnp.zeros_like(out_ref)

    is_x = lax.broadcasted_iota(jnp.int32, (rows // SLAB, SLAB, step), 1) < SUB

    @pl.loop(0, depth // step)
    def _(i):
        cols = pl.ds(pl.multiple_of(i * step, step), step)
        raw = got_ref[:, cols]
        wide = raw.astype(jnp.float32).reshape(rows // SLAB, SLAB, step)
        product = wide * pltpu.roll(wide, SUB, 1)
        second = jnp.where(is_x, product * wide, product)
        second = second.reshape(rows, step).astype(jnp.bfloat16)
        right = moved_ref[cols, :]
        out_ref[0] += jnp.dot(raw, right, preferred_element_type=jnp.float32)
        out_ref[1] += jnp.dot(second, right, preferred_element_type=jnp.float32)


def sums(got, moved):
    rows, width = got.shape
    depth = min(2048, width)
    return pl.pallas_call(
        sums_kernel,
        grid=(width // depth,),
        out_shape=jax.ShapeDtypeStruct((2, rows, moved.shape[1]), jnp.float32),
        in_specs=[
            pl.BlockSpec((rows, depth), lambda i: (0, i)),
            pl.BlockSpec((depth, moved.shape[1]), lambda i: (i, 0)),
        ],
        out_specs=pl.BlockSpec((2, rows, moved.shape[1]), lambda i: (0, 0, 0)),
        compiler_params=params(),
        cost_estimate=pl.CostEstimate(
            flops=4 * rows * width * moved.shape[1],
            bytes_accessed=2 * width * (rows + moved.shape[1]),
            transcendentals=0,
        ),
        name="sums",
    )(got, moved)


def pearson(share, blk):
    first, second = share[0], share[1]
    total_w = first[:, SUB:, :, :blk]
    sum_x = first[:, SUB:, :, blk : 2 * blk]
    sum_xx = first[:, SUB:, :, 2 * blk : 3 * blk]
    sum_y = second[:, SUB:, :, :blk]
    sum_xy = second[:, SUB:, :, blk : 2 * blk]
    sum_yy = second[:, :SUB, :, :blk]
    numer = total_w * sum_xy - sum_x * sum_y
    var_x = jnp.maximum(total_w * sum_xx - sum_x * sum_x, 0.05 * total_w * sum_xx)
    var_y = jnp.maximum(total_w * sum_yy - sum_y * sum_y, 0.05 * total_w * sum_yy)
    return numer / jnp.sqrt(var_x * var_y)


def weigh_kernel(x_ref, obs_ref, qw_ref, out_ref):
    blk = x_ref.shape[0]
    weights = obs_ref[...].astype(jnp.float32) * qw_ref[...].astype(jnp.float32)
    out_ref[:blk, :] = x_ref[...]
    out_ref[blk:, :] = weights.astype(jnp.bfloat16)


def weigh(x, observed, qweights, part):
    blk, width = x.shape
    depth = min(2048, width // HALVES)
    count = width // HALVES // depth
    spec = pl.BlockSpec((blk, depth), lambda i: (0, part * count + i))
    return pl.pallas_call(
        weigh_kernel,
        grid=(count,),
        out_shape=jax.ShapeDtypeStruct((2 * blk, width // HALVES), jnp.bfloat16),
        in_specs=[spec] * 3,
        out_specs=pl.BlockSpec((2 * blk, depth), lambda i: (0, i)),
        compiler_params=params(16),
        cost_estimate=pl.CostEstimate(
            flops=blk * width, bytes_accessed=blk * width * 12 // HALVES, transcendentals=0
        ),
        name="weigh",
    )(x, observed, qweights)


def fill_slabs(slabs, xw_ref, offset):
    blk, width = xw_ref.shape[0] // 2, xw_ref.shape[1]
    step = min(512, width)

    @pl.loop(0, width // step)
    def _(i):
        start = pl.multiple_of(i * step, step)
        wide = xw_ref[:, pl.ds(start, step)].astype(jnp.float32)
        for g in range(blk // SUB):
            rows = slice(g * SUB, (g + 1) * SUB)
            slab = jnp.concatenate([wide[:blk][rows], wide[blk:][rows]], 0)
            slabs[g, :, pl.ds(offset + start, step)] = slab.astype(jnp.bfloat16)


def send_slabs(slabs, pick_ref, send_ref, sems):
    mine = lax.div(lax.axis_index("dp"), PLANE)
    partner = mine + 1 - 2 * lax.rem(mine, 2)
    copies = []
    for c in range(PLANE):
        for t, plane in enumerate((mine, partner)):
            group = pick_ref[plane * PLANE + c]
            copies.append(pltpu.make_async_copy(slabs.at[group], send_ref.at[c, t], sems.at[c, t]))
    for copy in copies:
        copy.start()
    for copy in copies:
        copy.wait()


def own_pack_kernel(pick_ref, *refs):
    halves, (send_ref, slabs, sems) = refs[:HALVES], refs[HALVES:]
    for part, ref in enumerate(halves):
        fill_slabs(slabs, ref, part * ref.shape[1])
    send_slabs(slabs, pick_ref, send_ref, sems)


def far_pack_kernel(pick_ref, outer_ref, inner_ref, after_ref, send_ref, slabs, sems):
    plane = lax.div(lax.axis_index("dp"), PLANE)
    inner = (plane == 1) | (plane == 2)

    @pl.when(inner)
    def _():
        fill_slabs(slabs, inner_ref, 0)

    @pl.when(jnp.logical_not(inner))
    def _():
        fill_slabs(slabs, outer_ref, 0)

    send_slabs(slabs, pick_ref, send_ref, sems)


def pack_call(kernel, name, specs, blk, width, weight, *operands):
    return pl.pallas_call(
        kernel,
        out_shape=jax.ShapeDtypeStruct((PLANE, 2, SLAB, width), jnp.bfloat16),
        in_specs=[pl.BlockSpec(memory_space=pltpu.SMEM)] + specs,
        out_specs=pl.BlockSpec(memory_space=pl.ANY),
        scratch_shapes=[pltpu.VMEM((blk // SUB, SLAB, width), jnp.bfloat16), pltpu.SemaphoreType.DMA((PLANE, 2))],
        compiler_params=params(16),
        cost_estimate=pl.CostEstimate(
            flops=blk * width * 4, bytes_accessed=weight * (PLANE * 2 * SLAB * 2 + blk * 4) * width, transcendentals=0
        ),
        name=name,
    )(*operands)


def own_pack(pick, halves):
    rows, width = halves[0].shape
    specs = [pl.BlockSpec(memory_space=pltpu.VMEM)] * HALVES
    return pack_call(own_pack_kernel, "own_pack", specs, rows // 2, HALVES * width, 1, pick, *halves)


def far_pack(pick, outer, inner, after):
    rows, width = outer.shape
    specs = [pl.BlockSpec(memory_space=pltpu.VMEM)] * 2 + [pl.BlockSpec(memory_space=pl.ANY)]
    return pack_call(far_pack_kernel, "far_pack", specs, rows // 2, width, 60, pick, outer, inner, after)


def place_kernel(flips, joined, ops_ref, *refs):
    count = len(flips)
    blocks, refs = refs[: 2 * HALVES], refs[2 * HALVES :]
    earlier_ref, refs = refs[0], refs[2 if joined else 1 :]
    outs, tables, targets = refs[: -2 * count], refs[-2 * count : -count], refs[-count:]
    rows, depth = blocks[0].shape
    blk = rows // 2
    width = targets[0].shape[0]
    chunks = width // HALVES // depth
    step = min(512, width)
    size = min(256, depth)

    def fill(one_ref, two_ref):
        diagonal = lax.broadcasted_iota(jnp.int32, (size, size), 0) == lax.broadcasted_iota(
            jnp.int32, (size, size), 1
        )
        identity = jnp.where(diagonal, 1.0, 0.0).astype(jnp.bfloat16)
        for table, flip in zip(tables, flips):
            pair = (two_ref, one_ref) if flip else (one_ref, two_ref)
            for i in range(depth // size):
                cols = slice(i * size, (i + 1) * size)
                four = [ref[:blk, cols] for ref in pair] + [ref[blk:, cols] for ref in pair]
                table[cols, :] = lax.dot_general(
                    identity,
                    jnp.concatenate(four, 0),
                    (((1,), (1,)), ((), ())),
                    preferred_element_type=jnp.float32,
                )

    for part in range(HALVES):

        @pl.when(lax.div(pl.program_id(0), chunks) == part)
        def _():
            fill(blocks[part], blocks[HALVES + part])

    @pl.loop(0, depth // UNROLL)
    def _(i):
        base = pl.multiple_of(i * UNROLL, UNROLL)
        for j in range(UNROLL):
            for k, (table, target) in enumerate(zip(tables, targets)):
                target[pl.ds(ops_ref[k, 0, base + j], 1), :] = table[pl.ds(base + j, 1), :]

    @pl.when(pl.program_id(0) == pl.num_programs(0) - 1)
    def _():
        lane = lax.broadcasted_iota(jnp.int32, (step, LANES), 1)
        first = lax.rem(lane, 2 * blk) < blk

        @pl.loop(0, width // step)
        def _(i):
            here = pl.ds(pl.multiple_of(i * step, step), step)
            values = [target[here, :] for target in targets]
            if joined:
                values.insert(0, earlier_ref[here, :].astype(jnp.float32))
            if len(values) == 2:
                outs[0][here, :] = jnp.where(first, *values).astype(jnp.bfloat16)
                outs[1][here, :] = jnp.where(first, *values[::-1]).astype(jnp.bfloat16)
            else:
                outs[0][here, :] = values[0].astype(jnp.bfloat16)


def place(ops, first, count, one, two, earlier, after, weight):
    width = ops.shape[2]
    rows, span = one[0].shape
    depth = min(2048, span)
    chunks = span // depth
    some = [
        pl.BlockSpec((rows, depth), lambda i, part=part: (0, jnp.clip(i - part * chunks, 0, chunks - 1)))
        for part in range(HALVES)
    ]
    anywhere = pl.BlockSpec(memory_space=pl.ANY)
    whole = pl.BlockSpec((width, LANES), lambda i: (0, 0))
    joined = earlier is not None
    outputs = 2 if joined or count == 2 else 1
    flips = (True,) if joined else (False, True)[:count]
    outs = pl.pallas_call(
        functools.partial(place_kernel, flips, joined),
        grid=(HALVES * chunks,),
        out_shape=(jax.ShapeDtypeStruct((width, LANES), jnp.bfloat16),) * outputs,
        in_specs=[
            pl.BlockSpec((count, 1, depth), lambda i: (first, 0, i), memory_space=pltpu.SMEM),
            *some,
            *some,
            *([whole] if joined else []),
            anywhere,
        ],
        out_specs=(whole,) * outputs,
        scratch_shapes=[pltpu.VMEM((depth, LANES), jnp.float32)] * count
        + [pltpu.VMEM((width, LANES), jnp.float32)] * count,
        compiler_params=params(40),
        cost_estimate=pl.CostEstimate(flops=0, bytes_accessed=weight * width * LANES, transcendentals=0),
        name="place",
    )(ops, *one, *two, *((earlier,) if joined else ()), after)
    return outs if outputs == 2 else outs[0]


def ratio(total_w, sum_x, sum_xx, sum_y, sum_xy, sum_yy):
    numer = total_w * sum_xy - sum_x * sum_y
    var_x = jnp.maximum(total_w * sum_xx - sum_x * sum_x, 0.05 * total_w * sum_xx)
    var_y = jnp.maximum(total_w * sum_yy - sum_y * sum_y, 0.05 * total_w * sum_yy)
    return numer / jnp.sqrt(var_x * var_y)


def plane_sums_kernel(begun, ended, own_ref, far_ref, *refs):
    moved_refs, (before_ref, *outs) = refs[:4], refs[4:]
    acc = outs[-1]
    rows, depth = own_ref.shape
    step = min(1024, depth)
    half = LANES // 2
    slabs = rows // SLAB // 2

    @pl.when(pl.program_id(0) == 0)
    def _():
        if begun:
            acc[...] = before_ref[...]
        else:
            acc[...] = jnp.zeros_like(acc)

    for i in range(depth // step):
        cols = slice(i * step, (i + 1) * step)
        is_x = lax.broadcasted_iota(jnp.int32, (slabs, SLAB, step), 1) < SUB
        weights, products = ([], []), ([], [])
        for ref in (own_ref, far_ref):
            full = ref[:, cols].astype(jnp.float32).reshape(slabs, 2, SLAB, step)
            for t in range(2):
                wide = full[:, t]
                rolled = pltpu.roll(wide, SUB, 1)
                product = wide * rolled
                both = jnp.where(is_x, product * wide, product)
                products[t].append(both.reshape(slabs * SLAB, step))
                even = rolled.reshape(slabs // 2, 2, SLAB, step)[:, 0]
                odd = wide.reshape(slabs // 2, 2, SLAB, step)[:, 1]
                pair = jnp.where(is_x[: slabs // 2], even, odd)
                weights[t].append(pair.reshape(slabs // 2 * SLAB, step))
        low = lax.broadcasted_iota(jnp.int32, (step, LANES), 1) < half
        for t in range(2):
            linear, square = [], []
            for a in range(2):
                values = moved_refs[2 * t + a][cols, :].astype(jnp.float32)
                swapped = pltpu.roll(values, half, 1)
                product = values * swapped
                linear.append(jnp.where(low, product, values).astype(jnp.bfloat16))
                square.append(product * (values if a == 0 else swapped))
            right = jnp.concatenate(linear + [jnp.where(low, *square).astype(jnp.bfloat16)], 1)
            left = jnp.concatenate(weights[t] + products[t], 0).astype(jnp.bfloat16)
            acc[t] += jnp.dot(left, right, preferred_element_type=jnp.float32)

    if not ended:
        return

    @pl.when(pl.program_id(0) == pl.num_programs(0) - 1)
    def _():
        near_ref, back_ref = outs[0], outs[1]
        count = 2 * slabs * SUB
        tiles = count // SLAB
        top = lax.broadcasted_iota(jnp.int32, (tiles, SLAB, LANES), 1) < SUB
        low = lax.broadcasted_iota(jnp.int32, (count, LANES), 1) < half
        early = lax.rem(lax.broadcasted_iota(jnp.int32, (count, LANES), 1), half) < half // 2
        me = lax.axis_index("dp")
        results = []
        for t in range(2):
            ratios = []
            for a in range(2):
                lanes = slice(a * LANES, (a + 1) * LANES)
                with_w = acc[t, :count, lanes]
                with_y = acc[t, count:, lanes].reshape(tiles, 2, SLAB, LANES)
                even, odd = with_y[:, 0], with_y[:, 1]
                y = jnp.where(top, pltpu.roll(even, SUB, 1), odd).reshape(count, LANES)
                yy = jnp.where(top, even, pltpu.roll(odd, SUB, 1)).reshape(count, LANES)
                sum_xx = acc[t, :count, 2 * LANES :]
                if a == 1:
                    sum_xx = pltpu.roll(sum_xx, half, 1)
                ratios.append(
                    ratio(
                        pltpu.roll(with_w, half, 1), with_w, sum_xx, pltpu.roll(y, half, 1), y, pltpu.roll(yy, half, 1)
                    )
                )
            kept, got = ratios
            got = jnp.where(early, pltpu.roll(got, LANES - half // 2, 1), pltpu.roll(got, half // 2, 1))
            straight = jnp.where(low, kept, pltpu.roll(got, half, 1))
            crossed = jnp.where(low, got, pltpu.roll(kept, half, 1))
            results.append(jnp.where(lax.rem(me, 2) == 0, straight, crossed))
        mine, near = results
        near_ref[...] = near
        back_ref[0] = mine
        back_ref[1] = near


def plane_sums(part, own, far, moved, before):
    rows, width = far.shape
    depth = min(2048, width)
    chunks = width // depth
    begun, ended = before is not None, part == HALVES - 1
    total = (2, 2 * rows * 3 // 4, 3 * LANES)
    count = rows // 2
    placed = pl.BlockSpec((depth, LANES), lambda i: (part * chunks + i, 0))
    entire = pl.BlockSpec(total, lambda i: (0, 0, 0))
    if ended:
        shapes = ((count, LANES), (2, count, LANES))
        out_specs = (pl.BlockSpec(shapes[0], lambda i: (0, 0)), pl.BlockSpec(shapes[1], lambda i: (0, 0, 0)))
    else:
        shapes, out_specs = (total,), (entire,)
    outs = pl.pallas_call(
        functools.partial(plane_sums_kernel, begun, ended),
        grid=(chunks,),
        out_shape=tuple(jax.ShapeDtypeStruct(shape, jnp.float32) for shape in shapes),
        in_specs=[
            pl.BlockSpec((rows, depth), lambda i: (0, part * chunks + i)),
            pl.BlockSpec((rows, depth), lambda i: (0, i)),
            placed,
            placed,
            placed,
            placed,
            entire if begun else pl.BlockSpec(memory_space=pl.ANY),
        ],
        out_specs=out_specs,
        scratch_shapes=[pltpu.VMEM(total, jnp.float32)] if ended else [],
        compiler_params=params(32),
        cost_estimate=pl.CostEstimate(
            flops=18 * rows * width * LANES,
            bytes_accessed=width * (4 * rows + 8 * LANES),
            transcendentals=0,
        ),
        name="plane_sums",
    )(own, far, *moved, before if begun else far)
    return outs if ended else outs[0]


def shards_by_plane(intensities, observed, qweights, ops, pick):
    blk = intensities.shape[0]
    groups = PLANES * PLANE
    swap = [(i, i ^ 1) for i in range(groups)]
    beside = [(i, i ^ PLANE) for i in range(groups)]
    across = [(i, i ^ (2 * PLANE)) for i in range(groups)]
    middle = [(i, 3 * PLANE + 2 * (i % PLANE) - i) for i in range(PLANE, 3 * PLANE)]
    outward = [(i, i - PLANE if i < 2 * PLANE else i + PLANE) for i in range(PLANE, 3 * PLANE)]
    rings = [[z * PLANE + c for c in range(PLANE)] for z in range(PLANES)]
    plane = lax.axis_index("dp") // PLANE
    odd, upper = plane % 2 == 1, plane >= 2

    def spread(send):
        got = lax.all_to_all(send, "dp", split_axis=0, concat_axis=0, axis_index_groups=rings, tiled=True)
        return got.reshape(PLANE * 2 * SLAB, send.shape[-1])

    own_pick = pick[:, 0]
    core = lax.axis_index("dp") % 2
    ops = lax.dynamic_slice_in_dim(ops, core * (NOPS // 2), NOPS // 2, 0)[:, None, :]
    mine = [weigh(intensities, observed, qweights, part) for part in range(HALVES)]
    near = [lax.ppermute(rows, "dp", beside) for rows in mine]
    mid = [lax.ppermute(rows, "dp", middle) for rows in mine]
    other = [lax.ppermute(rows, "dp", swap) for rows in mine]
    far_pick = lax.ppermute(own_pick, "dp", across)

    own_send = own_pack(own_pick, mine)
    own_send, other = lax.optimization_barrier((own_send, other))
    own_got = spread(own_send)
    keep, give = place(ops, 0, 2, mine, other, None, own_pick, 4)
    own_moved = [keep, lax.ppermute(give, "dp", swap)]

    near, mid, far_pick, keep = lax.optimization_barrier((near, mid, far_pick, keep))
    own_moved[0] = keep
    near_other = [lax.ppermute(rows, "dp", swap) for rows in near]
    outer_0 = lax.ppermute(mid[0], "dp", outward)
    inner_0 = lax.ppermute(near[0], "dp", middle)
    placed = place(ops, 0, 1, near, near_other, None, own_got, 32)
    outer_0, inner_0, mid_1, near_1 = lax.optimization_barrier((outer_0, inner_0, mid[1], near[1]))
    outer_1 = lax.ppermute(mid_1, "dp", outward)
    inner_1 = lax.ppermute(near_1, "dp", middle)
    far_send_0 = far_pack(far_pick, outer_0, inner_0, placed)
    far_got_0 = spread(far_send_0)
    keep, give = place(ops, 1, 1, near, near_other, placed, far_send_0, 32)
    far_send_1 = far_pack(far_pick, outer_1, inner_1, keep)
    moved = own_moved + [keep, lax.ppermute(give, "dp", swap)]
    far_got_1 = spread(far_send_1)
    sums = plane_sums(0, own_got, far_got_0, moved, None)
    theirs, both = plane_sums(1, own_got, far_got_1, moved, sums)
    both = both.reshape(2, 2, PLANE, SUB, NOPS * blk)

    from_near = lax.ppermute(theirs, "dp", beside).reshape(2, PLANE, SUB, NOPS * blk)
    pair = jnp.stack([both[0], from_near], 1)
    pair = jnp.where(odd, pair[:, ::-1], pair)
    pair = jnp.where(upper, pair[::-1], pair)
    corr = pair.reshape(groups * SUB, NOPS * blk).T.reshape(NOPS, blk, groups * SUB)

    both = jnp.transpose(both, (1, 2, 0, 3, 4))
    both = jnp.where(upper, both[::-1], both).reshape(2, 1, PLANE, 2 * SUB, NOPS * blk)
    back = jnp.broadcast_to(both, (2, 2, PLANE, 2 * SUB, NOPS * blk)).reshape(groups, 2 * SUB, NOPS * blk)
    back = lax.all_to_all(back, "dp", split_axis=0, concat_axis=0, tiled=True)
    back = back.reshape(2, 2, PLANE, 2, SUB, NOPS, blk)
    back = jnp.where(odd, back[:, 1, :, ::-1], back[:, 0])
    returned = jnp.transpose(back, (4, 0, 2, 1, 3, 5)).reshape(NOPS, 1, groups, SUB, blk)
    return (corr, returned)


def shards(intensities, observed, qweights, ops, pick):
    if lax.axis_size("dp") == PLANES * PLANE and lax.axis_size("refl") == 1:
        return shards_by_plane(intensities, observed, qweights, ops, pick)
    return shards_direct(intensities, observed, qweights, ops, pick)


def shards_direct(intensities, observed, qweights, ops, pick):
    blk, width = intensities.shape
    groups = lax.axis_size("dp")
    shares = lax.axis_size("refl")
    local_ops = ops - lax.axis_index("refl") * width
    send, own_w = pack(pick[:, 0], intensities, observed, qweights)
    got = lax.all_to_all(send, "dp", split_axis=0, concat_axis=0, tiled=True)
    moved = move(local_ops, intensities, own_w)
    stats = sums(got.reshape(groups * SLAB, width), moved)
    if shares > 1:
        stats = lax.psum(stats, "refl")
    stats = stats.reshape(2, groups, SLAB, NOPS, LANES)
    full = pearson(stats, blk)
    rows = blk // shares
    if shares > 1:
        full = lax.dynamic_slice_in_dim(full, lax.axis_index("refl") * rows, rows, 3)
    corr = jnp.transpose(full, (2, 3, 0, 1)).reshape(NOPS, rows, groups * SUB)
    back = lax.all_to_all(full, "dp", split_axis=0, concat_axis=0, tiled=True)
    returned = jnp.transpose(back, (2, 0, 1, 3))[:, None]
    return (corr, returned)


def solution(mesh):
    return jax.shard_map(
        shards,
        mesh=mesh,
        in_specs=(
            P("dp", "refl"),
            P("dp", "refl"),
            P("dp", "refl"),
            P(None, "refl"),
            P(None, "dp"),
        ),
        out_specs=(P(None, ("dp", "refl"), None), P(None, "dp", None, None, "refl")),
        check_vma=False,
    )
```

```python
import functools

import jax
import jax.numpy as jnp
from jax import lax
from jax.experimental import pallas as pl
from jax.experimental.pallas import tpu as pltpu
from jax.sharding import PartitionSpec as P

SUB = 4
NOPS = 4
LANES = 128
SLAB = 2 * SUB
VMEM_LIMIT = 56 * 1024 * 1024
PLANES = 4
PLANE = 8
UNROLL = 64
BATCH = 16
HALVES = 2


def params():
    return pltpu.CompilerParams(vmem_limit_bytes=VMEM_LIMIT)


def pack_kernel(pick_ref, x_ref, obs_ref, qw_ref, send_ref, w_ref, slabs, sems):
    blk, width = x_ref.shape
    step = min(512, width)

    @pl.loop(0, width // step)
    def _(i):
        cols = pl.ds(pl.multiple_of(i * step, step), step)
        wide_w = obs_ref[:, cols].astype(jnp.float32) * qw_ref[:, cols].astype(jnp.float32)
        wide_x = x_ref[:, cols].astype(jnp.float32)
        w_ref[:, cols] = wide_w.astype(jnp.bfloat16)
        for g in range(blk // SUB):
            rows = slice(g * SUB, (g + 1) * SUB)
            slab = jnp.concatenate([wide_x[rows], wide_w[rows]], 0)
            slabs[g, :, cols] = slab.astype(jnp.bfloat16)

    groups = send_ref.shape[0]

    def copy(d):
        return pltpu.make_async_copy(slabs.at[pick_ref[d]], send_ref.at[d], sems.at[d])

    @pl.loop(0, groups)
    def _(d):
        copy(d).start()

    @pl.loop(0, groups)
    def _(d):
        copy(d).wait()


def pack(pick, intensities, observed, qweights):
    blk, width = intensities.shape
    groups = pick.shape[0]
    whole = pl.BlockSpec(memory_space=pltpu.VMEM)
    return pl.pallas_call(
        pack_kernel,
        out_shape=(
            jax.ShapeDtypeStruct((groups, SLAB, width), jnp.bfloat16),
            jax.ShapeDtypeStruct((blk, width), jnp.bfloat16),
        ),
        in_specs=[pl.BlockSpec(memory_space=pltpu.SMEM), whole, whole, whole],
        out_specs=(pl.BlockSpec(memory_space=pl.ANY), whole),
        scratch_shapes=[
            pltpu.VMEM((blk // SUB, SLAB, width), jnp.bfloat16),
            pltpu.SemaphoreType.DMA((groups,)),
        ],
        compiler_params=params(),
        cost_estimate=pl.CostEstimate(
            flops=blk * width * 4, bytes_accessed=(groups * SLAB * 2 + blk * 10) * width, transcendentals=0
        ),
        name="pack",
    )(pick, intensities, observed, qweights)


def move_kernel(ops_ref, x_ref, w_ref, moved_ref, table, target):
    blk, width = x_ref.shape

    @pl.when(pl.program_id(0) == 0)
    def _():
        @pl.loop(0, width // LANES)
        def _(i):
            cols = pl.ds(pl.multiple_of(i * LANES, LANES), LANES)
            wide_x = x_ref[:, cols].astype(jnp.float32)
            wide_w = w_ref[:, cols].astype(jnp.float32)
            wx = (wide_w * wide_x).astype(jnp.bfloat16).astype(jnp.float32)
            wxx = (wide_w * wide_x * wide_x).astype(jnp.bfloat16).astype(jnp.float32)
            stacked = jnp.concatenate([wide_w, wx, wxx, jnp.zeros((LANES - 3 * blk, LANES), jnp.float32)], 0)
            table[cols, :] = stacked.T

    unroll = 16

    @pl.loop(0, width // unroll)
    def _(i):
        base = pl.multiple_of(i * unroll, unroll)
        for j in range(unroll):
            to = ops_ref[0, 0, base + j]
            target[pl.ds(to, 1), :] = table[pl.ds(base + j, 1), :]

    step = min(512, width)

    @pl.loop(0, width // step)
    def _(i):
        rows = pl.ds(pl.multiple_of(i * step, step), step)
        moved_ref[rows, :] = target[rows, :].astype(jnp.bfloat16)


def move(local_ops, intensities, own_w):
    blk, width = intensities.shape
    whole = pl.BlockSpec(memory_space=pltpu.VMEM)
    return pl.pallas_call(
        move_kernel,
        grid=(NOPS,),
        out_shape=jax.ShapeDtypeStruct((width, NOPS * LANES), jnp.bfloat16),
        in_specs=[
            pl.BlockSpec((1, 1, width), lambda k: (k, 0, 0), memory_space=pltpu.SMEM),
            whole,
            whole,
        ],
        out_specs=pl.BlockSpec((width, LANES), lambda k: (0, k)),
        scratch_shapes=[
            pltpu.VMEM((width, LANES), jnp.float32),
            pltpu.VMEM((width, LANES), jnp.float32),
        ],
        compiler_params=params(),
        cost_estimate=pl.CostEstimate(
            flops=0, bytes_accessed=NOPS * width * LANES * 100, transcendentals=0
        ),
        name="move",
    )(local_ops[:, None, :], intensities, own_w)


def sums_kernel(got_ref, moved_ref, out_ref):
    rows, depth = got_ref.shape
    step = min(512, depth)

    @pl.when(pl.program_id(0) == 0)
    def _():
        out_ref[...] = jnp.zeros_like(out_ref)

    is_x = lax.broadcasted_iota(jnp.int32, (rows // SLAB, SLAB, step), 1) < SUB

    @pl.loop(0, depth // step)
    def _(i):
        cols = pl.ds(pl.multiple_of(i * step, step), step)
        raw = got_ref[:, cols]
        wide = raw.astype(jnp.float32).reshape(rows // SLAB, SLAB, step)
        product = wide * pltpu.roll(wide, SUB, 1)
        second = jnp.where(is_x, product * wide, product)
        second = second.reshape(rows, step).astype(jnp.bfloat16)
        right = moved_ref[cols, :]
        out_ref[0] += jnp.dot(raw, right, preferred_element_type=jnp.float32)
        out_ref[1] += jnp.dot(second, right, preferred_element_type=jnp.float32)


def sums(got, moved):
    rows, width = got.shape
    depth = min(2048, width)
    return pl.pallas_call(
        sums_kernel,
        grid=(width // depth,),
        out_shape=jax.ShapeDtypeStruct((2, rows, moved.shape[1]), jnp.float32),
        in_specs=[
            pl.BlockSpec((rows, depth), lambda i: (0, i)),
            pl.BlockSpec((depth, moved.shape[1]), lambda i: (i, 0)),
        ],
        out_specs=pl.BlockSpec((2, rows, moved.shape[1]), lambda i: (0, 0, 0)),
        compiler_params=params(),
        cost_estimate=pl.CostEstimate(
            flops=4 * rows * width * moved.shape[1],
            bytes_accessed=2 * width * (rows + moved.shape[1]),
            transcendentals=0,
        ),
        name="sums",
    )(got, moved)


def pearson(share, blk):
    first, second = share[0], share[1]
    total_w = first[:, SUB:, :, :blk]
    sum_x = first[:, SUB:, :, blk : 2 * blk]
    sum_xx = first[:, SUB:, :, 2 * blk : 3 * blk]
    sum_y = second[:, SUB:, :, :blk]
    sum_xy = second[:, SUB:, :, blk : 2 * blk]
    sum_yy = second[:, :SUB, :, :blk]
    numer = total_w * sum_xy - sum_x * sum_y
    var_x = jnp.maximum(total_w * sum_xx - sum_x * sum_x, 0.05 * total_w * sum_xx)
    var_y = jnp.maximum(total_w * sum_yy - sum_y * sum_y, 0.05 * total_w * sum_yy)
    return numer / jnp.sqrt(var_x * var_y)


def weigh_kernel(x_ref, obs_ref, qw_ref, out_ref):
    blk = x_ref.shape[0]
    weights = obs_ref[...].astype(jnp.float32) * qw_ref[...].astype(jnp.float32)
    out_ref[:blk, :] = x_ref[...]
    out_ref[blk:, :] = weights.astype(jnp.bfloat16)


def weigh(x, observed, qweights, part):
    blk, width = x.shape
    depth = min(2048, width // HALVES)
    count = width // HALVES // depth
    spec = pl.BlockSpec((blk, depth), lambda i: (0, part * count + i))
    return pl.pallas_call(
        weigh_kernel,
        grid=(count,),
        out_shape=jax.ShapeDtypeStruct((2 * blk, width // HALVES), jnp.bfloat16),
        in_specs=[spec] * 3,
        out_specs=pl.BlockSpec((2 * blk, depth), lambda i: (0, i)),
        compiler_params=params(),
        cost_estimate=pl.CostEstimate(
            flops=blk * width, bytes_accessed=blk * width * 12 // HALVES, transcendentals=0
        ),
        name="weigh",
    )(x, observed, qweights)


def fill_slabs(slabs, xw_ref):
    blk, width = xw_ref.shape[0] // 2, xw_ref.shape[1]
    step = min(512, width)

    @pl.loop(0, width // step)
    def _(i):
        cols = pl.ds(pl.multiple_of(i * step, step), step)
        wide = xw_ref[:, cols].astype(jnp.float32)
        for g in range(blk // SUB):
            rows = slice(g * SUB, (g + 1) * SUB)
            slab = jnp.concatenate([wide[:blk][rows], wide[blk:][rows]], 0)
            slabs[g, :, cols] = slab.astype(jnp.bfloat16)


def send_slabs(slabs, pick_ref, send_ref, source, sems):
    mine = lax.div(lax.axis_index("dp"), PLANE)
    partner = mine + 1 - 2 * lax.rem(mine, 2)
    copies = []
    for c in range(PLANE):
        for t, plane in enumerate((mine, partner)):
            group = pick_ref[plane * PLANE + c]
            copies.append(pltpu.make_async_copy(slabs.at[group], send_ref.at[c, source, t], sems.at[c, t]))
    for copy in copies:
        copy.start()
    for copy in copies:
        copy.wait()


def own_pack_kernel(pick_ref, mine_ref, send_ref, slabs, sems):
    fill_slabs(slabs, mine_ref)
    send_slabs(slabs, pick_ref, send_ref, 0, sems)


def far_pack_kernel(pick_ref, outer_ref, inner_ref, own_ref, after_ref, send_ref, slabs, sems):
    plane = lax.div(lax.axis_index("dp"), PLANE)
    inner = (plane == 1) | (plane == 2)

    @pl.when(inner)
    def _():
        fill_slabs(slabs, inner_ref)

    @pl.when(jnp.logical_not(inner))
    def _():
        fill_slabs(slabs, outer_ref)

    send_slabs(slabs, pick_ref, send_ref, 1, sems)


def pack_call(kernel, name, specs, aliases, blk, width, *operands):
    return pl.pallas_call(
        kernel,
        out_shape=jax.ShapeDtypeStruct((PLANE, 2, 2, SLAB, width), jnp.bfloat16),
        in_specs=[pl.BlockSpec(memory_space=pltpu.SMEM)] + specs,
        out_specs=pl.BlockSpec(memory_space=pl.ANY),
        scratch_shapes=[pltpu.VMEM((blk // SUB, SLAB, width), jnp.bfloat16), pltpu.SemaphoreType.DMA((PLANE, 2))],
        input_output_aliases=aliases,
        compiler_params=params(),
        cost_estimate=pl.CostEstimate(
            flops=blk * width * 4, bytes_accessed=(PLANE * 2 * SLAB * 2 + blk * 4) * width, transcendentals=0
        ),
        name=name,
    )(*operands)


def own_pack(pick, mine):
    rows, width = mine.shape
    return pack_call(own_pack_kernel, "own_pack", [pl.BlockSpec(memory_space=pltpu.VMEM)], {}, rows // 2, width, pick, mine)


def far_pack(pick, outer, inner, send, after):
    rows, width = outer.shape
    specs = [pl.BlockSpec(memory_space=pltpu.VMEM)] * 2 + [pl.BlockSpec(memory_space=pl.ANY)] * 2
    return pack_call(far_pack_kernel, "far_pack", specs, {3: 0}, rows // 2, width, pick, outer, inner, send, after)


def place_kernel(begun, ops_ref, mine_ref, near_ref, before_ref, after_ref, moved_ref, table, target):
    rows, depth = mine_ref.shape
    blk = rows // 2
    width = target.shape[0]
    step = min(512, width)
    part = pl.multiple_of(pl.program_id(1) * depth, depth)

    @pl.when(pl.program_id(0) == 0)
    def _():
        size = min(256, depth)
        diagonal = lax.broadcasted_iota(jnp.int32, (size, size), 0) == lax.broadcasted_iota(
            jnp.int32, (size, size), 1
        )
        identity = jnp.where(diagonal, 1.0, 0.0).astype(jnp.bfloat16)
        for i in range(depth // size):
            cols = slice(i * size, (i + 1) * size)
            both = [mine_ref[:blk, cols], near_ref[:blk, cols], mine_ref[blk:, cols], near_ref[blk:, cols]]
            table[pl.ds(part + i * size, size), :] = lax.dot_general(
                identity,
                jnp.concatenate(both, 0),
                (((1,), (1,)), ((), ())),
                preferred_element_type=jnp.float32,
            )

    if begun:

        @pl.when(pl.program_id(1) == 0)
        def _():
            @pl.loop(0, width // step)
            def _(i):
                here = pl.ds(pl.multiple_of(i * step, step), step)
                target[here, :] = before_ref[here, :].astype(jnp.float32)

    @pl.loop(0, depth // UNROLL)
    def _(i):
        base = pl.multiple_of(i * UNROLL, UNROLL)
        row = pl.multiple_of(part + base, UNROLL)
        for start in range(0, UNROLL, BATCH):
            span = range(start, start + BATCH)
            places = [ops_ref[0, 0, base + j] for j in span]
            values = [table[pl.ds(row + j, 1), :] for j in span]
            for to, value in zip(places, values):
                target[pl.ds(to, 1), :] = value

    @pl.when(pl.program_id(1) == pl.num_programs(1) - 1)
    def _():
        @pl.loop(0, width // step)
        def _(i):
            here = pl.ds(pl.multiple_of(i * step, step), step)
            moved_ref[here, :] = target[here, :].astype(jnp.bfloat16)


def place(ops, first, count, part, mine, near, before, after):
    width = ops.shape[2]
    rows, span = mine.shape
    depth = min(2048, span)
    chunks = span // depth
    some = pl.BlockSpec((rows, depth), lambda k, i: (0, jnp.where(k == 0, i, chunks - 1)))
    anywhere = pl.BlockSpec(memory_space=pl.ANY)
    begun = before is not None
    return pl.pallas_call(
        functools.partial(place_kernel, begun),
        grid=(count, chunks),
        out_shape=jax.ShapeDtypeStruct((width, count * LANES), jnp.bfloat16),
        in_specs=[
            pl.BlockSpec((1, 1, depth), lambda k, i: (first + k, 0, part * chunks + i), memory_space=pltpu.SMEM),
            some,
            some,
            pl.BlockSpec((width, LANES), lambda k, i: (0, first + k)) if begun else anywhere,
            anywhere,
        ],
        out_specs=pl.BlockSpec((width, LANES), lambda k, i: (0, k)),
        scratch_shapes=[pltpu.VMEM((span, LANES), jnp.float32), pltpu.VMEM((width, LANES), jnp.float32)],
        compiler_params=params(),
        cost_estimate=pl.CostEstimate(
            flops=0, bytes_accessed=count * span * LANES * 64, transcendentals=0
        ),
        name="place",
    )(ops, mine, near, before if begun else after, after)


def ratio(total_w, sum_x, sum_xx, sum_y, sum_xy, sum_yy):
    numer = total_w * sum_xy - sum_x * sum_y
    var_x = jnp.maximum(total_w * sum_xx - sum_x * sum_x, 0.05 * total_w * sum_xx)
    var_y = jnp.maximum(total_w * sum_yy - sum_y * sum_y, 0.05 * total_w * sum_yy)
    return numer / jnp.sqrt(var_x * var_y)


def plane_sums_kernel(begun, ended, got_ref, first_ref, second_ref, before_ref, out_ref, *scratch):
    rows, depth = got_ref.shape[0] // 2, got_ref.shape[1]
    step = min(1024, depth)
    half = LANES // 2
    slabs = rows // SLAB
    blk = half // 2

    acc = scratch[0] if ended else out_ref

    @pl.when(pl.program_id(0) == 0)
    def _():
        if begun:
            acc[...] = before_ref[...]
        else:
            acc[...] = jnp.zeros_like(acc)

    for i in range(depth // step):
        cols = slice(i * step, (i + 1) * step)
        is_x = lax.broadcasted_iota(jnp.int32, (2 * slabs, SLAB, step), 1) < SUB
        wide = got_ref[:, cols].astype(jnp.float32).reshape(2 * slabs, SLAB, step)
        rolled = pltpu.roll(wide, SUB, 1)
        product = wide * rolled
        both = jnp.where(is_x, product * wide, product)
        products = both.reshape(2 * rows, step).astype(jnp.bfloat16)
        mine = rolled.reshape(slabs, 2, SLAB, step)[:, 0]
        partner = wide.reshape(slabs, 2, SLAB, step)[:, 1]
        weights = jnp.where(is_x[:slabs], mine, partner).reshape(rows, step).astype(jnp.bfloat16)
        low = lax.broadcasted_iota(jnp.int32, (step, LANES), 1) < half
        linear, square = [], []
        for ref in (first_ref, second_ref):
            even, odd = None, None
            for k in range(2):
                values = ref[cols, k * LANES : (k + 1) * LANES].astype(jnp.float32)
                swapped = pltpu.roll(values, half, 1)
                product = values * swapped
                linear.append(jnp.where(low, product, values).astype(jnp.bfloat16))
                if k == 0:
                    even = product * values
                else:
                    odd = product * swapped
            square.append(jnp.where(low, even, odd).astype(jnp.bfloat16))
        left = jnp.concatenate([weights, products], 0)
        right = jnp.concatenate(linear + square, 1)
        acc[...] += jnp.dot(left, right, preferred_element_type=jnp.float32)

    if not ended:
        return

    @pl.when(pl.program_id(0) == pl.num_programs(0) - 1)
    def _():
        tiles = slabs
        top = lax.broadcasted_iota(jnp.int32, (tiles, SLAB, LANES), 1) < SUB
        lane = lax.broadcasted_iota(jnp.int32, (tiles * SLAB, LANES), 1)
        result = jnp.zeros((tiles * SLAB, LANES), jnp.float32)
        for k in range(NOPS):
            lanes = slice(k * LANES, (k + 1) * LANES)
            squares = slice((NOPS + k // 2) * LANES, (NOPS + k // 2 + 1) * LANES)
            with_w = acc[:rows, lanes]
            with_y = acc[rows:, lanes].reshape(tiles, 2, SLAB, LANES)
            mine, partner = with_y[:, 0], with_y[:, 1]
            y = jnp.where(top, pltpu.roll(mine, SUB, 1), partner).reshape(tiles * SLAB, LANES)
            yy = jnp.where(top, mine, pltpu.roll(partner, SUB, 1)).reshape(tiles * SLAB, LANES)
            sum_xx = acc[:rows, squares]
            if k % 2 == 1:
                sum_xx = pltpu.roll(sum_xx, half, 1)
            both = ratio(
                pltpu.roll(with_w, half, 1), with_w, sum_xx, pltpu.roll(y, half, 1), y, pltpu.roll(yy, half, 1)
            )
            both = jnp.where(
                top.reshape(tiles * SLAB, LANES), both, pltpu.roll(both, LANES - blk, 1)
            )
            moved = both if k == 0 else pltpu.roll(both, k * blk, 1)
            result = jnp.where((lane >= k * blk) & (lane < (k + 1) * blk), moved, result)
        out_ref[...] = result


def plane_sums(part, got, first, second, before):
    rows, width = got.shape[0] // 2, got.shape[1]
    depth = min(4096, width)
    chunks = width // depth
    lanes = (NOPS + NOPS // 2) * LANES
    moved = pl.BlockSpec((depth, 2 * LANES), lambda i: (part * chunks + i, 0))
    begun, ended = before is not None, part == HALVES - 1
    total = (3 * rows, lanes)
    shape = (rows, LANES) if ended else total
    return pl.pallas_call(
        functools.partial(plane_sums_kernel, begun, ended),
        grid=(chunks,),
        out_shape=jax.ShapeDtypeStruct(shape, jnp.float32),
        in_specs=[
            pl.BlockSpec((2 * rows, depth), lambda i: (0, i)),
            moved,
            moved,
            pl.BlockSpec(total, lambda i: (0, 0)) if begun else pl.BlockSpec(memory_space=pl.ANY),
        ],
        out_specs=pl.BlockSpec(shape, lambda i: (0, 0)),
        scratch_shapes=[pltpu.VMEM(total, jnp.float32)] if ended else [],
        compiler_params=params(),
        cost_estimate=pl.CostEstimate(
            flops=6 * rows * width * lanes,
            bytes_accessed=width * (4 * rows + 8 * LANES),
            transcendentals=0,
        ),
        name="plane_sums",
    )(got, first, second, before if begun else got)


def shards_by_plane(intensities, observed, qweights, ops, pick):
    blk = intensities.shape[0]
    groups = PLANES * PLANE
    near = [(i, i ^ PLANE) for i in range(groups)]
    far = [(i, i ^ (2 * PLANE)) for i in range(groups)]
    middle = [(i, 3 * PLANE + 2 * (i % PLANE) - i) for i in range(PLANE, 3 * PLANE)]
    outward = [(i, i - PLANE if i < 2 * PLANE else i + PLANE) for i in range(PLANE, 3 * PLANE)]
    rings = [[z * PLANE + c for c in range(PLANE)] for z in range(PLANES)]
    plane = lax.axis_index("dp") // PLANE
    odd, upper = plane % 2 == 1, plane >= 2

    def spread(send):
        got = lax.all_to_all(send, "dp", split_axis=0, concat_axis=0, axis_index_groups=rings, tiled=True)
        return got.reshape(4 * PLANE * SLAB, send.shape[-1])

    own_pick = pick[:, 0]
    ops = ops[:, None, :]
    mine_0 = weigh(intensities, observed, qweights, 0)
    near_0 = lax.ppermute(mine_0, "dp", near)
    mid_0 = lax.ppermute(mine_0, "dp", middle)
    far_pick = lax.ppermute(own_pick, "dp", far)
    mine_1 = weigh(intensities, observed, qweights, 1)
    own_send_0 = own_pack(own_pick, mine_0)
    own_send_1 = own_pack(own_pick, mine_1)
    near_0, mid_0, far_pick, later_1 = lax.optimization_barrier((near_0, mid_0, far_pick, mine_1))
    near_1 = lax.ppermute(later_1, "dp", near)
    mid_1 = lax.ppermute(later_1, "dp", middle)
    outer_0 = lax.ppermute(mid_0, "dp", outward)
    inner_0 = lax.ppermute(near_0, "dp", middle)
    moved_0 = place(ops, 0, NOPS, 0, mine_0, near_0, None, own_send_1)
    near_1, mid_1, outer_0, inner_0 = lax.optimization_barrier((near_1, mid_1, outer_0, inner_0))
    outer_1 = lax.ppermute(mid_1, "dp", outward)
    inner_1 = lax.ppermute(near_1, "dp", middle)
    send_0 = far_pack(far_pick, outer_0, inner_0, own_send_0, moved_0)
    got_0 = spread(send_0)
    first = place(ops, 0, NOPS // 2, 1, mine_1, near_1, moved_0, send_0)
    send_1 = far_pack(far_pick, outer_1, inner_1, own_send_1, first)
    got_1 = spread(send_1)
    second = place(ops, NOPS // 2, NOPS // 2, 1, mine_1, near_1, moved_0, send_1)
    sums_0 = plane_sums(0, got_0, first, second, None)
    stats = plane_sums(1, got_1, first, second, sums_0)
    stats = jnp.transpose(stats.reshape(PLANE, 2, 2, SUB, NOPS * blk), (1, 0, 2, 3, 4))
    mine, other = stats[:, :, 0], stats[:, :, 1]

    from_near = lax.ppermute(other, "dp", near)
    pair = jnp.stack([mine, from_near], 1)
    pair = jnp.where(odd, pair[:, ::-1], pair)
    pair = jnp.where(upper, pair[::-1], pair)
    corr = pair.reshape(groups * SUB, NOPS * blk).T.reshape(NOPS, blk, groups * SUB)

    both = jnp.where(upper, stats[::-1], stats).reshape(2, 1, PLANE, 2 * SUB, NOPS * blk)
    back = jnp.broadcast_to(both, (2, 2, PLANE, 2 * SUB, NOPS * blk)).reshape(groups, 2 * SUB, NOPS * blk)
    back = lax.all_to_all(back, "dp", split_axis=0, concat_axis=0, tiled=True)
    back = back.reshape(2, 2, PLANE, 2, SUB, NOPS, blk)
    back = jnp.where(odd, back[:, 1, :, ::-1], back[:, 0])
    returned = jnp.transpose(back, (4, 0, 2, 1, 3, 5)).reshape(NOPS, 1, groups, SUB, blk)
    return (corr, returned)


def shards(intensities, observed, qweights, ops, pick):
    if lax.axis_size("dp") == PLANES * PLANE and lax.axis_size("refl") == 1:
        return shards_by_plane(intensities, observed, qweights, ops, pick)
    return shards_direct(intensities, observed, qweights, ops, pick)


def shards_direct(intensities, observed, qweights, ops, pick):
    blk, width = intensities.shape
    groups = lax.axis_size("dp")
    shares = lax.axis_size("refl")
    local_ops = ops - lax.axis_index("refl") * width
    send, own_w = pack(pick[:, 0], intensities, observed, qweights)
    got = lax.all_to_all(send, "dp", split_axis=0, concat_axis=0, tiled=True)
    moved = move(local_ops, intensities, own_w)
    stats = sums(got.reshape(groups * SLAB, width), moved)
    if shares > 1:
        stats = lax.psum(stats, "refl")
    stats = stats.reshape(2, groups, SLAB, NOPS, LANES)
    full = pearson(stats, blk)
    rows = blk // shares
    if shares > 1:
        full = lax.dynamic_slice_in_dim(full, lax.axis_index("refl") * rows, rows, 3)
    corr = jnp.transpose(full, (2, 3, 0, 1)).reshape(NOPS, rows, groups * SUB)
    back = lax.all_to_all(full, "dp", split_axis=0, concat_axis=0, tiled=True)
    returned = jnp.transpose(back, (2, 0, 1, 3))[:, None]
    return (corr, returned)


def solution(mesh):
    return jax.shard_map(
        shards,
        mesh=mesh,
        in_specs=(
            P("dp", "refl"),
            P("dp", "refl"),
            P("dp", "refl"),
            P(None, "refl"),
            P(None, "dp"),
        ),
        out_specs=(P(None, ("dp", "refl"), None), P(None, "dp", None, None, "refl")),
        check_vma=False,
    )
```

```python
import functools

import jax
import jax.numpy as jnp
from jax import lax
from jax.experimental import pallas as pl
from jax.experimental.pallas import tpu as pltpu
from jax.sharding import PartitionSpec as P

SUB = 4
NOPS = 4
LANES = 128
SLAB = 2 * SUB
VMEM_LIMIT = 56 * 1024 * 1024
PLANES = 4
PLANE = 8
UNROLL = 64


def params():
    return pltpu.CompilerParams(vmem_limit_bytes=VMEM_LIMIT)


def pack_kernel(pick_ref, x_ref, obs_ref, qw_ref, send_ref, w_ref, slabs, sems):
    blk, width = x_ref.shape
    step = min(512, width)

    @pl.loop(0, width // step)
    def _(i):
        cols = pl.ds(pl.multiple_of(i * step, step), step)
        wide_w = obs_ref[:, cols].astype(jnp.float32) * qw_ref[:, cols].astype(jnp.float32)
        wide_x = x_ref[:, cols].astype(jnp.float32)
        w_ref[:, cols] = wide_w.astype(jnp.bfloat16)
        for g in range(blk // SUB):
            rows = slice(g * SUB, (g + 1) * SUB)
            slab = jnp.concatenate([wide_x[rows], wide_w[rows]], 0)
            slabs[g, :, cols] = slab.astype(jnp.bfloat16)

    groups = send_ref.shape[0]

    def copy(d):
        return pltpu.make_async_copy(slabs.at[pick_ref[d]], send_ref.at[d], sems.at[d])

    @pl.loop(0, groups)
    def _(d):
        copy(d).start()

    @pl.loop(0, groups)
    def _(d):
        copy(d).wait()


def pack(pick, intensities, observed, qweights):
    blk, width = intensities.shape
    groups = pick.shape[0]
    whole = pl.BlockSpec(memory_space=pltpu.VMEM)
    return pl.pallas_call(
        pack_kernel,
        out_shape=(
            jax.ShapeDtypeStruct((groups, SLAB, width), jnp.bfloat16),
            jax.ShapeDtypeStruct((blk, width), jnp.bfloat16),
        ),
        in_specs=[pl.BlockSpec(memory_space=pltpu.SMEM), whole, whole, whole],
        out_specs=(pl.BlockSpec(memory_space=pl.ANY), whole),
        scratch_shapes=[
            pltpu.VMEM((blk // SUB, SLAB, width), jnp.bfloat16),
            pltpu.SemaphoreType.DMA((groups,)),
        ],
        compiler_params=params(),
        cost_estimate=pl.CostEstimate(
            flops=blk * width * 4, bytes_accessed=(groups * SLAB * 2 + blk * 10) * width, transcendentals=0
        ),
        name="pack",
    )(pick, intensities, observed, qweights)


def move_kernel(ops_ref, x_ref, w_ref, moved_ref, table, target):
    blk, width = x_ref.shape

    @pl.when(pl.program_id(0) == 0)
    def _():
        @pl.loop(0, width // LANES)
        def _(i):
            cols = pl.ds(pl.multiple_of(i * LANES, LANES), LANES)
            wide_x = x_ref[:, cols].astype(jnp.float32)
            wide_w = w_ref[:, cols].astype(jnp.float32)
            wx = (wide_w * wide_x).astype(jnp.bfloat16).astype(jnp.float32)
            wxx = (wide_w * wide_x * wide_x).astype(jnp.bfloat16).astype(jnp.float32)
            stacked = jnp.concatenate([wide_w, wx, wxx, jnp.zeros((LANES - 3 * blk, LANES), jnp.float32)], 0)
            table[cols, :] = stacked.T

    unroll = 16

    @pl.loop(0, width // unroll)
    def _(i):
        base = pl.multiple_of(i * unroll, unroll)
        for j in range(unroll):
            to = ops_ref[0, 0, base + j]
            target[pl.ds(to, 1), :] = table[pl.ds(base + j, 1), :]

    step = min(512, width)

    @pl.loop(0, width // step)
    def _(i):
        rows = pl.ds(pl.multiple_of(i * step, step), step)
        moved_ref[rows, :] = target[rows, :].astype(jnp.bfloat16)


def move(local_ops, intensities, own_w):
    blk, width = intensities.shape
    whole = pl.BlockSpec(memory_space=pltpu.VMEM)
    return pl.pallas_call(
        move_kernel,
        grid=(NOPS,),
        out_shape=jax.ShapeDtypeStruct((width, NOPS * LANES), jnp.bfloat16),
        in_specs=[
            pl.BlockSpec((1, 1, width), lambda k: (k, 0, 0), memory_space=pltpu.SMEM),
            whole,
            whole,
        ],
        out_specs=pl.BlockSpec((width, LANES), lambda k: (0, k)),
        scratch_shapes=[
            pltpu.VMEM((width, LANES), jnp.float32),
            pltpu.VMEM((width, LANES), jnp.float32),
        ],
        compiler_params=params(),
        cost_estimate=pl.CostEstimate(
            flops=0, bytes_accessed=NOPS * width * LANES * 100, transcendentals=0
        ),
        name="move",
    )(local_ops[:, None, :], intensities, own_w)


def sums_kernel(got_ref, moved_ref, out_ref):
    rows, depth = got_ref.shape
    step = min(512, depth)

    @pl.when(pl.program_id(0) == 0)
    def _():
        out_ref[...] = jnp.zeros_like(out_ref)

    is_x = lax.broadcasted_iota(jnp.int32, (rows // SLAB, SLAB, step), 1) < SUB

    @pl.loop(0, depth // step)
    def _(i):
        cols = pl.ds(pl.multiple_of(i * step, step), step)
        raw = got_ref[:, cols]
        wide = raw.astype(jnp.float32).reshape(rows // SLAB, SLAB, step)
        product = wide * pltpu.roll(wide, SUB, 1)
        second = jnp.where(is_x, product * wide, product)
        second = second.reshape(rows, step).astype(jnp.bfloat16)
        right = moved_ref[cols, :]
        out_ref[0] += jnp.dot(raw, right, preferred_element_type=jnp.float32)
        out_ref[1] += jnp.dot(second, right, preferred_element_type=jnp.float32)


def sums(got, moved):
    rows, width = got.shape
    depth = min(2048, width)
    return pl.pallas_call(
        sums_kernel,
        grid=(width // depth,),
        out_shape=jax.ShapeDtypeStruct((2, rows, moved.shape[1]), jnp.float32),
        in_specs=[
            pl.BlockSpec((rows, depth), lambda i: (0, i)),
            pl.BlockSpec((depth, moved.shape[1]), lambda i: (i, 0)),
        ],
        out_specs=pl.BlockSpec((2, rows, moved.shape[1]), lambda i: (0, 0, 0)),
        compiler_params=params(),
        cost_estimate=pl.CostEstimate(
            flops=4 * rows * width * moved.shape[1],
            bytes_accessed=2 * width * (rows + moved.shape[1]),
            transcendentals=0,
        ),
        name="sums",
    )(got, moved)


def pearson(share, blk):
    first, second = share[0], share[1]
    total_w = first[:, SUB:, :, :blk]
    sum_x = first[:, SUB:, :, blk : 2 * blk]
    sum_xx = first[:, SUB:, :, 2 * blk : 3 * blk]
    sum_y = second[:, SUB:, :, :blk]
    sum_xy = second[:, SUB:, :, blk : 2 * blk]
    sum_yy = second[:, :SUB, :, :blk]
    numer = total_w * sum_xy - sum_x * sum_y
    var_x = jnp.maximum(total_w * sum_xx - sum_x * sum_x, 0.05 * total_w * sum_xx)
    var_y = jnp.maximum(total_w * sum_yy - sum_y * sum_y, 0.05 * total_w * sum_yy)
    return numer / jnp.sqrt(var_x * var_y)


def fill_slabs(slabs, x_ref, w_ref):
    blk, width = x_ref.shape
    step = min(512, width)

    @pl.loop(0, width // step)
    def _(i):
        cols = pl.ds(pl.multiple_of(i * step, step), step)
        wide_x = x_ref[:, cols].astype(jnp.float32)
        wide_w = w_ref[:, cols].astype(jnp.float32)
        for g in range(blk // SUB):
            rows = slice(g * SUB, (g + 1) * SUB)
            slab = jnp.concatenate([wide_x[rows], wide_w[rows]], 0)
            slabs[g, :, cols] = slab.astype(jnp.bfloat16)


def send_slabs(slabs, pick_ref, send_ref, sems):
    mine = lax.div(lax.axis_index("dp"), PLANE)
    partner = mine + 1 - 2 * lax.rem(mine, 2)
    copies = []
    for c in range(PLANE):
        for t, plane in enumerate((mine, partner)):
            group = pick_ref[plane * PLANE + c]
            copies.append(pltpu.make_async_copy(slabs.at[group], send_ref.at[c, t], sems.at[c, t]))
    for copy in copies:
        copy.start()
    for copy in copies:
        copy.wait()


def own_pack_kernel(pick_ref, x_ref, w_ref, send_ref, slabs, sems):
    fill_slabs(slabs, x_ref, w_ref)
    send_slabs(slabs, pick_ref, send_ref, sems)


def far_pack_kernel(pick_ref, xo_ref, wo_ref, xi_ref, wi_ref, after_ref, send_ref, x_buf, w_buf, slabs, sems, in_sems):
    plane = lax.div(lax.axis_index("dp"), PLANE)
    inner = (plane == 1) | (plane == 2)

    def fetch(x_ref, w_ref):
        copies = (
            pltpu.make_async_copy(x_ref, x_buf, in_sems.at[0]),
            pltpu.make_async_copy(w_ref, w_buf, in_sems.at[1]),
        )
        for copy in copies:
            copy.start()
        for copy in copies:
            copy.wait()

    @pl.when(inner)
    def _():
        fetch(xi_ref, wi_ref)

    @pl.when(jnp.logical_not(inner))
    def _():
        fetch(xo_ref, wo_ref)

    fill_slabs(slabs, x_buf, w_buf)
    send_slabs(slabs, pick_ref, send_ref, sems)


def pack_call(kernel, name, specs, scratch, blk, width, *operands):
    return pl.pallas_call(
        kernel,
        out_shape=jax.ShapeDtypeStruct((PLANE, 2, SLAB, width), jnp.bfloat16),
        in_specs=[pl.BlockSpec(memory_space=pltpu.SMEM)] + specs,
        out_specs=pl.BlockSpec(memory_space=pl.ANY),
        scratch_shapes=scratch
        + [pltpu.VMEM((blk // SUB, SLAB, width), jnp.bfloat16), pltpu.SemaphoreType.DMA((PLANE, 2))],
        compiler_params=params(),
        cost_estimate=pl.CostEstimate(
            flops=blk * width * 4, bytes_accessed=(PLANE * 2 * SLAB * 2 + blk * 4) * width, transcendentals=0
        ),
        name=name,
    )(*operands)


def own_pack(pick, x, w):
    specs = [pl.BlockSpec(memory_space=pltpu.VMEM)] * 2
    return pack_call(own_pack_kernel, "own_pack", specs, [], *x.shape, pick, x, w)


def far_pack(pick, x_outer, w_outer, x_inner, w_inner, after):
    blk, width = x_outer.shape
    buf = pltpu.VMEM((blk, width), jnp.bfloat16)

    def kernel(pick_ref, xo, wo, xi, wi, after_ref, send_ref, x_buf, w_buf, in_sems, slabs, sems):
        far_pack_kernel(pick_ref, xo, wo, xi, wi, after_ref, send_ref, x_buf, w_buf, slabs, sems, in_sems)

    return pack_call(
        kernel, "far_pack", [pl.BlockSpec(memory_space=pl.ANY)] * 5,
        [buf, buf, pltpu.SemaphoreType.DMA((2,))], blk, width,
        pick, x_outer, w_outer, x_inner, w_inner, after,
    )


def place_kernel(ops_ref, x_ref, x1_ref, w_ref, w1_ref, after_ref, moved_ref, table, target):
    depth = x_ref.shape[1]
    width = target.shape[0]
    part = pl.multiple_of(pl.program_id(1) * depth, depth)

    @pl.when(pl.program_id(0) == 0)
    def _():
        step = min(256, depth)
        diagonal = lax.broadcasted_iota(jnp.int32, (step, step), 0) == lax.broadcasted_iota(
            jnp.int32, (step, step), 1
        )
        identity = jnp.where(diagonal, 1.0, 0.0).astype(jnp.bfloat16)
        for i in range(depth // step):
            cols = slice(i * step, (i + 1) * step)
            rows = jnp.concatenate([x_ref[:, cols], x1_ref[:, cols], w_ref[:, cols], w1_ref[:, cols]], 0)
            table[pl.ds(part + i * step, step), :] = lax.dot_general(
                identity, rows, (((1,), (1,)), ((), ())), preferred_element_type=jnp.float32
            )

    @pl.loop(0, depth // UNROLL)
    def _(i):
        base = pl.multiple_of(i * UNROLL, UNROLL)
        row = pl.multiple_of(part + base, UNROLL)
        for j in range(UNROLL):
            to = ops_ref[0, 0, base + j]
            target[pl.ds(to, 1), :] = table[pl.ds(row + j, 1), :]

    @pl.when(pl.program_id(1) == pl.num_programs(1) - 1)
    def _():
        step = min(512, width)

        @pl.loop(0, width // step)
        def _(i):
            rows = pl.ds(pl.multiple_of(i * step, step), step)
            moved_ref[rows, :] = target[rows, :].astype(jnp.bfloat16)


def place(ops, x, x1, w, w1, after):
    count = ops.shape[0]
    blk, width = x.shape
    depth = min(2048, width)
    last = width // depth - 1
    part = pl.BlockSpec((blk, depth), lambda k, i: (0, jnp.where(k == 0, i, last)))
    return pl.pallas_call(
        place_kernel,
        grid=(count, width // depth),
        out_shape=jax.ShapeDtypeStruct((width, count * LANES), jnp.bfloat16),
        in_specs=[
            pl.BlockSpec((1, 1, depth), lambda k, i: (k, 0, i), memory_space=pltpu.SMEM),
            part,
            part,
            part,
            part,
            pl.BlockSpec(memory_space=pl.ANY),
        ],
        out_specs=pl.BlockSpec((width, LANES), lambda k, i: (0, k)),
        scratch_shapes=[pltpu.VMEM((width, LANES), jnp.float32)] * 2,
        compiler_params=params(),
        cost_estimate=pl.CostEstimate(
            flops=0, bytes_accessed=count * width * LANES * 64, transcendentals=0
        ),
        name="place",
    )(ops[:, None, :], x, x1, w, w1, after)


def ratio(total_w, sum_x, sum_xx, sum_y, sum_xy, sum_yy):
    numer = total_w * sum_xy - sum_x * sum_y
    var_x = jnp.maximum(total_w * sum_xx - sum_x * sum_x, 0.05 * total_w * sum_xx)
    var_y = jnp.maximum(total_w * sum_yy - sum_y * sum_y, 0.05 * total_w * sum_yy)
    return numer / jnp.sqrt(var_x * var_y)


def add_sums(acc, got_ref, cols, right):
    rows = got_ref.shape[0]
    slabs = rows // SLAB
    wide = got_ref[:, cols].astype(jnp.float32).reshape(slabs, SLAB, -1)
    is_x = lax.broadcasted_iota(jnp.int32, wide.shape, 1) < SUB
    rolled = pltpu.roll(wide, SUB, 1)
    product = wide * rolled
    products = jnp.where(is_x, product * wide, product).reshape(rows, -1)
    mine = rolled.reshape(slabs // 2, 2, SLAB, -1)[:, 0]
    partner = wide.reshape(slabs // 2, 2, SLAB, -1)[:, 1]
    weights = jnp.where(is_x[: slabs // 2], mine, partner).reshape(rows // 2, -1)
    left = jnp.concatenate([weights, products], 0).astype(jnp.bfloat16)
    acc[...] += jnp.dot(left, right, preferred_element_type=jnp.float32)


def correlations(acc):
    rows = acc.shape[0] // 3
    half = LANES // 2
    blk = half // 2
    tiles = rows // SLAB
    top = lax.broadcasted_iota(jnp.int32, (tiles, SLAB, LANES), 1) < SUB
    lane = lax.broadcasted_iota(jnp.int32, (rows, LANES), 1)
    result = jnp.zeros((rows, LANES), jnp.float32)
    for k in range(NOPS):
        lanes = slice(k * LANES, (k + 1) * LANES)
        squares = slice((NOPS + k // 2) * LANES, (NOPS + k // 2 + 1) * LANES)
        with_w = acc[:rows, lanes]
        with_y = acc[rows:, lanes].reshape(tiles, 2, SLAB, LANES)
        mine, partner = with_y[:, 0], with_y[:, 1]
        y = jnp.where(top, pltpu.roll(mine, SUB, 1), partner).reshape(rows, LANES)
        yy = jnp.where(top, mine, pltpu.roll(partner, SUB, 1)).reshape(rows, LANES)
        sum_xx = acc[:rows, squares]
        if k % 2 == 1:
            sum_xx = pltpu.roll(sum_xx, half, 1)
        both = ratio(
            pltpu.roll(with_w, half, 1), with_w, sum_xx, pltpu.roll(y, half, 1), y, pltpu.roll(yy, half, 1)
        )
        both = jnp.where(top.reshape(rows, LANES), both, pltpu.roll(both, LANES - blk, 1))
        moved = both if k == 0 else pltpu.roll(both, k * blk, 1)
        result = jnp.where((lane >= k * blk) & (lane < (k + 1) * blk), moved, result)
    return result


def own_sums_kernel(got_ref, first_ref, second_ref, out_ref, right_ref, acc):
    depth = got_ref.shape[1]
    step = min(1024, depth)
    half = LANES // 2

    @pl.when(pl.program_id(0) == 0)
    def _():
        acc[...] = jnp.zeros_like(acc)

    low = lax.broadcasted_iota(jnp.int32, (step, LANES), 1) < half
    for i in range(depth // step):
        cols = slice(i * step, (i + 1) * step)
        linear, square = [], []
        for ref in (first_ref, second_ref):
            even, odd = None, None
            for k in range(2):
                values = ref[cols, k * LANES : (k + 1) * LANES].astype(jnp.float32)
                swapped = pltpu.roll(values, half, 1)
                product = values * swapped
                linear.append(jnp.where(low, product, values).astype(jnp.bfloat16))
                if k == 0:
                    even = product * values
                else:
                    odd = product * swapped
            square.append(jnp.where(low, even, odd).astype(jnp.bfloat16))
        right = jnp.concatenate(linear + square, 1)
        right_ref[cols, :] = right
        add_sums(acc, got_ref, cols, right)

    @pl.when(pl.program_id(0) == pl.num_programs(0) - 1)
    def _():
        out_ref[...] = correlations(acc)


def far_sums_kernel(got_ref, right_ref, own_ref, mine_ref, other_ref, back_ref, acc):
    depth = got_ref.shape[1]
    step = min(1024, depth)

    @pl.when(pl.program_id(0) == 0)
    def _():
        acc[...] = jnp.zeros_like(acc)

    for i in range(depth // step):
        cols = slice(i * step, (i + 1) * step)
        add_sums(acc, got_ref, cols, right_ref[cols, :])

    @pl.when(pl.program_id(0) == pl.num_programs(0) - 1)
    def _():
        upper = lax.div(lax.axis_index("dp"), 2 * PLANE)
        count = own_ref.shape[0] // 2
        for part, result in enumerate((own_ref[...], correlations(acc))):
            tiles = result.reshape(PLANE, SLAB, LANES)
            slot = part + upper - 2 * part * upper
            for twin in range(2):
                back_ref[slot, twin] = tiles
            pairs = result.reshape(PLANE // 2, 2, SLAB, LANES)
            even, odd = pairs[:, 0], pairs[:, 1]
            top = lax.broadcasted_iota(jnp.int32, even.shape, 1) < SUB
            here = slice(part * count, (part + 1) * count)
            mine_ref[here, :] = jnp.where(top, even, pltpu.roll(odd, SUB, 1)).reshape(count, LANES)
            other_ref[here, :] = jnp.where(top, pltpu.roll(even, SUB, 1), odd).reshape(count, LANES)


def own_sums(got, first, second):
    rows, width = got.shape
    depth = min(2048, width)
    lanes = (NOPS + NOPS // 2) * LANES
    moved = pl.BlockSpec((depth, 2 * LANES), lambda i: (i, 0))
    return pl.pallas_call(
        own_sums_kernel,
        grid=(width // depth,),
        out_shape=(
            jax.ShapeDtypeStruct((rows // 2, LANES), jnp.float32),
            jax.ShapeDtypeStruct((width, lanes), jnp.bfloat16),
        ),
        in_specs=[pl.BlockSpec((rows, depth), lambda i: (0, i)), moved, moved],
        out_specs=(
            pl.BlockSpec((rows // 2, LANES), lambda i: (0, 0)),
            pl.BlockSpec((depth, lanes), lambda i: (i, 0)),
        ),
        scratch_shapes=[pltpu.VMEM((rows * 3 // 2, lanes), jnp.float32)],
        compiler_params=params(),
        cost_estimate=pl.CostEstimate(
            flops=3 * rows * width * lanes,
            bytes_accessed=2 * width * (rows + 4 * LANES + lanes),
            transcendentals=0,
        ),
        name="own_sums",
    )(got, first, second)


def far_sums(got, right, own):
    rows, width = got.shape
    depth = min(2048, width)
    lanes = right.shape[1]
    shapes = (own.shape, own.shape, (2, 2, PLANE, SLAB, LANES))
    return pl.pallas_call(
        far_sums_kernel,
        grid=(width // depth,),
        out_shape=tuple(jax.ShapeDtypeStruct(shape, jnp.float32) for shape in shapes),
        in_specs=[
            pl.BlockSpec((rows, depth), lambda i: (0, i)),
            pl.BlockSpec((depth, lanes), lambda i: (i, 0)),
            pl.BlockSpec(own.shape, lambda i: (0, 0)),
        ],
        out_specs=tuple(pl.BlockSpec(shape, lambda i, shape=shape: (0,) * len(shape)) for shape in shapes),
        scratch_shapes=[pltpu.VMEM((rows * 3 // 2, lanes), jnp.float32)],
        compiler_params=params(),
        cost_estimate=pl.CostEstimate(
            flops=3 * rows * width * lanes, bytes_accessed=2 * width * (rows + lanes), transcendentals=0
        ),
        name="far_sums",
    )(got, right, own)


def shards_by_plane(intensities, observed, qweights, ops, pick):
    blk, width = intensities.shape
    groups = PLANES * PLANE
    near = [(i, i ^ PLANE) for i in range(groups)]
    far = [(i, i ^ (2 * PLANE)) for i in range(groups)]
    middle = [(i, 3 * PLANE + 2 * (i % PLANE) - i) for i in range(PLANE, 3 * PLANE)]
    outward = [(i, i - PLANE if i < 2 * PLANE else i + PLANE) for i in range(PLANE, 3 * PLANE)]
    rings = [[z * PLANE + c for c in range(PLANE)] for z in range(PLANES)]
    plane = lax.axis_index("dp") // PLANE
    odd, upper = plane % 2 == 1, plane >= 2

    def spread(send):
        got = lax.all_to_all(send, "dp", split_axis=0, concat_axis=0, axis_index_groups=rings, tiled=True)
        return got.reshape(PLANE * 2 * SLAB, width)

    own_pick = pick[:, 0]
    near_x = lax.ppermute(intensities, "dp", near)
    mid_x = lax.ppermute(intensities, "dp", middle)
    far_pick = lax.ppermute(own_pick, "dp", far)
    own_w = (observed.astype(jnp.float32) * qweights.astype(jnp.float32)).astype(jnp.bfloat16)
    near_w = lax.ppermute(own_w, "dp", near)
    mid_w = lax.ppermute(own_w, "dp", middle)
    own_got = spread(own_pack(own_pick, intensities, own_w))
    near_x, mid_x, near_w, mid_w, far_pick = lax.optimization_barrier((near_x, mid_x, near_w, mid_w, far_pick))
    outer_x = lax.ppermute(mid_x, "dp", outward)
    inner_x = lax.ppermute(near_x, "dp", middle)
    outer_w = lax.ppermute(mid_w, "dp", outward)
    inner_w = lax.ppermute(near_w, "dp", middle)
    first = place(ops[:2], intensities, near_x, own_w, near_w, own_pick)
    far_send = far_pack(far_pick, outer_x, outer_w, inner_x, inner_w, first)
    far_got = spread(far_send)
    second = place(ops[2:], intensities, near_x, own_w, near_w, far_send)
    own_corr, right = own_sums(own_got, first, second)
    mine, other, back = far_sums(far_got, right, own_corr)

    from_near = lax.ppermute(other, "dp", near)
    pair = [each.reshape(2, PLANE, SUB, NOPS * blk) for each in (mine, from_near)]
    pair = jnp.stack(pair, 1)
    pair = jnp.where(odd, pair[:, ::-1], pair)
    pair = jnp.where(upper, pair[::-1], pair)
    corr = pair.reshape(groups * SUB, NOPS * blk).T.reshape(NOPS, blk, groups * SUB)

    back = back.reshape(groups, 2 * SUB, NOPS * blk)
    back = lax.all_to_all(back, "dp", split_axis=0, concat_axis=0, tiled=True)
    back = back.reshape(2, 2, PLANE, 2, SUB, NOPS, blk)
    back = jnp.where(odd, back[:, 1, :, ::-1], back[:, 0])
    returned = jnp.transpose(back, (4, 0, 2, 1, 3, 5)).reshape(NOPS, 1, groups, SUB, blk)
    return (corr, returned)


def shards(intensities, observed, qweights, ops, pick):
    if lax.axis_size("dp") == PLANES * PLANE and lax.axis_size("refl") == 1:
        return shards_by_plane(intensities, observed, qweights, ops, pick)
    return shards_direct(intensities, observed, qweights, ops, pick)


def shards_direct(intensities, observed, qweights, ops, pick):
    blk, width = intensities.shape
    groups = lax.axis_size("dp")
    shares = lax.axis_size("refl")
    local_ops = ops - lax.axis_index("refl") * width
    send, own_w = pack(pick[:, 0], intensities, observed, qweights)
    got = lax.all_to_all(send, "dp", split_axis=0, concat_axis=0, tiled=True)
    moved = move(local_ops, intensities, own_w)
    stats = sums(got.reshape(groups * SLAB, width), moved)
    if shares > 1:
        stats = lax.psum(stats, "refl")
    stats = stats.reshape(2, groups, SLAB, NOPS, LANES)
    full = pearson(stats, blk)
    rows = blk // shares
    if shares > 1:
        full = lax.dynamic_slice_in_dim(full, lax.axis_index("refl") * rows, rows, 3)
    corr = jnp.transpose(full, (2, 3, 0, 1)).reshape(NOPS, rows, groups * SUB)
    back = lax.all_to_all(full, "dp", split_axis=0, concat_axis=0, tiled=True)
    returned = jnp.transpose(back, (2, 0, 1, 3))[:, None]
    return (corr, returned)


def solution(mesh):
    return jax.shard_map(
        shards,
        mesh=mesh,
        in_specs=(
            P("dp", "refl"),
            P("dp", "refl"),
            P("dp", "refl"),
            P(None, "refl"),
            P(None, "dp"),
        ),
        out_specs=(P(None, ("dp", "refl"), None), P(None, "dp", None, None, "refl")),
        check_vma=False,
    )
```

```python
import functools

import jax
import jax.numpy as jnp
from jax import lax
from jax.experimental import pallas as pl
from jax.experimental.pallas import tpu as pltpu
from jax.sharding import PartitionSpec as P

SUB = 4
NOPS = 4
LANES = 128
SLAB = 2 * SUB
MIB = 1024 * 1024
PLANES = 4
PLANE = 8
UNROLL = 64
HALVES = 2


def params():
    return pltpu.CompilerParams(vmem_limit_bytes=56 * MIB)


def pack_kernel(pick_ref, x_ref, obs_ref, qw_ref, send_ref, w_ref, slabs, sems):
    blk, width = x_ref.shape
    step = min(512, width)

    @pl.loop(0, width // step)
    def _(i):
        cols = pl.ds(pl.multiple_of(i * step, step), step)
        wide_w = obs_ref[:, cols].astype(jnp.float32) * qw_ref[:, cols].astype(jnp.float32)
        wide_x = x_ref[:, cols].astype(jnp.float32)
        w_ref[:, cols] = wide_w.astype(jnp.bfloat16)
        for g in range(blk // SUB):
            rows = slice(g * SUB, (g + 1) * SUB)
            slab = jnp.concatenate([wide_x[rows], wide_w[rows]], 0)
            slabs[g, :, cols] = slab.astype(jnp.bfloat16)

    groups = send_ref.shape[0]

    def copy(d):
        return pltpu.make_async_copy(slabs.at[pick_ref[d]], send_ref.at[d], sems.at[d])

    @pl.loop(0, groups)
    def _(d):
        copy(d).start()

    @pl.loop(0, groups)
    def _(d):
        copy(d).wait()


def pack(pick, intensities, observed, qweights):
    blk, width = intensities.shape
    groups = pick.shape[0]
    whole = pl.BlockSpec(memory_space=pltpu.VMEM)
    return pl.pallas_call(
        pack_kernel,
        out_shape=(
            jax.ShapeDtypeStruct((groups, SLAB, width), jnp.bfloat16),
            jax.ShapeDtypeStruct((blk, width), jnp.bfloat16),
        ),
        in_specs=[pl.BlockSpec(memory_space=pltpu.SMEM), whole, whole, whole],
        out_specs=(pl.BlockSpec(memory_space=pl.ANY), whole),
        scratch_shapes=[
            pltpu.VMEM((blk // SUB, SLAB, width), jnp.bfloat16),
            pltpu.SemaphoreType.DMA((groups,)),
        ],
        compiler_params=params(),
        cost_estimate=pl.CostEstimate(
            flops=blk * width * 4, bytes_accessed=(groups * SLAB * 2 + blk * 10) * width, transcendentals=0
        ),
        name="pack",
    )(pick, intensities, observed, qweights)


def move_kernel(ops_ref, x_ref, w_ref, moved_ref, table, target):
    blk, width = x_ref.shape

    @pl.when(pl.program_id(0) == 0)
    def _():
        @pl.loop(0, width // LANES)
        def _(i):
            cols = pl.ds(pl.multiple_of(i * LANES, LANES), LANES)
            wide_x = x_ref[:, cols].astype(jnp.float32)
            wide_w = w_ref[:, cols].astype(jnp.float32)
            wx = (wide_w * wide_x).astype(jnp.bfloat16).astype(jnp.float32)
            wxx = (wide_w * wide_x * wide_x).astype(jnp.bfloat16).astype(jnp.float32)
            stacked = jnp.concatenate([wide_w, wx, wxx, jnp.zeros((LANES - 3 * blk, LANES), jnp.float32)], 0)
            table[cols, :] = stacked.T

    unroll = 16

    @pl.loop(0, width // unroll)
    def _(i):
        base = pl.multiple_of(i * unroll, unroll)
        for j in range(unroll):
            to = ops_ref[0, 0, base + j]
            target[pl.ds(to, 1), :] = table[pl.ds(base + j, 1), :]

    step = min(512, width)

    @pl.loop(0, width // step)
    def _(i):
        rows = pl.ds(pl.multiple_of(i * step, step), step)
        moved_ref[rows, :] = target[rows, :].astype(jnp.bfloat16)


def move(local_ops, intensities, own_w):
    blk, width = intensities.shape
    whole = pl.BlockSpec(memory_space=pltpu.VMEM)
    return pl.pallas_call(
        move_kernel,
        grid=(NOPS,),
        out_shape=jax.ShapeDtypeStruct((width, NOPS * LANES), jnp.bfloat16),
        in_specs=[
            pl.BlockSpec((1, 1, width), lambda k: (k, 0, 0), memory_space=pltpu.SMEM),
            whole,
            whole,
        ],
        out_specs=pl.BlockSpec((width, LANES), lambda k: (0, k)),
        scratch_shapes=[
            pltpu.VMEM((width, LANES), jnp.float32),
            pltpu.VMEM((width, LANES), jnp.float32),
        ],
        compiler_params=params(),
        cost_estimate=pl.CostEstimate(
            flops=0, bytes_accessed=NOPS * width * LANES * 100, transcendentals=0
        ),
        name="move",
    )(local_ops[:, None, :], intensities, own_w)


def sums_kernel(got_ref, moved_ref, out_ref):
    rows, depth = got_ref.shape
    step = min(512, depth)

    @pl.when(pl.program_id(0) == 0)
    def _():
        out_ref[...] = jnp.zeros_like(out_ref)

    is_x = lax.broadcasted_iota(jnp.int32, (rows // SLAB, SLAB, step), 1) < SUB

    @pl.loop(0, depth // step)
    def _(i):
        cols = pl.ds(pl.multiple_of(i * step, step), step)
        raw = got_ref[:, cols]
        wide = raw.astype(jnp.float32).reshape(rows // SLAB, SLAB, step)
        product = wide * pltpu.roll(wide, SUB, 1)
        second = jnp.where(is_x, product * wide, product)
        second = second.reshape(rows, step).astype(jnp.bfloat16)
        right = moved_ref[cols, :]
        out_ref[0] += jnp.dot(raw, right, preferred_element_type=jnp.float32)
        out_ref[1] += jnp.dot(second, right, preferred_element_type=jnp.float32)


def sums(got, moved):
    rows, width = got.shape
    depth = min(2048, width)
    return pl.pallas_call(
        sums_kernel,
        grid=(width // depth,),
        out_shape=jax.ShapeDtypeStruct((2, rows, moved.shape[1]), jnp.float32),
        in_specs=[
            pl.BlockSpec((rows, depth), lambda i: (0, i)),
            pl.BlockSpec((depth, moved.shape[1]), lambda i: (i, 0)),
        ],
        out_specs=pl.BlockSpec((2, rows, moved.shape[1]), lambda i: (0, 0, 0)),
        compiler_params=params(),
        cost_estimate=pl.CostEstimate(
            flops=4 * rows * width * moved.shape[1],
            bytes_accessed=2 * width * (rows + moved.shape[1]),
            transcendentals=0,
        ),
        name="sums",
    )(got, moved)


def pearson(share, blk):
    first, second = share[0], share[1]
    total_w = first[:, SUB:, :, :blk]
    sum_x = first[:, SUB:, :, blk : 2 * blk]
    sum_xx = first[:, SUB:, :, 2 * blk : 3 * blk]
    sum_y = second[:, SUB:, :, :blk]
    sum_xy = second[:, SUB:, :, blk : 2 * blk]
    sum_yy = second[:, :SUB, :, :blk]
    numer = total_w * sum_xy - sum_x * sum_y
    var_x = jnp.maximum(total_w * sum_xx - sum_x * sum_x, 0.05 * total_w * sum_xx)
    var_y = jnp.maximum(total_w * sum_yy - sum_y * sum_y, 0.05 * total_w * sum_yy)
    return numer / jnp.sqrt(var_x * var_y)


def weigh_kernel(x_ref, obs_ref, qw_ref, out_ref):
    blk = x_ref.shape[0]
    weights = obs_ref[...].astype(jnp.float32) * qw_ref[...].astype(jnp.float32)
    out_ref[:blk, :] = x_ref[...]
    out_ref[blk:, :] = weights.astype(jnp.bfloat16)


def weigh(x, observed, qweights, part):
    blk, width = x.shape
    depth = min(2048, width // HALVES)
    count = width // HALVES // depth
    spec = pl.BlockSpec((blk, depth), lambda i: (0, part * count + i))
    return pl.pallas_call(
        weigh_kernel,
        grid=(count,),
        out_shape=jax.ShapeDtypeStruct((2 * blk, width // HALVES), jnp.bfloat16),
        in_specs=[spec] * 3,
        out_specs=pl.BlockSpec((2 * blk, depth), lambda i: (0, i)),
        compiler_params=params(),
        cost_estimate=pl.CostEstimate(
            flops=blk * width, bytes_accessed=blk * width * 12 // HALVES, transcendentals=0
        ),
        name="weigh",
    )(x, observed, qweights)


def fill_slabs(slabs, xw_ref, offset):
    blk, width = xw_ref.shape[0] // 2, xw_ref.shape[1]
    step = min(512, width)

    @pl.loop(0, width // step)
    def _(i):
        start = pl.multiple_of(i * step, step)
        wide = xw_ref[:, pl.ds(start, step)].astype(jnp.float32)
        for g in range(blk // SUB):
            rows = slice(g * SUB, (g + 1) * SUB)
            slab = jnp.concatenate([wide[:blk][rows], wide[blk:][rows]], 0)
            slabs[g, :, pl.ds(offset + start, step)] = slab.astype(jnp.bfloat16)


def send_slabs(slabs, pick_ref, send_ref, sems):
    mine = lax.div(lax.axis_index("dp"), PLANE)
    partner = mine + 1 - 2 * lax.rem(mine, 2)
    copies = []
    for c in range(PLANE):
        for t, plane in enumerate((mine, partner)):
            group = pick_ref[plane * PLANE + c]
            copies.append(pltpu.make_async_copy(slabs.at[group], send_ref.at[c, t], sems.at[c, t]))
    for copy in copies:
        copy.start()
    for copy in copies:
        copy.wait()


def own_pack_kernel(pick_ref, *refs):
    halves, (send_ref, slabs, sems) = refs[:HALVES], refs[HALVES:]
    for part, ref in enumerate(halves):
        fill_slabs(slabs, ref, part * ref.shape[1])
    send_slabs(slabs, pick_ref, send_ref, sems)


def far_pack_kernel(pick_ref, *refs):
    outer, inner = refs[:HALVES], refs[HALVES : 2 * HALVES]
    send_ref, slabs, sems = refs[2 * HALVES + 1 :]
    plane = lax.div(lax.axis_index("dp"), PLANE)
    is_inner = (plane == 1) | (plane == 2)

    @pl.when(is_inner)
    def _():
        for part, ref in enumerate(inner):
            fill_slabs(slabs, ref, part * ref.shape[1])

    @pl.when(jnp.logical_not(is_inner))
    def _():
        for part, ref in enumerate(outer):
            fill_slabs(slabs, ref, part * ref.shape[1])

    send_slabs(slabs, pick_ref, send_ref, sems)


def pack_call(kernel, name, specs, blk, width, weight, *operands):
    return pl.pallas_call(
        kernel,
        out_shape=jax.ShapeDtypeStruct((PLANE, 2, SLAB, width), jnp.bfloat16),
        in_specs=[pl.BlockSpec(memory_space=pltpu.SMEM)] + specs,
        out_specs=pl.BlockSpec(memory_space=pl.ANY),
        scratch_shapes=[pltpu.VMEM((blk // SUB, SLAB, width), jnp.bfloat16), pltpu.SemaphoreType.DMA((PLANE, 2))],
        compiler_params=params(),
        cost_estimate=pl.CostEstimate(
            flops=blk * width * 4, bytes_accessed=weight * (PLANE * 2 * SLAB * 2 + blk * 4) * width, transcendentals=0
        ),
        name=name,
    )(*operands)


def own_pack(pick, halves):
    rows, width = halves[0].shape
    specs = [pl.BlockSpec(memory_space=pltpu.VMEM)] * HALVES
    return pack_call(own_pack_kernel, "own_pack", specs, rows // 2, HALVES * width, 1, pick, *halves)


def far_pack(pick, outer, inner, after):
    rows, width = outer[0].shape
    specs = [pl.BlockSpec(memory_space=pltpu.VMEM)] * (2 * HALVES) + [pl.BlockSpec(memory_space=pl.ANY)]
    return pack_call(
        far_pack_kernel, "far_pack", specs, rows // 2, HALVES * width, 1, pick, *outer, *inner, after
    )


def place_kernel(ops_ref, *refs):
    blocks, (after_ref, keep_ref, give_ref, table, *targets) = refs[: 2 * HALVES], refs[2 * HALVES :]
    rows, depth = blocks[0].shape
    blk = rows // 2
    width = targets[0].shape[0]
    chunks = width // HALVES // depth
    step = min(512, width)
    size = min(256, depth)
    now = pl.program_id(1)

    def fill(one_ref, two_ref):
        diagonal = lax.broadcasted_iota(jnp.int32, (size, size), 0) == lax.broadcasted_iota(
            jnp.int32, (size, size), 1
        )
        identity = jnp.where(diagonal, 1.0, 0.0).astype(jnp.bfloat16)
        for i in range(depth // size):
            cols = slice(i * size, (i + 1) * size)
            four = [one_ref[:blk, cols], two_ref[:blk, cols], one_ref[blk:, cols], two_ref[blk:, cols]]
            table[cols, :] = lax.dot_general(
                identity,
                jnp.concatenate(four, 0),
                (((1,), (1,)), ((), ())),
                preferred_element_type=jnp.float32,
            )

    for k, target in enumerate(targets):
        for part in range(HALVES):
            pair = (blocks[part], blocks[HALVES + part])

            @pl.when((pl.program_id(0) == k) & (lax.div(now, chunks) == part))
            def _():
                fill(*(pair if k == 0 else pair[::-1]))

        @pl.when(pl.program_id(0) == k)
        def _():
            @pl.loop(0, depth // UNROLL)
            def _(i):
                base = pl.multiple_of(i * UNROLL, UNROLL)
                for j in range(UNROLL):
                    target[pl.ds(ops_ref[0, 0, base + j], 1), :] = table[pl.ds(base + j, 1), :]

    @pl.when((pl.program_id(0) == pl.num_programs(0) - 1) & (now == pl.num_programs(1) - 1))
    def _():
        lane = lax.broadcasted_iota(jnp.int32, (step, LANES), 1)
        first = lax.rem(lane, 2 * blk) < blk

        @pl.loop(0, width // step)
        def _(i):
            here = pl.ds(pl.multiple_of(i * step, step), step)
            values = [target[here, :] for target in targets]
            keep_ref[here, :] = jnp.where(first, *values).astype(jnp.bfloat16)
            give_ref[here, :] = jnp.where(first, *values[::-1]).astype(jnp.bfloat16)


def place(ops, one, two, after, weight):
    count, _, width = ops.shape
    rows, span = one[0].shape
    depth = min(2048, span)
    chunks = span // depth
    some = [
        pl.BlockSpec((rows, depth), lambda k, i, part=part: (0, jnp.clip(i - part * chunks, 0, chunks - 1)))
        for part in range(HALVES)
    ]
    whole = pl.BlockSpec((width, LANES), lambda k, i: (0, 0))
    return pl.pallas_call(
        place_kernel,
        grid=(count, HALVES * chunks),
        out_shape=(jax.ShapeDtypeStruct((width, LANES), jnp.bfloat16),) * 2,
        in_specs=[
            pl.BlockSpec((1, 1, depth), lambda k, i: (k, 0, i), memory_space=pltpu.SMEM),
            *some,
            *some,
            pl.BlockSpec(memory_space=pl.ANY),
        ],
        out_specs=(whole, whole),
        scratch_shapes=[pltpu.VMEM((depth, LANES), jnp.float32)] + [pltpu.VMEM((width, LANES), jnp.float32)] * count,
        compiler_params=params(),
        cost_estimate=pl.CostEstimate(flops=0, bytes_accessed=weight * width * LANES, transcendentals=0),
        name="place",
    )(ops, *one, *two, after)


def ratio(total_w, sum_x, sum_xx, sum_y, sum_xy, sum_yy):
    numer = total_w * sum_xy - sum_x * sum_y
    var_x = jnp.maximum(total_w * sum_xx - sum_x * sum_x, 0.05 * total_w * sum_xx)
    var_y = jnp.maximum(total_w * sum_yy - sum_y * sum_y, 0.05 * total_w * sum_yy)
    return numer / jnp.sqrt(var_x * var_y)


def plane_sums_kernel(ended, got_ref, *refs):
    moved_refs, before, outs, acc = refs[:4], refs[4 : 4 + ended], refs[4 + ended : -1], refs[-1]
    rows, depth = got_ref.shape
    step = min(1024, depth)
    half = LANES // 2
    slabs = rows // SLAB // 2

    @pl.when(pl.program_id(0) == 0)
    def _():
        acc[...] = jnp.zeros_like(acc)

    for i in range(depth // step):
        cols = slice(i * step, (i + 1) * step)
        is_x = lax.broadcasted_iota(jnp.int32, (slabs, SLAB, step), 1) < SUB
        low = lax.broadcasted_iota(jnp.int32, (step, LANES), 1) < half
        full = got_ref[:, cols].astype(jnp.float32).reshape(slabs, 2, SLAB, step)
        for t in range(2):
            wide = full[:, t]
            rolled = pltpu.roll(wide, SUB, 1)
            product = wide * rolled
            both = jnp.where(is_x, product * wide, product).reshape(slabs * SLAB, step)
            even = rolled.reshape(slabs // 2, 2, SLAB, step)[:, 0]
            odd = wide.reshape(slabs // 2, 2, SLAB, step)[:, 1]
            weights = jnp.where(is_x[: slabs // 2], even, odd).reshape(slabs // 2 * SLAB, step)
            linear, square = [], []
            for a in range(2):
                values = moved_refs[2 * t + a][cols, :].astype(jnp.float32)
                swapped = pltpu.roll(values, half, 1)
                product = values * swapped
                linear.append(jnp.where(low, product, values).astype(jnp.bfloat16))
                square.append(product * (values if a == 0 else swapped))
            right = jnp.concatenate(linear + [jnp.where(low, *square).astype(jnp.bfloat16)], 1)
            left = jnp.concatenate([weights, both], 0).astype(jnp.bfloat16)
            acc[t] += jnp.dot(left, right, preferred_element_type=jnp.float32)

    @pl.when(pl.program_id(0) == pl.num_programs(0) - 1)
    def _():
        count = slabs * SUB
        tiles = count // SLAB
        top = lax.broadcasted_iota(jnp.int32, (tiles, SLAB, LANES), 1) < SUB
        low = lax.broadcasted_iota(jnp.int32, (count, LANES), 1) < half
        early = lax.rem(lax.broadcasted_iota(jnp.int32, (count, LANES), 1), half) < half // 2
        me = lax.axis_index("dp")
        results = []
        for t in range(2):
            ratios = []
            for a in range(2):
                lanes = slice(a * LANES, (a + 1) * LANES)
                with_w = acc[t, :count, lanes]
                with_y = acc[t, count:, lanes].reshape(tiles, 2, SLAB, LANES)
                even, odd = with_y[:, 0], with_y[:, 1]
                y = jnp.where(top, pltpu.roll(even, SUB, 1), odd).reshape(count, LANES)
                yy = jnp.where(top, even, pltpu.roll(odd, SUB, 1)).reshape(count, LANES)
                sum_xx = acc[t, :count, 2 * LANES :]
                if a == 1:
                    sum_xx = pltpu.roll(sum_xx, half, 1)
                ratios.append(
                    ratio(
                        pltpu.roll(with_w, half, 1), with_w, sum_xx, pltpu.roll(y, half, 1), y, pltpu.roll(yy, half, 1)
                    )
                )
            kept, got = ratios
            got = jnp.where(early, pltpu.roll(got, LANES - half // 2, 1), pltpu.roll(got, half // 2, 1))
            straight = jnp.where(low, kept, pltpu.roll(got, half, 1))
            crossed = jnp.where(low, got, pltpu.roll(kept, half, 1))
            results.append(jnp.where(lax.rem(me, 2) == 0, straight, crossed))
        if not ended:
            for t in range(2):
                outs[0][t] = results[t]
            return
        mine_ref, near_ref, back_ref = outs
        upper = lax.div(me, 2 * PLANE)
        for part, (mine, near) in enumerate(((before[0][0], before[0][1]), results)):
            mine_ref[part] = mine
            near_ref[part] = near
            mine, near = mine.reshape(tiles, SLAB, LANES), near.reshape(tiles, SLAB, LANES)
            slot = part + upper - 2 * part * upper
            even = jnp.where(top, mine, pltpu.roll(near, SUB, 1))
            odd = jnp.where(top, pltpu.roll(mine, SUB, 1), near)
            for i in range(tiles):
                for twin in range(2):
                    back_ref[slot, twin, 2 * i] = even[i]
                    back_ref[slot, twin, 2 * i + 1] = odd[i]


def plane_sums(got, moved, before):
    rows, width = got.shape
    depth = min(2048, width)
    ended = before is not None
    count = rows // 4
    placed = pl.BlockSpec((depth, LANES), lambda i: (i, 0))
    result = (2, count, LANES)
    shapes = (result, result, (2, 2, PLANE, SLAB, LANES)) if ended else (result,)
    entire = [pl.BlockSpec(shape, lambda i, shape=shape: (0,) * len(shape)) for shape in shapes]
    outs = pl.pallas_call(
        functools.partial(plane_sums_kernel, ended),
        grid=(width // depth,),
        out_shape=tuple(jax.ShapeDtypeStruct(shape, jnp.float32) for shape in shapes),
        in_specs=[pl.BlockSpec((rows, depth), lambda i: (0, i)), placed, placed, placed, placed]
        + ([entire[0]] if ended else []),
        out_specs=tuple(entire),
        scratch_shapes=[pltpu.VMEM((2, 3 * count, 3 * LANES), jnp.float32)],
        compiler_params=params(),
        cost_estimate=pl.CostEstimate(
            flops=9 * rows * width * LANES, bytes_accessed=width * (2 * rows + 8 * LANES), transcendentals=0
        ),
        name="plane_sums",
    )(got, *moved, *((before,) if ended else ()))
    return outs if ended else outs[0]


def shards_by_plane(intensities, observed, qweights, ops, pick):
    blk = intensities.shape[0]
    groups = PLANES * PLANE
    swap = [(i, i ^ 1) for i in range(groups)]
    beside = [(i, i ^ PLANE) for i in range(groups)]
    across = [(i, i ^ (2 * PLANE)) for i in range(groups)]
    middle = [(i, 3 * PLANE + 2 * (i % PLANE) - i) for i in range(PLANE, 3 * PLANE)]
    outward = [(i, i - PLANE if i < 2 * PLANE else i + PLANE) for i in range(PLANE, 3 * PLANE)]
    rings = [[z * PLANE + c for c in range(PLANE)] for z in range(PLANES)]
    plane = lax.axis_index("dp") // PLANE
    odd, upper = plane % 2 == 1, plane >= 2

    def spread(send):
        got = lax.all_to_all(send, "dp", split_axis=0, concat_axis=0, axis_index_groups=rings, tiled=True)
        return got.reshape(PLANE * 2 * SLAB, send.shape[-1])

    own_pick = pick[:, 0]
    core = lax.axis_index("dp") % 2
    ops = lax.dynamic_slice_in_dim(ops, core * (NOPS // 2), NOPS // 2, 0)[:, None, :]
    mine = [weigh(intensities, observed, qweights, part) for part in range(HALVES)]
    near = [lax.ppermute(rows, "dp", beside) for rows in mine]
    mid = [lax.ppermute(rows, "dp", middle) for rows in mine]
    other = [lax.ppermute(rows, "dp", swap) for rows in mine]
    far_pick = lax.ppermute(own_pick, "dp", across)

    own_got = spread(own_pack(own_pick, mine))
    keep, give = place(ops, mine, other, own_pick, 4)
    own_moved = [keep, lax.ppermute(give, "dp", swap)]

    near, mid, far_pick, keep = lax.optimization_barrier((near, mid, far_pick, keep))
    own_moved[0] = keep
    outer = [lax.ppermute(rows, "dp", outward) for rows in mid]
    inner = [lax.ppermute(rows, "dp", middle) for rows in near]
    near_other = [lax.ppermute(rows, "dp", swap) for rows in near]
    keep, give = place(ops, near, near_other, own_pick, 256)
    far_send = far_pack(far_pick, outer, inner, keep)
    far_send, give = lax.optimization_barrier((far_send, give))
    far_got = spread(far_send)
    moved = own_moved + [keep, lax.ppermute(give, "dp", swap)]
    own_corr = plane_sums(own_got, moved, None)
    ours, theirs, back = plane_sums(far_got, moved, own_corr)

    from_near = lax.ppermute(theirs, "dp", beside)
    pair = [each.reshape(2, PLANE, SUB, NOPS * blk) for each in (ours, from_near)]
    pair = jnp.stack(pair, 1)
    pair = jnp.where(odd, pair[:, ::-1], pair)
    pair = jnp.where(upper, pair[::-1], pair)
    corr = pair.reshape(groups * SUB, NOPS * blk).T.reshape(NOPS, blk, groups * SUB)

    back = back.reshape(groups, 2 * SUB, NOPS * blk)
    back = lax.all_to_all(back, "dp", split_axis=0, concat_axis=0, tiled=True)
    back = back.reshape(2, 2, PLANE, 2, SUB, NOPS, blk)
    back = jnp.where(odd, back[:, 1, :, ::-1], back[:, 0])
    returned = jnp.transpose(back, (4, 0, 2, 1, 3, 5)).reshape(NOPS, 1, groups, SUB, blk)
    return (corr, returned)


def shards(intensities, observed, qweights, ops, pick):
    if lax.axis_size("dp") == PLANES * PLANE and lax.axis_size("refl") == 1:
        return shards_by_plane(intensities, observed, qweights, ops, pick)
    return shards_direct(intensities, observed, qweights, ops, pick)


def shards_direct(intensities, observed, qweights, ops, pick):
    blk, width = intensities.shape
    groups = lax.axis_size("dp")
    shares = lax.axis_size("refl")
    local_ops = ops - lax.axis_index("refl") * width
    send, own_w = pack(pick[:, 0], intensities, observed, qweights)
    got = lax.all_to_all(send, "dp", split_axis=0, concat_axis=0, tiled=True)
    moved = move(local_ops, intensities, own_w)
    stats = sums(got.reshape(groups * SLAB, width), moved)
    if shares > 1:
        stats = lax.psum(stats, "refl")
    stats = stats.reshape(2, groups, SLAB, NOPS, LANES)
    full = pearson(stats, blk)
    rows = blk // shares
    if shares > 1:
        full = lax.dynamic_slice_in_dim(full, lax.axis_index("refl") * rows, rows, 3)
    corr = jnp.transpose(full, (2, 3, 0, 1)).reshape(NOPS, rows, groups * SUB)
    back = lax.all_to_all(full, "dp", split_axis=0, concat_axis=0, tiled=True)
    returned = jnp.transpose(back, (2, 0, 1, 3))[:, None]
    return (corr, returned)


def solution(mesh):
    return jax.shard_map(
        shards,
        mesh=mesh,
        in_specs=(
            P("dp", "refl"),
            P("dp", "refl"),
            P("dp", "refl"),
            P(None, "refl"),
            P(None, "dp"),
        ),
        out_specs=(P(None, ("dp", "refl"), None), P(None, "dp", None, None, "refl")),
        check_vma=False,
    )
```

```python
import functools

import jax
import jax.numpy as jnp
from jax import lax
from jax.experimental import pallas as pl
from jax.experimental.pallas import tpu as pltpu
from jax.sharding import PartitionSpec as P

SUB = 4
NOPS = 4
LANES = 128
SLAB = 2 * SUB
VMEM_LIMIT = 56 * 1024 * 1024
PLANES = 4
PLANE = 8
UNROLL = 64


def params():
    return pltpu.CompilerParams(vmem_limit_bytes=VMEM_LIMIT)


def pack_kernel(pick_ref, x_ref, obs_ref, qw_ref, send_ref, w_ref, slabs, sems):
    blk, width = x_ref.shape
    step = min(512, width)

    @pl.loop(0, width // step)
    def _(i):
        cols = pl.ds(pl.multiple_of(i * step, step), step)
        wide_w = obs_ref[:, cols].astype(jnp.float32) * qw_ref[:, cols].astype(jnp.float32)
        wide_x = x_ref[:, cols].astype(jnp.float32)
        w_ref[:, cols] = wide_w.astype(jnp.bfloat16)
        for g in range(blk // SUB):
            rows = slice(g * SUB, (g + 1) * SUB)
            slab = jnp.concatenate([wide_x[rows], wide_w[rows]], 0)
            slabs[g, :, cols] = slab.astype(jnp.bfloat16)

    groups = send_ref.shape[0]

    def copy(d):
        return pltpu.make_async_copy(slabs.at[pick_ref[d]], send_ref.at[d], sems.at[d])

    @pl.loop(0, groups)
    def _(d):
        copy(d).start()

    @pl.loop(0, groups)
    def _(d):
        copy(d).wait()


def pack(pick, intensities, observed, qweights):
    blk, width = intensities.shape
    groups = pick.shape[0]
    whole = pl.BlockSpec(memory_space=pltpu.VMEM)
    return pl.pallas_call(
        pack_kernel,
        out_shape=(
            jax.ShapeDtypeStruct((groups, SLAB, width), jnp.bfloat16),
            jax.ShapeDtypeStruct((blk, width), jnp.bfloat16),
        ),
        in_specs=[pl.BlockSpec(memory_space=pltpu.SMEM), whole, whole, whole],
        out_specs=(pl.BlockSpec(memory_space=pl.ANY), whole),
        scratch_shapes=[
            pltpu.VMEM((blk // SUB, SLAB, width), jnp.bfloat16),
            pltpu.SemaphoreType.DMA((groups,)),
        ],
        compiler_params=params(),
        cost_estimate=pl.CostEstimate(
            flops=blk * width * 4, bytes_accessed=(groups * SLAB * 2 + blk * 10) * width, transcendentals=0
        ),
        name="pack",
    )(pick, intensities, observed, qweights)


def move_kernel(ops_ref, x_ref, w_ref, moved_ref, table, target):
    blk, width = x_ref.shape

    @pl.when(pl.program_id(0) == 0)
    def _():
        @pl.loop(0, width // LANES)
        def _(i):
            cols = pl.ds(pl.multiple_of(i * LANES, LANES), LANES)
            wide_x = x_ref[:, cols].astype(jnp.float32)
            wide_w = w_ref[:, cols].astype(jnp.float32)
            wx = (wide_w * wide_x).astype(jnp.bfloat16).astype(jnp.float32)
            wxx = (wide_w * wide_x * wide_x).astype(jnp.bfloat16).astype(jnp.float32)
            stacked = jnp.concatenate([wide_w, wx, wxx, jnp.zeros((LANES - 3 * blk, LANES), jnp.float32)], 0)
            table[cols, :] = stacked.T

    unroll = 16

    @pl.loop(0, width // unroll)
    def _(i):
        base = pl.multiple_of(i * unroll, unroll)
        for j in range(unroll):
            to = ops_ref[0, 0, base + j]
            target[pl.ds(to, 1), :] = table[pl.ds(base + j, 1), :]

    step = min(512, width)

    @pl.loop(0, width // step)
    def _(i):
        rows = pl.ds(pl.multiple_of(i * step, step), step)
        moved_ref[rows, :] = target[rows, :].astype(jnp.bfloat16)


def move(local_ops, intensities, own_w):
    blk, width = intensities.shape
    whole = pl.BlockSpec(memory_space=pltpu.VMEM)
    return pl.pallas_call(
        move_kernel,
        grid=(NOPS,),
        out_shape=jax.ShapeDtypeStruct((width, NOPS * LANES), jnp.bfloat16),
        in_specs=[
            pl.BlockSpec((1, 1, width), lambda k: (k, 0, 0), memory_space=pltpu.SMEM),
            whole,
            whole,
        ],
        out_specs=pl.BlockSpec((width, LANES), lambda k: (0, k)),
        scratch_shapes=[
            pltpu.VMEM((width, LANES), jnp.float32),
            pltpu.VMEM((width, LANES), jnp.float32),
        ],
        compiler_params=params(),
        cost_estimate=pl.CostEstimate(
            flops=0, bytes_accessed=NOPS * width * LANES * 100, transcendentals=0
        ),
        name="move",
    )(local_ops[:, None, :], intensities, own_w)


def sums_kernel(got_ref, moved_ref, out_ref):
    rows, depth = got_ref.shape
    step = min(512, depth)

    @pl.when(pl.program_id(0) == 0)
    def _():
        out_ref[...] = jnp.zeros_like(out_ref)

    is_x = lax.broadcasted_iota(jnp.int32, (rows // SLAB, SLAB, step), 1) < SUB

    @pl.loop(0, depth // step)
    def _(i):
        cols = pl.ds(pl.multiple_of(i * step, step), step)
        raw = got_ref[:, cols]
        wide = raw.astype(jnp.float32).reshape(rows // SLAB, SLAB, step)
        product = wide * pltpu.roll(wide, SUB, 1)
        second = jnp.where(is_x, product * wide, product)
        second = second.reshape(rows, step).astype(jnp.bfloat16)
        right = moved_ref[cols, :]
        out_ref[0] += jnp.dot(raw, right, preferred_element_type=jnp.float32)
        out_ref[1] += jnp.dot(second, right, preferred_element_type=jnp.float32)


def sums(got, moved):
    rows, width = got.shape
    depth = min(2048, width)
    return pl.pallas_call(
        sums_kernel,
        grid=(width // depth,),
        out_shape=jax.ShapeDtypeStruct((2, rows, moved.shape[1]), jnp.float32),
        in_specs=[
            pl.BlockSpec((rows, depth), lambda i: (0, i)),
            pl.BlockSpec((depth, moved.shape[1]), lambda i: (i, 0)),
        ],
        out_specs=pl.BlockSpec((2, rows, moved.shape[1]), lambda i: (0, 0, 0)),
        compiler_params=params(),
        cost_estimate=pl.CostEstimate(
            flops=4 * rows * width * moved.shape[1],
            bytes_accessed=2 * width * (rows + moved.shape[1]),
            transcendentals=0,
        ),
        name="sums",
    )(got, moved)


def pearson(share, blk):
    first, second = share[0], share[1]
    total_w = first[:, SUB:, :, :blk]
    sum_x = first[:, SUB:, :, blk : 2 * blk]
    sum_xx = first[:, SUB:, :, 2 * blk : 3 * blk]
    sum_y = second[:, SUB:, :, :blk]
    sum_xy = second[:, SUB:, :, blk : 2 * blk]
    sum_yy = second[:, :SUB, :, :blk]
    numer = total_w * sum_xy - sum_x * sum_y
    var_x = jnp.maximum(total_w * sum_xx - sum_x * sum_x, 0.05 * total_w * sum_xx)
    var_y = jnp.maximum(total_w * sum_yy - sum_y * sum_y, 0.05 * total_w * sum_yy)
    return numer / jnp.sqrt(var_x * var_y)


def fill_slabs(slabs, x_ref, w_ref):
    blk, width = x_ref.shape
    step = min(512, width)

    @pl.loop(0, width // step)
    def _(i):
        cols = pl.ds(pl.multiple_of(i * step, step), step)
        wide_x = x_ref[:, cols].astype(jnp.float32)
        wide_w = w_ref[:, cols].astype(jnp.float32)
        for g in range(blk // SUB):
            rows = slice(g * SUB, (g + 1) * SUB)
            slab = jnp.concatenate([wide_x[rows], wide_w[rows]], 0)
            slabs[g, :, cols] = slab.astype(jnp.bfloat16)


def send_slabs(slabs, pick_ref, send_refs, sems):
    me = lax.axis_index("dp")
    mine, here = lax.div(me, PLANE), lax.rem(me, PLANE)
    partner = mine + 1 - 2 * lax.rem(mine, 2)
    copies = []
    for r, send_ref in enumerate(send_refs):
        for t, plane in enumerate((mine, partner)):
            group = pick_ref[plane * PLANE + lax.bitwise_xor(here, r)]
            copies.append(pltpu.make_async_copy(slabs.at[group], send_ref.at[t], sems.at[r, t]))
    for copy in copies:
        copy.start()
    for copy in copies:
        copy.wait()


def own_pack_kernel(pick_ref, x_ref, w_ref, *refs):
    send_refs, (slabs, sems) = refs[:PLANE], refs[PLANE:]
    fill_slabs(slabs, x_ref, w_ref)
    send_slabs(slabs, pick_ref, send_refs, sems)


def far_pack_kernel(pick_ref, xo_ref, wo_ref, xi_ref, wi_ref, after_ref, *refs):
    send_refs, (x_buf, w_buf, in_sems, slabs, sems) = refs[:PLANE], refs[PLANE:]
    plane = lax.div(lax.axis_index("dp"), PLANE)
    inner = (plane == 1) | (plane == 2)

    def fetch(x_ref, w_ref):
        copies = (
            pltpu.make_async_copy(x_ref, x_buf, in_sems.at[0]),
            pltpu.make_async_copy(w_ref, w_buf, in_sems.at[1]),
        )
        for copy in copies:
            copy.start()
        for copy in copies:
            copy.wait()

    @pl.when(inner)
    def _():
        fetch(xi_ref, wi_ref)

    @pl.when(jnp.logical_not(inner))
    def _():
        fetch(xo_ref, wo_ref)

    fill_slabs(slabs, x_buf, w_buf)
    send_slabs(slabs, pick_ref, send_refs, sems)


def pack_call(kernel, name, specs, scratch, blk, width, *operands):
    return pl.pallas_call(
        kernel,
        out_shape=(jax.ShapeDtypeStruct((2, SLAB, width), jnp.bfloat16),) * PLANE,
        in_specs=[pl.BlockSpec(memory_space=pltpu.SMEM)] + specs,
        out_specs=(pl.BlockSpec(memory_space=pl.ANY),) * PLANE,
        scratch_shapes=scratch
        + [pltpu.VMEM((blk // SUB, SLAB, width), jnp.bfloat16), pltpu.SemaphoreType.DMA((PLANE, 2))],
        compiler_params=params(),
        cost_estimate=pl.CostEstimate(
            flops=blk * width * 4, bytes_accessed=(PLANE * 2 * SLAB * 2 + blk * 4) * width, transcendentals=0
        ),
        name=name,
    )(*operands)


def own_pack(pick, x, w):
    specs = [pl.BlockSpec(memory_space=pltpu.VMEM)] * 2
    return pack_call(own_pack_kernel, "own_pack", specs, [], *x.shape, pick, x, w)


def far_pack(pick, x_outer, w_outer, x_inner, w_inner, after):
    blk, width = x_outer.shape
    buf = pltpu.VMEM((blk, width), jnp.bfloat16)

    return pack_call(
        far_pack_kernel, "far_pack", [pl.BlockSpec(memory_space=pl.ANY)] * 5,
        [buf, buf, pltpu.SemaphoreType.DMA((2,))], blk, width,
        pick, x_outer, w_outer, x_inner, w_inner, after,
    )


def place_kernel(ops_ref, x_ref, x1_ref, w_ref, w1_ref, after_ref, moved_ref, table, target):
    depth = x_ref.shape[1]
    width = target.shape[0]
    part = pl.multiple_of(pl.program_id(1) * depth, depth)

    @pl.when(pl.program_id(0) == 0)
    def _():
        step = min(256, depth)
        diagonal = lax.broadcasted_iota(jnp.int32, (step, step), 0) == lax.broadcasted_iota(
            jnp.int32, (step, step), 1
        )
        identity = jnp.where(diagonal, 1.0, 0.0).astype(jnp.bfloat16)
        for i in range(depth // step):
            cols = slice(i * step, (i + 1) * step)
            rows = jnp.concatenate([x_ref[:, cols], x1_ref[:, cols], w_ref[:, cols], w1_ref[:, cols]], 0)
            table[pl.ds(part + i * step, step), :] = lax.dot_general(
                identity, rows, (((1,), (1,)), ((), ())), preferred_element_type=jnp.float32
            )

    @pl.loop(0, depth // UNROLL)
    def _(i):
        base = pl.multiple_of(i * UNROLL, UNROLL)
        row = pl.multiple_of(part + base, UNROLL)
        for j in range(UNROLL):
            to = ops_ref[0, 0, base + j]
            target[pl.ds(to, 1), :] = table[pl.ds(row + j, 1), :]

    @pl.when(pl.program_id(1) == pl.num_programs(1) - 1)
    def _():
        step = min(512, width)

        @pl.loop(0, width // step)
        def _(i):
            rows = pl.ds(pl.multiple_of(i * step, step), step)
            moved_ref[rows, :] = target[rows, :].astype(jnp.bfloat16)


def place(ops, x, x1, w, w1, after):
    count = ops.shape[0]
    blk, width = x.shape
    depth = min(2048, width)
    last = width // depth - 1
    part = pl.BlockSpec((blk, depth), lambda k, i: (0, jnp.where(k == 0, i, last)))
    return pl.pallas_call(
        place_kernel,
        grid=(count, width // depth),
        out_shape=jax.ShapeDtypeStruct((width, count * LANES), jnp.bfloat16),
        in_specs=[
            pl.BlockSpec((1, 1, depth), lambda k, i: (k, 0, i), memory_space=pltpu.SMEM),
            part,
            part,
            part,
            part,
            pl.BlockSpec(memory_space=pl.ANY),
        ],
        out_specs=pl.BlockSpec((width, LANES), lambda k, i: (0, k)),
        scratch_shapes=[pltpu.VMEM((width, LANES), jnp.float32)] * 2,
        compiler_params=params(),
        cost_estimate=pl.CostEstimate(
            flops=0, bytes_accessed=count * width * LANES * 64, transcendentals=0
        ),
        name="place",
    )(ops[:, None, :], x, x1, w, w1, after)


def ratio(total_w, sum_x, sum_xx, sum_y, sum_xy, sum_yy):
    numer = total_w * sum_xy - sum_x * sum_y
    var_x = jnp.maximum(total_w * sum_xx - sum_x * sum_x, 0.05 * total_w * sum_xx)
    var_y = jnp.maximum(total_w * sum_yy - sum_y * sum_y, 0.05 * total_w * sum_yy)
    return numer / jnp.sqrt(var_x * var_y)


def plane_sums_kernel(*refs):
    own_refs, far_refs = refs[:PLANE], refs[PLANE : 2 * PLANE]
    first_ref, second_ref, out_ref, acc = refs[2 * PLANE :]
    depth = first_ref.shape[0]
    rows = 2 * SLAB * PLANE
    step = min(1024, depth)
    half = LANES // 2
    slabs = rows // SLAB
    blk = half // 2

    @pl.when(pl.program_id(0) == 0)
    def _():
        acc[...] = jnp.zeros_like(acc)

    @pl.loop(0, depth // step)
    def _(i):
        cols = pl.ds(pl.multiple_of(i * step, step), step)
        is_x = lax.broadcasted_iota(jnp.int32, (slabs, SLAB, step), 1) < SUB
        weights, products = [], []
        for group in (own_refs, far_refs):
            wide = jnp.concatenate([ref[:, :, cols].astype(jnp.float32) for ref in group], 0)
            rolled = pltpu.roll(wide, SUB, 1)
            product = wide * rolled
            both = jnp.where(is_x, product * wide, product)
            products.append(both.reshape(rows, step).astype(jnp.bfloat16))
            mine = rolled.reshape(slabs // 2, 2, SLAB, step)[:, 0]
            partner = wide.reshape(slabs // 2, 2, SLAB, step)[:, 1]
            pair = jnp.where(is_x[: slabs // 2], mine, partner)
            weights.append(pair.reshape(rows // 2, step).astype(jnp.bfloat16))
        low = lax.broadcasted_iota(jnp.int32, (step, LANES), 1) < half
        linear, square = [], []
        for ref in (first_ref, second_ref):
            even, odd = None, None
            for k in range(2):
                values = ref[cols, k * LANES : (k + 1) * LANES].astype(jnp.float32)
                swapped = pltpu.roll(values, half, 1)
                product = values * swapped
                linear.append(jnp.where(low, product, values).astype(jnp.bfloat16))
                if k == 0:
                    even = product * values
                else:
                    odd = product * swapped
            square.append(jnp.where(low, even, odd).astype(jnp.bfloat16))
        left = jnp.concatenate(weights + products, 0)
        right = jnp.concatenate(linear + square, 1)
        acc[...] += jnp.dot(left, right, preferred_element_type=jnp.float32)

    @pl.when(pl.program_id(0) == pl.num_programs(0) - 1)
    def _():
        tiles = slabs
        top = lax.broadcasted_iota(jnp.int32, (tiles, SLAB, LANES), 1) < SUB
        lane = lax.broadcasted_iota(jnp.int32, (tiles * SLAB, LANES), 1)
        result = jnp.zeros((tiles * SLAB, LANES), jnp.float32)
        for k in range(NOPS):
            lanes = slice(k * LANES, (k + 1) * LANES)
            squares = slice((NOPS + k // 2) * LANES, (NOPS + k // 2 + 1) * LANES)
            with_w = acc[:rows, lanes]
            with_y = acc[rows:, lanes].reshape(tiles, 2, SLAB, LANES)
            mine, partner = with_y[:, 0], with_y[:, 1]
            y = jnp.where(top, pltpu.roll(mine, SUB, 1), partner).reshape(tiles * SLAB, LANES)
            yy = jnp.where(top, mine, pltpu.roll(partner, SUB, 1)).reshape(tiles * SLAB, LANES)
            sum_xx = acc[:rows, squares]
            if k % 2 == 1:
                sum_xx = pltpu.roll(sum_xx, half, 1)
            both = ratio(
                pltpu.roll(with_w, half, 1), with_w, sum_xx, pltpu.roll(y, half, 1), y, pltpu.roll(yy, half, 1)
            )
            both = jnp.where(
                top.reshape(tiles * SLAB, LANES), both, pltpu.roll(both, LANES - blk, 1)
            )
            moved = both if k == 0 else pltpu.roll(both, k * blk, 1)
            result = jnp.where((lane >= k * blk) & (lane < (k + 1) * blk), moved, result)
        here = lax.rem(lax.axis_index("dp"), PLANE)
        for tile in range(tiles):
            part, r = tile // PLANE, tile % PLANE
            out_ref[part * PLANE + lax.bitwise_xor(here, r)] = result[tile * SLAB : (tile + 1) * SLAB]


def plane_sums(own, far, first, second):
    _, slab, width = own[0].shape
    rows = 2 * slab * PLANE
    depth = min(2048, width)
    lanes = (NOPS + NOPS // 2) * LANES
    part = pl.BlockSpec((2, slab, depth), lambda i: (0, 0, i))
    moved = pl.BlockSpec((depth, 2 * LANES), lambda i: (i, 0))
    return pl.pallas_call(
        plane_sums_kernel,
        grid=(width // depth,),
        out_shape=jax.ShapeDtypeStruct((2 * PLANE, slab, LANES), jnp.float32),
        in_specs=[part] * (2 * PLANE) + [moved, moved],
        out_specs=pl.BlockSpec((2 * PLANE, slab, LANES), lambda i: (0, 0, 0)),
        scratch_shapes=[pltpu.VMEM((3 * rows, lanes), jnp.float32)],
        compiler_params=params(),
        cost_estimate=pl.CostEstimate(
            flops=6 * rows * width * lanes,
            bytes_accessed=width * (4 * rows + 8 * LANES),
            transcendentals=0,
        ),
        name="plane_sums",
    )(*own, *far, first, second)


def shards_by_plane(intensities, observed, qweights, ops, pick):
    blk, width = intensities.shape
    groups = PLANES * PLANE
    near = [(i, i ^ PLANE) for i in range(groups)]
    far = [(i, i ^ (2 * PLANE)) for i in range(groups)]
    middle = [(i, 3 * PLANE + 2 * (i % PLANE) - i) for i in range(PLANE, 3 * PLANE)]
    outward = [(i, i - PLANE if i < 2 * PLANE else i + PLANE) for i in range(PLANE, 3 * PLANE)]
    couples = [[z * PLANE + c for z in (odd, odd + 2) for c in range(PLANE)] for odd in range(2)]
    plane = lax.axis_index("dp") // PLANE
    odd, upper = plane % 2 == 1, plane >= 2

    def spread(send):
        got = [send[0]]
        for r in range(1, PLANE):
            got.append(lax.ppermute(send[r], "dp", [(i, i ^ r) for i in range(groups)]))
        return got

    own_pick = pick[:, 0]
    near_x = lax.ppermute(intensities, "dp", near)
    mid_x = lax.ppermute(intensities, "dp", middle)
    far_pick = lax.ppermute(own_pick, "dp", far)
    own_w = (observed.astype(jnp.float32) * qweights.astype(jnp.float32)).astype(jnp.bfloat16)
    near_w = lax.ppermute(own_w, "dp", near)
    mid_w = lax.ppermute(own_w, "dp", middle)
    own_got = spread(own_pack(own_pick, intensities, own_w))
    near_x, mid_x, near_w, mid_w, far_pick = lax.optimization_barrier((near_x, mid_x, near_w, mid_w, far_pick))
    outer_x = lax.ppermute(mid_x, "dp", outward)
    inner_x = lax.ppermute(near_x, "dp", middle)
    outer_w = lax.ppermute(mid_w, "dp", outward)
    inner_w = lax.ppermute(near_w, "dp", middle)
    first = place(ops[:2], intensities, near_x, own_w, near_w, own_pick)
    far_send = far_pack(far_pick, outer_x, outer_w, inner_x, inner_w, first)
    far_got = spread(far_send)
    second = place(ops[2:], intensities, near_x, own_w, near_w, far_send[0])
    stats = plane_sums(own_got, far_got, first, second)
    stats = stats.reshape(2, PLANE, 2, SUB, NOPS * blk)
    mine, other = stats[:, :, 0], stats[:, :, 1]

    from_near = lax.ppermute(other, "dp", near)
    pair = jnp.stack([mine, from_near], 1)
    pair = jnp.where(odd, pair[:, ::-1], pair)
    pair = jnp.where(upper, pair[::-1], pair)
    corr = pair.reshape(groups * SUB, NOPS * blk).T.reshape(NOPS, blk, groups * SUB)

    back = jnp.where(upper, stats[::-1], stats).reshape(2 * PLANE, 2 * SUB, NOPS * blk)
    back = lax.all_to_all(back, "dp", split_axis=0, concat_axis=0, axis_index_groups=couples, tiled=True)
    back = back.reshape(2, PLANE, 2, SUB, NOPS, blk)
    back = jnp.where(odd, back[:, :, ::-1], back)
    returned = jnp.transpose(back, (4, 0, 2, 1, 3, 5)).reshape(NOPS, 1, groups, SUB, blk)
    return (corr, returned)


def shards(intensities, observed, qweights, ops, pick):
    if lax.axis_size("dp") == PLANES * PLANE and lax.axis_size("refl") == 1:
        return shards_by_plane(intensities, observed, qweights, ops, pick)
    return shards_direct(intensities, observed, qweights, ops, pick)


def shards_direct(intensities, observed, qweights, ops, pick):
    blk, width = intensities.shape
    groups = lax.axis_size("dp")
    shares = lax.axis_size("refl")
    local_ops = ops - lax.axis_index("refl") * width
    send, own_w = pack(pick[:, 0], intensities, observed, qweights)
    got = lax.all_to_all(send, "dp", split_axis=0, concat_axis=0, tiled=True)
    moved = move(local_ops, intensities, own_w)
    stats = sums(got.reshape(groups * SLAB, width), moved)
    if shares > 1:
        stats = lax.psum(stats, "refl")
    stats = stats.reshape(2, groups, SLAB, NOPS, LANES)
    full = pearson(stats, blk)
    rows = blk // shares
    if shares > 1:
        full = lax.dynamic_slice_in_dim(full, lax.axis_index("refl") * rows, rows, 3)
    corr = jnp.transpose(full, (2, 3, 0, 1)).reshape(NOPS, rows, groups * SUB)
    back = lax.all_to_all(full, "dp", split_axis=0, concat_axis=0, tiled=True)
    returned = jnp.transpose(back, (2, 0, 1, 3))[:, None]
    return (corr, returned)


def solution(mesh):
    return jax.shard_map(
        shards,
        mesh=mesh,
        in_specs=(
            P("dp", "refl"),
            P("dp", "refl"),
            P("dp", "refl"),
            P(None, "refl"),
            P(None, "dp"),
        ),
        out_specs=(P(None, ("dp", "refl"), None), P(None, "dp", None, None, "refl")),
        check_vma=False,
    )
```

```python
import functools

import jax
import jax.numpy as jnp
from jax import lax
from jax.experimental import pallas as pl
from jax.experimental.pallas import tpu as pltpu
from jax.sharding import PartitionSpec as P

SUB = 4
NOPS = 4
LANES = 128
SLAB = 2 * SUB
MIB = 1024 * 1024
PLANES = 4
PLANE = 8
UNROLL = 64
HALVES = 2


def params():
    return pltpu.CompilerParams(vmem_limit_bytes=56 * MIB)


def pack_kernel(pick_ref, x_ref, obs_ref, qw_ref, send_ref, w_ref, slabs, sems):
    blk, width = x_ref.shape
    step = min(512, width)

    @pl.loop(0, width // step)
    def _(i):
        cols = pl.ds(pl.multiple_of(i * step, step), step)
        wide_w = obs_ref[:, cols].astype(jnp.float32) * qw_ref[:, cols].astype(jnp.float32)
        wide_x = x_ref[:, cols].astype(jnp.float32)
        w_ref[:, cols] = wide_w.astype(jnp.bfloat16)
        for g in range(blk // SUB):
            rows = slice(g * SUB, (g + 1) * SUB)
            slab = jnp.concatenate([wide_x[rows], wide_w[rows]], 0)
            slabs[g, :, cols] = slab.astype(jnp.bfloat16)

    groups = send_ref.shape[0]

    def copy(d):
        return pltpu.make_async_copy(slabs.at[pick_ref[d]], send_ref.at[d], sems.at[d])

    @pl.loop(0, groups)
    def _(d):
        copy(d).start()

    @pl.loop(0, groups)
    def _(d):
        copy(d).wait()


def pack(pick, intensities, observed, qweights):
    blk, width = intensities.shape
    groups = pick.shape[0]
    whole = pl.BlockSpec(memory_space=pltpu.VMEM)
    return pl.pallas_call(
        pack_kernel,
        out_shape=(
            jax.ShapeDtypeStruct((groups, SLAB, width), jnp.bfloat16),
            jax.ShapeDtypeStruct((blk, width), jnp.bfloat16),
        ),
        in_specs=[pl.BlockSpec(memory_space=pltpu.SMEM), whole, whole, whole],
        out_specs=(pl.BlockSpec(memory_space=pl.ANY), whole),
        scratch_shapes=[
            pltpu.VMEM((blk // SUB, SLAB, width), jnp.bfloat16),
            pltpu.SemaphoreType.DMA((groups,)),
        ],
        compiler_params=params(),
        cost_estimate=pl.CostEstimate(
            flops=blk * width * 4, bytes_accessed=(groups * SLAB * 2 + blk * 10) * width, transcendentals=0
        ),
        name="pack",
    )(pick, intensities, observed, qweights)


def move_kernel(ops_ref, x_ref, w_ref, moved_ref, table, target):
    blk, width = x_ref.shape

    @pl.when(pl.program_id(0) == 0)
    def _():
        @pl.loop(0, width // LANES)
        def _(i):
            cols = pl.ds(pl.multiple_of(i * LANES, LANES), LANES)
            wide_x = x_ref[:, cols].astype(jnp.float32)
            wide_w = w_ref[:, cols].astype(jnp.float32)
            wx = (wide_w * wide_x).astype(jnp.bfloat16).astype(jnp.float32)
            wxx = (wide_w * wide_x * wide_x).astype(jnp.bfloat16).astype(jnp.float32)
            stacked = jnp.concatenate([wide_w, wx, wxx, jnp.zeros((LANES - 3 * blk, LANES), jnp.float32)], 0)
            table[cols, :] = stacked.T

    unroll = 16

    @pl.loop(0, width // unroll)
    def _(i):
        base = pl.multiple_of(i * unroll, unroll)
        for j in range(unroll):
            to = ops_ref[0, 0, base + j]
            target[pl.ds(to, 1), :] = table[pl.ds(base + j, 1), :]

    step = min(512, width)

    @pl.loop(0, width // step)
    def _(i):
        rows = pl.ds(pl.multiple_of(i * step, step), step)
        moved_ref[rows, :] = target[rows, :].astype(jnp.bfloat16)


def move(local_ops, intensities, own_w):
    blk, width = intensities.shape
    whole = pl.BlockSpec(memory_space=pltpu.VMEM)
    return pl.pallas_call(
        move_kernel,
        grid=(NOPS,),
        out_shape=jax.ShapeDtypeStruct((width, NOPS * LANES), jnp.bfloat16),
        in_specs=[
            pl.BlockSpec((1, 1, width), lambda k: (k, 0, 0), memory_space=pltpu.SMEM),
            whole,
            whole,
        ],
        out_specs=pl.BlockSpec((width, LANES), lambda k: (0, k)),
        scratch_shapes=[
            pltpu.VMEM((width, LANES), jnp.float32),
            pltpu.VMEM((width, LANES), jnp.float32),
        ],
        compiler_params=params(),
        cost_estimate=pl.CostEstimate(
            flops=0, bytes_accessed=NOPS * width * LANES * 100, transcendentals=0
        ),
        name="move",
    )(local_ops[:, None, :], intensities, own_w)


def sums_kernel(got_ref, moved_ref, out_ref):
    rows, depth = got_ref.shape
    step = min(512, depth)

    @pl.when(pl.program_id(0) == 0)
    def _():
        out_ref[...] = jnp.zeros_like(out_ref)

    is_x = lax.broadcasted_iota(jnp.int32, (rows // SLAB, SLAB, step), 1) < SUB

    @pl.loop(0, depth // step)
    def _(i):
        cols = pl.ds(pl.multiple_of(i * step, step), step)
        raw = got_ref[:, cols]
        wide = raw.astype(jnp.float32).reshape(rows // SLAB, SLAB, step)
        product = wide * pltpu.roll(wide, SUB, 1)
        second = jnp.where(is_x, product * wide, product)
        second = second.reshape(rows, step).astype(jnp.bfloat16)
        right = moved_ref[cols, :]
        out_ref[0] += jnp.dot(raw, right, preferred_element_type=jnp.float32)
        out_ref[1] += jnp.dot(second, right, preferred_element_type=jnp.float32)


def sums(got, moved):
    rows, width = got.shape
    depth = min(2048, width)
    return pl.pallas_call(
        sums_kernel,
        grid=(width // depth,),
        out_shape=jax.ShapeDtypeStruct((2, rows, moved.shape[1]), jnp.float32),
        in_specs=[
            pl.BlockSpec((rows, depth), lambda i: (0, i)),
            pl.BlockSpec((depth, moved.shape[1]), lambda i: (i, 0)),
        ],
        out_specs=pl.BlockSpec((2, rows, moved.shape[1]), lambda i: (0, 0, 0)),
        compiler_params=params(),
        cost_estimate=pl.CostEstimate(
            flops=4 * rows * width * moved.shape[1],
            bytes_accessed=2 * width * (rows + moved.shape[1]),
            transcendentals=0,
        ),
        name="sums",
    )(got, moved)


def pearson(share, blk):
    first, second = share[0], share[1]
    total_w = first[:, SUB:, :, :blk]
    sum_x = first[:, SUB:, :, blk : 2 * blk]
    sum_xx = first[:, SUB:, :, 2 * blk : 3 * blk]
    sum_y = second[:, SUB:, :, :blk]
    sum_xy = second[:, SUB:, :, blk : 2 * blk]
    sum_yy = second[:, :SUB, :, :blk]
    numer = total_w * sum_xy - sum_x * sum_y
    var_x = jnp.maximum(total_w * sum_xx - sum_x * sum_x, 0.05 * total_w * sum_xx)
    var_y = jnp.maximum(total_w * sum_yy - sum_y * sum_y, 0.05 * total_w * sum_yy)
    return numer / jnp.sqrt(var_x * var_y)


def weigh_kernel(x_ref, obs_ref, qw_ref, out_ref):
    blk = x_ref.shape[0]
    weights = obs_ref[...].astype(jnp.float32) * qw_ref[...].astype(jnp.float32)
    out_ref[:blk, :] = x_ref[...]
    out_ref[blk:, :] = weights.astype(jnp.bfloat16)


def weigh(x, observed, qweights, part):
    blk, width = x.shape
    depth = min(2048, width // HALVES)
    count = width // HALVES // depth
    spec = pl.BlockSpec((blk, depth), lambda i: (0, part * count + i))
    return pl.pallas_call(
        weigh_kernel,
        grid=(count,),
        out_shape=jax.ShapeDtypeStruct((2 * blk, width // HALVES), jnp.bfloat16),
        in_specs=[spec] * 3,
        out_specs=pl.BlockSpec((2 * blk, depth), lambda i: (0, i)),
        compiler_params=params(),
        cost_estimate=pl.CostEstimate(
            flops=blk * width, bytes_accessed=blk * width * 12 // HALVES, transcendentals=0
        ),
        name="weigh",
    )(x, observed, qweights)


def fill_slabs(slabs, xw_ref, offset):
    blk, width = xw_ref.shape[0] // 2, xw_ref.shape[1]
    step = min(512, width)

    @pl.loop(0, width // step)
    def _(i):
        start = pl.multiple_of(i * step, step)
        wide = xw_ref[:, pl.ds(start, step)].astype(jnp.float32)
        for g in range(blk // SUB):
            rows = slice(g * SUB, (g + 1) * SUB)
            slab = jnp.concatenate([wide[:blk][rows], wide[blk:][rows]], 0)
            slabs[g, :, pl.ds(offset + start, step)] = slab.astype(jnp.bfloat16)


def send_slabs(slabs, pick_ref, send_ref, sems):
    mine = lax.div(lax.axis_index("dp"), PLANE)
    partner = mine + 1 - 2 * lax.rem(mine, 2)
    copies = []
    for c in range(PLANE):
        for t, plane in enumerate((mine, partner)):
            group = pick_ref[plane * PLANE + c]
            copies.append(pltpu.make_async_copy(slabs.at[group], send_ref.at[c, t], sems.at[c, t]))
    for copy in copies:
        copy.start()
    for copy in copies:
        copy.wait()


def own_pack_kernel(pick_ref, *refs):
    halves, (send_ref, slabs, sems) = refs[:HALVES], refs[HALVES:]
    for part, ref in enumerate(halves):
        fill_slabs(slabs, ref, part * ref.shape[1])
    send_slabs(slabs, pick_ref, send_ref, sems)


def far_pack_kernel(pick_ref, *refs):
    outer, inner = refs[:HALVES], refs[HALVES : 2 * HALVES]
    send_ref, slabs, sems = refs[2 * HALVES + 1 :]
    plane = lax.div(lax.axis_index("dp"), PLANE)
    is_inner = (plane == 1) | (plane == 2)

    @pl.when(is_inner)
    def _():
        for part, ref in enumerate(inner):
            fill_slabs(slabs, ref, part * ref.shape[1])

    @pl.when(jnp.logical_not(is_inner))
    def _():
        for part, ref in enumerate(outer):
            fill_slabs(slabs, ref, part * ref.shape[1])

    send_slabs(slabs, pick_ref, send_ref, sems)


def pack_call(kernel, name, specs, blk, width, weight, *operands):
    return pl.pallas_call(
        kernel,
        out_shape=jax.ShapeDtypeStruct((PLANE, 2, SLAB, width), jnp.bfloat16),
        in_specs=[pl.BlockSpec(memory_space=pltpu.SMEM)] + specs,
        out_specs=pl.BlockSpec(memory_space=pl.ANY),
        scratch_shapes=[pltpu.VMEM((blk // SUB, SLAB, width), jnp.bfloat16), pltpu.SemaphoreType.DMA((PLANE, 2))],
        compiler_params=params(),
        cost_estimate=pl.CostEstimate(
            flops=blk * width * 4, bytes_accessed=weight * (PLANE * 2 * SLAB * 2 + blk * 4) * width, transcendentals=0
        ),
        name=name,
    )(*operands)


def own_pack(pick, halves):
    rows, width = halves[0].shape
    specs = [pl.BlockSpec(memory_space=pltpu.VMEM)] * HALVES
    return pack_call(own_pack_kernel, "own_pack", specs, rows // 2, HALVES * width, 1, pick, *halves)


def far_pack(pick, outer, inner, after):
    rows, width = outer[0].shape
    specs = [pl.BlockSpec(memory_space=pltpu.VMEM)] * (2 * HALVES) + [pl.BlockSpec(memory_space=pl.ANY)]
    return pack_call(
        far_pack_kernel, "far_pack", specs, rows // 2, HALVES * width, 1, pick, *outer, *inner, after
    )


def place_kernel(ops_ref, *refs):
    blocks, (after_ref, keep_ref, give_ref, table, *targets) = refs[: 2 * HALVES], refs[2 * HALVES :]
    rows, depth = blocks[0].shape
    blk = rows // 2
    width = targets[0].shape[0]
    chunks = width // HALVES // depth
    step = min(512, width)
    size = min(256, depth)
    now = pl.program_id(1)

    def fill(one_ref, two_ref):
        diagonal = lax.broadcasted_iota(jnp.int32, (size, size), 0) == lax.broadcasted_iota(
            jnp.int32, (size, size), 1
        )
        identity = jnp.where(diagonal, 1.0, 0.0).astype(jnp.bfloat16)
        for i in range(depth // size):
            cols = slice(i * size, (i + 1) * size)
            four = [one_ref[:blk, cols], two_ref[:blk, cols], one_ref[blk:, cols], two_ref[blk:, cols]]
            table[cols, :] = lax.dot_general(
                identity,
                jnp.concatenate(four, 0),
                (((1,), (1,)), ((), ())),
                preferred_element_type=jnp.float32,
            )

    for k, target in enumerate(targets):
        for part in range(HALVES):
            pair = (blocks[part], blocks[HALVES + part])

            @pl.when((pl.program_id(0) == k) & (lax.div(now, chunks) == part))
            def _():
                fill(*(pair if k == 0 else pair[::-1]))

        @pl.when(pl.program_id(0) == k)
        def _():
            @pl.loop(0, depth // UNROLL)
            def _(i):
                base = pl.multiple_of(i * UNROLL, UNROLL)
                for j in range(UNROLL):
                    target[pl.ds(ops_ref[0, 0, base + j], 1), :] = table[pl.ds(base + j, 1), :]

    @pl.when((pl.program_id(0) == pl.num_programs(0) - 1) & (now == pl.num_programs(1) - 1))
    def _():
        lane = lax.broadcasted_iota(jnp.int32, (step, LANES), 1)
        first = lax.rem(lane, 2 * blk) < blk

        @pl.loop(0, width // step)
        def _(i):
            here = pl.ds(pl.multiple_of(i * step, step), step)
            values = [target[here, :] for target in targets]
            keep_ref[here, :] = jnp.where(first, *values).astype(jnp.bfloat16)
            give_ref[here, :] = jnp.where(first, *values[::-1]).astype(jnp.bfloat16)


def place(ops, one, two, after, weight):
    count, _, width = ops.shape
    rows, span = one[0].shape
    depth = min(2048, span)
    chunks = span // depth
    some = [
        pl.BlockSpec((rows, depth), lambda k, i, part=part: (0, jnp.clip(i - part * chunks, 0, chunks - 1)))
        for part in range(HALVES)
    ]
    whole = pl.BlockSpec((width, LANES), lambda k, i: (0, 0))
    return pl.pallas_call(
        place_kernel,
        grid=(count, HALVES * chunks),
        out_shape=(jax.ShapeDtypeStruct((width, LANES), jnp.bfloat16),) * 2,
        in_specs=[
            pl.BlockSpec((1, 1, depth), lambda k, i: (k, 0, i), memory_space=pltpu.SMEM),
            *some,
            *some,
            pl.BlockSpec(memory_space=pl.ANY),
        ],
        out_specs=(whole, whole),
        scratch_shapes=[pltpu.VMEM((depth, LANES), jnp.float32)] + [pltpu.VMEM((width, LANES), jnp.float32)] * count,
        compiler_params=params(),
        cost_estimate=pl.CostEstimate(flops=0, bytes_accessed=weight * width * LANES, transcendentals=0),
        name="place",
    )(ops, *one, *two, after)


def ratio(total_w, sum_x, sum_xx, sum_y, sum_xy, sum_yy):
    numer = total_w * sum_xy - sum_x * sum_y
    var_x = jnp.maximum(total_w * sum_xx - sum_x * sum_x, 0.05 * total_w * sum_xx)
    var_y = jnp.maximum(total_w * sum_yy - sum_y * sum_y, 0.05 * total_w * sum_yy)
    return numer / jnp.sqrt(var_x * var_y)


def plane_sums_kernel(own_ref, far_ref, *refs):
    moved_refs, (mine_ref, near_ref, back_ref, acc) = refs[:4], refs[4:]
    rows, depth = own_ref.shape
    step = min(1024, depth)
    half = LANES // 2
    slabs = rows // SLAB // 2

    @pl.when(pl.program_id(0) == 0)
    def _():
        acc[...] = jnp.zeros_like(acc)

    for i in range(depth // step):
        cols = slice(i * step, (i + 1) * step)
        is_x = lax.broadcasted_iota(jnp.int32, (slabs, SLAB, step), 1) < SUB
        low = lax.broadcasted_iota(jnp.int32, (step, LANES), 1) < half
        fulls = [
            ref[:, cols].astype(jnp.float32).reshape(slabs, 2, SLAB, step) for ref in (own_ref, far_ref)
        ]
        for t in range(2):
            weights, products = [], []
            for full in fulls:
                wide = full[:, t]
                rolled = pltpu.roll(wide, SUB, 1)
                product = wide * rolled
                products.append(jnp.where(is_x, product * wide, product).reshape(slabs * SLAB, step))
                even = rolled.reshape(slabs // 2, 2, SLAB, step)[:, 0]
                odd = wide.reshape(slabs // 2, 2, SLAB, step)[:, 1]
                weights.append(jnp.where(is_x[: slabs // 2], even, odd).reshape(slabs // 2 * SLAB, step))
            linear, square = [], []
            for a in range(2):
                values = moved_refs[2 * t + a][cols, :].astype(jnp.float32)
                swapped = pltpu.roll(values, half, 1)
                product = values * swapped
                linear.append(jnp.where(low, product, values).astype(jnp.bfloat16))
                square.append(product * (values if a == 0 else swapped))
            right = jnp.concatenate(linear + [jnp.where(low, *square).astype(jnp.bfloat16)], 1)
            left = jnp.concatenate(weights + products, 0).astype(jnp.bfloat16)
            acc[t] += jnp.dot(left, right, preferred_element_type=jnp.float32)

    @pl.when(pl.program_id(0) == pl.num_programs(0) - 1)
    def _():
        count = 2 * slabs * SUB
        tiles = count // SLAB
        top = lax.broadcasted_iota(jnp.int32, (tiles, SLAB, LANES), 1) < SUB
        low = lax.broadcasted_iota(jnp.int32, (count, LANES), 1) < half
        early = lax.rem(lax.broadcasted_iota(jnp.int32, (count, LANES), 1), half) < half // 2
        me = lax.axis_index("dp")
        results = []
        for t in range(2):
            ratios = []
            for a in range(2):
                lanes = slice(a * LANES, (a + 1) * LANES)
                with_w = acc[t, :count, lanes]
                with_y = acc[t, count:, lanes].reshape(tiles, 2, SLAB, LANES)
                even, odd = with_y[:, 0], with_y[:, 1]
                y = jnp.where(top, pltpu.roll(even, SUB, 1), odd).reshape(count, LANES)
                yy = jnp.where(top, even, pltpu.roll(odd, SUB, 1)).reshape(count, LANES)
                sum_xx = acc[t, :count, 2 * LANES :]
                if a == 1:
                    sum_xx = pltpu.roll(sum_xx, half, 1)
                ratios.append(
                    ratio(
                        pltpu.roll(with_w, half, 1), with_w, sum_xx, pltpu.roll(y, half, 1), y, pltpu.roll(yy, half, 1)
                    )
                )
            kept, got = ratios
            got = jnp.where(early, pltpu.roll(got, LANES - half // 2, 1), pltpu.roll(got, half // 2, 1))
            straight = jnp.where(low, kept, pltpu.roll(got, half, 1))
            crossed = jnp.where(low, got, pltpu.roll(kept, half, 1))
            results.append(jnp.where(lax.rem(me, 2) == 0, straight, crossed))
        mine, near = results
        mine_ref[...] = mine
        near_ref[...] = near
        mine, near = mine.reshape(tiles, SLAB, LANES), near.reshape(tiles, SLAB, LANES)
        even = jnp.where(top, mine, pltpu.roll(near, SUB, 1))
        odd = jnp.where(top, pltpu.roll(mine, SUB, 1), near)
        upper = lax.div(me, 2 * PLANE)
        for i in range(tiles):
            part, c = 2 * i // slabs, 2 * i % slabs
            slot = part + upper - 2 * part * upper
            back_ref[slot, c] = even[i]
            back_ref[slot, c + 1] = odd[i]


def plane_sums(own, far, moved):
    rows, width = own.shape
    depth = min(2048, width)
    count = rows // 2
    part = pl.BlockSpec((rows, depth), lambda i: (0, i))
    placed = pl.BlockSpec((depth, LANES), lambda i: (i, 0))
    shapes = ((count, LANES), (count, LANES), (2, PLANE, SLAB, LANES))
    return pl.pallas_call(
        plane_sums_kernel,
        grid=(width // depth,),
        out_shape=tuple(jax.ShapeDtypeStruct(shape, jnp.float32) for shape in shapes),
        in_specs=[part, part, placed, placed, placed, placed],
        out_specs=tuple(pl.BlockSpec(shape, lambda i, shape=shape: (0,) * len(shape)) for shape in shapes),
        scratch_shapes=[pltpu.VMEM((2, 3 * count, 3 * LANES), jnp.float32)],
        compiler_params=params(),
        cost_estimate=pl.CostEstimate(
            flops=18 * rows * width * LANES, bytes_accessed=width * (4 * rows + 8 * LANES), transcendentals=0
        ),
        name="plane_sums",
    )(own, far, *moved)


def shards_by_plane(intensities, observed, qweights, ops, pick):
    blk = intensities.shape[0]
    groups = PLANES * PLANE
    swap = [(i, i ^ 1) for i in range(groups)]
    beside = [(i, i ^ PLANE) for i in range(groups)]
    across = [(i, i ^ (2 * PLANE)) for i in range(groups)]
    middle = [(i, 3 * PLANE + 2 * (i % PLANE) - i) for i in range(PLANE, 3 * PLANE)]
    outward = [(i, i - PLANE if i < 2 * PLANE else i + PLANE) for i in range(PLANE, 3 * PLANE)]
    rings = [[z * PLANE + c for c in range(PLANE)] for z in range(PLANES)]
    couples = [[z * PLANE + c for z in (odd, odd + 2) for c in range(PLANE)] for odd in range(2)]
    plane = lax.axis_index("dp") // PLANE
    odd, upper = plane % 2 == 1, plane >= 2

    def spread(send):
        got = lax.all_to_all(send, "dp", split_axis=0, concat_axis=0, axis_index_groups=rings, tiled=True)
        return got.reshape(PLANE * 2 * SLAB, send.shape[-1])

    own_pick = pick[:, 0]
    core = lax.axis_index("dp") % 2
    ops = lax.dynamic_slice_in_dim(ops, core * (NOPS // 2), NOPS // 2, 0)[:, None, :]
    mine = [weigh(intensities, observed, qweights, part) for part in range(HALVES)]
    near = [lax.ppermute(rows, "dp", beside) for rows in mine]
    mid = [lax.ppermute(rows, "dp", middle) for rows in mine]
    other = [lax.ppermute(rows, "dp", swap) for rows in mine]
    far_pick = lax.ppermute(own_pick, "dp", across)

    own_got = spread(own_pack(own_pick, mine))
    keep, give = place(ops, mine, other, own_pick, 4)
    own_moved = [keep, lax.ppermute(give, "dp", swap)]

    near, mid, far_pick, keep = lax.optimization_barrier((near, mid, far_pick, keep))
    own_moved[0] = keep
    outer = [lax.ppermute(rows, "dp", outward) for rows in mid]
    inner = [lax.ppermute(rows, "dp", middle) for rows in near]
    near_other = [lax.ppermute(rows, "dp", swap) for rows in near]
    keep, give = place(ops, near, near_other, own_pick, 256)
    far_send = far_pack(far_pick, outer, inner, keep)
    far_got = spread(far_send)
    moved = own_moved + [keep, lax.ppermute(give, "dp", swap)]
    ours, theirs, back = plane_sums(own_got, far_got, moved)

    from_near = lax.ppermute(theirs, "dp", beside)
    pair = [each.reshape(2, PLANE, SUB, NOPS * blk) for each in (ours, from_near)]
    pair = jnp.stack(pair, 1)
    pair = jnp.where(odd, pair[:, ::-1], pair)
    pair = jnp.where(upper, pair[::-1], pair)
    corr = pair.reshape(groups * SUB, NOPS * blk).T.reshape(NOPS, blk, groups * SUB)

    back = back.reshape(2 * PLANE, 2 * SUB, NOPS * blk)
    back = lax.all_to_all(back, "dp", split_axis=0, concat_axis=0, axis_index_groups=couples, tiled=True)
    back = back.reshape(2, PLANE, 2, SUB, NOPS, blk)
    back = jnp.where(odd, back[:, :, ::-1], back)
    returned = jnp.transpose(back, (4, 0, 2, 1, 3, 5)).reshape(NOPS, 1, groups, SUB, blk)
    return (corr, returned)


def shards(intensities, observed, qweights, ops, pick):
    if lax.axis_size("dp") == PLANES * PLANE and lax.axis_size("refl") == 1:
        return shards_by_plane(intensities, observed, qweights, ops, pick)
    return shards_direct(intensities, observed, qweights, ops, pick)


def shards_direct(intensities, observed, qweights, ops, pick):
    blk, width = intensities.shape
    groups = lax.axis_size("dp")
    shares = lax.axis_size("refl")
    local_ops = ops - lax.axis_index("refl") * width
    send, own_w = pack(pick[:, 0], intensities, observed, qweights)
    got = lax.all_to_all(send, "dp", split_axis=0, concat_axis=0, tiled=True)
    moved = move(local_ops, intensities, own_w)
    stats = sums(got.reshape(groups * SLAB, width), moved)
    if shares > 1:
        stats = lax.psum(stats, "refl")
    stats = stats.reshape(2, groups, SLAB, NOPS, LANES)
    full = pearson(stats, blk)
    rows = blk // shares
    if shares > 1:
        full = lax.dynamic_slice_in_dim(full, lax.axis_index("refl") * rows, rows, 3)
    corr = jnp.transpose(full, (2, 3, 0, 1)).reshape(NOPS, rows, groups * SUB)
    back = lax.all_to_all(full, "dp", split_axis=0, concat_axis=0, tiled=True)
    returned = jnp.transpose(back, (2, 0, 1, 3))[:, None]
    return (corr, returned)


def solution(mesh):
    return jax.shard_map(
        shards,
        mesh=mesh,
        in_specs=(
            P("dp", "refl"),
            P("dp", "refl"),
            P("dp", "refl"),
            P(None, "refl"),
            P(None, "dp"),
        ),
        out_specs=(P(None, ("dp", "refl"), None), P(None, "dp", None, None, "refl")),
        check_vma=False,
    )
```

```python
import functools

import jax
import jax.numpy as jnp
from jax import lax
from jax.experimental import pallas as pl
from jax.experimental.pallas import tpu as pltpu
from jax.sharding import PartitionSpec as P

SUB = 4
NOPS = 4
LANES = 128
SLAB = 2 * SUB
MIB = 1024 * 1024
PLANES = 4
PLANE = 8
UNROLL = 64
HALVES = 2


def params():
    return pltpu.CompilerParams(vmem_limit_bytes=56 * MIB)


def pack_kernel(pick_ref, x_ref, obs_ref, qw_ref, send_ref, w_ref, slabs, sems):
    blk, width = x_ref.shape
    step = min(512, width)

    @pl.loop(0, width // step)
    def _(i):
        cols = pl.ds(pl.multiple_of(i * step, step), step)
        wide_w = obs_ref[:, cols].astype(jnp.float32) * qw_ref[:, cols].astype(jnp.float32)
        wide_x = x_ref[:, cols].astype(jnp.float32)
        w_ref[:, cols] = wide_w.astype(jnp.bfloat16)
        for g in range(blk // SUB):
            rows = slice(g * SUB, (g + 1) * SUB)
            slab = jnp.concatenate([wide_x[rows], wide_w[rows]], 0)
            slabs[g, :, cols] = slab.astype(jnp.bfloat16)

    groups = send_ref.shape[0]

    def copy(d):
        return pltpu.make_async_copy(slabs.at[pick_ref[d]], send_ref.at[d], sems.at[d])

    @pl.loop(0, groups)
    def _(d):
        copy(d).start()

    @pl.loop(0, groups)
    def _(d):
        copy(d).wait()


def pack(pick, intensities, observed, qweights):
    blk, width = intensities.shape
    groups = pick.shape[0]
    whole = pl.BlockSpec(memory_space=pltpu.VMEM)
    return pl.pallas_call(
        pack_kernel,
        out_shape=(
            jax.ShapeDtypeStruct((groups, SLAB, width), jnp.bfloat16),
            jax.ShapeDtypeStruct((blk, width), jnp.bfloat16),
        ),
        in_specs=[pl.BlockSpec(memory_space=pltpu.SMEM), whole, whole, whole],
        out_specs=(pl.BlockSpec(memory_space=pl.ANY), whole),
        scratch_shapes=[
            pltpu.VMEM((blk // SUB, SLAB, width), jnp.bfloat16),
            pltpu.SemaphoreType.DMA((groups,)),
        ],
        compiler_params=params(),
        cost_estimate=pl.CostEstimate(
            flops=blk * width * 4, bytes_accessed=(groups * SLAB * 2 + blk * 10) * width, transcendentals=0
        ),
        name="pack",
    )(pick, intensities, observed, qweights)


def move_kernel(ops_ref, x_ref, w_ref, moved_ref, table, target):
    blk, width = x_ref.shape

    @pl.when(pl.program_id(0) == 0)
    def _():
        @pl.loop(0, width // LANES)
        def _(i):
            cols = pl.ds(pl.multiple_of(i * LANES, LANES), LANES)
            wide_x = x_ref[:, cols].astype(jnp.float32)
            wide_w = w_ref[:, cols].astype(jnp.float32)
            wx = (wide_w * wide_x).astype(jnp.bfloat16).astype(jnp.float32)
            wxx = (wide_w * wide_x * wide_x).astype(jnp.bfloat16).astype(jnp.float32)
            stacked = jnp.concatenate([wide_w, wx, wxx, jnp.zeros((LANES - 3 * blk, LANES), jnp.float32)], 0)
            table[cols, :] = stacked.T

    unroll = 16

    @pl.loop(0, width // unroll)
    def _(i):
        base = pl.multiple_of(i * unroll, unroll)
        for j in range(unroll):
            to = ops_ref[0, 0, base + j]
            target[pl.ds(to, 1), :] = table[pl.ds(base + j, 1), :]

    step = min(512, width)

    @pl.loop(0, width // step)
    def _(i):
        rows = pl.ds(pl.multiple_of(i * step, step), step)
        moved_ref[rows, :] = target[rows, :].astype(jnp.bfloat16)


def move(local_ops, intensities, own_w):
    blk, width = intensities.shape
    whole = pl.BlockSpec(memory_space=pltpu.VMEM)
    return pl.pallas_call(
        move_kernel,
        grid=(NOPS,),
        out_shape=jax.ShapeDtypeStruct((width, NOPS * LANES), jnp.bfloat16),
        in_specs=[
            pl.BlockSpec((1, 1, width), lambda k: (k, 0, 0), memory_space=pltpu.SMEM),
            whole,
            whole,
        ],
        out_specs=pl.BlockSpec((width, LANES), lambda k: (0, k)),
        scratch_shapes=[
            pltpu.VMEM((width, LANES), jnp.float32),
            pltpu.VMEM((width, LANES), jnp.float32),
        ],
        compiler_params=params(),
        cost_estimate=pl.CostEstimate(
            flops=0, bytes_accessed=NOPS * width * LANES * 100, transcendentals=0
        ),
        name="move",
    )(local_ops[:, None, :], intensities, own_w)


def sums_kernel(got_ref, moved_ref, out_ref):
    rows, depth = got_ref.shape
    step = min(512, depth)

    @pl.when(pl.program_id(0) == 0)
    def _():
        out_ref[...] = jnp.zeros_like(out_ref)

    is_x = lax.broadcasted_iota(jnp.int32, (rows // SLAB, SLAB, step), 1) < SUB

    @pl.loop(0, depth // step)
    def _(i):
        cols = pl.ds(pl.multiple_of(i * step, step), step)
        raw = got_ref[:, cols]
        wide = raw.astype(jnp.float32).reshape(rows // SLAB, SLAB, step)
        product = wide * pltpu.roll(wide, SUB, 1)
        second = jnp.where(is_x, product * wide, product)
        second = second.reshape(rows, step).astype(jnp.bfloat16)
        right = moved_ref[cols, :]
        out_ref[0] += jnp.dot(raw, right, preferred_element_type=jnp.float32)
        out_ref[1] += jnp.dot(second, right, preferred_element_type=jnp.float32)


def sums(got, moved):
    rows, width = got.shape
    depth = min(2048, width)
    return pl.pallas_call(
        sums_kernel,
        grid=(width // depth,),
        out_shape=jax.ShapeDtypeStruct((2, rows, moved.shape[1]), jnp.float32),
        in_specs=[
            pl.BlockSpec((rows, depth), lambda i: (0, i)),
            pl.BlockSpec((depth, moved.shape[1]), lambda i: (i, 0)),
        ],
        out_specs=pl.BlockSpec((2, rows, moved.shape[1]), lambda i: (0, 0, 0)),
        compiler_params=params(),
        cost_estimate=pl.CostEstimate(
            flops=4 * rows * width * moved.shape[1],
            bytes_accessed=2 * width * (rows + moved.shape[1]),
            transcendentals=0,
        ),
        name="sums",
    )(got, moved)


def pearson(share, blk):
    first, second = share[0], share[1]
    total_w = first[:, SUB:, :, :blk]
    sum_x = first[:, SUB:, :, blk : 2 * blk]
    sum_xx = first[:, SUB:, :, 2 * blk : 3 * blk]
    sum_y = second[:, SUB:, :, :blk]
    sum_xy = second[:, SUB:, :, blk : 2 * blk]
    sum_yy = second[:, :SUB, :, :blk]
    numer = total_w * sum_xy - sum_x * sum_y
    var_x = jnp.maximum(total_w * sum_xx - sum_x * sum_x, 0.05 * total_w * sum_xx)
    var_y = jnp.maximum(total_w * sum_yy - sum_y * sum_y, 0.05 * total_w * sum_yy)
    return numer / jnp.sqrt(var_x * var_y)


def weigh_kernel(x_ref, obs_ref, qw_ref, out_ref):
    blk = x_ref.shape[0]
    weights = obs_ref[...].astype(jnp.float32) * qw_ref[...].astype(jnp.float32)
    out_ref[:blk, :] = x_ref[...]
    out_ref[blk:, :] = weights.astype(jnp.bfloat16)


def weigh(x, observed, qweights, part):
    blk, width = x.shape
    depth = min(2048, width // HALVES)
    count = width // HALVES // depth
    spec = pl.BlockSpec((blk, depth), lambda i: (0, part * count + i))
    return pl.pallas_call(
        weigh_kernel,
        grid=(count,),
        out_shape=jax.ShapeDtypeStruct((2 * blk, width // HALVES), jnp.bfloat16),
        in_specs=[spec] * 3,
        out_specs=pl.BlockSpec((2 * blk, depth), lambda i: (0, i)),
        compiler_params=params(),
        cost_estimate=pl.CostEstimate(
            flops=blk * width, bytes_accessed=blk * width * 12 // HALVES, transcendentals=0
        ),
        name="weigh",
    )(x, observed, qweights)


def fill_slabs(slabs, xw_ref, offset):
    blk, width = xw_ref.shape[0] // 2, xw_ref.shape[1]
    step = min(512, width)

    @pl.loop(0, width // step)
    def _(i):
        start = pl.multiple_of(i * step, step)
        wide = xw_ref[:, pl.ds(start, step)].astype(jnp.float32)
        for g in range(blk // SUB):
            rows = slice(g * SUB, (g + 1) * SUB)
            slab = jnp.concatenate([wide[:blk][rows], wide[blk:][rows]], 0)
            slabs[g, :, pl.ds(offset + start, step)] = slab.astype(jnp.bfloat16)


def send_slabs(slabs, pick_ref, send_ref, sems):
    mine = lax.div(lax.axis_index("dp"), PLANE)
    partner = mine + 1 - 2 * lax.rem(mine, 2)
    copies = []
    for c in range(PLANE):
        for t, plane in enumerate((mine, partner)):
            group = pick_ref[plane * PLANE + c]
            copies.append(pltpu.make_async_copy(slabs.at[group], send_ref.at[c, t], sems.at[c, t]))
    for copy in copies:
        copy.start()
    for copy in copies:
        copy.wait()


def own_pack_kernel(pick_ref, *refs):
    halves, (send_ref, slabs, sems) = refs[:HALVES], refs[HALVES:]
    for part, ref in enumerate(halves):
        fill_slabs(slabs, ref, part * ref.shape[1])
    send_slabs(slabs, pick_ref, send_ref, sems)


def far_pack_kernel(pick_ref, *refs):
    outer, inner = refs[:HALVES], refs[HALVES : 2 * HALVES]
    send_ref, slabs, sems = refs[2 * HALVES + 1 :]
    plane = lax.div(lax.axis_index("dp"), PLANE)
    is_inner = (plane == 1) | (plane == 2)

    @pl.when(is_inner)
    def _():
        for part, ref in enumerate(inner):
            fill_slabs(slabs, ref, part * ref.shape[1])

    @pl.when(jnp.logical_not(is_inner))
    def _():
        for part, ref in enumerate(outer):
            fill_slabs(slabs, ref, part * ref.shape[1])

    send_slabs(slabs, pick_ref, send_ref, sems)


def pack_call(kernel, name, specs, blk, width, weight, *operands):
    return pl.pallas_call(
        kernel,
        out_shape=jax.ShapeDtypeStruct((PLANE, 2, SLAB, width), jnp.bfloat16),
        in_specs=[pl.BlockSpec(memory_space=pltpu.SMEM)] + specs,
        out_specs=pl.BlockSpec(memory_space=pl.ANY),
        scratch_shapes=[pltpu.VMEM((blk // SUB, SLAB, width), jnp.bfloat16), pltpu.SemaphoreType.DMA((PLANE, 2))],
        compiler_params=params(),
        cost_estimate=pl.CostEstimate(
            flops=blk * width * 4, bytes_accessed=weight * (PLANE * 2 * SLAB * 2 + blk * 4) * width, transcendentals=0
        ),
        name=name,
    )(*operands)


def own_pack(pick, halves):
    rows, width = halves[0].shape
    specs = [pl.BlockSpec(memory_space=pltpu.VMEM)] * HALVES
    return pack_call(own_pack_kernel, "own_pack", specs, rows // 2, HALVES * width, 1, pick, *halves)


def far_pack(pick, outer, inner, after):
    rows, width = outer[0].shape
    specs = [pl.BlockSpec(memory_space=pltpu.VMEM)] * (2 * HALVES) + [pl.BlockSpec(memory_space=pl.ANY)]
    return pack_call(
        far_pack_kernel, "far_pack", specs, rows // 2, HALVES * width, 1, pick, *outer, *inner, after
    )


def place_kernel(ops_ref, *refs):
    blocks, (after_ref, keep_ref, give_ref, table, *targets) = refs[: 2 * HALVES], refs[2 * HALVES :]
    rows, depth = blocks[0].shape
    blk = rows // 2
    width = targets[0].shape[0]
    chunks = width // HALVES // depth
    step = min(512, width)
    size = min(256, depth)
    now = pl.program_id(1)

    def fill(one_ref, two_ref):
        diagonal = lax.broadcasted_iota(jnp.int32, (size, size), 0) == lax.broadcasted_iota(
            jnp.int32, (size, size), 1
        )
        identity = jnp.where(diagonal, 1.0, 0.0).astype(jnp.bfloat16)
        for i in range(depth // size):
            cols = slice(i * size, (i + 1) * size)
            four = [one_ref[:blk, cols], two_ref[:blk, cols], one_ref[blk:, cols], two_ref[blk:, cols]]
            table[cols, :] = lax.dot_general(
                identity,
                jnp.concatenate(four, 0),
                (((1,), (1,)), ((), ())),
                preferred_element_type=jnp.float32,
            )

    for k, target in enumerate(targets):
        for part in range(HALVES):
            pair = (blocks[part], blocks[HALVES + part])

            @pl.when((pl.program_id(0) == k) & (lax.div(now, chunks) == part))
            def _():
                fill(*(pair if k == 0 else pair[::-1]))

        @pl.when(pl.program_id(0) == k)
        def _():
            @pl.loop(0, depth // UNROLL)
            def _(i):
                base = pl.multiple_of(i * UNROLL, UNROLL)
                for j in range(UNROLL):
                    target[pl.ds(ops_ref[0, 0, base + j], 1), :] = table[pl.ds(base + j, 1), :]

    @pl.when((pl.program_id(0) == pl.num_programs(0) - 1) & (now == pl.num_programs(1) - 1))
    def _():
        lane = lax.broadcasted_iota(jnp.int32, (step, LANES), 1)
        first = lax.rem(lane, 2 * blk) < blk

        @pl.loop(0, width // step)
        def _(i):
            here = pl.ds(pl.multiple_of(i * step, step), step)
            values = [target[here, :] for target in targets]
            keep_ref[here, :] = jnp.where(first, *values).astype(jnp.bfloat16)
            give_ref[here, :] = jnp.where(first, *values[::-1]).astype(jnp.bfloat16)


def place(ops, one, two, after, weight):
    count, _, width = ops.shape
    rows, span = one[0].shape
    depth = min(2048, span)
    chunks = span // depth
    some = [
        pl.BlockSpec((rows, depth), lambda k, i, part=part: (0, jnp.clip(i - part * chunks, 0, chunks - 1)))
        for part in range(HALVES)
    ]
    whole = pl.BlockSpec((width, LANES), lambda k, i: (0, 0))
    return pl.pallas_call(
        place_kernel,
        grid=(count, HALVES * chunks),
        out_shape=(jax.ShapeDtypeStruct((width, LANES), jnp.bfloat16),) * 2,
        in_specs=[
            pl.BlockSpec((1, 1, depth), lambda k, i: (k, 0, i), memory_space=pltpu.SMEM),
            *some,
            *some,
            pl.BlockSpec(memory_space=pl.ANY),
        ],
        out_specs=(whole, whole),
        scratch_shapes=[pltpu.VMEM((depth, LANES), jnp.float32)] + [pltpu.VMEM((width, LANES), jnp.float32)] * count,
        compiler_params=params(),
        cost_estimate=pl.CostEstimate(flops=0, bytes_accessed=weight * width * LANES, transcendentals=0),
        name="place",
    )(ops, *one, *two, after)


def ratio(total_w, sum_x, sum_xx, sum_y, sum_xy, sum_yy):
    numer = total_w * sum_xy - sum_x * sum_y
    var_x = jnp.maximum(total_w * sum_xx - sum_x * sum_x, 0.05 * total_w * sum_xx)
    var_y = jnp.maximum(total_w * sum_yy - sum_y * sum_y, 0.05 * total_w * sum_yy)
    return numer / jnp.sqrt(var_x * var_y)


def plane_sums_kernel(own_ref, far_ref, *refs):
    moved_refs, (mine_ref, near_ref, back_ref, acc) = refs[:4], refs[4:]
    rows, depth = own_ref.shape
    step = min(1024, depth)
    half = LANES // 2
    slabs = rows // SLAB // 2

    @pl.when(pl.program_id(0) == 0)
    def _():
        acc[...] = jnp.zeros_like(acc)

    for i in range(depth // step):
        cols = slice(i * step, (i + 1) * step)
        is_x = lax.broadcasted_iota(jnp.int32, (slabs, SLAB, step), 1) < SUB
        low = lax.broadcasted_iota(jnp.int32, (step, LANES), 1) < half
        fulls = [
            ref[:, cols].astype(jnp.float32).reshape(slabs, 2, SLAB, step) for ref in (own_ref, far_ref)
        ]
        for t in range(2):
            weights, products = [], []
            for full in fulls:
                wide = full[:, t]
                rolled = pltpu.roll(wide, SUB, 1)
                product = wide * rolled
                products.append(jnp.where(is_x, product * wide, product).reshape(slabs * SLAB, step))
                even = rolled.reshape(slabs // 2, 2, SLAB, step)[:, 0]
                odd = wide.reshape(slabs // 2, 2, SLAB, step)[:, 1]
                weights.append(jnp.where(is_x[: slabs // 2], even, odd).reshape(slabs // 2 * SLAB, step))
            linear, square = [], []
            for a in range(2):
                values = moved_refs[2 * t + a][cols, :].astype(jnp.float32)
                swapped = pltpu.roll(values, half, 1)
                product = values * swapped
                linear.append(jnp.where(low, product, values).astype(jnp.bfloat16))
                square.append(product * (values if a == 0 else swapped))
            right = jnp.concatenate(linear + [jnp.where(low, *square).astype(jnp.bfloat16)], 1)
            left = jnp.concatenate(weights + products, 0).astype(jnp.bfloat16)
            acc[t] += jnp.dot(left, right, preferred_element_type=jnp.float32)

    @pl.when(pl.program_id(0) == pl.num_programs(0) - 1)
    def _():
        count = 2 * slabs * SUB
        tiles = count // SLAB
        top = lax.broadcasted_iota(jnp.int32, (tiles, SLAB, LANES), 1) < SUB
        low = lax.broadcasted_iota(jnp.int32, (count, LANES), 1) < half
        early = lax.rem(lax.broadcasted_iota(jnp.int32, (count, LANES), 1), half) < half // 2
        me = lax.axis_index("dp")
        results = []
        for t in range(2):
            ratios = []
            for a in range(2):
                lanes = slice(a * LANES, (a + 1) * LANES)
                with_w = acc[t, :count, lanes]
                with_y = acc[t, count:, lanes].reshape(tiles, 2, SLAB, LANES)
                even, odd = with_y[:, 0], with_y[:, 1]
                y = jnp.where(top, pltpu.roll(even, SUB, 1), odd).reshape(count, LANES)
                yy = jnp.where(top, even, pltpu.roll(odd, SUB, 1)).reshape(count, LANES)
                sum_xx = acc[t, :count, 2 * LANES :]
                if a == 1:
                    sum_xx = pltpu.roll(sum_xx, half, 1)
                ratios.append(
                    ratio(
                        pltpu.roll(with_w, half, 1), with_w, sum_xx, pltpu.roll(y, half, 1), y, pltpu.roll(yy, half, 1)
                    )
                )
            kept, got = ratios
            got = jnp.where(early, pltpu.roll(got, LANES - half // 2, 1), pltpu.roll(got, half // 2, 1))
            straight = jnp.where(low, kept, pltpu.roll(got, half, 1))
            crossed = jnp.where(low, got, pltpu.roll(kept, half, 1))
            results.append(jnp.where(lax.rem(me, 2) == 0, straight, crossed))
        mine, near = results
        mine_ref[...] = mine
        near_ref[...] = near
        mine, near = mine.reshape(tiles, SLAB, LANES), near.reshape(tiles, SLAB, LANES)
        even = jnp.where(top, mine, pltpu.roll(near, SUB, 1))
        odd = jnp.where(top, pltpu.roll(mine, SUB, 1), near)
        upper = lax.div(me, 2 * PLANE)
        for i in range(tiles):
            part, c = 2 * i // slabs, 2 * i % slabs
            slot = part + upper - 2 * part * upper
            back_ref[slot, c] = even[i]
            back_ref[slot, c + 1] = odd[i]


def plane_sums(own, far, moved):
    rows, width = own.shape
    depth = min(2048, width)
    count = rows // 2
    part = pl.BlockSpec((rows, depth), lambda i: (0, i))
    placed = pl.BlockSpec((depth, LANES), lambda i: (i, 0))
    shapes = ((count, LANES), (count, LANES), (2, PLANE, SLAB, LANES))
    return pl.pallas_call(
        plane_sums_kernel,
        grid=(width // depth,),
        out_shape=tuple(jax.ShapeDtypeStruct(shape, jnp.float32) for shape in shapes),
        in_specs=[part, part, placed, placed, placed, placed],
        out_specs=tuple(pl.BlockSpec(shape, lambda i, shape=shape: (0,) * len(shape)) for shape in shapes),
        scratch_shapes=[pltpu.VMEM((2, 3 * count, 3 * LANES), jnp.float32)],
        compiler_params=params(),
        cost_estimate=pl.CostEstimate(
            flops=18 * rows * width * LANES, bytes_accessed=width * (4 * rows + 8 * LANES), transcendentals=0
        ),
        name="plane_sums",
    )(own, far, *moved)


def shards_by_plane(intensities, observed, qweights, ops, pick):
    blk = intensities.shape[0]
    groups = PLANES * PLANE
    swap = [(i, i ^ 1) for i in range(groups)]
    beside = [(i, i ^ PLANE) for i in range(groups)]
    across = [(i, i ^ (2 * PLANE)) for i in range(groups)]
    middle = [(i, 3 * PLANE + 2 * (i % PLANE) - i) for i in range(PLANE, 3 * PLANE)]
    outward = [(i, i - PLANE if i < 2 * PLANE else i + PLANE) for i in range(PLANE, 3 * PLANE)]
    rings = [[z * PLANE + c for c in range(PLANE)] for z in range(PLANES)]
    couples = [[z * PLANE + c for z in (odd, odd + 2) for c in range(PLANE)] for odd in range(2)]
    plane = lax.axis_index("dp") // PLANE
    odd, upper = plane % 2 == 1, plane >= 2

    def spread(send):
        got = lax.all_to_all(send, "dp", split_axis=0, concat_axis=0, axis_index_groups=rings, tiled=True)
        return got.reshape(PLANE * 2 * SLAB, send.shape[-1])

    own_pick = pick[:, 0]
    core = lax.axis_index("dp") % 2
    ops = lax.dynamic_slice_in_dim(ops, core * (NOPS // 2), NOPS // 2, 0)[:, None, :]
    mine = [weigh(intensities, observed, qweights, part) for part in range(HALVES)]
    near = [lax.ppermute(rows, "dp", beside) for rows in mine]
    mid = [lax.ppermute(rows, "dp", middle) for rows in mine]
    other = [lax.ppermute(rows, "dp", swap) for rows in mine]
    far_pick = lax.ppermute(own_pick, "dp", across)

    own_got = spread(own_pack(own_pick, mine))
    keep, give = place(ops, mine, other, own_pick, 4)
    own_moved = [keep, lax.ppermute(give, "dp", swap)]

    near, mid, far_pick, keep = lax.optimization_barrier((near, mid, far_pick, keep))
    own_moved[0] = keep
    outer = [lax.ppermute(rows, "dp", outward) for rows in mid]
    inner = [lax.ppermute(rows, "dp", middle) for rows in near]
    near_other = [lax.ppermute(rows, "dp", swap) for rows in near]
    keep, give = place(ops, near, near_other, own_pick, 256)
    far_send = far_pack(far_pick, outer, inner, keep)
    near_moved = [keep, lax.ppermute(give, "dp", swap)]
    far_send, own_moved[1], near_moved[1] = lax.optimization_barrier((far_send, own_moved[1], near_moved[1]))
    far_got = spread(far_send)
    moved = own_moved + near_moved
    ours, theirs, back = plane_sums(own_got, far_got, moved)

    from_near = lax.ppermute(theirs, "dp", beside)
    pair = [each.reshape(2, PLANE, SUB, NOPS * blk) for each in (ours, from_near)]
    pair = jnp.stack(pair, 1)
    pair = jnp.where(odd, pair[:, ::-1], pair)
    pair = jnp.where(upper, pair[::-1], pair)
    corr = pair.reshape(groups * SUB, NOPS * blk).T.reshape(NOPS, blk, groups * SUB)

    back = back.reshape(2 * PLANE, 2 * SUB, NOPS * blk)
    back = lax.all_to_all(back, "dp", split_axis=0, concat_axis=0, axis_index_groups=couples, tiled=True)
    back = back.reshape(2, PLANE, 2, SUB, NOPS, blk)
    back = jnp.where(odd, back[:, :, ::-1], back)
    returned = jnp.transpose(back, (4, 0, 2, 1, 3, 5)).reshape(NOPS, 1, groups, SUB, blk)
    return (corr, returned)


def shards(intensities, observed, qweights, ops, pick):
    if lax.axis_size("dp") == PLANES * PLANE and lax.axis_size("refl") == 1:
        return shards_by_plane(intensities, observed, qweights, ops, pick)
    return shards_direct(intensities, observed, qweights, ops, pick)


def shards_direct(intensities, observed, qweights, ops, pick):
    blk, width = intensities.shape
    groups = lax.axis_size("dp")
    shares = lax.axis_size("refl")
    local_ops = ops - lax.axis_index("refl") * width
    send, own_w = pack(pick[:, 0], intensities, observed, qweights)
    got = lax.all_to_all(send, "dp", split_axis=0, concat_axis=0, tiled=True)
    moved = move(local_ops, intensities, own_w)
    stats = sums(got.reshape(groups * SLAB, width), moved)
    if shares > 1:
        stats = lax.psum(stats, "refl")
    stats = stats.reshape(2, groups, SLAB, NOPS, LANES)
    full = pearson(stats, blk)
    rows = blk // shares
    if shares > 1:
        full = lax.dynamic_slice_in_dim(full, lax.axis_index("refl") * rows, rows, 3)
    corr = jnp.transpose(full, (2, 3, 0, 1)).reshape(NOPS, rows, groups * SUB)
    back = lax.all_to_all(full, "dp", split_axis=0, concat_axis=0, tiled=True)
    returned = jnp.transpose(back, (2, 0, 1, 3))[:, None]
    return (corr, returned)


def solution(mesh):
    return jax.shard_map(
        shards,
        mesh=mesh,
        in_specs=(
            P("dp", "refl"),
            P("dp", "refl"),
            P("dp", "refl"),
            P(None, "refl"),
            P(None, "dp"),
        ),
        out_specs=(P(None, ("dp", "refl"), None), P(None, "dp", None, None, "refl")),
        check_vma=False,
    )
```

```python
import functools

import jax
import jax.numpy as jnp
from jax import lax
from jax.experimental import pallas as pl
from jax.experimental.pallas import tpu as pltpu
from jax.sharding import PartitionSpec as P

SUB = 4
NOPS = 4
LANES = 128
SLAB = 2 * SUB
VMEM_LIMIT = 56 * 1024 * 1024
PLANES = 4
PLANE = 8
UNROLL = 64


def params():
    return pltpu.CompilerParams(vmem_limit_bytes=VMEM_LIMIT)


def pack_kernel(pick_ref, x_ref, obs_ref, qw_ref, send_ref, w_ref, slabs, sems):
    blk, width = x_ref.shape
    step = min(512, width)

    @pl.loop(0, width // step)
    def _(i):
        cols = pl.ds(pl.multiple_of(i * step, step), step)
        wide_w = obs_ref[:, cols].astype(jnp.float32) * qw_ref[:, cols].astype(jnp.float32)
        wide_x = x_ref[:, cols].astype(jnp.float32)
        w_ref[:, cols] = wide_w.astype(jnp.bfloat16)
        for g in range(blk // SUB):
            rows = slice(g * SUB, (g + 1) * SUB)
            slab = jnp.concatenate([wide_x[rows], wide_w[rows]], 0)
            slabs[g, :, cols] = slab.astype(jnp.bfloat16)

    groups = send_ref.shape[0]

    def copy(d):
        return pltpu.make_async_copy(slabs.at[pick_ref[d]], send_ref.at[d], sems.at[d])

    @pl.loop(0, groups)
    def _(d):
        copy(d).start()

    @pl.loop(0, groups)
    def _(d):
        copy(d).wait()


def pack(pick, intensities, observed, qweights):
    blk, width = intensities.shape
    groups = pick.shape[0]
    whole = pl.BlockSpec(memory_space=pltpu.VMEM)
    return pl.pallas_call(
        pack_kernel,
        out_shape=(
            jax.ShapeDtypeStruct((groups, SLAB, width), jnp.bfloat16),
            jax.ShapeDtypeStruct((blk, width), jnp.bfloat16),
        ),
        in_specs=[pl.BlockSpec(memory_space=pltpu.SMEM), whole, whole, whole],
        out_specs=(pl.BlockSpec(memory_space=pl.ANY), whole),
        scratch_shapes=[
            pltpu.VMEM((blk // SUB, SLAB, width), jnp.bfloat16),
            pltpu.SemaphoreType.DMA((groups,)),
        ],
        compiler_params=params(),
        cost_estimate=pl.CostEstimate(
            flops=blk * width * 4, bytes_accessed=(groups * SLAB * 2 + blk * 10) * width, transcendentals=0
        ),
        name="pack",
    )(pick, intensities, observed, qweights)


def move_kernel(ops_ref, x_ref, w_ref, moved_ref, table, target):
    blk, width = x_ref.shape

    @pl.when(pl.program_id(0) == 0)
    def _():
        @pl.loop(0, width // LANES)
        def _(i):
            cols = pl.ds(pl.multiple_of(i * LANES, LANES), LANES)
            wide_x = x_ref[:, cols].astype(jnp.float32)
            wide_w = w_ref[:, cols].astype(jnp.float32)
            wx = (wide_w * wide_x).astype(jnp.bfloat16).astype(jnp.float32)
            wxx = (wide_w * wide_x * wide_x).astype(jnp.bfloat16).astype(jnp.float32)
            stacked = jnp.concatenate([wide_w, wx, wxx, jnp.zeros((LANES - 3 * blk, LANES), jnp.float32)], 0)
            table[cols, :] = stacked.T

    unroll = 16

    @pl.loop(0, width // unroll)
    def _(i):
        base = pl.multiple_of(i * unroll, unroll)
        for j in range(unroll):
            to = ops_ref[0, 0, base + j]
            target[pl.ds(to, 1), :] = table[pl.ds(base + j, 1), :]

    step = min(512, width)

    @pl.loop(0, width // step)
    def _(i):
        rows = pl.ds(pl.multiple_of(i * step, step), step)
        moved_ref[rows, :] = target[rows, :].astype(jnp.bfloat16)


def move(local_ops, intensities, own_w):
    blk, width = intensities.shape
    whole = pl.BlockSpec(memory_space=pltpu.VMEM)
    return pl.pallas_call(
        move_kernel,
        grid=(NOPS,),
        out_shape=jax.ShapeDtypeStruct((width, NOPS * LANES), jnp.bfloat16),
        in_specs=[
            pl.BlockSpec((1, 1, width), lambda k: (k, 0, 0), memory_space=pltpu.SMEM),
            whole,
            whole,
        ],
        out_specs=pl.BlockSpec((width, LANES), lambda k: (0, k)),
        scratch_shapes=[
            pltpu.VMEM((width, LANES), jnp.float32),
            pltpu.VMEM((width, LANES), jnp.float32),
        ],
        compiler_params=params(),
        cost_estimate=pl.CostEstimate(
            flops=0, bytes_accessed=NOPS * width * LANES * 100, transcendentals=0
        ),
        name="move",
    )(local_ops[:, None, :], intensities, own_w)


def sums_kernel(got_ref, moved_ref, out_ref):
    rows, depth = got_ref.shape
    step = min(512, depth)

    @pl.when(pl.program_id(0) == 0)
    def _():
        out_ref[...] = jnp.zeros_like(out_ref)

    is_x = lax.broadcasted_iota(jnp.int32, (rows // SLAB, SLAB, step), 1) < SUB

    @pl.loop(0, depth // step)
    def _(i):
        cols = pl.ds(pl.multiple_of(i * step, step), step)
        raw = got_ref[:, cols]
        wide = raw.astype(jnp.float32).reshape(rows // SLAB, SLAB, step)
        product = wide * pltpu.roll(wide, SUB, 1)
        second = jnp.where(is_x, product * wide, product)
        second = second.reshape(rows, step).astype(jnp.bfloat16)
        right = moved_ref[cols, :]
        out_ref[0] += jnp.dot(raw, right, preferred_element_type=jnp.float32)
        out_ref[1] += jnp.dot(second, right, preferred_element_type=jnp.float32)


def sums(got, moved):
    rows, width = got.shape
    depth = min(2048, width)
    return pl.pallas_call(
        sums_kernel,
        grid=(width // depth,),
        out_shape=jax.ShapeDtypeStruct((2, rows, moved.shape[1]), jnp.float32),
        in_specs=[
            pl.BlockSpec((rows, depth), lambda i: (0, i)),
            pl.BlockSpec((depth, moved.shape[1]), lambda i: (i, 0)),
        ],
        out_specs=pl.BlockSpec((2, rows, moved.shape[1]), lambda i: (0, 0, 0)),
        compiler_params=params(),
        cost_estimate=pl.CostEstimate(
            flops=4 * rows * width * moved.shape[1],
            bytes_accessed=2 * width * (rows + moved.shape[1]),
            transcendentals=0,
        ),
        name="sums",
    )(got, moved)


def pearson(share, blk):
    first, second = share[0], share[1]
    total_w = first[:, SUB:, :, :blk]
    sum_x = first[:, SUB:, :, blk : 2 * blk]
    sum_xx = first[:, SUB:, :, 2 * blk : 3 * blk]
    sum_y = second[:, SUB:, :, :blk]
    sum_xy = second[:, SUB:, :, blk : 2 * blk]
    sum_yy = second[:, :SUB, :, :blk]
    numer = total_w * sum_xy - sum_x * sum_y
    var_x = jnp.maximum(total_w * sum_xx - sum_x * sum_x, 0.05 * total_w * sum_xx)
    var_y = jnp.maximum(total_w * sum_yy - sum_y * sum_y, 0.05 * total_w * sum_yy)
    return numer / jnp.sqrt(var_x * var_y)


def fill_slabs(slabs, x_ref, w_ref):
    blk, width = x_ref.shape
    step = min(512, width)

    @pl.loop(0, width // step)
    def _(i):
        cols = pl.ds(pl.multiple_of(i * step, step), step)
        wide_x = x_ref[:, cols].astype(jnp.float32)
        wide_w = w_ref[:, cols].astype(jnp.float32)
        for g in range(blk // SUB):
            rows = slice(g * SUB, (g + 1) * SUB)
            slab = jnp.concatenate([wide_x[rows], wide_w[rows]], 0)
            slabs[g, :, cols] = slab.astype(jnp.bfloat16)


def send_slabs(slabs, pick_ref, send_ref, sems):
    mine = lax.div(lax.axis_index("dp"), PLANE)
    partner = mine + 1 - 2 * lax.rem(mine, 2)
    copies = []
    for c in range(PLANE):
        for t, plane in enumerate((mine, partner)):
            group = pick_ref[plane * PLANE + c]
            copies.append(pltpu.make_async_copy(slabs.at[group], send_ref.at[c, t], sems.at[c, t]))
    for copy in copies:
        copy.start()
    for copy in copies:
        copy.wait()


def own_pack_kernel(pick_ref, x_ref, w_ref, send_ref, slabs, sems):
    fill_slabs(slabs, x_ref, w_ref)
    send_slabs(slabs, pick_ref, send_ref, sems)


def far_pack_kernel(pick_ref, xo_ref, wo_ref, xi_ref, wi_ref, after_ref, send_ref, x_buf, w_buf, slabs, sems, in_sems):
    plane = lax.div(lax.axis_index("dp"), PLANE)
    inner = (plane == 1) | (plane == 2)

    def fetch(x_ref, w_ref):
        copies = (
            pltpu.make_async_copy(x_ref, x_buf, in_sems.at[0]),
            pltpu.make_async_copy(w_ref, w_buf, in_sems.at[1]),
        )
        for copy in copies:
            copy.start()
        for copy in copies:
            copy.wait()

    @pl.when(inner)
    def _():
        fetch(xi_ref, wi_ref)

    @pl.when(jnp.logical_not(inner))
    def _():
        fetch(xo_ref, wo_ref)

    fill_slabs(slabs, x_buf, w_buf)
    send_slabs(slabs, pick_ref, send_ref, sems)


def pack_call(kernel, name, specs, scratch, blk, width, *operands):
    return pl.pallas_call(
        kernel,
        out_shape=jax.ShapeDtypeStruct((PLANE, 2, SLAB, width), jnp.bfloat16),
        in_specs=[pl.BlockSpec(memory_space=pltpu.SMEM)] + specs,
        out_specs=pl.BlockSpec(memory_space=pl.ANY),
        scratch_shapes=scratch
        + [pltpu.VMEM((blk // SUB, SLAB, width), jnp.bfloat16), pltpu.SemaphoreType.DMA((PLANE, 2))],
        compiler_params=params(),
        cost_estimate=pl.CostEstimate(
            flops=blk * width * 4, bytes_accessed=(PLANE * 2 * SLAB * 2 + blk * 4) * width, transcendentals=0
        ),
        name=name,
    )(*operands)


def own_pack(pick, x, w):
    specs = [pl.BlockSpec(memory_space=pltpu.VMEM)] * 2
    return pack_call(own_pack_kernel, "own_pack", specs, [], *x.shape, pick, x, w)


def far_pack(pick, x_outer, w_outer, x_inner, w_inner, after):
    blk, width = x_outer.shape
    buf = pltpu.VMEM((blk, width), jnp.bfloat16)

    def kernel(pick_ref, xo, wo, xi, wi, after_ref, send_ref, x_buf, w_buf, in_sems, slabs, sems):
        far_pack_kernel(pick_ref, xo, wo, xi, wi, after_ref, send_ref, x_buf, w_buf, slabs, sems, in_sems)

    return pack_call(
        kernel, "far_pack", [pl.BlockSpec(memory_space=pl.ANY)] * 5,
        [buf, buf, pltpu.SemaphoreType.DMA((2,))], blk, width,
        pick, x_outer, w_outer, x_inner, w_inner, after,
    )


def place_kernel(ops_ref, x_ref, x1_ref, w_ref, w1_ref, after_ref, moved_ref, table, target):
    depth = x_ref.shape[1]
    width = target.shape[0]
    part = pl.multiple_of(pl.program_id(1) * depth, depth)

    @pl.when(pl.program_id(0) == 0)
    def _():
        step = min(256, depth)
        diagonal = lax.broadcasted_iota(jnp.int32, (step, step), 0) == lax.broadcasted_iota(
            jnp.int32, (step, step), 1
        )
        identity = jnp.where(diagonal, 1.0, 0.0).astype(jnp.bfloat16)
        for i in range(depth // step):
            cols = slice(i * step, (i + 1) * step)
            rows = jnp.concatenate([x_ref[:, cols], x1_ref[:, cols], w_ref[:, cols], w1_ref[:, cols]], 0)
            table[pl.ds(part + i * step, step), :] = lax.dot_general(
                identity, rows, (((1,), (1,)), ((), ())), preferred_element_type=jnp.float32
            )

    @pl.loop(0, depth // UNROLL)
    def _(i):
        base = pl.multiple_of(i * UNROLL, UNROLL)
        row = pl.multiple_of(part + base, UNROLL)
        for j in range(UNROLL):
            to = ops_ref[0, 0, base + j]
            target[pl.ds(to, 1), :] = table[pl.ds(row + j, 1), :]

    @pl.when(pl.program_id(1) == pl.num_programs(1) - 1)
    def _():
        step = min(512, width)

        @pl.loop(0, width // step)
        def _(i):
            rows = pl.ds(pl.multiple_of(i * step, step), step)
            moved_ref[rows, :] = target[rows, :].astype(jnp.bfloat16)


def place(ops, first, count, x, x1, w, w1, after):
    blk, width = x.shape
    depth = min(2048, width)
    last = width // depth - 1
    part = pl.BlockSpec((blk, depth), lambda k, i: (0, jnp.where(k == 0, i, last)))
    return pl.pallas_call(
        place_kernel,
        grid=(count, width // depth),
        out_shape=jax.ShapeDtypeStruct((width, count * LANES), jnp.bfloat16),
        in_specs=[
            pl.BlockSpec((1, 1, depth), lambda k, i: (first + k, 0, i), memory_space=pltpu.SMEM),
            part,
            part,
            part,
            part,
            pl.BlockSpec(memory_space=pl.ANY),
        ],
        out_specs=pl.BlockSpec((width, LANES), lambda k, i: (0, k)),
        scratch_shapes=[pltpu.VMEM((width, LANES), jnp.float32)] * 2,
        compiler_params=params(),
        cost_estimate=pl.CostEstimate(
            flops=0, bytes_accessed=count * width * LANES * 64, transcendentals=0
        ),
        name="place",
    )(ops, x, x1, w, w1, after)


def ratio(total_w, sum_x, sum_xx, sum_y, sum_xy, sum_yy):
    numer = total_w * sum_xy - sum_x * sum_y
    var_x = jnp.maximum(total_w * sum_xx - sum_x * sum_x, 0.05 * total_w * sum_xx)
    var_y = jnp.maximum(total_w * sum_yy - sum_y * sum_y, 0.05 * total_w * sum_yy)
    return numer / jnp.sqrt(var_x * var_y)


def add_sums(acc, got_ref, cols, right):
    rows = got_ref.shape[0]
    slabs = rows // SLAB
    wide = got_ref[:, cols].astype(jnp.float32).reshape(slabs, SLAB, -1)
    is_x = lax.broadcasted_iota(jnp.int32, wide.shape, 1) < SUB
    rolled = pltpu.roll(wide, SUB, 1)
    product = wide * rolled
    products = jnp.where(is_x, product * wide, product).reshape(rows, -1)
    mine = rolled.reshape(slabs // 2, 2, SLAB, -1)[:, 0]
    partner = wide.reshape(slabs // 2, 2, SLAB, -1)[:, 1]
    weights = jnp.where(is_x[: slabs // 2], mine, partner).reshape(rows // 2, -1)
    left = jnp.concatenate([weights, products], 0).astype(jnp.bfloat16)
    acc[...] += jnp.dot(left, right, preferred_element_type=jnp.float32)


def correlations(acc):
    rows = acc.shape[0] // 3
    half = LANES // 2
    blk = half // 2
    tiles = rows // SLAB
    top = lax.broadcasted_iota(jnp.int32, (tiles, SLAB, LANES), 1) < SUB
    lane = lax.broadcasted_iota(jnp.int32, (rows, LANES), 1)
    result = jnp.zeros((rows, LANES), jnp.float32)
    for k in range(NOPS):
        lanes = slice(k * LANES, (k + 1) * LANES)
        squares = slice((NOPS + k // 2) * LANES, (NOPS + k // 2 + 1) * LANES)
        with_w = acc[:rows, lanes]
        with_y = acc[rows:, lanes].reshape(tiles, 2, SLAB, LANES)
        mine, partner = with_y[:, 0], with_y[:, 1]
        y = jnp.where(top, pltpu.roll(mine, SUB, 1), partner).reshape(rows, LANES)
        yy = jnp.where(top, mine, pltpu.roll(partner, SUB, 1)).reshape(rows, LANES)
        sum_xx = acc[:rows, squares]
        if k % 2 == 1:
            sum_xx = pltpu.roll(sum_xx, half, 1)
        both = ratio(
            pltpu.roll(with_w, half, 1), with_w, sum_xx, pltpu.roll(y, half, 1), y, pltpu.roll(yy, half, 1)
        )
        both = jnp.where(top.reshape(rows, LANES), both, pltpu.roll(both, LANES - blk, 1))
        moved = both if k == 0 else pltpu.roll(both, k * blk, 1)
        result = jnp.where((lane >= k * blk) & (lane < (k + 1) * blk), moved, result)
    return result


def plane_sums_kernel(ended, got_ref, first_ref, second_ref, *refs):
    acc = refs[-1]
    depth = got_ref.shape[1]
    step = min(1024, depth)
    half = LANES // 2

    @pl.when(pl.program_id(0) == 0)
    def _():
        acc[...] = jnp.zeros_like(acc)

    low = lax.broadcasted_iota(jnp.int32, (step, LANES), 1) < half
    for i in range(depth // step):
        cols = slice(i * step, (i + 1) * step)
        linear, square = [], []
        for ref in (first_ref, second_ref):
            even, odd = None, None
            for k in range(2):
                values = ref[cols, k * LANES : (k + 1) * LANES].astype(jnp.float32)
                swapped = pltpu.roll(values, half, 1)
                product = values * swapped
                linear.append(jnp.where(low, product, values).astype(jnp.bfloat16))
                if k == 0:
                    even = product * values
                else:
                    odd = product * swapped
            square.append(jnp.where(low, even, odd).astype(jnp.bfloat16))
        add_sums(acc, got_ref, cols, jnp.concatenate(linear + square, 1))

    @pl.when(pl.program_id(0) == pl.num_programs(0) - 1)
    def _():
        if not ended:
            refs[0][...] = correlations(acc)
            return
        own_ref, mine_ref, other_ref, back_ref = refs[:-1]
        upper = lax.div(lax.axis_index("dp"), 2 * PLANE)
        count = own_ref.shape[0] // 2
        for part, result in enumerate((own_ref[...], correlations(acc))):
            slot = part + upper - 2 * part * upper
            back_ref[slot] = result.reshape(PLANE, SLAB, LANES)
            pairs = result.reshape(PLANE // 2, 2, SLAB, LANES)
            even, odd = pairs[:, 0], pairs[:, 1]
            top = lax.broadcasted_iota(jnp.int32, even.shape, 1) < SUB
            here = slice(part * count, (part + 1) * count)
            mine_ref[here, :] = jnp.where(top, even, pltpu.roll(odd, SUB, 1)).reshape(count, LANES)
            other_ref[here, :] = jnp.where(top, pltpu.roll(even, SUB, 1), odd).reshape(count, LANES)


def plane_sums(got, first, second, own):
    rows, width = got.shape
    depth = min(2048, width)
    lanes = (NOPS + NOPS // 2) * LANES
    ended = own is not None
    moved = pl.BlockSpec((depth, 2 * LANES), lambda i: (i, 0))
    result = (rows // 2, LANES)
    shapes = (result, result, (2, PLANE, SLAB, LANES)) if ended else (result,)
    entire = [pl.BlockSpec(shape, lambda i, shape=shape: (0,) * len(shape)) for shape in shapes]
    outs = pl.pallas_call(
        functools.partial(plane_sums_kernel, ended),
        grid=(width // depth,),
        out_shape=tuple(jax.ShapeDtypeStruct(shape, jnp.float32) for shape in shapes),
        in_specs=[pl.BlockSpec((rows, depth), lambda i: (0, i)), moved, moved] + ([entire[0]] if ended else []),
        out_specs=tuple(entire),
        scratch_shapes=[pltpu.VMEM((rows * 3 // 2, lanes), jnp.float32)],
        compiler_params=params(),
        cost_estimate=pl.CostEstimate(
            flops=3 * rows * width * lanes, bytes_accessed=2 * width * (rows + 4 * LANES), transcendentals=0
        ),
        name="plane_sums",
    )(got, first, second, *((own,) if ended else ()))
    return outs if ended else outs[0]


def shards_by_plane(intensities, observed, qweights, ops, pick):
    blk, width = intensities.shape
    groups = PLANES * PLANE
    near = [(i, i ^ PLANE) for i in range(groups)]
    far = [(i, i ^ (2 * PLANE)) for i in range(groups)]
    middle = [(i, 3 * PLANE + 2 * (i % PLANE) - i) for i in range(PLANE, 3 * PLANE)]
    outward = [(i, i - PLANE if i < 2 * PLANE else i + PLANE) for i in range(PLANE, 3 * PLANE)]
    rings = [[z * PLANE + c for c in range(PLANE)] for z in range(PLANES)]
    couples = [[z * PLANE + c for z in (odd, odd + 2) for c in range(PLANE)] for odd in range(2)]
    plane = lax.axis_index("dp") // PLANE
    odd, upper = plane % 2 == 1, plane >= 2

    def spread(send):
        got = lax.all_to_all(send, "dp", split_axis=0, concat_axis=0, axis_index_groups=rings, tiled=True)
        return got.reshape(PLANE * 2 * SLAB, width)

    own_pick = pick[:, 0]
    ops = ops[:, None, :]
    near_x = lax.ppermute(intensities, "dp", near)
    mid_x = lax.ppermute(intensities, "dp", middle)
    far_pick = lax.ppermute(own_pick, "dp", far)
    own_w = (observed.astype(jnp.float32) * qweights.astype(jnp.float32)).astype(jnp.bfloat16)
    near_w = lax.ppermute(own_w, "dp", near)
    mid_w = lax.ppermute(own_w, "dp", middle)
    own_got = spread(own_pack(own_pick, intensities, own_w))
    near_x, mid_x, near_w, mid_w, far_pick = lax.optimization_barrier((near_x, mid_x, near_w, mid_w, far_pick))
    outer_x = lax.ppermute(mid_x, "dp", outward)
    inner_x = lax.ppermute(near_x, "dp", middle)
    outer_w = lax.ppermute(mid_w, "dp", outward)
    inner_w = lax.ppermute(near_w, "dp", middle)
    first = place(ops, 0, 2, intensities, near_x, own_w, near_w, own_pick)
    far_send = far_pack(far_pick, outer_x, outer_w, inner_x, inner_w, first)
    far_got = spread(far_send)
    second = place(ops, 2, 2, intensities, near_x, own_w, near_w, far_send)
    own_corr = plane_sums(own_got, first, second, None)
    mine, other, back = plane_sums(far_got, first, second, own_corr)

    from_near = lax.ppermute(other, "dp", near)
    pair = [each.reshape(2, PLANE, SUB, NOPS * blk) for each in (mine, from_near)]
    pair = jnp.stack(pair, 1)
    pair = jnp.where(odd, pair[:, ::-1], pair)
    pair = jnp.where(upper, pair[::-1], pair)
    corr = pair.reshape(groups * SUB, NOPS * blk).T.reshape(NOPS, blk, groups * SUB)

    back = back.reshape(2 * PLANE, 2 * SUB, NOPS * blk)
    back = lax.all_to_all(back, "dp", split_axis=0, concat_axis=0, axis_index_groups=couples, tiled=True)
    back = back.reshape(2, PLANE, 2, SUB, NOPS, blk)
    back = jnp.where(odd, back[:, :, ::-1], back)
    returned = jnp.transpose(back, (4, 0, 2, 1, 3, 5)).reshape(NOPS, 1, groups, SUB, blk)
    return (corr, returned)


def shards(intensities, observed, qweights, ops, pick):
    if lax.axis_size("dp") == PLANES * PLANE and lax.axis_size("refl") == 1:
        return shards_by_plane(intensities, observed, qweights, ops, pick)
    return shards_direct(intensities, observed, qweights, ops, pick)


def shards_direct(intensities, observed, qweights, ops, pick):
    blk, width = intensities.shape
    groups = lax.axis_size("dp")
    shares = lax.axis_size("refl")
    local_ops = ops - lax.axis_index("refl") * width
    send, own_w = pack(pick[:, 0], intensities, observed, qweights)
    got = lax.all_to_all(send, "dp", split_axis=0, concat_axis=0, tiled=True)
    moved = move(local_ops, intensities, own_w)
    stats = sums(got.reshape(groups * SLAB, width), moved)
    if shares > 1:
        stats = lax.psum(stats, "refl")
    stats = stats.reshape(2, groups, SLAB, NOPS, LANES)
    full = pearson(stats, blk)
    rows = blk // shares
    if shares > 1:
        full = lax.dynamic_slice_in_dim(full, lax.axis_index("refl") * rows, rows, 3)
    corr = jnp.transpose(full, (2, 3, 0, 1)).reshape(NOPS, rows, groups * SUB)
    back = lax.all_to_all(full, "dp", split_axis=0, concat_axis=0, tiled=True)
    returned = jnp.transpose(back, (2, 0, 1, 3))[:, None]
    return (corr, returned)


def solution(mesh):
    return jax.shard_map(
        shards,
        mesh=mesh,
        in_specs=(
            P("dp", "refl"),
            P("dp", "refl"),
            P("dp", "refl"),
            P(None, "refl"),
            P(None, "dp"),
        ),
        out_specs=(P(None, ("dp", "refl"), None), P(None, "dp", None, None, "refl")),
        check_vma=False,
    )
```

```python
import functools

import jax
import jax.numpy as jnp
from jax import lax
from jax.experimental import pallas as pl
from jax.experimental.pallas import tpu as pltpu
from jax.sharding import PartitionSpec as P

SUB = 4
NOPS = 4
LANES = 128
SLAB = 2 * SUB
VMEM_LIMIT = 56 * 1024 * 1024
PLANES = 4
PLANE = 8
UNROLL = 64


def params():
    return pltpu.CompilerParams(vmem_limit_bytes=VMEM_LIMIT)


def pack_kernel(pick_ref, x_ref, obs_ref, qw_ref, send_ref, w_ref, slabs, sems):
    blk, width = x_ref.shape
    step = min(512, width)

    @pl.loop(0, width // step)
    def _(i):
        cols = pl.ds(pl.multiple_of(i * step, step), step)
        wide_w = obs_ref[:, cols].astype(jnp.float32) * qw_ref[:, cols].astype(jnp.float32)
        wide_x = x_ref[:, cols].astype(jnp.float32)
        w_ref[:, cols] = wide_w.astype(jnp.bfloat16)
        for g in range(blk // SUB):
            rows = slice(g * SUB, (g + 1) * SUB)
            slab = jnp.concatenate([wide_x[rows], wide_w[rows]], 0)
            slabs[g, :, cols] = slab.astype(jnp.bfloat16)

    groups = send_ref.shape[0]

    def copy(d):
        return pltpu.make_async_copy(slabs.at[pick_ref[d]], send_ref.at[d], sems.at[d])

    @pl.loop(0, groups)
    def _(d):
        copy(d).start()

    @pl.loop(0, groups)
    def _(d):
        copy(d).wait()


def pack(pick, intensities, observed, qweights):
    blk, width = intensities.shape
    groups = pick.shape[0]
    whole = pl.BlockSpec(memory_space=pltpu.VMEM)
    return pl.pallas_call(
        pack_kernel,
        out_shape=(
            jax.ShapeDtypeStruct((groups, SLAB, width), jnp.bfloat16),
            jax.ShapeDtypeStruct((blk, width), jnp.bfloat16),
        ),
        in_specs=[pl.BlockSpec(memory_space=pltpu.SMEM), whole, whole, whole],
        out_specs=(pl.BlockSpec(memory_space=pl.ANY), whole),
        scratch_shapes=[
            pltpu.VMEM((blk // SUB, SLAB, width), jnp.bfloat16),
            pltpu.SemaphoreType.DMA((groups,)),
        ],
        compiler_params=params(),
        cost_estimate=pl.CostEstimate(
            flops=blk * width * 4, bytes_accessed=(groups * SLAB * 2 + blk * 10) * width, transcendentals=0
        ),
        name="pack",
    )(pick, intensities, observed, qweights)


def move_kernel(ops_ref, x_ref, w_ref, moved_ref, table, target):
    blk, width = x_ref.shape

    @pl.when(pl.program_id(0) == 0)
    def _():
        @pl.loop(0, width // LANES)
        def _(i):
            cols = pl.ds(pl.multiple_of(i * LANES, LANES), LANES)
            wide_x = x_ref[:, cols].astype(jnp.float32)
            wide_w = w_ref[:, cols].astype(jnp.float32)
            wx = (wide_w * wide_x).astype(jnp.bfloat16).astype(jnp.float32)
            wxx = (wide_w * wide_x * wide_x).astype(jnp.bfloat16).astype(jnp.float32)
            stacked = jnp.concatenate([wide_w, wx, wxx, jnp.zeros((LANES - 3 * blk, LANES), jnp.float32)], 0)
            table[cols, :] = stacked.T

    unroll = 16

    @pl.loop(0, width // unroll)
    def _(i):
        base = pl.multiple_of(i * unroll, unroll)
        for j in range(unroll):
            to = ops_ref[0, 0, base + j]
            target[pl.ds(to, 1), :] = table[pl.ds(base + j, 1), :]

    step = min(512, width)

    @pl.loop(0, width // step)
    def _(i):
        rows = pl.ds(pl.multiple_of(i * step, step), step)
        moved_ref[rows, :] = target[rows, :].astype(jnp.bfloat16)


def move(local_ops, intensities, own_w):
    blk, width = intensities.shape
    whole = pl.BlockSpec(memory_space=pltpu.VMEM)
    return pl.pallas_call(
        move_kernel,
        grid=(NOPS,),
        out_shape=jax.ShapeDtypeStruct((width, NOPS * LANES), jnp.bfloat16),
        in_specs=[
            pl.BlockSpec((1, 1, width), lambda k: (k, 0, 0), memory_space=pltpu.SMEM),
            whole,
            whole,
        ],
        out_specs=pl.BlockSpec((width, LANES), lambda k: (0, k)),
        scratch_shapes=[
            pltpu.VMEM((width, LANES), jnp.float32),
            pltpu.VMEM((width, LANES), jnp.float32),
        ],
        compiler_params=params(),
        cost_estimate=pl.CostEstimate(
            flops=0, bytes_accessed=NOPS * width * LANES * 100, transcendentals=0
        ),
        name="move",
    )(local_ops[:, None, :], intensities, own_w)


def sums_kernel(got_ref, moved_ref, out_ref):
    rows, depth = got_ref.shape
    step = min(512, depth)

    @pl.when(pl.program_id(0) == 0)
    def _():
        out_ref[...] = jnp.zeros_like(out_ref)

    is_x = lax.broadcasted_iota(jnp.int32, (rows // SLAB, SLAB, step), 1) < SUB

    @pl.loop(0, depth // step)
    def _(i):
        cols = pl.ds(pl.multiple_of(i * step, step), step)
        raw = got_ref[:, cols]
        wide = raw.astype(jnp.float32).reshape(rows // SLAB, SLAB, step)
        product = wide * pltpu.roll(wide, SUB, 1)
        second = jnp.where(is_x, product * wide, product)
        second = second.reshape(rows, step).astype(jnp.bfloat16)
        right = moved_ref[cols, :]
        out_ref[0] += jnp.dot(raw, right, preferred_element_type=jnp.float32)
        out_ref[1] += jnp.dot(second, right, preferred_element_type=jnp.float32)


def sums(got, moved):
    rows, width = got.shape
    depth = min(2048, width)
    return pl.pallas_call(
        sums_kernel,
        grid=(width // depth,),
        out_shape=jax.ShapeDtypeStruct((2, rows, moved.shape[1]), jnp.float32),
        in_specs=[
            pl.BlockSpec((rows, depth), lambda i: (0, i)),
            pl.BlockSpec((depth, moved.shape[1]), lambda i: (i, 0)),
        ],
        out_specs=pl.BlockSpec((2, rows, moved.shape[1]), lambda i: (0, 0, 0)),
        compiler_params=params(),
        cost_estimate=pl.CostEstimate(
            flops=4 * rows * width * moved.shape[1],
            bytes_accessed=2 * width * (rows + moved.shape[1]),
            transcendentals=0,
        ),
        name="sums",
    )(got, moved)


def pearson(share, blk):
    first, second = share[0], share[1]
    total_w = first[:, SUB:, :, :blk]
    sum_x = first[:, SUB:, :, blk : 2 * blk]
    sum_xx = first[:, SUB:, :, 2 * blk : 3 * blk]
    sum_y = second[:, SUB:, :, :blk]
    sum_xy = second[:, SUB:, :, blk : 2 * blk]
    sum_yy = second[:, :SUB, :, :blk]
    numer = total_w * sum_xy - sum_x * sum_y
    var_x = jnp.maximum(total_w * sum_xx - sum_x * sum_x, 0.05 * total_w * sum_xx)
    var_y = jnp.maximum(total_w * sum_yy - sum_y * sum_y, 0.05 * total_w * sum_yy)
    return numer / jnp.sqrt(var_x * var_y)


def fill_slabs(slabs, x_ref, w_ref):
    blk, width = x_ref.shape
    step = min(512, width)

    @pl.loop(0, width // step)
    def _(i):
        cols = pl.ds(pl.multiple_of(i * step, step), step)
        wide_x = x_ref[:, cols].astype(jnp.float32)
        wide_w = w_ref[:, cols].astype(jnp.float32)
        for g in range(blk // SUB):
            rows = slice(g * SUB, (g + 1) * SUB)
            slab = jnp.concatenate([wide_x[rows], wide_w[rows]], 0)
            slabs[g, :, cols] = slab.astype(jnp.bfloat16)


def send_slabs(slabs, pick_ref, send_ref, sems):
    mine = lax.div(lax.axis_index("dp"), PLANE)
    partner = mine + 1 - 2 * lax.rem(mine, 2)
    copies = []
    for c in range(PLANE):
        for t, plane in enumerate((mine, partner)):
            group = pick_ref[plane * PLANE + c]
            copies.append(pltpu.make_async_copy(slabs.at[group], send_ref.at[c, t], sems.at[c, t]))
    for copy in copies:
        copy.start()
    for copy in copies:
        copy.wait()


def own_pack_kernel(pick_ref, x_ref, w_ref, send_ref, slabs, sems):
    fill_slabs(slabs, x_ref, w_ref)
    send_slabs(slabs, pick_ref, send_ref, sems)


def far_pack_kernel(pick_ref, xo_ref, wo_ref, xi_ref, wi_ref, after_ref, send_ref, x_buf, w_buf, slabs, sems, in_sems):
    plane = lax.div(lax.axis_index("dp"), PLANE)
    inner = (plane == 1) | (plane == 2)

    def fetch(x_ref, w_ref):
        copies = (
            pltpu.make_async_copy(x_ref, x_buf, in_sems.at[0]),
            pltpu.make_async_copy(w_ref, w_buf, in_sems.at[1]),
        )
        for copy in copies:
            copy.start()
        for copy in copies:
            copy.wait()

    @pl.when(inner)
    def _():
        fetch(xi_ref, wi_ref)

    @pl.when(jnp.logical_not(inner))
    def _():
        fetch(xo_ref, wo_ref)

    fill_slabs(slabs, x_buf, w_buf)
    send_slabs(slabs, pick_ref, send_ref, sems)


def pack_call(kernel, name, specs, scratch, blk, width, *operands):
    return pl.pallas_call(
        kernel,
        out_shape=jax.ShapeDtypeStruct((PLANE, 2, SLAB, width), jnp.bfloat16),
        in_specs=[pl.BlockSpec(memory_space=pltpu.SMEM)] + specs,
        out_specs=pl.BlockSpec(memory_space=pl.ANY),
        scratch_shapes=scratch
        + [pltpu.VMEM((blk // SUB, SLAB, width), jnp.bfloat16), pltpu.SemaphoreType.DMA((PLANE, 2))],
        compiler_params=params(),
        cost_estimate=pl.CostEstimate(
            flops=blk * width * 4, bytes_accessed=(PLANE * 2 * SLAB * 2 + blk * 4) * width, transcendentals=0
        ),
        name=name,
    )(*operands)


def own_pack(pick, x, w):
    specs = [pl.BlockSpec(memory_space=pltpu.VMEM)] * 2
    return pack_call(own_pack_kernel, "own_pack", specs, [], *x.shape, pick, x, w)


def far_pack(pick, x_outer, w_outer, x_inner, w_inner, after):
    blk, width = x_outer.shape
    buf = pltpu.VMEM((blk, width), jnp.bfloat16)

    def kernel(pick_ref, xo, wo, xi, wi, after_ref, send_ref, x_buf, w_buf, in_sems, slabs, sems):
        far_pack_kernel(pick_ref, xo, wo, xi, wi, after_ref, send_ref, x_buf, w_buf, slabs, sems, in_sems)

    return pack_call(
        kernel, "far_pack", [pl.BlockSpec(memory_space=pl.ANY)] * 5,
        [buf, buf, pltpu.SemaphoreType.DMA((2,))], blk, width,
        pick, x_outer, w_outer, x_inner, w_inner, after,
    )


def place_kernel(ops_ref, x_ref, x1_ref, w_ref, w1_ref, after_ref, moved_ref, table, target):
    depth = x_ref.shape[1]
    width = target.shape[0]
    part = pl.multiple_of(pl.program_id(1) * depth, depth)

    @pl.when(pl.program_id(0) == 0)
    def _():
        step = min(256, depth)
        diagonal = lax.broadcasted_iota(jnp.int32, (step, step), 0) == lax.broadcasted_iota(
            jnp.int32, (step, step), 1
        )
        identity = jnp.where(diagonal, 1.0, 0.0).astype(jnp.bfloat16)
        for i in range(depth // step):
            cols = slice(i * step, (i + 1) * step)
            rows = jnp.concatenate([x_ref[:, cols], x1_ref[:, cols], w_ref[:, cols], w1_ref[:, cols]], 0)
            table[pl.ds(part + i * step, step), :] = lax.dot_general(
                identity, rows, (((1,), (1,)), ((), ())), preferred_element_type=jnp.float32
            )

    @pl.loop(0, depth // UNROLL)
    def _(i):
        base = pl.multiple_of(i * UNROLL, UNROLL)
        row = pl.multiple_of(part + base, UNROLL)
        for j in range(UNROLL):
            to = ops_ref[0, 0, base + j]
            target[pl.ds(to, 1), :] = table[pl.ds(row + j, 1), :]

    @pl.when(pl.program_id(1) == pl.num_programs(1) - 1)
    def _():
        step = min(512, width)

        @pl.loop(0, width // step)
        def _(i):
            rows = pl.ds(pl.multiple_of(i * step, step), step)
            moved_ref[rows, :] = target[rows, :].astype(jnp.bfloat16)


def place(ops, x, x1, w, w1, after):
    count = ops.shape[0]
    blk, width = x.shape
    depth = min(2048, width)
    last = width // depth - 1
    part = pl.BlockSpec((blk, depth), lambda k, i: (0, jnp.where(k == 0, i, last)))
    return pl.pallas_call(
        place_kernel,
        grid=(count, width // depth),
        out_shape=jax.ShapeDtypeStruct((width, count * LANES), jnp.bfloat16),
        in_specs=[
            pl.BlockSpec((1, 1, depth), lambda k, i: (k, 0, i), memory_space=pltpu.SMEM),
            part,
            part,
            part,
            part,
            pl.BlockSpec(memory_space=pl.ANY),
        ],
        out_specs=pl.BlockSpec((width, LANES), lambda k, i: (0, k)),
        scratch_shapes=[pltpu.VMEM((width, LANES), jnp.float32)] * 2,
        compiler_params=params(),
        cost_estimate=pl.CostEstimate(
            flops=0, bytes_accessed=count * width * LANES * 64, transcendentals=0
        ),
        name="place",
    )(ops[:, None, :], x, x1, w, w1, after)


def ratio(total_w, sum_x, sum_xx, sum_y, sum_xy, sum_yy):
    numer = total_w * sum_xy - sum_x * sum_y
    var_x = jnp.maximum(total_w * sum_xx - sum_x * sum_x, 0.05 * total_w * sum_xx)
    var_y = jnp.maximum(total_w * sum_yy - sum_y * sum_y, 0.05 * total_w * sum_yy)
    return numer / jnp.sqrt(var_x * var_y)


def add_sums(acc, got_ref, cols, right):
    rows = got_ref.shape[0]
    slabs = rows // SLAB
    wide = got_ref[:, cols].astype(jnp.float32).reshape(slabs, SLAB, -1)
    is_x = lax.broadcasted_iota(jnp.int32, wide.shape, 1) < SUB
    rolled = pltpu.roll(wide, SUB, 1)
    product = wide * rolled
    products = jnp.where(is_x, product * wide, product).reshape(rows, -1)
    mine = rolled.reshape(slabs // 2, 2, SLAB, -1)[:, 0]
    partner = wide.reshape(slabs // 2, 2, SLAB, -1)[:, 1]
    weights = jnp.where(is_x[: slabs // 2], mine, partner).reshape(rows // 2, -1)
    left = jnp.concatenate([weights, products], 0).astype(jnp.bfloat16)
    acc[...] += jnp.dot(left, right, preferred_element_type=jnp.float32)


def correlations(acc):
    rows = acc.shape[0] // 3
    half = LANES // 2
    blk = half // 2
    tiles = rows // SLAB
    top = lax.broadcasted_iota(jnp.int32, (tiles, SLAB, LANES), 1) < SUB
    lane = lax.broadcasted_iota(jnp.int32, (rows, LANES), 1)
    result = jnp.zeros((rows, LANES), jnp.float32)
    count = acc.shape[1] * 2 // 3 // LANES
    for k in range(count):
        lanes = slice(k * LANES, (k + 1) * LANES)
        squares = slice((count + k // 2) * LANES, (count + k // 2 + 1) * LANES)
        with_w = acc[:rows, lanes]
        with_y = acc[rows:, lanes].reshape(tiles, 2, SLAB, LANES)
        mine, partner = with_y[:, 0], with_y[:, 1]
        y = jnp.where(top, pltpu.roll(mine, SUB, 1), partner).reshape(rows, LANES)
        yy = jnp.where(top, mine, pltpu.roll(partner, SUB, 1)).reshape(rows, LANES)
        sum_xx = acc[:rows, squares]
        if k % 2 == 1:
            sum_xx = pltpu.roll(sum_xx, half, 1)
        both = ratio(
            pltpu.roll(with_w, half, 1), with_w, sum_xx, pltpu.roll(y, half, 1), y, pltpu.roll(yy, half, 1)
        )
        both = jnp.where(top.reshape(rows, LANES), both, pltpu.roll(both, LANES - blk, 1))
        moved = both if k == 0 else pltpu.roll(both, k * blk, 1)
        result = jnp.where((lane >= k * blk) & (lane < (k + 1) * blk), moved, result)
    return result


def plane_sums_kernel(pairs, got_ref, *refs):
    moved_refs, refs, acc = refs[:pairs], refs[pairs:-1], refs[-1]
    depth = got_ref.shape[1]
    step = min(1024, depth)
    half = LANES // 2

    @pl.when(pl.program_id(0) == 0)
    def _():
        acc[...] = jnp.zeros_like(acc)

    low = lax.broadcasted_iota(jnp.int32, (step, LANES), 1) < half
    for i in range(depth // step):
        cols = slice(i * step, (i + 1) * step)
        linear, square = [], []
        for ref in moved_refs:
            even, odd = None, None
            for k in range(2):
                values = ref[cols, k * LANES : (k + 1) * LANES].astype(jnp.float32)
                swapped = pltpu.roll(values, half, 1)
                product = values * swapped
                linear.append(jnp.where(low, product, values).astype(jnp.bfloat16))
                if k == 0:
                    even = product * values
                else:
                    odd = product * swapped
            square.append(jnp.where(low, even, odd).astype(jnp.bfloat16))
        add_sums(acc, got_ref, cols, jnp.concatenate(linear + square, 1))

    @pl.when(pl.program_id(0) == pl.num_programs(0) - 1)
    def _():
        if len(refs) == 1:
            refs[0][...] = correlations(acc)
            return
        first_ref, second_ref, mine_ref, other_ref, back_ref = refs
        upper = lax.div(lax.axis_index("dp"), 2 * PLANE)
        count = first_ref.shape[0] // 2
        low = lax.broadcasted_iota(jnp.int32, first_ref.shape, 1) < half
        own = jnp.where(low, first_ref[...], pltpu.roll(second_ref[...], half, 1))
        for part, result in enumerate((own, correlations(acc))):
            slot = part + upper - 2 * part * upper
            back_ref[slot] = result.reshape(PLANE, SLAB, LANES)
            pairs = result.reshape(PLANE // 2, 2, SLAB, LANES)
            even, odd = pairs[:, 0], pairs[:, 1]
            top = lax.broadcasted_iota(jnp.int32, even.shape, 1) < SUB
            here = slice(part * count, (part + 1) * count)
            mine_ref[here, :] = jnp.where(top, even, pltpu.roll(odd, SUB, 1)).reshape(count, LANES)
            other_ref[here, :] = jnp.where(top, pltpu.roll(even, SUB, 1), odd).reshape(count, LANES)


def plane_sums(got, moved, own):
    rows, width = got.shape
    depth = min(2048, width)
    lanes = 3 * len(moved) * LANES
    ended = len(own) > 0
    placed = pl.BlockSpec((depth, 2 * LANES), lambda i: (i, 0))
    result = (rows // 2, LANES)
    shapes = (result, result, (2, PLANE, SLAB, LANES)) if ended else (result,)
    entire = [pl.BlockSpec(shape, lambda i, shape=shape: (0,) * len(shape)) for shape in shapes]
    outs = pl.pallas_call(
        functools.partial(plane_sums_kernel, len(moved)),
        grid=(width // depth,),
        out_shape=tuple(jax.ShapeDtypeStruct(shape, jnp.float32) for shape in shapes),
        in_specs=[pl.BlockSpec((rows, depth), lambda i: (0, i))] + [placed] * len(moved) + [entire[0]] * len(own),
        out_specs=tuple(entire),
        scratch_shapes=[pltpu.VMEM((rows * 3 // 2, lanes), jnp.float32)],
        compiler_params=params(),
        cost_estimate=pl.CostEstimate(
            flops=3 * rows * width * lanes, bytes_accessed=2 * width * (rows + 2 * len(moved) * LANES), transcendentals=0
        ),
        name="plane_sums",
    )(got, *moved, *own)
    return outs if ended else outs[0]


def shards_by_plane(intensities, observed, qweights, ops, pick):
    blk, width = intensities.shape
    groups = PLANES * PLANE
    near = [(i, i ^ PLANE) for i in range(groups)]
    far = [(i, i ^ (2 * PLANE)) for i in range(groups)]
    middle = [(i, 3 * PLANE + 2 * (i % PLANE) - i) for i in range(PLANE, 3 * PLANE)]
    outward = [(i, i - PLANE if i < 2 * PLANE else i + PLANE) for i in range(PLANE, 3 * PLANE)]
    rings = [[z * PLANE + c for c in range(PLANE)] for z in range(PLANES)]
    couples = [[z * PLANE + c for z in (odd, odd + 2) for c in range(PLANE)] for odd in range(2)]
    plane = lax.axis_index("dp") // PLANE
    odd, upper = plane % 2 == 1, plane >= 2

    def spread(send):
        got = lax.all_to_all(send, "dp", split_axis=0, concat_axis=0, axis_index_groups=rings, tiled=True)
        return got.reshape(PLANE * 2 * SLAB, width)

    own_pick = pick[:, 0]
    near_x = lax.ppermute(intensities, "dp", near)
    mid_x = lax.ppermute(intensities, "dp", middle)
    far_pick = lax.ppermute(own_pick, "dp", far)
    own_w = (observed.astype(jnp.float32) * qweights.astype(jnp.float32)).astype(jnp.bfloat16)
    near_w = lax.ppermute(own_w, "dp", near)
    mid_w = lax.ppermute(own_w, "dp", middle)
    own_got = spread(own_pack(own_pick, intensities, own_w))
    near_x, mid_x, near_w, mid_w, far_pick = lax.optimization_barrier((near_x, mid_x, near_w, mid_w, far_pick))
    outer_x = lax.ppermute(mid_x, "dp", outward)
    inner_x = lax.ppermute(near_x, "dp", middle)
    outer_w = lax.ppermute(mid_w, "dp", outward)
    inner_w = lax.ppermute(near_w, "dp", middle)
    first = place(ops[:2], intensities, near_x, own_w, near_w, own_pick)
    own_first = plane_sums(own_got, (first,), ())
    far_send = far_pack(far_pick, outer_x, outer_w, inner_x, inner_w, own_first)
    far_got = spread(far_send)
    second = place(ops[2:], intensities, near_x, own_w, near_w, far_send)
    own_second = plane_sums(own_got, (second,), ())
    mine, other, back = plane_sums(far_got, (first, second), (own_first, own_second))

    from_near = lax.ppermute(other, "dp", near)
    pair = [each.reshape(2, PLANE, SUB, NOPS * blk) for each in (mine, from_near)]
    pair = jnp.stack(pair, 1)
    pair = jnp.where(odd, pair[:, ::-1], pair)
    pair = jnp.where(upper, pair[::-1], pair)
    corr = pair.reshape(groups * SUB, NOPS * blk).T.reshape(NOPS, blk, groups * SUB)

    back = back.reshape(2 * PLANE, 2 * SUB, NOPS * blk)
    back = lax.all_to_all(back, "dp", split_axis=0, concat_axis=0, axis_index_groups=couples, tiled=True)
    back = back.reshape(2, PLANE, 2, SUB, NOPS, blk)
    back = jnp.where(odd, back[:, :, ::-1], back)
    returned = jnp.transpose(back, (4, 0, 2, 1, 3, 5)).reshape(NOPS, 1, groups, SUB, blk)
    return (corr, returned)


def shards(intensities, observed, qweights, ops, pick):
    if lax.axis_size("dp") == PLANES * PLANE and lax.axis_size("refl") == 1:
        return shards_by_plane(intensities, observed, qweights, ops, pick)
    return shards_direct(intensities, observed, qweights, ops, pick)


def shards_direct(intensities, observed, qweights, ops, pick):
    blk, width = intensities.shape
    groups = lax.axis_size("dp")
    shares = lax.axis_size("refl")
    local_ops = ops - lax.axis_index("refl") * width
    send, own_w = pack(pick[:, 0], intensities, observed, qweights)
    got = lax.all_to_all(send, "dp", split_axis=0, concat_axis=0, tiled=True)
    moved = move(local_ops, intensities, own_w)
    stats = sums(got.reshape(groups * SLAB, width), moved)
    if shares > 1:
        stats = lax.psum(stats, "refl")
    stats = stats.reshape(2, groups, SLAB, NOPS, LANES)
    full = pearson(stats, blk)
    rows = blk // shares
    if shares > 1:
        full = lax.dynamic_slice_in_dim(full, lax.axis_index("refl") * rows, rows, 3)
    corr = jnp.transpose(full, (2, 3, 0, 1)).reshape(NOPS, rows, groups * SUB)
    back = lax.all_to_all(full, "dp", split_axis=0, concat_axis=0, tiled=True)
    returned = jnp.transpose(back, (2, 0, 1, 3))[:, None]
    return (corr, returned)


def solution(mesh):
    return jax.shard_map(
        shards,
        mesh=mesh,
        in_specs=(
            P("dp", "refl"),
            P("dp", "refl"),
            P("dp", "refl"),
            P(None, "refl"),
            P(None, "dp"),
        ),
        out_specs=(P(None, ("dp", "refl"), None), P(None, "dp", None, None, "refl")),
        check_vma=False,
    )
```

```python
import functools

import jax
import jax.numpy as jnp
from jax import lax
from jax.experimental import pallas as pl
from jax.experimental.pallas import tpu as pltpu
from jax.sharding import PartitionSpec as P

SUB = 4
NOPS = 4
LANES = 128
SLAB = 2 * SUB
VMEM_LIMIT = 56 * 1024 * 1024
PLANES = 4
PLANE = 8
UNROLL = 64


def params():
    return pltpu.CompilerParams(vmem_limit_bytes=VMEM_LIMIT)


def pack_kernel(pick_ref, x_ref, obs_ref, qw_ref, send_ref, w_ref, slabs, sems):
    blk, width = x_ref.shape
    step = min(512, width)

    @pl.loop(0, width // step)
    def _(i):
        cols = pl.ds(pl.multiple_of(i * step, step), step)
        wide_w = obs_ref[:, cols].astype(jnp.float32) * qw_ref[:, cols].astype(jnp.float32)
        wide_x = x_ref[:, cols].astype(jnp.float32)
        w_ref[:, cols] = wide_w.astype(jnp.bfloat16)
        for g in range(blk // SUB):
            rows = slice(g * SUB, (g + 1) * SUB)
            slab = jnp.concatenate([wide_x[rows], wide_w[rows]], 0)
            slabs[g, :, cols] = slab.astype(jnp.bfloat16)

    groups = send_ref.shape[0]

    def copy(d):
        return pltpu.make_async_copy(slabs.at[pick_ref[d]], send_ref.at[d], sems.at[d])

    @pl.loop(0, groups)
    def _(d):
        copy(d).start()

    @pl.loop(0, groups)
    def _(d):
        copy(d).wait()


def pack(pick, intensities, observed, qweights):
    blk, width = intensities.shape
    groups = pick.shape[0]
    whole = pl.BlockSpec(memory_space=pltpu.VMEM)
    return pl.pallas_call(
        pack_kernel,
        out_shape=(
            jax.ShapeDtypeStruct((groups, SLAB, width), jnp.bfloat16),
            jax.ShapeDtypeStruct((blk, width), jnp.bfloat16),
        ),
        in_specs=[pl.BlockSpec(memory_space=pltpu.SMEM), whole, whole, whole],
        out_specs=(pl.BlockSpec(memory_space=pl.ANY), whole),
        scratch_shapes=[
            pltpu.VMEM((blk // SUB, SLAB, width), jnp.bfloat16),
            pltpu.SemaphoreType.DMA((groups,)),
        ],
        compiler_params=params(),
        cost_estimate=pl.CostEstimate(
            flops=blk * width * 4, bytes_accessed=(groups * SLAB * 2 + blk * 10) * width, transcendentals=0
        ),
        name="pack",
    )(pick, intensities, observed, qweights)


def move_kernel(ops_ref, x_ref, w_ref, moved_ref, table, target):
    blk, width = x_ref.shape

    @pl.when(pl.program_id(0) == 0)
    def _():
        @pl.loop(0, width // LANES)
        def _(i):
            cols = pl.ds(pl.multiple_of(i * LANES, LANES), LANES)
            wide_x = x_ref[:, cols].astype(jnp.float32)
            wide_w = w_ref[:, cols].astype(jnp.float32)
            wx = (wide_w * wide_x).astype(jnp.bfloat16).astype(jnp.float32)
            wxx = (wide_w * wide_x * wide_x).astype(jnp.bfloat16).astype(jnp.float32)
            stacked = jnp.concatenate([wide_w, wx, wxx, jnp.zeros((LANES - 3 * blk, LANES), jnp.float32)], 0)
            table[cols, :] = stacked.T

    unroll = 16

    @pl.loop(0, width // unroll)
    def _(i):
        base = pl.multiple_of(i * unroll, unroll)
        for j in range(unroll):
            to = ops_ref[0, 0, base + j]
            target[pl.ds(to, 1), :] = table[pl.ds(base + j, 1), :]

    step = min(512, width)

    @pl.loop(0, width // step)
    def _(i):
        rows = pl.ds(pl.multiple_of(i * step, step), step)
        moved_ref[rows, :] = target[rows, :].astype(jnp.bfloat16)


def move(local_ops, intensities, own_w):
    blk, width = intensities.shape
    whole = pl.BlockSpec(memory_space=pltpu.VMEM)
    return pl.pallas_call(
        move_kernel,
        grid=(NOPS,),
        out_shape=jax.ShapeDtypeStruct((width, NOPS * LANES), jnp.bfloat16),
        in_specs=[
            pl.BlockSpec((1, 1, width), lambda k: (k, 0, 0), memory_space=pltpu.SMEM),
            whole,
            whole,
        ],
        out_specs=pl.BlockSpec((width, LANES), lambda k: (0, k)),
        scratch_shapes=[
            pltpu.VMEM((width, LANES), jnp.float32),
            pltpu.VMEM((width, LANES), jnp.float32),
        ],
        compiler_params=params(),
        cost_estimate=pl.CostEstimate(
            flops=0, bytes_accessed=NOPS * width * LANES * 100, transcendentals=0
        ),
        name="move",
    )(local_ops[:, None, :], intensities, own_w)


def sums_kernel(got_ref, moved_ref, out_ref):
    rows, depth = got_ref.shape
    step = min(512, depth)

    @pl.when(pl.program_id(0) == 0)
    def _():
        out_ref[...] = jnp.zeros_like(out_ref)

    is_x = lax.broadcasted_iota(jnp.int32, (rows // SLAB, SLAB, step), 1) < SUB

    @pl.loop(0, depth // step)
    def _(i):
        cols = pl.ds(pl.multiple_of(i * step, step), step)
        raw = got_ref[:, cols]
        wide = raw.astype(jnp.float32).reshape(rows // SLAB, SLAB, step)
        product = wide * pltpu.roll(wide, SUB, 1)
        second = jnp.where(is_x, product * wide, product)
        second = second.reshape(rows, step).astype(jnp.bfloat16)
        right = moved_ref[cols, :]
        out_ref[0] += jnp.dot(raw, right, preferred_element_type=jnp.float32)
        out_ref[1] += jnp.dot(second, right, preferred_element_type=jnp.float32)


def sums(got, moved):
    rows, width = got.shape
    depth = min(2048, width)
    return pl.pallas_call(
        sums_kernel,
        grid=(width // depth,),
        out_shape=jax.ShapeDtypeStruct((2, rows, moved.shape[1]), jnp.float32),
        in_specs=[
            pl.BlockSpec((rows, depth), lambda i: (0, i)),
            pl.BlockSpec((depth, moved.shape[1]), lambda i: (i, 0)),
        ],
        out_specs=pl.BlockSpec((2, rows, moved.shape[1]), lambda i: (0, 0, 0)),
        compiler_params=params(),
        cost_estimate=pl.CostEstimate(
            flops=4 * rows * width * moved.shape[1],
            bytes_accessed=2 * width * (rows + moved.shape[1]),
            transcendentals=0,
        ),
        name="sums",
    )(got, moved)


def pearson(share, blk):
    first, second = share[0], share[1]
    total_w = first[:, SUB:, :, :blk]
    sum_x = first[:, SUB:, :, blk : 2 * blk]
    sum_xx = first[:, SUB:, :, 2 * blk : 3 * blk]
    sum_y = second[:, SUB:, :, :blk]
    sum_xy = second[:, SUB:, :, blk : 2 * blk]
    sum_yy = second[:, :SUB, :, :blk]
    numer = total_w * sum_xy - sum_x * sum_y
    var_x = jnp.maximum(total_w * sum_xx - sum_x * sum_x, 0.05 * total_w * sum_xx)
    var_y = jnp.maximum(total_w * sum_yy - sum_y * sum_y, 0.05 * total_w * sum_yy)
    return numer / jnp.sqrt(var_x * var_y)


def fill_slabs(slabs, xw_ref):
    blk, width = xw_ref.shape[0] // 2, xw_ref.shape[1]
    step = min(512, width)

    @pl.loop(0, width // step)
    def _(i):
        cols = pl.ds(pl.multiple_of(i * step, step), step)
        wide = xw_ref[:, cols].astype(jnp.float32)
        for g in range(blk // SUB):
            rows = slice(g * SUB, (g + 1) * SUB)
            slab = jnp.concatenate([wide[:blk][rows], wide[blk:][rows]], 0)
            slabs[g, :, cols] = slab.astype(jnp.bfloat16)


def send_slabs(slabs, pick_ref, send_ref, sems):
    mine = lax.div(lax.axis_index("dp"), PLANE)
    partner = mine + 1 - 2 * lax.rem(mine, 2)
    copies = []
    for c in range(PLANE):
        for t, plane in enumerate((mine, partner)):
            group = pick_ref[plane * PLANE + c]
            copies.append(pltpu.make_async_copy(slabs.at[group], send_ref.at[c, t], sems.at[c, t]))
    for copy in copies:
        copy.start()
    for copy in copies:
        copy.wait()


def own_pack_kernel(pick_ref, xw_ref, send_ref, slabs, sems):
    fill_slabs(slabs, xw_ref)
    send_slabs(slabs, pick_ref, send_ref, sems)


def far_pack_kernel(pick_ref, outer_ref, inner_ref, after_ref, send_ref, buf, in_sem, slabs, sems):
    plane = lax.div(lax.axis_index("dp"), PLANE)
    is_inner = (plane == 1) | (plane == 2)

    def fetch(ref):
        copy = pltpu.make_async_copy(ref, buf, in_sem)
        copy.start()
        copy.wait()

    @pl.when(is_inner)
    def _():
        fetch(inner_ref)

    @pl.when(jnp.logical_not(is_inner))
    def _():
        fetch(outer_ref)

    fill_slabs(slabs, buf)
    send_slabs(slabs, pick_ref, send_ref, sems)


def pack_call(kernel, name, specs, scratch, blk, width, *operands):
    return pl.pallas_call(
        kernel,
        out_shape=jax.ShapeDtypeStruct((PLANE, 2, SLAB, width), jnp.bfloat16),
        in_specs=[pl.BlockSpec(memory_space=pltpu.SMEM)] + specs,
        out_specs=pl.BlockSpec(memory_space=pl.ANY),
        scratch_shapes=scratch
        + [pltpu.VMEM((blk // SUB, SLAB, width), jnp.bfloat16), pltpu.SemaphoreType.DMA((PLANE, 2))],
        compiler_params=params(),
        cost_estimate=pl.CostEstimate(
            flops=blk * width * 4, bytes_accessed=(PLANE * 2 * SLAB * 2 + blk * 4) * width, transcendentals=0
        ),
        name=name,
    )(*operands)


def own_pack(pick, xw):
    rows, width = xw.shape
    specs = [pl.BlockSpec(memory_space=pltpu.VMEM)]
    return pack_call(own_pack_kernel, "own_pack", specs, [], rows // 2, width, pick, xw)


def far_pack(pick, outer, inner, after):
    rows, width = outer.shape
    scratch = [pltpu.VMEM((rows, width), jnp.bfloat16), pltpu.SemaphoreType.DMA]
    specs = [pl.BlockSpec(memory_space=pl.ANY)] * 3
    return pack_call(far_pack_kernel, "far_pack", specs, scratch, rows // 2, width, pick, outer, inner, after)


def place_kernel(ops_ref, mine_ref, near_ref, after_ref, moved_ref, table, target):
    blk, depth = mine_ref.shape[0] // 2, mine_ref.shape[1]
    width = target.shape[0]
    part = pl.multiple_of(pl.program_id(1) * depth, depth)

    @pl.when(pl.program_id(0) == 0)
    def _():
        step = min(256, depth)
        diagonal = lax.broadcasted_iota(jnp.int32, (step, step), 0) == lax.broadcasted_iota(
            jnp.int32, (step, step), 1
        )
        identity = jnp.where(diagonal, 1.0, 0.0).astype(jnp.bfloat16)
        for i in range(depth // step):
            cols = slice(i * step, (i + 1) * step)
            pair = (mine_ref, near_ref)
            rows = jnp.concatenate([ref[:blk, cols] for ref in pair] + [ref[blk:, cols] for ref in pair], 0)
            table[pl.ds(part + i * step, step), :] = lax.dot_general(
                identity, rows, (((1,), (1,)), ((), ())), preferred_element_type=jnp.float32
            )

    @pl.loop(0, depth // UNROLL)
    def _(i):
        base = pl.multiple_of(i * UNROLL, UNROLL)
        row = pl.multiple_of(part + base, UNROLL)
        for j in range(UNROLL):
            to = ops_ref[0, 0, base + j]
            target[pl.ds(to, 1), :] = table[pl.ds(row + j, 1), :]

    @pl.when(pl.program_id(1) == pl.num_programs(1) - 1)
    def _():
        step = min(512, width)

        @pl.loop(0, width // step)
        def _(i):
            rows = pl.ds(pl.multiple_of(i * step, step), step)
            moved_ref[rows, :] = target[rows, :].astype(jnp.bfloat16)


def place(ops, mine, near, after):
    count = ops.shape[0]
    rows, width = mine.shape
    depth = min(2048, width)
    last = width // depth - 1
    part = pl.BlockSpec((rows, depth), lambda k, i: (0, jnp.where(k == 0, i, last)))
    return pl.pallas_call(
        place_kernel,
        grid=(count, width // depth),
        out_shape=jax.ShapeDtypeStruct((width, count * LANES), jnp.bfloat16),
        in_specs=[
            pl.BlockSpec((1, 1, depth), lambda k, i: (k, 0, i), memory_space=pltpu.SMEM),
            part,
            part,
            pl.BlockSpec(memory_space=pl.ANY),
        ],
        out_specs=pl.BlockSpec((width, LANES), lambda k, i: (0, k)),
        scratch_shapes=[pltpu.VMEM((width, LANES), jnp.float32)] * 2,
        compiler_params=params(),
        cost_estimate=pl.CostEstimate(
            flops=0, bytes_accessed=count * width * LANES * 64, transcendentals=0
        ),
        name="place",
    )(ops[:, None, :], mine, near, after)


def ratio(total_w, sum_x, sum_xx, sum_y, sum_xy, sum_yy):
    numer = total_w * sum_xy - sum_x * sum_y
    var_x = jnp.maximum(total_w * sum_xx - sum_x * sum_x, 0.05 * total_w * sum_xx)
    var_y = jnp.maximum(total_w * sum_yy - sum_y * sum_y, 0.05 * total_w * sum_yy)
    return numer / jnp.sqrt(var_x * var_y)


def add_sums(acc, got_ref, cols, right):
    rows = got_ref.shape[0]
    slabs = rows // SLAB
    wide = got_ref[:, cols].astype(jnp.float32).reshape(slabs, SLAB, -1)
    is_x = lax.broadcasted_iota(jnp.int32, wide.shape, 1) < SUB
    rolled = pltpu.roll(wide, SUB, 1)
    product = wide * rolled
    products = jnp.where(is_x, product * wide, product).reshape(rows, -1)
    mine = rolled.reshape(slabs // 2, 2, SLAB, -1)[:, 0]
    partner = wide.reshape(slabs // 2, 2, SLAB, -1)[:, 1]
    weights = jnp.where(is_x[: slabs // 2], mine, partner).reshape(rows // 2, -1)
    left = jnp.concatenate([weights, products], 0).astype(jnp.bfloat16)
    acc[...] += jnp.dot(left, right, preferred_element_type=jnp.float32)


def correlations(acc):
    rows = acc.shape[0] // 3
    half = LANES // 2
    blk = half // 2
    tiles = rows // SLAB
    top = lax.broadcasted_iota(jnp.int32, (tiles, SLAB, LANES), 1) < SUB
    lane = lax.broadcasted_iota(jnp.int32, (rows, LANES), 1)
    result = jnp.zeros((rows, LANES), jnp.float32)
    count = acc.shape[1] * 2 // 3 // LANES
    for k in range(count):
        lanes = slice(k * LANES, (k + 1) * LANES)
        squares = slice((count + k // 2) * LANES, (count + k // 2 + 1) * LANES)
        with_w = acc[:rows, lanes]
        with_y = acc[rows:, lanes].reshape(tiles, 2, SLAB, LANES)
        mine, partner = with_y[:, 0], with_y[:, 1]
        y = jnp.where(top, pltpu.roll(mine, SUB, 1), partner).reshape(rows, LANES)
        yy = jnp.where(top, mine, pltpu.roll(partner, SUB, 1)).reshape(rows, LANES)
        sum_xx = acc[:rows, squares]
        if k % 2 == 1:
            sum_xx = pltpu.roll(sum_xx, half, 1)
        both = ratio(
            pltpu.roll(with_w, half, 1), with_w, sum_xx, pltpu.roll(y, half, 1), y, pltpu.roll(yy, half, 1)
        )
        both = jnp.where(top.reshape(rows, LANES), both, pltpu.roll(both, LANES - blk, 1))
        moved = both if k == 0 else pltpu.roll(both, k * blk, 1)
        result = jnp.where((lane >= k * blk) & (lane < (k + 1) * blk), moved, result)
    return result


def plane_sums_kernel(pairs, got_ref, *refs):
    moved_refs, refs, acc = refs[:pairs], refs[pairs:-1], refs[-1]
    depth = got_ref.shape[1]
    step = min(1024, depth)
    half = LANES // 2

    @pl.when(pl.program_id(0) == 0)
    def _():
        acc[...] = jnp.zeros_like(acc)

    low = lax.broadcasted_iota(jnp.int32, (step, LANES), 1) < half
    for i in range(depth // step):
        cols = slice(i * step, (i + 1) * step)
        linear, square = [], []
        for ref in moved_refs:
            even, odd = None, None
            for k in range(2):
                values = ref[cols, k * LANES : (k + 1) * LANES].astype(jnp.float32)
                swapped = pltpu.roll(values, half, 1)
                product = values * swapped
                linear.append(jnp.where(low, product, values).astype(jnp.bfloat16))
                if k == 0:
                    even = product * values
                else:
                    odd = product * swapped
            square.append(jnp.where(low, even, odd).astype(jnp.bfloat16))
        add_sums(acc, got_ref, cols, jnp.concatenate(linear + square, 1))

    @pl.when(pl.program_id(0) == pl.num_programs(0) - 1)
    def _():
        if len(refs) == 1:
            refs[0][...] = correlations(acc)
            return
        first_ref, second_ref, mine_ref, other_ref, back_ref = refs
        upper = lax.div(lax.axis_index("dp"), 2 * PLANE)
        count = first_ref.shape[0] // 2
        low = lax.broadcasted_iota(jnp.int32, first_ref.shape, 1) < half
        own = jnp.where(low, first_ref[...], pltpu.roll(second_ref[...], half, 1))
        for part, result in enumerate((own, correlations(acc))):
            slot = part + upper - 2 * part * upper
            back_ref[slot] = result.reshape(PLANE, SLAB, LANES)
            pairs = result.reshape(PLANE // 2, 2, SLAB, LANES)
            even, odd = pairs[:, 0], pairs[:, 1]
            top = lax.broadcasted_iota(jnp.int32, even.shape, 1) < SUB
            here = slice(part * count, (part + 1) * count)
            mine_ref[here, :] = jnp.where(top, even, pltpu.roll(odd, SUB, 1)).reshape(count, LANES)
            other_ref[here, :] = jnp.where(top, pltpu.roll(even, SUB, 1), odd).reshape(count, LANES)


def plane_sums(got, moved, own):
    rows, width = got.shape
    depth = min(2048, width)
    lanes = 3 * len(moved) * LANES
    ended = len(own) > 0
    placed = pl.BlockSpec((depth, 2 * LANES), lambda i: (i, 0))
    result = (rows // 2, LANES)
    shapes = (result, result, (2, PLANE, SLAB, LANES)) if ended else (result,)
    entire = [pl.BlockSpec(shape, lambda i, shape=shape: (0,) * len(shape)) for shape in shapes]
    outs = pl.pallas_call(
        functools.partial(plane_sums_kernel, len(moved)),
        grid=(width // depth,),
        out_shape=tuple(jax.ShapeDtypeStruct(shape, jnp.float32) for shape in shapes),
        in_specs=[pl.BlockSpec((rows, depth), lambda i: (0, i))] + [placed] * len(moved) + [entire[0]] * len(own),
        out_specs=tuple(entire),
        scratch_shapes=[pltpu.VMEM((rows * 3 // 2, lanes), jnp.float32)],
        compiler_params=params(),
        cost_estimate=pl.CostEstimate(
            flops=3 * rows * width * lanes, bytes_accessed=2 * width * (rows + 2 * len(moved) * LANES), transcendentals=0
        ),
        name="plane_sums",
    )(got, *moved, *own)
    return outs if ended else outs[0]


def shards_by_plane(intensities, observed, qweights, ops, pick):
    blk, width = intensities.shape
    groups = PLANES * PLANE
    near = [(i, i ^ PLANE) for i in range(groups)]
    far = [(i, i ^ (2 * PLANE)) for i in range(groups)]
    middle = [(i, 3 * PLANE + 2 * (i % PLANE) - i) for i in range(PLANE, 3 * PLANE)]
    outward = [(i, i - PLANE if i < 2 * PLANE else i + PLANE) for i in range(PLANE, 3 * PLANE)]
    rings = [[z * PLANE + c for c in range(PLANE)] for z in range(PLANES)]
    couples = [[z * PLANE + c for z in (odd, odd + 2) for c in range(PLANE)] for odd in range(2)]
    plane = lax.axis_index("dp") // PLANE
    odd, upper = plane % 2 == 1, plane >= 2

    def spread(send):
        got = lax.all_to_all(send, "dp", split_axis=0, concat_axis=0, axis_index_groups=rings, tiled=True)
        return got.reshape(PLANE * 2 * SLAB, width)

    own_pick = pick[:, 0]
    own_w = (observed.astype(jnp.float32) * qweights.astype(jnp.float32)).astype(jnp.bfloat16)
    mine_xw = jnp.concatenate([intensities, own_w], 0)
    near_xw = lax.ppermute(mine_xw, "dp", near)
    mid_xw = lax.ppermute(mine_xw, "dp", middle)
    far_pick = lax.ppermute(own_pick, "dp", far)
    own_got = spread(own_pack(own_pick, mine_xw))
    near_xw, mid_xw, far_pick = lax.optimization_barrier((near_xw, mid_xw, far_pick))
    outer_xw = lax.ppermute(mid_xw, "dp", outward)
    inner_xw = lax.ppermute(near_xw, "dp", middle)
    first = place(ops[:2], mine_xw, near_xw, own_pick)
    own_first = plane_sums(own_got, (first,), ())
    far_send = far_pack(far_pick, outer_xw, inner_xw, own_first)
    far_got = spread(far_send)
    second = place(ops[2:], mine_xw, near_xw, far_send)
    own_second = plane_sums(own_got, (second,), ())
    mine, other, back = plane_sums(far_got, (first, second), (own_first, own_second))

    from_near = lax.ppermute(other, "dp", near)
    pair = [each.reshape(2, PLANE, SUB, NOPS * blk) for each in (mine, from_near)]
    pair = jnp.stack(pair, 1)
    pair = jnp.where(odd, pair[:, ::-1], pair)
    pair = jnp.where(upper, pair[::-1], pair)
    corr = pair.reshape(groups * SUB, NOPS * blk).T.reshape(NOPS, blk, groups * SUB)

    back = back.reshape(2 * PLANE, 2 * SUB, NOPS * blk)
    back = lax.all_to_all(back, "dp", split_axis=0, concat_axis=0, axis_index_groups=couples, tiled=True)
    back = back.reshape(2, PLANE, 2, SUB, NOPS, blk)
    back = jnp.where(odd, back[:, :, ::-1], back)
    returned = jnp.transpose(back, (4, 0, 2, 1, 3, 5)).reshape(NOPS, 1, groups, SUB, blk)
    return (corr, returned)


def shards(intensities, observed, qweights, ops, pick):
    if lax.axis_size("dp") == PLANES * PLANE and lax.axis_size("refl") == 1:
        return shards_by_plane(intensities, observed, qweights, ops, pick)
    return shards_direct(intensities, observed, qweights, ops, pick)


def shards_direct(intensities, observed, qweights, ops, pick):
    blk, width = intensities.shape
    groups = lax.axis_size("dp")
    shares = lax.axis_size("refl")
    local_ops = ops - lax.axis_index("refl") * width
    send, own_w = pack(pick[:, 0], intensities, observed, qweights)
    got = lax.all_to_all(send, "dp", split_axis=0, concat_axis=0, tiled=True)
    moved = move(local_ops, intensities, own_w)
    stats = sums(got.reshape(groups * SLAB, width), moved)
    if shares > 1:
        stats = lax.psum(stats, "refl")
    stats = stats.reshape(2, groups, SLAB, NOPS, LANES)
    full = pearson(stats, blk)
    rows = blk // shares
    if shares > 1:
        full = lax.dynamic_slice_in_dim(full, lax.axis_index("refl") * rows, rows, 3)
    corr = jnp.transpose(full, (2, 3, 0, 1)).reshape(NOPS, rows, groups * SUB)
    back = lax.all_to_all(full, "dp", split_axis=0, concat_axis=0, tiled=True)
    returned = jnp.transpose(back, (2, 0, 1, 3))[:, None]
    return (corr, returned)


def solution(mesh):
    return jax.shard_map(
        shards,
        mesh=mesh,
        in_specs=(
            P("dp", "refl"),
            P("dp", "refl"),
            P("dp", "refl"),
            P(None, "refl"),
            P(None, "dp"),
        ),
        out_specs=(P(None, ("dp", "refl"), None), P(None, "dp", None, None, "refl")),
        check_vma=False,
    )
```

```python
import functools

import jax
import jax.numpy as jnp
from jax import lax
from jax.experimental import pallas as pl
from jax.experimental.pallas import tpu as pltpu
from jax.sharding import PartitionSpec as P

SUB = 4
NOPS = 4
LANES = 128
SLAB = 2 * SUB
VMEM_LIMIT = 56 * 1024 * 1024
PLANES = 4
PLANE = 8
UNROLL = 64
PARTS = 4


def params():
    return pltpu.CompilerParams(vmem_limit_bytes=VMEM_LIMIT)


def pack_kernel(pick_ref, x_ref, obs_ref, qw_ref, send_ref, w_ref, slabs, sems):
    blk, width = x_ref.shape
    step = min(512, width)

    @pl.loop(0, width // step)
    def _(i):
        cols = pl.ds(pl.multiple_of(i * step, step), step)
        wide_w = obs_ref[:, cols].astype(jnp.float32) * qw_ref[:, cols].astype(jnp.float32)
        wide_x = x_ref[:, cols].astype(jnp.float32)
        w_ref[:, cols] = wide_w.astype(jnp.bfloat16)
        for g in range(blk // SUB):
            rows = slice(g * SUB, (g + 1) * SUB)
            slab = jnp.concatenate([wide_x[rows], wide_w[rows]], 0)
            slabs[g, :, cols] = slab.astype(jnp.bfloat16)

    groups = send_ref.shape[0]

    def copy(d):
        return pltpu.make_async_copy(slabs.at[pick_ref[d]], send_ref.at[d], sems.at[d])

    @pl.loop(0, groups)
    def _(d):
        copy(d).start()

    @pl.loop(0, groups)
    def _(d):
        copy(d).wait()


def pack(pick, intensities, observed, qweights):
    blk, width = intensities.shape
    groups = pick.shape[0]
    whole = pl.BlockSpec(memory_space=pltpu.VMEM)
    return pl.pallas_call(
        pack_kernel,
        out_shape=(
            jax.ShapeDtypeStruct((groups, SLAB, width), jnp.bfloat16),
            jax.ShapeDtypeStruct((blk, width), jnp.bfloat16),
        ),
        in_specs=[pl.BlockSpec(memory_space=pltpu.SMEM), whole, whole, whole],
        out_specs=(pl.BlockSpec(memory_space=pl.ANY), whole),
        scratch_shapes=[
            pltpu.VMEM((blk // SUB, SLAB, width), jnp.bfloat16),
            pltpu.SemaphoreType.DMA((groups,)),
        ],
        compiler_params=params(),
        cost_estimate=pl.CostEstimate(
            flops=blk * width * 4, bytes_accessed=(groups * SLAB * 2 + blk * 10) * width, transcendentals=0
        ),
        name="pack",
    )(pick, intensities, observed, qweights)


def move_kernel(ops_ref, x_ref, w_ref, moved_ref, table, target):
    blk, width = x_ref.shape

    @pl.when(pl.program_id(0) == 0)
    def _():
        @pl.loop(0, width // LANES)
        def _(i):
            cols = pl.ds(pl.multiple_of(i * LANES, LANES), LANES)
            wide_x = x_ref[:, cols].astype(jnp.float32)
            wide_w = w_ref[:, cols].astype(jnp.float32)
            wx = (wide_w * wide_x).astype(jnp.bfloat16).astype(jnp.float32)
            wxx = (wide_w * wide_x * wide_x).astype(jnp.bfloat16).astype(jnp.float32)
            stacked = jnp.concatenate([wide_w, wx, wxx, jnp.zeros((LANES - 3 * blk, LANES), jnp.float32)], 0)
            table[cols, :] = stacked.T

    unroll = 16

    @pl.loop(0, width // unroll)
    def _(i):
        base = pl.multiple_of(i * unroll, unroll)
        for j in range(unroll):
            to = ops_ref[0, 0, base + j]
            target[pl.ds(to, 1), :] = table[pl.ds(base + j, 1), :]

    step = min(512, width)

    @pl.loop(0, width // step)
    def _(i):
        rows = pl.ds(pl.multiple_of(i * step, step), step)
        moved_ref[rows, :] = target[rows, :].astype(jnp.bfloat16)


def move(local_ops, intensities, own_w):
    blk, width = intensities.shape
    whole = pl.BlockSpec(memory_space=pltpu.VMEM)
    return pl.pallas_call(
        move_kernel,
        grid=(NOPS,),
        out_shape=jax.ShapeDtypeStruct((width, NOPS * LANES), jnp.bfloat16),
        in_specs=[
            pl.BlockSpec((1, 1, width), lambda k: (k, 0, 0), memory_space=pltpu.SMEM),
            whole,
            whole,
        ],
        out_specs=pl.BlockSpec((width, LANES), lambda k: (0, k)),
        scratch_shapes=[
            pltpu.VMEM((width, LANES), jnp.float32),
            pltpu.VMEM((width, LANES), jnp.float32),
        ],
        compiler_params=params(),
        cost_estimate=pl.CostEstimate(
            flops=0, bytes_accessed=NOPS * width * LANES * 100, transcendentals=0
        ),
        name="move",
    )(local_ops[:, None, :], intensities, own_w)


def sums_kernel(got_ref, moved_ref, out_ref):
    rows, depth = got_ref.shape
    step = min(512, depth)

    @pl.when(pl.program_id(0) == 0)
    def _():
        out_ref[...] = jnp.zeros_like(out_ref)

    is_x = lax.broadcasted_iota(jnp.int32, (rows // SLAB, SLAB, step), 1) < SUB

    @pl.loop(0, depth // step)
    def _(i):
        cols = pl.ds(pl.multiple_of(i * step, step), step)
        raw = got_ref[:, cols]
        wide = raw.astype(jnp.float32).reshape(rows // SLAB, SLAB, step)
        product = wide * pltpu.roll(wide, SUB, 1)
        second = jnp.where(is_x, product * wide, product)
        second = second.reshape(rows, step).astype(jnp.bfloat16)
        right = moved_ref[cols, :]
        out_ref[0] += jnp.dot(raw, right, preferred_element_type=jnp.float32)
        out_ref[1] += jnp.dot(second, right, preferred_element_type=jnp.float32)


def sums(got, moved):
    rows, width = got.shape
    depth = min(2048, width)
    return pl.pallas_call(
        sums_kernel,
        grid=(width // depth,),
        out_shape=jax.ShapeDtypeStruct((2, rows, moved.shape[1]), jnp.float32),
        in_specs=[
            pl.BlockSpec((rows, depth), lambda i: (0, i)),
            pl.BlockSpec((depth, moved.shape[1]), lambda i: (i, 0)),
        ],
        out_specs=pl.BlockSpec((2, rows, moved.shape[1]), lambda i: (0, 0, 0)),
        compiler_params=params(),
        cost_estimate=pl.CostEstimate(
            flops=4 * rows * width * moved.shape[1],
            bytes_accessed=2 * width * (rows + moved.shape[1]),
            transcendentals=0,
        ),
        name="sums",
    )(got, moved)


def pearson(share, blk):
    first, second = share[0], share[1]
    total_w = first[:, SUB:, :, :blk]
    sum_x = first[:, SUB:, :, blk : 2 * blk]
    sum_xx = first[:, SUB:, :, 2 * blk : 3 * blk]
    sum_y = second[:, SUB:, :, :blk]
    sum_xy = second[:, SUB:, :, blk : 2 * blk]
    sum_yy = second[:, :SUB, :, :blk]
    numer = total_w * sum_xy - sum_x * sum_y
    var_x = jnp.maximum(total_w * sum_xx - sum_x * sum_x, 0.05 * total_w * sum_xx)
    var_y = jnp.maximum(total_w * sum_yy - sum_y * sum_y, 0.05 * total_w * sum_yy)
    return numer / jnp.sqrt(var_x * var_y)


def fill_slabs(slabs, xw_ref, offset, width):
    blk = xw_ref.shape[0] // 2
    step = min(512, width)

    @pl.loop(0, width // step)
    def _(i):
        cols = pl.ds(pl.multiple_of(offset + i * step, step), step)
        wide = xw_ref[:, cols].astype(jnp.float32)
        for g in range(blk // SUB):
            rows = slice(g * SUB, (g + 1) * SUB)
            slab = jnp.concatenate([wide[:blk][rows], wide[blk:][rows]], 0)
            slabs[g, :, cols] = slab.astype(jnp.bfloat16)


def send_slabs(xw_ref, pick_ref, send_ref, slabs, sems, ready):
    mine = lax.div(lax.axis_index("dp"), PLANE)
    partner = mine + 1 - 2 * lax.rem(mine, 2)
    span = xw_ref.shape[1] // PARTS
    copies = []
    for part in range(PARTS):
        ready(part)
        fill_slabs(slabs, xw_ref, part * span, span)
        cols = pl.ds(part * span, span)
        for c in range(PLANE):
            for t, plane in enumerate((mine, partner)):
                group = pick_ref[plane * PLANE + c]
                copy = pltpu.make_async_copy(
                    slabs.at[group, :, cols], send_ref.at[c, t, :, cols], sems.at[c, t, part]
                )
                copy.start()
                copies.append(copy)
    for copy in copies:
        copy.wait()


def own_pack_kernel(pick_ref, xw_ref, send_ref, slabs, sems):
    send_slabs(xw_ref, pick_ref, send_ref, slabs, sems, lambda part: None)


def far_pack_kernel(pick_ref, outer_ref, inner_ref, after_ref, send_ref, buf, in_sems, slabs, sems):
    plane = lax.div(lax.axis_index("dp"), PLANE)
    is_inner = (plane == 1) | (plane == 2)
    span = buf.shape[1] // PARTS

    def forward(ref):
        fetches = []
        for part in range(PARTS):
            cols = pl.ds(part * span, span)
            fetches.append(pltpu.make_async_copy(ref.at[:, cols], buf.at[:, cols], in_sems.at[part]))
        for fetch in fetches:
            fetch.start()
        send_slabs(buf, pick_ref, send_ref, slabs, sems, lambda part: fetches[part].wait())

    @pl.when(is_inner)
    def _():
        forward(inner_ref)

    @pl.when(jnp.logical_not(is_inner))
    def _():
        forward(outer_ref)


def pack_call(kernel, name, specs, scratch, blk, width, *operands):
    return pl.pallas_call(
        kernel,
        out_shape=jax.ShapeDtypeStruct((PLANE, 2, SLAB, width), jnp.bfloat16),
        in_specs=[pl.BlockSpec(memory_space=pltpu.SMEM)] + specs,
        out_specs=pl.BlockSpec(memory_space=pl.ANY),
        scratch_shapes=scratch
        + [pltpu.VMEM((blk // SUB, SLAB, width), jnp.bfloat16), pltpu.SemaphoreType.DMA((PLANE, 2, PARTS))],
        compiler_params=params(),
        cost_estimate=pl.CostEstimate(
            flops=blk * width * 4, bytes_accessed=(PLANE * 2 * SLAB * 2 + blk * 4) * width, transcendentals=0
        ),
        name=name,
    )(*operands)


def own_pack(pick, xw):
    rows, width = xw.shape
    specs = [pl.BlockSpec(memory_space=pltpu.VMEM)]
    return pack_call(own_pack_kernel, "own_pack", specs, [], rows // 2, width, pick, xw)


def far_pack(pick, outer, inner, after):
    rows, width = outer.shape
    scratch = [pltpu.VMEM((rows, width), jnp.bfloat16), pltpu.SemaphoreType.DMA((PARTS,))]
    specs = [pl.BlockSpec(memory_space=pl.ANY)] * 3
    return pack_call(far_pack_kernel, "far_pack", specs, scratch, rows // 2, width, pick, outer, inner, after)


def place_kernel(ops_ref, mine_ref, near_ref, after_ref, moved_ref, table, target):
    blk, depth = mine_ref.shape[0] // 2, mine_ref.shape[1]
    width = target.shape[0]
    part = pl.multiple_of(pl.program_id(1) * depth, depth)

    @pl.when(pl.program_id(0) == 0)
    def _():
        step = min(256, depth)
        diagonal = lax.broadcasted_iota(jnp.int32, (step, step), 0) == lax.broadcasted_iota(
            jnp.int32, (step, step), 1
        )
        identity = jnp.where(diagonal, 1.0, 0.0).astype(jnp.bfloat16)
        for i in range(depth // step):
            cols = slice(i * step, (i + 1) * step)
            pair = (mine_ref, near_ref)
            rows = jnp.concatenate([ref[:blk, cols] for ref in pair] + [ref[blk:, cols] for ref in pair], 0)
            table[pl.ds(part + i * step, step), :] = lax.dot_general(
                identity, rows, (((1,), (1,)), ((), ())), preferred_element_type=jnp.float32
            )

    @pl.loop(0, depth // UNROLL)
    def _(i):
        base = pl.multiple_of(i * UNROLL, UNROLL)
        row = pl.multiple_of(part + base, UNROLL)
        for j in range(UNROLL):
            to = ops_ref[0, 0, base + j]
            target[pl.ds(to, 1), :] = table[pl.ds(row + j, 1), :]

    @pl.when(pl.program_id(1) == pl.num_programs(1) - 1)
    def _():
        step = min(512, width)

        @pl.loop(0, width // step)
        def _(i):
            rows = pl.ds(pl.multiple_of(i * step, step), step)
            moved_ref[rows, :] = target[rows, :].astype(jnp.bfloat16)


def place(ops, mine, near, after):
    count = ops.shape[0]
    rows, width = mine.shape
    depth = min(2048, width)
    last = width // depth - 1
    part = pl.BlockSpec((rows, depth), lambda k, i: (0, jnp.where(k == 0, i, last)))
    return pl.pallas_call(
        place_kernel,
        grid=(count, width // depth),
        out_shape=jax.ShapeDtypeStruct((width, count * LANES), jnp.bfloat16),
        in_specs=[
            pl.BlockSpec((1, 1, depth), lambda k, i: (k, 0, i), memory_space=pltpu.SMEM),
            part,
            part,
            pl.BlockSpec(memory_space=pl.ANY),
        ],
        out_specs=pl.BlockSpec((width, LANES), lambda k, i: (0, k)),
        scratch_shapes=[pltpu.VMEM((width, LANES), jnp.float32)] * 2,
        compiler_params=params(),
        cost_estimate=pl.CostEstimate(
            flops=0, bytes_accessed=count * width * LANES * 64, transcendentals=0
        ),
        name="place",
    )(ops[:, None, :], mine, near, after)


def ratio(total_w, sum_x, sum_xx, sum_y, sum_xy, sum_yy):
    numer = total_w * sum_xy - sum_x * sum_y
    var_x = jnp.maximum(total_w * sum_xx - sum_x * sum_x, 0.05 * total_w * sum_xx)
    var_y = jnp.maximum(total_w * sum_yy - sum_y * sum_y, 0.05 * total_w * sum_yy)
    return numer / jnp.sqrt(var_x * var_y)


def add_sums(acc, got_ref, cols, right):
    rows = got_ref.shape[0]
    slabs = rows // SLAB
    wide = got_ref[:, cols].astype(jnp.float32).reshape(slabs, SLAB, -1)
    is_x = lax.broadcasted_iota(jnp.int32, wide.shape, 1) < SUB
    rolled = pltpu.roll(wide, SUB, 1)
    product = wide * rolled
    products = jnp.where(is_x, product * wide, product).reshape(rows, -1)
    mine = rolled.reshape(slabs // 2, 2, SLAB, -1)[:, 0]
    partner = wide.reshape(slabs // 2, 2, SLAB, -1)[:, 1]
    weights = jnp.where(is_x[: slabs // 2], mine, partner).reshape(rows // 2, -1)
    left = jnp.concatenate([weights, products], 0).astype(jnp.bfloat16)
    acc[...] += jnp.dot(left, right, preferred_element_type=jnp.float32)


def correlations(acc):
    rows = acc.shape[0] // 3
    half = LANES // 2
    blk = half // 2
    tiles = rows // SLAB
    top = lax.broadcasted_iota(jnp.int32, (tiles, SLAB, LANES), 1) < SUB
    lane = lax.broadcasted_iota(jnp.int32, (rows, LANES), 1)
    result = jnp.zeros((rows, LANES), jnp.float32)
    count = acc.shape[1] * 2 // 3 // LANES
    for k in range(count):
        lanes = slice(k * LANES, (k + 1) * LANES)
        squares = slice((count + k // 2) * LANES, (count + k // 2 + 1) * LANES)
        with_w = acc[:rows, lanes]
        with_y = acc[rows:, lanes].reshape(tiles, 2, SLAB, LANES)
        mine, partner = with_y[:, 0], with_y[:, 1]
        y = jnp.where(top, pltpu.roll(mine, SUB, 1), partner).reshape(rows, LANES)
        yy = jnp.where(top, mine, pltpu.roll(partner, SUB, 1)).reshape(rows, LANES)
        sum_xx = acc[:rows, squares]
        if k % 2 == 1:
            sum_xx = pltpu.roll(sum_xx, half, 1)
        both = ratio(
            pltpu.roll(with_w, half, 1), with_w, sum_xx, pltpu.roll(y, half, 1), y, pltpu.roll(yy, half, 1)
        )
        both = jnp.where(top.reshape(rows, LANES), both, pltpu.roll(both, LANES - blk, 1))
        moved = both if k == 0 else pltpu.roll(both, k * blk, 1)
        result = jnp.where((lane >= k * blk) & (lane < (k + 1) * blk), moved, result)
    return result


def plane_sums_kernel(pairs, got_ref, *refs):
    moved_refs, refs, acc = refs[:pairs], refs[pairs:-1], refs[-1]
    depth = got_ref.shape[1]
    step = min(1024, depth)
    half = LANES // 2

    @pl.when(pl.program_id(0) == 0)
    def _():
        acc[...] = jnp.zeros_like(acc)

    low = lax.broadcasted_iota(jnp.int32, (step, LANES), 1) < half
    for i in range(depth // step):
        cols = slice(i * step, (i + 1) * step)
        linear, square = [], []
        for ref in moved_refs:
            even, odd = None, None
            for k in range(2):
                values = ref[cols, k * LANES : (k + 1) * LANES].astype(jnp.float32)
                swapped = pltpu.roll(values, half, 1)
                product = values * swapped
                linear.append(jnp.where(low, product, values).astype(jnp.bfloat16))
                if k == 0:
                    even = product * values
                else:
                    odd = product * swapped
            square.append(jnp.where(low, even, odd).astype(jnp.bfloat16))
        add_sums(acc, got_ref, cols, jnp.concatenate(linear + square, 1))

    @pl.when(pl.program_id(0) == pl.num_programs(0) - 1)
    def _():
        if len(refs) == 1:
            refs[0][...] = correlations(acc)
            return
        first_ref, second_ref, mine_ref, other_ref, back_ref = refs
        upper = lax.div(lax.axis_index("dp"), 2 * PLANE)
        count = first_ref.shape[0] // 2
        low = lax.broadcasted_iota(jnp.int32, first_ref.shape, 1) < half
        own = jnp.where(low, first_ref[...], pltpu.roll(second_ref[...], half, 1))
        for part, result in enumerate((own, correlations(acc))):
            slot = part + upper - 2 * part * upper
            back_ref[slot] = result.reshape(PLANE, SLAB, LANES)
            pairs = result.reshape(PLANE // 2, 2, SLAB, LANES)
            even, odd = pairs[:, 0], pairs[:, 1]
            top = lax.broadcasted_iota(jnp.int32, even.shape, 1) < SUB
            here = slice(part * count, (part + 1) * count)
            mine_ref[here, :] = jnp.where(top, even, pltpu.roll(odd, SUB, 1)).reshape(count, LANES)
            other_ref[here, :] = jnp.where(top, pltpu.roll(even, SUB, 1), odd).reshape(count, LANES)


def plane_sums(got, moved, own):
    rows, width = got.shape
    depth = min(4096, width)
    lanes = 3 * len(moved) * LANES
    ended = len(own) > 0
    placed = pl.BlockSpec((depth, 2 * LANES), lambda i: (i, 0))
    result = (rows // 2, LANES)
    shapes = (result, result, (2, PLANE, SLAB, LANES)) if ended else (result,)
    entire = [pl.BlockSpec(shape, lambda i, shape=shape: (0,) * len(shape)) for shape in shapes]
    outs = pl.pallas_call(
        functools.partial(plane_sums_kernel, len(moved)),
        grid=(width // depth,),
        out_shape=tuple(jax.ShapeDtypeStruct(shape, jnp.float32) for shape in shapes),
        in_specs=[pl.BlockSpec((rows, depth), lambda i: (0, i))] + [placed] * len(moved) + [entire[0]] * len(own),
        out_specs=tuple(entire),
        scratch_shapes=[pltpu.VMEM((rows * 3 // 2, lanes), jnp.float32)],
        compiler_params=params(),
        cost_estimate=pl.CostEstimate(
            flops=3 * rows * width * lanes, bytes_accessed=2 * width * (rows + 2 * len(moved) * LANES), transcendentals=0
        ),
        name="plane_sums",
    )(got, *moved, *own)
    return outs if ended else outs[0]


def shards_by_plane(intensities, observed, qweights, ops, pick):
    blk, width = intensities.shape
    groups = PLANES * PLANE
    near = [(i, i ^ PLANE) for i in range(groups)]
    far = [(i, i ^ (2 * PLANE)) for i in range(groups)]
    middle = [(i, 3 * PLANE + 2 * (i % PLANE) - i) for i in range(PLANE, 3 * PLANE)]
    outward = [(i, i - PLANE if i < 2 * PLANE else i + PLANE) for i in range(PLANE, 3 * PLANE)]
    rings = [[z * PLANE + c for c in range(PLANE)] for z in range(PLANES)]
    couples = [[z * PLANE + c for z in (odd, odd + 2) for c in range(PLANE)] for odd in range(2)]
    plane = lax.axis_index("dp") // PLANE
    odd, upper = plane % 2 == 1, plane >= 2

    def spread(send):
        got = lax.all_to_all(send, "dp", split_axis=0, concat_axis=0, axis_index_groups=rings, tiled=True)
        return got.reshape(PLANE * 2 * SLAB, width)

    own_pick = pick[:, 0]
    own_w = (observed.astype(jnp.float32) * qweights.astype(jnp.float32)).astype(jnp.bfloat16)
    mine_xw = jnp.concatenate([intensities, own_w], 0)
    near_xw = lax.ppermute(mine_xw, "dp", near)
    mid_xw = lax.ppermute(mine_xw, "dp", middle)
    far_pick = lax.ppermute(own_pick, "dp", far)
    own_got = spread(own_pack(own_pick, mine_xw))
    near_xw, mid_xw, far_pick = lax.optimization_barrier((near_xw, mid_xw, far_pick))
    outer_xw = lax.ppermute(mid_xw, "dp", outward)
    inner_xw = lax.ppermute(near_xw, "dp", middle)
    first = place(ops[:2], mine_xw, near_xw, own_pick)
    own_first = plane_sums(own_got, (first,), ())
    far_send = far_pack(far_pick, outer_xw, inner_xw, own_first)
    far_got = spread(far_send)
    second = place(ops[2:], mine_xw, near_xw, far_send)
    own_second = plane_sums(own_got, (second,), ())
    mine, other, back = plane_sums(far_got, (first, second), (own_first, own_second))

    from_near = lax.ppermute(other, "dp", near)
    pair = [each.reshape(2, PLANE, SUB, NOPS * blk) for each in (mine, from_near)]
    pair = jnp.stack(pair, 1)
    pair = jnp.where(odd, pair[:, ::-1], pair)
    pair = jnp.where(upper, pair[::-1], pair)
    corr = pair.reshape(groups * SUB, NOPS * blk).T.reshape(NOPS, blk, groups * SUB)

    back = back.reshape(2 * PLANE, 2 * SUB, NOPS * blk)
    back = lax.all_to_all(back, "dp", split_axis=0, concat_axis=0, axis_index_groups=couples, tiled=True)
    back = back.reshape(2, PLANE, 2, SUB, NOPS, blk)
    back = jnp.where(odd, back[:, :, ::-1], back)
    returned = jnp.transpose(back, (4, 0, 2, 1, 3, 5)).reshape(NOPS, 1, groups, SUB, blk)
    return (corr, returned)


def shards(intensities, observed, qweights, ops, pick):
    if lax.axis_size("dp") == PLANES * PLANE and lax.axis_size("refl") == 1:
        return shards_by_plane(intensities, observed, qweights, ops, pick)
    return shards_direct(intensities, observed, qweights, ops, pick)


def shards_direct(intensities, observed, qweights, ops, pick):
    blk, width = intensities.shape
    groups = lax.axis_size("dp")
    shares = lax.axis_size("refl")
    local_ops = ops - lax.axis_index("refl") * width
    send, own_w = pack(pick[:, 0], intensities, observed, qweights)
    got = lax.all_to_all(send, "dp", split_axis=0, concat_axis=0, tiled=True)
    moved = move(local_ops, intensities, own_w)
    stats = sums(got.reshape(groups * SLAB, width), moved)
    if shares > 1:
        stats = lax.psum(stats, "refl")
    stats = stats.reshape(2, groups, SLAB, NOPS, LANES)
    full = pearson(stats, blk)
    rows = blk // shares
    if shares > 1:
        full = lax.dynamic_slice_in_dim(full, lax.axis_index("refl") * rows, rows, 3)
    corr = jnp.transpose(full, (2, 3, 0, 1)).reshape(NOPS, rows, groups * SUB)
    back = lax.all_to_all(full, "dp", split_axis=0, concat_axis=0, tiled=True)
    returned = jnp.transpose(back, (2, 0, 1, 3))[:, None]
    return (corr, returned)


def solution(mesh):
    return jax.shard_map(
        shards,
        mesh=mesh,
        in_specs=(
            P("dp", "refl"),
            P("dp", "refl"),
            P("dp", "refl"),
            P(None, "refl"),
            P(None, "dp"),
        ),
        out_specs=(P(None, ("dp", "refl"), None), P(None, "dp", None, None, "refl")),
        check_vma=False,
    )
```

```python
import functools

import jax
import jax.numpy as jnp
from jax import lax
from jax.experimental import pallas as pl
from jax.experimental.pallas import tpu as pltpu
from jax.sharding import PartitionSpec as P

SUB = 4
NOPS = 4
LANES = 128
SLAB = 2 * SUB
VMEM_LIMIT = 56 * 1024 * 1024
PLANES = 4
PLANE = 8
UNROLL = 128
PARTS = 4


def params():
    return pltpu.CompilerParams(vmem_limit_bytes=VMEM_LIMIT)


def pack_kernel(pick_ref, x_ref, obs_ref, qw_ref, send_ref, w_ref, slabs, sems):
    blk, width = x_ref.shape
    step = min(512, width)

    @pl.loop(0, width // step)
    def _(i):
        cols = pl.ds(pl.multiple_of(i * step, step), step)
        wide_w = obs_ref[:, cols].astype(jnp.float32) * qw_ref[:, cols].astype(jnp.float32)
        wide_x = x_ref[:, cols].astype(jnp.float32)
        w_ref[:, cols] = wide_w.astype(jnp.bfloat16)
        for g in range(blk // SUB):
            rows = slice(g * SUB, (g + 1) * SUB)
            slab = jnp.concatenate([wide_x[rows], wide_w[rows]], 0)
            slabs[g, :, cols] = slab.astype(jnp.bfloat16)

    groups = send_ref.shape[0]

    def copy(d):
        return pltpu.make_async_copy(slabs.at[pick_ref[d]], send_ref.at[d], sems.at[d])

    @pl.loop(0, groups)
    def _(d):
        copy(d).start()

    @pl.loop(0, groups)
    def _(d):
        copy(d).wait()


def pack(pick, intensities, observed, qweights):
    blk, width = intensities.shape
    groups = pick.shape[0]
    whole = pl.BlockSpec(memory_space=pltpu.VMEM)
    return pl.pallas_call(
        pack_kernel,
        out_shape=(
            jax.ShapeDtypeStruct((groups, SLAB, width), jnp.bfloat16),
            jax.ShapeDtypeStruct((blk, width), jnp.bfloat16),
        ),
        in_specs=[pl.BlockSpec(memory_space=pltpu.SMEM), whole, whole, whole],
        out_specs=(pl.BlockSpec(memory_space=pl.ANY), whole),
        scratch_shapes=[
            pltpu.VMEM((blk // SUB, SLAB, width), jnp.bfloat16),
            pltpu.SemaphoreType.DMA((groups,)),
        ],
        compiler_params=params(),
        cost_estimate=pl.CostEstimate(
            flops=blk * width * 4, bytes_accessed=(groups * SLAB * 2 + blk * 10) * width, transcendentals=0
        ),
        name="pack",
    )(pick, intensities, observed, qweights)


def move_kernel(ops_ref, x_ref, w_ref, moved_ref, table, target):
    blk, width = x_ref.shape

    @pl.when(pl.program_id(0) == 0)
    def _():
        @pl.loop(0, width // LANES)
        def _(i):
            cols = pl.ds(pl.multiple_of(i * LANES, LANES), LANES)
            wide_x = x_ref[:, cols].astype(jnp.float32)
            wide_w = w_ref[:, cols].astype(jnp.float32)
            wx = (wide_w * wide_x).astype(jnp.bfloat16).astype(jnp.float32)
            wxx = (wide_w * wide_x * wide_x).astype(jnp.bfloat16).astype(jnp.float32)
            stacked = jnp.concatenate([wide_w, wx, wxx, jnp.zeros((LANES - 3 * blk, LANES), jnp.float32)], 0)
            table[cols, :] = stacked.T

    unroll = 16

    @pl.loop(0, width // unroll)
    def _(i):
        base = pl.multiple_of(i * unroll, unroll)
        for j in range(unroll):
            to = ops_ref[0, 0, base + j]
            target[pl.ds(to, 1), :] = table[pl.ds(base + j, 1), :]

    step = min(512, width)

    @pl.loop(0, width // step)
    def _(i):
        rows = pl.ds(pl.multiple_of(i * step, step), step)
        moved_ref[rows, :] = target[rows, :].astype(jnp.bfloat16)


def move(local_ops, intensities, own_w):
    blk, width = intensities.shape
    whole = pl.BlockSpec(memory_space=pltpu.VMEM)
    return pl.pallas_call(
        move_kernel,
        grid=(NOPS,),
        out_shape=jax.ShapeDtypeStruct((width, NOPS * LANES), jnp.bfloat16),
        in_specs=[
            pl.BlockSpec((1, 1, width), lambda k: (k, 0, 0), memory_space=pltpu.SMEM),
            whole,
            whole,
        ],
        out_specs=pl.BlockSpec((width, LANES), lambda k: (0, k)),
        scratch_shapes=[
            pltpu.VMEM((width, LANES), jnp.float32),
            pltpu.VMEM((width, LANES), jnp.float32),
        ],
        compiler_params=params(),
        cost_estimate=pl.CostEstimate(
            flops=0, bytes_accessed=NOPS * width * LANES * 100, transcendentals=0
        ),
        name="move",
    )(local_ops[:, None, :], intensities, own_w)


def sums_kernel(got_ref, moved_ref, out_ref):
    rows, depth = got_ref.shape
    step = min(512, depth)

    @pl.when(pl.program_id(0) == 0)
    def _():
        out_ref[...] = jnp.zeros_like(out_ref)

    is_x = lax.broadcasted_iota(jnp.int32, (rows // SLAB, SLAB, step), 1) < SUB

    @pl.loop(0, depth // step)
    def _(i):
        cols = pl.ds(pl.multiple_of(i * step, step), step)
        raw = got_ref[:, cols]
        wide = raw.astype(jnp.float32).reshape(rows // SLAB, SLAB, step)
        product = wide * pltpu.roll(wide, SUB, 1)
        second = jnp.where(is_x, product * wide, product)
        second = second.reshape(rows, step).astype(jnp.bfloat16)
        right = moved_ref[cols, :]
        out_ref[0] += jnp.dot(raw, right, preferred_element_type=jnp.float32)
        out_ref[1] += jnp.dot(second, right, preferred_element_type=jnp.float32)


def sums(got, moved):
    rows, width = got.shape
    depth = min(2048, width)
    return pl.pallas_call(
        sums_kernel,
        grid=(width // depth,),
        out_shape=jax.ShapeDtypeStruct((2, rows, moved.shape[1]), jnp.float32),
        in_specs=[
            pl.BlockSpec((rows, depth), lambda i: (0, i)),
            pl.BlockSpec((depth, moved.shape[1]), lambda i: (i, 0)),
        ],
        out_specs=pl.BlockSpec((2, rows, moved.shape[1]), lambda i: (0, 0, 0)),
        compiler_params=params(),
        cost_estimate=pl.CostEstimate(
            flops=4 * rows * width * moved.shape[1],
            bytes_accessed=2 * width * (rows + moved.shape[1]),
            transcendentals=0,
        ),
        name="sums",
    )(got, moved)


def pearson(share, blk):
    first, second = share[0], share[1]
    total_w = first[:, SUB:, :, :blk]
    sum_x = first[:, SUB:, :, blk : 2 * blk]
    sum_xx = first[:, SUB:, :, 2 * blk : 3 * blk]
    sum_y = second[:, SUB:, :, :blk]
    sum_xy = second[:, SUB:, :, blk : 2 * blk]
    sum_yy = second[:, :SUB, :, :blk]
    numer = total_w * sum_xy - sum_x * sum_y
    var_x = jnp.maximum(total_w * sum_xx - sum_x * sum_x, 0.05 * total_w * sum_xx)
    var_y = jnp.maximum(total_w * sum_yy - sum_y * sum_y, 0.05 * total_w * sum_yy)
    return numer / jnp.sqrt(var_x * var_y)


def fill_slabs(slabs, xw_ref, offset, width):
    blk = xw_ref.shape[0] // 2
    step = min(512, width)

    @pl.loop(0, width // step)
    def _(i):
        cols = pl.ds(pl.multiple_of(offset + i * step, step), step)
        wide = xw_ref[:, cols].astype(jnp.float32)
        for g in range(blk // SUB):
            rows = slice(g * SUB, (g + 1) * SUB)
            slab = jnp.concatenate([wide[:blk][rows], wide[blk:][rows]], 0)
            slabs[g, :, cols] = slab.astype(jnp.bfloat16)


def send_slabs(xw_ref, pick_ref, send_ref, slabs, sems, ready):
    mine = lax.div(lax.axis_index("dp"), PLANE)
    partner = mine + 1 - 2 * lax.rem(mine, 2)
    span = xw_ref.shape[1] // PARTS
    copies = []
    for part in range(PARTS):
        ready(part)
        fill_slabs(slabs, xw_ref, part * span, span)
        cols = pl.ds(part * span, span)
        for c in range(PLANE):
            for t, plane in enumerate((mine, partner)):
                group = pick_ref[plane * PLANE + c]
                copy = pltpu.make_async_copy(
                    slabs.at[group, :, cols], send_ref.at[c, t, :, cols], sems.at[c, t, part]
                )
                copy.start()
                copies.append(copy)
    for copy in copies:
        copy.wait()


def own_pack_kernel(pick_ref, xw_ref, send_ref, slabs, sems):
    send_slabs(xw_ref, pick_ref, send_ref, slabs, sems, lambda part: None)


def far_pack_kernel(pick_ref, outer_ref, inner_ref, after_ref, send_ref, buf, in_sems, slabs, sems):
    plane = lax.div(lax.axis_index("dp"), PLANE)
    is_inner = (plane == 1) | (plane == 2)
    span = buf.shape[1] // PARTS

    def forward(ref):
        fetches = []
        for part in range(PARTS):
            cols = pl.ds(part * span, span)
            fetches.append(pltpu.make_async_copy(ref.at[:, cols], buf.at[:, cols], in_sems.at[part]))
        for fetch in fetches:
            fetch.start()
        send_slabs(buf, pick_ref, send_ref, slabs, sems, lambda part: fetches[part].wait())

    @pl.when(is_inner)
    def _():
        forward(inner_ref)

    @pl.when(jnp.logical_not(is_inner))
    def _():
        forward(outer_ref)


def pack_call(kernel, name, specs, scratch, blk, width, *operands):
    return pl.pallas_call(
        kernel,
        out_shape=jax.ShapeDtypeStruct((PLANE, 2, SLAB, width), jnp.bfloat16),
        in_specs=[pl.BlockSpec(memory_space=pltpu.SMEM)] + specs,
        out_specs=pl.BlockSpec(memory_space=pl.ANY),
        scratch_shapes=scratch
        + [pltpu.VMEM((blk // SUB, SLAB, width), jnp.bfloat16), pltpu.SemaphoreType.DMA((PLANE, 2, PARTS))],
        compiler_params=params(),
        cost_estimate=pl.CostEstimate(
            flops=blk * width * 4, bytes_accessed=(PLANE * 2 * SLAB * 2 + blk * 4) * width, transcendentals=0
        ),
        name=name,
    )(*operands)


def own_pack(pick, xw):
    rows, width = xw.shape
    specs = [pl.BlockSpec(memory_space=pltpu.VMEM)]
    return pack_call(own_pack_kernel, "own_pack", specs, [], rows // 2, width, pick, xw)


def far_pack(pick, outer, inner, after):
    rows, width = outer.shape
    scratch = [pltpu.VMEM((rows, width), jnp.bfloat16), pltpu.SemaphoreType.DMA((PARTS,))]
    specs = [pl.BlockSpec(memory_space=pl.ANY)] * 3
    return pack_call(far_pack_kernel, "far_pack", specs, scratch, rows // 2, width, pick, outer, inner, after)


def place_kernel(ops_ref, mine_ref, near_ref, after_ref, moved_ref, table, target):
    blk, depth = mine_ref.shape[0] // 2, mine_ref.shape[1]
    width = target.shape[0]
    part = pl.multiple_of(pl.program_id(1) * depth, depth)

    @pl.when(pl.program_id(0) == 0)
    def _():
        step = min(256, depth)
        diagonal = lax.broadcasted_iota(jnp.int32, (step, step), 0) == lax.broadcasted_iota(
            jnp.int32, (step, step), 1
        )
        identity = jnp.where(diagonal, 1.0, 0.0).astype(jnp.bfloat16)
        for i in range(depth // step):
            cols = slice(i * step, (i + 1) * step)
            pair = (mine_ref, near_ref)
            rows = jnp.concatenate([ref[:blk, cols] for ref in pair] + [ref[blk:, cols] for ref in pair], 0)
            table[pl.ds(part + i * step, step), :] = lax.dot_general(
                identity, rows, (((1,), (1,)), ((), ())), preferred_element_type=jnp.float32
            )

    @pl.loop(0, depth // UNROLL)
    def _(i):
        base = pl.multiple_of(i * UNROLL, UNROLL)
        row = pl.multiple_of(part + base, UNROLL)
        for j in range(UNROLL):
            to = ops_ref[0, 0, base + j]
            target[pl.ds(to, 1), :] = table[pl.ds(row + j, 1), :]

    @pl.when(pl.program_id(1) == pl.num_programs(1) - 1)
    def _():
        step = min(512, width)

        @pl.loop(0, width // step)
        def _(i):
            rows = pl.ds(pl.multiple_of(i * step, step), step)
            moved_ref[rows, :] = target[rows, :].astype(jnp.bfloat16)


def place(ops, mine, near, after):
    count = ops.shape[0]
    rows, width = mine.shape
    depth = min(2048, width)
    last = width // depth - 1
    part = pl.BlockSpec((rows, depth), lambda k, i: (0, jnp.where(k == 0, i, last)))
    return pl.pallas_call(
        place_kernel,
        grid=(count, width // depth),
        out_shape=jax.ShapeDtypeStruct((width, count * LANES), jnp.bfloat16),
        in_specs=[
            pl.BlockSpec((1, 1, depth), lambda k, i: (k, 0, i), memory_space=pltpu.SMEM),
            part,
            part,
            pl.BlockSpec(memory_space=pl.ANY),
        ],
        out_specs=pl.BlockSpec((width, LANES), lambda k, i: (0, k)),
        scratch_shapes=[pltpu.VMEM((width, LANES), jnp.float32)] * 2,
        compiler_params=params(),
        cost_estimate=pl.CostEstimate(
            flops=0, bytes_accessed=count * width * LANES * 64, transcendentals=0
        ),
        name="place",
    )(ops[:, None, :], mine, near, after)


def ratio(total_w, sum_x, sum_xx, sum_y, sum_xy, sum_yy):
    numer = total_w * sum_xy - sum_x * sum_y
    var_x = jnp.maximum(total_w * sum_xx - sum_x * sum_x, 0.05 * total_w * sum_xx)
    var_y = jnp.maximum(total_w * sum_yy - sum_y * sum_y, 0.05 * total_w * sum_yy)
    return numer / jnp.sqrt(var_x * var_y)


def add_sums(acc, got_ref, cols, right):
    rows = got_ref.shape[0]
    slabs = rows // SLAB
    wide = got_ref[:, cols].astype(jnp.float32).reshape(slabs, SLAB, -1)
    is_x = lax.broadcasted_iota(jnp.int32, wide.shape, 1) < SUB
    rolled = pltpu.roll(wide, SUB, 1)
    product = wide * rolled
    products = jnp.where(is_x, product * wide, product).reshape(rows, -1)
    mine = rolled.reshape(slabs // 2, 2, SLAB, -1)[:, 0]
    partner = wide.reshape(slabs // 2, 2, SLAB, -1)[:, 1]
    weights = jnp.where(is_x[: slabs // 2], mine, partner).reshape(rows // 2, -1)
    left = jnp.concatenate([weights, products], 0).astype(jnp.bfloat16)
    acc[...] += jnp.dot(left, right, preferred_element_type=jnp.float32)


def correlations(acc):
    rows = acc.shape[0] // 3
    half = LANES // 2
    blk = half // 2
    tiles = rows // SLAB
    top = lax.broadcasted_iota(jnp.int32, (tiles, SLAB, LANES), 1) < SUB
    lane = lax.broadcasted_iota(jnp.int32, (rows, LANES), 1)
    result = jnp.zeros((rows, LANES), jnp.float32)
    count = acc.shape[1] * 2 // 3 // LANES
    for k in range(count):
        lanes = slice(k * LANES, (k + 1) * LANES)
        squares = slice((count + k // 2) * LANES, (count + k // 2 + 1) * LANES)
        with_w = acc[:rows, lanes]
        with_y = acc[rows:, lanes].reshape(tiles, 2, SLAB, LANES)
        mine, partner = with_y[:, 0], with_y[:, 1]
        y = jnp.where(top, pltpu.roll(mine, SUB, 1), partner).reshape(rows, LANES)
        yy = jnp.where(top, mine, pltpu.roll(partner, SUB, 1)).reshape(rows, LANES)
        sum_xx = acc[:rows, squares]
        if k % 2 == 1:
            sum_xx = pltpu.roll(sum_xx, half, 1)
        both = ratio(
            pltpu.roll(with_w, half, 1), with_w, sum_xx, pltpu.roll(y, half, 1), y, pltpu.roll(yy, half, 1)
        )
        both = jnp.where(top.reshape(rows, LANES), both, pltpu.roll(both, LANES - blk, 1))
        moved = both if k == 0 else pltpu.roll(both, k * blk, 1)
        result = jnp.where((lane >= k * blk) & (lane < (k + 1) * blk), moved, result)
    return result


def plane_sums_kernel(pairs, got_ref, *refs):
    moved_refs, refs, acc = refs[:pairs], refs[pairs:-1], refs[-1]
    depth = got_ref.shape[1]
    step = min(2048, depth)
    half = LANES // 2

    @pl.when(pl.program_id(0) == 0)
    def _():
        acc[...] = jnp.zeros_like(acc)

    low = lax.broadcasted_iota(jnp.int32, (step, LANES), 1) < half
    for i in range(depth // step):
        cols = slice(i * step, (i + 1) * step)
        linear, square = [], []
        for ref in moved_refs:
            even, odd = None, None
            for k in range(2):
                values = ref[cols, k * LANES : (k + 1) * LANES].astype(jnp.float32)
                swapped = pltpu.roll(values, half, 1)
                product = values * swapped
                linear.append(jnp.where(low, product, values).astype(jnp.bfloat16))
                if k == 0:
                    even = product * values
                else:
                    odd = product * swapped
            square.append(jnp.where(low, even, odd).astype(jnp.bfloat16))
        add_sums(acc, got_ref, cols, jnp.concatenate(linear + square, 1))

    @pl.when(pl.program_id(0) == pl.num_programs(0) - 1)
    def _():
        if len(refs) == 1:
            refs[0][...] = correlations(acc)
            return
        first_ref, second_ref, mine_ref, other_ref, back_ref = refs
        upper = lax.div(lax.axis_index("dp"), 2 * PLANE)
        count = first_ref.shape[0] // 2
        low = lax.broadcasted_iota(jnp.int32, first_ref.shape, 1) < half
        own = jnp.where(low, first_ref[...], pltpu.roll(second_ref[...], half, 1))
        for part, result in enumerate((own, correlations(acc))):
            slot = part + upper - 2 * part * upper
            back_ref[slot] = result.reshape(PLANE, SLAB, LANES)
            pairs = result.reshape(PLANE // 2, 2, SLAB, LANES)
            even, odd = pairs[:, 0], pairs[:, 1]
            top = lax.broadcasted_iota(jnp.int32, even.shape, 1) < SUB
            here = slice(part * count, (part + 1) * count)
            mine_ref[here, :] = jnp.where(top, even, pltpu.roll(odd, SUB, 1)).reshape(count, LANES)
            other_ref[here, :] = jnp.where(top, pltpu.roll(even, SUB, 1), odd).reshape(count, LANES)


def plane_sums(got, moved, own):
    rows, width = got.shape
    depth = min(4096, width)
    lanes = 3 * len(moved) * LANES
    ended = len(own) > 0
    placed = pl.BlockSpec((depth, 2 * LANES), lambda i: (i, 0))
    result = (rows // 2, LANES)
    shapes = (result, result, (2, PLANE, SLAB, LANES)) if ended else (result,)
    entire = [pl.BlockSpec(shape, lambda i, shape=shape: (0,) * len(shape)) for shape in shapes]
    outs = pl.pallas_call(
        functools.partial(plane_sums_kernel, len(moved)),
        grid=(width // depth,),
        out_shape=tuple(jax.ShapeDtypeStruct(shape, jnp.float32) for shape in shapes),
        in_specs=[pl.BlockSpec((rows, depth), lambda i: (0, i))] + [placed] * len(moved) + [entire[0]] * len(own),
        out_specs=tuple(entire),
        scratch_shapes=[pltpu.VMEM((rows * 3 // 2, lanes), jnp.float32)],
        compiler_params=params(),
        cost_estimate=pl.CostEstimate(
            flops=3 * rows * width * lanes, bytes_accessed=2 * width * (rows + 2 * len(moved) * LANES), transcendentals=0
        ),
        name="plane_sums",
    )(got, *moved, *own)
    return outs if ended else outs[0]


def shards_by_plane(intensities, observed, qweights, ops, pick):
    blk, width = intensities.shape
    groups = PLANES * PLANE
    near = [(i, i ^ PLANE) for i in range(groups)]
    far = [(i, i ^ (2 * PLANE)) for i in range(groups)]
    middle = [(i, 3 * PLANE + 2 * (i % PLANE) - i) for i in range(PLANE, 3 * PLANE)]
    outward = [(i, i - PLANE if i < 2 * PLANE else i + PLANE) for i in range(PLANE, 3 * PLANE)]
    rings = [[z * PLANE + c for c in range(PLANE)] for z in range(PLANES)]
    couples = [[z * PLANE + c for z in (odd, odd + 2) for c in range(PLANE)] for odd in range(2)]
    plane = lax.axis_index("dp") // PLANE
    odd, upper = plane % 2 == 1, plane >= 2

    def spread(send):
        got = lax.all_to_all(send, "dp", split_axis=0, concat_axis=0, axis_index_groups=rings, tiled=True)
        return got.reshape(PLANE * 2 * SLAB, width)

    own_pick = pick[:, 0]
    own_w = (observed.astype(jnp.float32) * qweights.astype(jnp.float32)).astype(jnp.bfloat16)
    mine_xw = jnp.concatenate([intensities, own_w], 0)
    near_xw = lax.ppermute(mine_xw, "dp", near)
    mid_xw = lax.ppermute(mine_xw, "dp", middle)
    far_pick = lax.ppermute(own_pick, "dp", far)
    own_got = spread(own_pack(own_pick, mine_xw))
    near_xw, mid_xw, far_pick = lax.optimization_barrier((near_xw, mid_xw, far_pick))
    outer_xw = lax.ppermute(mid_xw, "dp", outward)
    inner_xw = lax.ppermute(near_xw, "dp", middle)
    first = place(ops[:2], mine_xw, near_xw, own_pick)
    own_first = plane_sums(own_got, (first,), ())
    far_send = far_pack(far_pick, outer_xw, inner_xw, own_first)
    far_got = spread(far_send)
    second = place(ops[2:], mine_xw, near_xw, far_send)
    own_second = plane_sums(own_got, (second,), ())
    mine, other, back = plane_sums(far_got, (first, second), (own_first, own_second))

    from_near = lax.ppermute(other, "dp", near)
    pair = [each.reshape(2, PLANE, SUB, NOPS * blk) for each in (mine, from_near)]
    pair = jnp.stack(pair, 1)
    pair = jnp.where(odd, pair[:, ::-1], pair)
    pair = jnp.where(upper, pair[::-1], pair)
    corr = pair.reshape(groups * SUB, NOPS * blk).T.reshape(NOPS, blk, groups * SUB)

    back = back.reshape(2 * PLANE, 2 * SUB, NOPS * blk)
    back = lax.all_to_all(back, "dp", split_axis=0, concat_axis=0, axis_index_groups=couples, tiled=True)
    back = back.reshape(2, PLANE, 2, SUB, NOPS, blk)
    back = jnp.where(odd, back[:, :, ::-1], back)
    returned = jnp.transpose(back, (4, 0, 2, 1, 3, 5)).reshape(NOPS, 1, groups, SUB, blk)
    return (corr, returned)


def shards(intensities, observed, qweights, ops, pick):
    if lax.axis_size("dp") == PLANES * PLANE and lax.axis_size("refl") == 1:
        return shards_by_plane(intensities, observed, qweights, ops, pick)
    return shards_direct(intensities, observed, qweights, ops, pick)


def shards_direct(intensities, observed, qweights, ops, pick):
    blk, width = intensities.shape
    groups = lax.axis_size("dp")
    shares = lax.axis_size("refl")
    local_ops = ops - lax.axis_index("refl") * width
    send, own_w = pack(pick[:, 0], intensities, observed, qweights)
    got = lax.all_to_all(send, "dp", split_axis=0, concat_axis=0, tiled=True)
    moved = move(local_ops, intensities, own_w)
    stats = sums(got.reshape(groups * SLAB, width), moved)
    if shares > 1:
        stats = lax.psum(stats, "refl")
    stats = stats.reshape(2, groups, SLAB, NOPS, LANES)
    full = pearson(stats, blk)
    rows = blk // shares
    if shares > 1:
        full = lax.dynamic_slice_in_dim(full, lax.axis_index("refl") * rows, rows, 3)
    corr = jnp.transpose(full, (2, 3, 0, 1)).reshape(NOPS, rows, groups * SUB)
    back = lax.all_to_all(full, "dp", split_axis=0, concat_axis=0, tiled=True)
    returned = jnp.transpose(back, (2, 0, 1, 3))[:, None]
    return (corr, returned)


def solution(mesh):
    return jax.shard_map(
        shards,
        mesh=mesh,
        in_specs=(
            P("dp", "refl"),
            P("dp", "refl"),
            P("dp", "refl"),
            P(None, "refl"),
            P(None, "dp"),
        ),
        out_specs=(P(None, ("dp", "refl"), None), P(None, "dp", None, None, "refl")),
        check_vma=False,
    )
```

```python
import functools

import jax
import jax.numpy as jnp
from jax import lax
from jax.experimental import pallas as pl
from jax.experimental.pallas import tpu as pltpu
from jax.sharding import PartitionSpec as P

SUB = 4
NOPS = 4
LANES = 128
SLAB = 2 * SUB
VMEM_LIMIT = 56 * 1024 * 1024
PLANES = 4
PLANE = 8
UNROLL = 128
PARTS = 4


def params():
    return pltpu.CompilerParams(vmem_limit_bytes=VMEM_LIMIT)


def pack_kernel(pick_ref, x_ref, obs_ref, qw_ref, send_ref, w_ref, slabs, sems):
    blk, width = x_ref.shape
    step = min(512, width)

    @pl.loop(0, width // step)
    def _(i):
        cols = pl.ds(pl.multiple_of(i * step, step), step)
        wide_w = obs_ref[:, cols].astype(jnp.float32) * qw_ref[:, cols].astype(jnp.float32)
        wide_x = x_ref[:, cols].astype(jnp.float32)
        w_ref[:, cols] = wide_w.astype(jnp.bfloat16)
        for g in range(blk // SUB):
            rows = slice(g * SUB, (g + 1) * SUB)
            slab = jnp.concatenate([wide_x[rows], wide_w[rows]], 0)
            slabs[g, :, cols] = slab.astype(jnp.bfloat16)

    groups = send_ref.shape[0]

    def copy(d):
        return pltpu.make_async_copy(slabs.at[pick_ref[d]], send_ref.at[d], sems.at[d])

    @pl.loop(0, groups)
    def _(d):
        copy(d).start()

    @pl.loop(0, groups)
    def _(d):
        copy(d).wait()


def pack(pick, intensities, observed, qweights):
    blk, width = intensities.shape
    groups = pick.shape[0]
    whole = pl.BlockSpec(memory_space=pltpu.VMEM)
    return pl.pallas_call(
        pack_kernel,
        out_shape=(
            jax.ShapeDtypeStruct((groups, SLAB, width), jnp.bfloat16),
            jax.ShapeDtypeStruct((blk, width), jnp.bfloat16),
        ),
        in_specs=[pl.BlockSpec(memory_space=pltpu.SMEM), whole, whole, whole],
        out_specs=(pl.BlockSpec(memory_space=pl.ANY), whole),
        scratch_shapes=[
            pltpu.VMEM((blk // SUB, SLAB, width), jnp.bfloat16),
            pltpu.SemaphoreType.DMA((groups,)),
        ],
        compiler_params=params(),
        cost_estimate=pl.CostEstimate(
            flops=blk * width * 4, bytes_accessed=(groups * SLAB * 2 + blk * 10) * width, transcendentals=0
        ),
        name="pack",
    )(pick, intensities, observed, qweights)


def move_kernel(ops_ref, x_ref, w_ref, moved_ref, table, target):
    blk, width = x_ref.shape

    @pl.when(pl.program_id(0) == 0)
    def _():
        @pl.loop(0, width // LANES)
        def _(i):
            cols = pl.ds(pl.multiple_of(i * LANES, LANES), LANES)
            wide_x = x_ref[:, cols].astype(jnp.float32)
            wide_w = w_ref[:, cols].astype(jnp.float32)
            wx = (wide_w * wide_x).astype(jnp.bfloat16).astype(jnp.float32)
            wxx = (wide_w * wide_x * wide_x).astype(jnp.bfloat16).astype(jnp.float32)
            stacked = jnp.concatenate([wide_w, wx, wxx, jnp.zeros((LANES - 3 * blk, LANES), jnp.float32)], 0)
            table[cols, :] = stacked.T

    unroll = 16

    @pl.loop(0, width // unroll)
    def _(i):
        base = pl.multiple_of(i * unroll, unroll)
        for j in range(unroll):
            to = ops_ref[0, 0, base + j]
            target[pl.ds(to, 1), :] = table[pl.ds(base + j, 1), :]

    step = min(512, width)

    @pl.loop(0, width // step)
    def _(i):
        rows = pl.ds(pl.multiple_of(i * step, step), step)
        moved_ref[rows, :] = target[rows, :].astype(jnp.bfloat16)


def move(local_ops, intensities, own_w):
    blk, width = intensities.shape
    whole = pl.BlockSpec(memory_space=pltpu.VMEM)
    return pl.pallas_call(
        move_kernel,
        grid=(NOPS,),
        out_shape=jax.ShapeDtypeStruct((width, NOPS * LANES), jnp.bfloat16),
        in_specs=[
            pl.BlockSpec((1, 1, width), lambda k: (k, 0, 0), memory_space=pltpu.SMEM),
            whole,
            whole,
        ],
        out_specs=pl.BlockSpec((width, LANES), lambda k: (0, k)),
        scratch_shapes=[
            pltpu.VMEM((width, LANES), jnp.float32),
            pltpu.VMEM((width, LANES), jnp.float32),
        ],
        compiler_params=params(),
        cost_estimate=pl.CostEstimate(
            flops=0, bytes_accessed=NOPS * width * LANES * 100, transcendentals=0
        ),
        name="move",
    )(local_ops[:, None, :], intensities, own_w)


def sums_kernel(got_ref, moved_ref, out_ref):
    rows, depth = got_ref.shape
    step = min(512, depth)

    @pl.when(pl.program_id(0) == 0)
    def _():
        out_ref[...] = jnp.zeros_like(out_ref)

    is_x = lax.broadcasted_iota(jnp.int32, (rows // SLAB, SLAB, step), 1) < SUB

    @pl.loop(0, depth // step)
    def _(i):
        cols = pl.ds(pl.multiple_of(i * step, step), step)
        raw = got_ref[:, cols]
        wide = raw.astype(jnp.float32).reshape(rows // SLAB, SLAB, step)
        product = wide * pltpu.roll(wide, SUB, 1)
        second = jnp.where(is_x, product * wide, product)
        second = second.reshape(rows, step).astype(jnp.bfloat16)
        right = moved_ref[cols, :]
        out_ref[0] += jnp.dot(raw, right, preferred_element_type=jnp.float32)
        out_ref[1] += jnp.dot(second, right, preferred_element_type=jnp.float32)


def sums(got, moved):
    rows, width = got.shape
    depth = min(2048, width)
    return pl.pallas_call(
        sums_kernel,
        grid=(width // depth,),
        out_shape=jax.ShapeDtypeStruct((2, rows, moved.shape[1]), jnp.float32),
        in_specs=[
            pl.BlockSpec((rows, depth), lambda i: (0, i)),
            pl.BlockSpec((depth, moved.shape[1]), lambda i: (i, 0)),
        ],
        out_specs=pl.BlockSpec((2, rows, moved.shape[1]), lambda i: (0, 0, 0)),
        compiler_params=params(),
        cost_estimate=pl.CostEstimate(
            flops=4 * rows * width * moved.shape[1],
            bytes_accessed=2 * width * (rows + moved.shape[1]),
            transcendentals=0,
        ),
        name="sums",
    )(got, moved)


def pearson(share, blk):
    first, second = share[0], share[1]
    total_w = first[:, SUB:, :, :blk]
    sum_x = first[:, SUB:, :, blk : 2 * blk]
    sum_xx = first[:, SUB:, :, 2 * blk : 3 * blk]
    sum_y = second[:, SUB:, :, :blk]
    sum_xy = second[:, SUB:, :, blk : 2 * blk]
    sum_yy = second[:, :SUB, :, :blk]
    numer = total_w * sum_xy - sum_x * sum_y
    var_x = jnp.maximum(total_w * sum_xx - sum_x * sum_x, 0.05 * total_w * sum_xx)
    var_y = jnp.maximum(total_w * sum_yy - sum_y * sum_y, 0.05 * total_w * sum_yy)
    return numer / jnp.sqrt(var_x * var_y)


def fill_slabs(slabs, xw_ref, offset, width):
    blk = xw_ref.shape[0] // 2
    step = min(512, width)

    @pl.loop(0, width // step)
    def _(i):
        cols = pl.ds(pl.multiple_of(offset + i * step, step), step)
        wide = xw_ref[:, cols].astype(jnp.float32)
        for g in range(blk // SUB):
            rows = slice(g * SUB, (g + 1) * SUB)
            slab = jnp.concatenate([wide[:blk][rows], wide[blk:][rows]], 0)
            slabs[g, :, cols] = slab.astype(jnp.bfloat16)


def send_slabs(xw_ref, pick_ref, send_ref, slabs, sems, ready):
    mine = lax.div(lax.axis_index("dp"), PLANE)
    partner = mine + 1 - 2 * lax.rem(mine, 2)
    span = xw_ref.shape[1] // PARTS
    copies = []
    for part in range(PARTS):
        ready(part)
        fill_slabs(slabs, xw_ref, part * span, span)
        cols = pl.ds(part * span, span)
        for c in range(PLANE):
            for t, plane in enumerate((mine, partner)):
                group = pick_ref[plane * PLANE + c]
                copy = pltpu.make_async_copy(
                    slabs.at[group, :, cols], send_ref.at[c, t, :, cols], sems.at[c, t, part]
                )
                copy.start()
                copies.append(copy)
    for copy in copies:
        copy.wait()


def own_pack_kernel(pick_ref, xw_ref, send_ref, slabs, sems):
    send_slabs(xw_ref, pick_ref, send_ref, slabs, sems, lambda part: None)


def far_pack_kernel(pick_ref, outer_ref, inner_ref, after_ref, send_ref, buf, in_sems, slabs, sems):
    plane = lax.div(lax.axis_index("dp"), PLANE)
    is_inner = (plane == 1) | (plane == 2)
    span = buf.shape[1] // PARTS

    def forward(ref):
        fetches = []
        for part in range(PARTS):
            cols = pl.ds(part * span, span)
            fetches.append(pltpu.make_async_copy(ref.at[:, cols], buf.at[:, cols], in_sems.at[part]))
        for fetch in fetches:
            fetch.start()
        send_slabs(buf, pick_ref, send_ref, slabs, sems, lambda part: fetches[part].wait())

    @pl.when(is_inner)
    def _():
        forward(inner_ref)

    @pl.when(jnp.logical_not(is_inner))
    def _():
        forward(outer_ref)


def pack_call(kernel, name, specs, scratch, blk, width, *operands):
    return pl.pallas_call(
        kernel,
        out_shape=jax.ShapeDtypeStruct((PLANE, 2, SLAB, width), jnp.bfloat16),
        in_specs=[pl.BlockSpec(memory_space=pltpu.SMEM)] + specs,
        out_specs=pl.BlockSpec(memory_space=pl.ANY),
        scratch_shapes=scratch
        + [pltpu.VMEM((blk // SUB, SLAB, width), jnp.bfloat16), pltpu.SemaphoreType.DMA((PLANE, 2, PARTS))],
        compiler_params=params(),
        cost_estimate=pl.CostEstimate(
            flops=blk * width * 4, bytes_accessed=(PLANE * 2 * SLAB * 2 + blk * 4) * width, transcendentals=0
        ),
        name=name,
    )(*operands)


def own_pack(pick, xw):
    rows, width = xw.shape
    specs = [pl.BlockSpec(memory_space=pltpu.VMEM)]
    return pack_call(own_pack_kernel, "own_pack", specs, [], rows // 2, width, pick, xw)


def far_pack(pick, outer, inner, after):
    rows, width = outer.shape
    scratch = [pltpu.VMEM((rows, width), jnp.bfloat16), pltpu.SemaphoreType.DMA((PARTS,))]
    specs = [pl.BlockSpec(memory_space=pl.ANY)] * 3
    return pack_call(far_pack_kernel, "far_pack", specs, scratch, rows // 2, width, pick, outer, inner, after)


def place_kernel(ops_ref, mine_ref, near_ref, after_ref, moved_ref, table, target):
    blk, depth = mine_ref.shape[0] // 2, mine_ref.shape[1]
    width = target.shape[0]
    part = pl.multiple_of(pl.program_id(1) * depth, depth)

    @pl.when(pl.program_id(0) == 0)
    def _():
        step = min(256, depth)
        diagonal = lax.broadcasted_iota(jnp.int32, (step, step), 0) == lax.broadcasted_iota(
            jnp.int32, (step, step), 1
        )
        identity = jnp.where(diagonal, 1.0, 0.0).astype(jnp.bfloat16)
        for i in range(depth // step):
            cols = slice(i * step, (i + 1) * step)
            pair = (mine_ref, near_ref)
            rows = jnp.concatenate([ref[:blk, cols] for ref in pair] + [ref[blk:, cols] for ref in pair], 0)
            table[pl.ds(part + i * step, step), :] = lax.dot_general(
                identity, rows, (((1,), (1,)), ((), ())), preferred_element_type=jnp.float32
            )

    @pl.loop(0, depth // UNROLL)
    def _(i):
        base = pl.multiple_of(i * UNROLL, UNROLL)
        row = pl.multiple_of(part + base, UNROLL)
        for j in range(UNROLL):
            to = ops_ref[0, 0, base + j]
            target[pl.ds(to, 1), :] = table[pl.ds(row + j, 1), :]

    @pl.when(pl.program_id(1) == pl.num_programs(1) - 1)
    def _():
        step = min(512, width)

        @pl.loop(0, width // step)
        def _(i):
            rows = pl.ds(pl.multiple_of(i * step, step), step)
            moved_ref[rows, :] = target[rows, :].astype(jnp.bfloat16)


def place(ops, mine, near, after):
    count = ops.shape[0]
    rows, width = mine.shape
    depth = min(4096, width)
    last = width // depth - 1
    part = pl.BlockSpec((rows, depth), lambda k, i: (0, jnp.where(k == 0, i, last)))
    return pl.pallas_call(
        place_kernel,
        grid=(count, width // depth),
        out_shape=jax.ShapeDtypeStruct((width, count * LANES), jnp.bfloat16),
        in_specs=[
            pl.BlockSpec((1, 1, depth), lambda k, i: (k, 0, i), memory_space=pltpu.SMEM),
            part,
            part,
            pl.BlockSpec(memory_space=pl.ANY),
        ],
        out_specs=pl.BlockSpec((width, LANES), lambda k, i: (0, k)),
        scratch_shapes=[pltpu.VMEM((width, LANES), jnp.float32)] * 2,
        compiler_params=params(),
        cost_estimate=pl.CostEstimate(
            flops=0, bytes_accessed=count * width * LANES * 64, transcendentals=0
        ),
        name="place",
    )(ops[:, None, :], mine, near, after)


def ratio(total_w, sum_x, sum_xx, sum_y, sum_xy, sum_yy):
    numer = total_w * sum_xy - sum_x * sum_y
    var_x = jnp.maximum(total_w * sum_xx - sum_x * sum_x, 0.05 * total_w * sum_xx)
    var_y = jnp.maximum(total_w * sum_yy - sum_y * sum_y, 0.05 * total_w * sum_yy)
    return numer / jnp.sqrt(var_x * var_y)


def add_sums(acc, got_ref, cols, right):
    rows = got_ref.shape[0]
    slabs = rows // SLAB
    wide = got_ref[:, cols].astype(jnp.float32).reshape(slabs, SLAB, -1)
    is_x = lax.broadcasted_iota(jnp.int32, wide.shape, 1) < SUB
    rolled = pltpu.roll(wide, SUB, 1)
    product = wide * rolled
    products = jnp.where(is_x, product * wide, product).reshape(rows, -1)
    mine = rolled.reshape(slabs // 2, 2, SLAB, -1)[:, 0]
    partner = wide.reshape(slabs // 2, 2, SLAB, -1)[:, 1]
    weights = jnp.where(is_x[: slabs // 2], mine, partner).reshape(rows // 2, -1)
    left = jnp.concatenate([weights, products], 0).astype(jnp.bfloat16)
    acc[...] += jnp.dot(left, right, preferred_element_type=jnp.float32)


def correlations(acc):
    rows = acc.shape[0] // 3
    half = LANES // 2
    blk = half // 2
    tiles = rows // SLAB
    top = lax.broadcasted_iota(jnp.int32, (tiles, SLAB, LANES), 1) < SUB
    lane = lax.broadcasted_iota(jnp.int32, (rows, LANES), 1)
    result = jnp.zeros((rows, LANES), jnp.float32)
    count = acc.shape[1] * 2 // 3 // LANES
    for k in range(count):
        lanes = slice(k * LANES, (k + 1) * LANES)
        squares = slice((count + k // 2) * LANES, (count + k // 2 + 1) * LANES)
        with_w = acc[:rows, lanes]
        with_y = acc[rows:, lanes].reshape(tiles, 2, SLAB, LANES)
        mine, partner = with_y[:, 0], with_y[:, 1]
        y = jnp.where(top, pltpu.roll(mine, SUB, 1), partner).reshape(rows, LANES)
        yy = jnp.where(top, mine, pltpu.roll(partner, SUB, 1)).reshape(rows, LANES)
        sum_xx = acc[:rows, squares]
        if k % 2 == 1:
            sum_xx = pltpu.roll(sum_xx, half, 1)
        both = ratio(
            pltpu.roll(with_w, half, 1), with_w, sum_xx, pltpu.roll(y, half, 1), y, pltpu.roll(yy, half, 1)
        )
        both = jnp.where(top.reshape(rows, LANES), both, pltpu.roll(both, LANES - blk, 1))
        moved = both if k == 0 else pltpu.roll(both, k * blk, 1)
        result = jnp.where((lane >= k * blk) & (lane < (k + 1) * blk), moved, result)
    return result


def plane_sums_kernel(pairs, got_ref, *refs):
    moved_refs, refs, acc = refs[:pairs], refs[pairs:-1], refs[-1]
    depth = got_ref.shape[1]
    step = min(2048, depth)
    half = LANES // 2

    @pl.when(pl.program_id(0) == 0)
    def _():
        acc[...] = jnp.zeros_like(acc)

    low = lax.broadcasted_iota(jnp.int32, (step, LANES), 1) < half
    for i in range(depth // step):
        cols = slice(i * step, (i + 1) * step)
        linear, square = [], []
        for ref in moved_refs:
            even, odd = None, None
            for k in range(2):
                values = ref[cols, k * LANES : (k + 1) * LANES].astype(jnp.float32)
                swapped = pltpu.roll(values, half, 1)
                product = values * swapped
                linear.append(jnp.where(low, product, values).astype(jnp.bfloat16))
                if k == 0:
                    even = product * values
                else:
                    odd = product * swapped
            square.append(jnp.where(low, even, odd).astype(jnp.bfloat16))
        add_sums(acc, got_ref, cols, jnp.concatenate(linear + square, 1))

    @pl.when(pl.program_id(0) == pl.num_programs(0) - 1)
    def _():
        if len(refs) == 1:
            refs[0][...] = correlations(acc)
            return
        first_ref, second_ref, mine_ref, other_ref, back_ref = refs
        upper = lax.div(lax.axis_index("dp"), 2 * PLANE)
        count = first_ref.shape[0] // 2
        low = lax.broadcasted_iota(jnp.int32, first_ref.shape, 1) < half
        own = jnp.where(low, first_ref[...], pltpu.roll(second_ref[...], half, 1))
        for part, result in enumerate((own, correlations(acc))):
            slot = part + upper - 2 * part * upper
            back_ref[slot] = result.reshape(PLANE, SLAB, LANES)
            pairs = result.reshape(PLANE // 2, 2, SLAB, LANES)
            even, odd = pairs[:, 0], pairs[:, 1]
            top = lax.broadcasted_iota(jnp.int32, even.shape, 1) < SUB
            here = slice(part * count, (part + 1) * count)
            mine_ref[here, :] = jnp.where(top, even, pltpu.roll(odd, SUB, 1)).reshape(count, LANES)
            other_ref[here, :] = jnp.where(top, pltpu.roll(even, SUB, 1), odd).reshape(count, LANES)


def plane_sums(got, moved, own):
    rows, width = got.shape
    depth = min(4096, width)
    lanes = 3 * len(moved) * LANES
    ended = len(own) > 0
    placed = pl.BlockSpec((depth, 2 * LANES), lambda i: (i, 0))
    result = (rows // 2, LANES)
    shapes = (result, result, (2, PLANE, SLAB, LANES)) if ended else (result,)
    entire = [pl.BlockSpec(shape, lambda i, shape=shape: (0,) * len(shape)) for shape in shapes]
    outs = pl.pallas_call(
        functools.partial(plane_sums_kernel, len(moved)),
        grid=(width // depth,),
        out_shape=tuple(jax.ShapeDtypeStruct(shape, jnp.float32) for shape in shapes),
        in_specs=[pl.BlockSpec((rows, depth), lambda i: (0, i))] + [placed] * len(moved) + [entire[0]] * len(own),
        out_specs=tuple(entire),
        scratch_shapes=[pltpu.VMEM((rows * 3 // 2, lanes), jnp.float32)],
        compiler_params=params(),
        cost_estimate=pl.CostEstimate(
            flops=3 * rows * width * lanes, bytes_accessed=2 * width * (rows + 2 * len(moved) * LANES), transcendentals=0
        ),
        name="plane_sums",
    )(got, *moved, *own)
    return outs if ended else outs[0]


def shards_by_plane(intensities, observed, qweights, ops, pick):
    blk, width = intensities.shape
    groups = PLANES * PLANE
    near = [(i, i ^ PLANE) for i in range(groups)]
    far = [(i, i ^ (2 * PLANE)) for i in range(groups)]
    middle = [(i, 3 * PLANE + 2 * (i % PLANE) - i) for i in range(PLANE, 3 * PLANE)]
    outward = [(i, i - PLANE if i < 2 * PLANE else i + PLANE) for i in range(PLANE, 3 * PLANE)]
    rings = [[z * PLANE + c for c in range(PLANE)] for z in range(PLANES)]
    couples = [[z * PLANE + c for z in (odd, odd + 2) for c in range(PLANE)] for odd in range(2)]
    plane = lax.axis_index("dp") // PLANE
    odd, upper = plane % 2 == 1, plane >= 2

    def spread(send):
        got = lax.all_to_all(send, "dp", split_axis=0, concat_axis=0, axis_index_groups=rings, tiled=True)
        return got.reshape(PLANE * 2 * SLAB, width)

    own_pick = pick[:, 0]
    own_w = (observed.astype(jnp.float32) * qweights.astype(jnp.float32)).astype(jnp.bfloat16)
    mine_xw = jnp.concatenate([intensities, own_w], 0)
    near_xw = lax.ppermute(mine_xw, "dp", near)
    mid_xw = lax.ppermute(mine_xw, "dp", middle)
    far_pick = lax.ppermute(own_pick, "dp", far)
    own_got = spread(own_pack(own_pick, mine_xw))
    near_xw, mid_xw, far_pick = lax.optimization_barrier((near_xw, mid_xw, far_pick))
    outer_xw = lax.ppermute(mid_xw, "dp", outward)
    inner_xw = lax.ppermute(near_xw, "dp", middle)
    first = place(ops[:2], mine_xw, near_xw, own_pick)
    own_first = plane_sums(own_got, (first,), ())
    far_send = far_pack(far_pick, outer_xw, inner_xw, own_first)
    far_got = spread(far_send)
    second = place(ops[2:], mine_xw, near_xw, far_send)
    own_second = plane_sums(own_got, (second,), ())
    mine, other, back = plane_sums(far_got, (first, second), (own_first, own_second))

    from_near = lax.ppermute(other, "dp", near)
    pair = [each.reshape(2, PLANE, SUB, NOPS * blk) for each in (mine, from_near)]
    pair = jnp.stack(pair, 1)
    pair = jnp.where(odd, pair[:, ::-1], pair)
    pair = jnp.where(upper, pair[::-1], pair)
    corr = pair.reshape(groups * SUB, NOPS * blk).T.reshape(NOPS, blk, groups * SUB)

    back = back.reshape(2 * PLANE, 2 * SUB, NOPS * blk)
    back = lax.all_to_all(back, "dp", split_axis=0, concat_axis=0, axis_index_groups=couples, tiled=True)
    back = back.reshape(2, PLANE, 2, SUB, NOPS, blk)
    back = jnp.where(odd, back[:, :, ::-1], back)
    returned = jnp.transpose(back, (4, 0, 2, 1, 3, 5)).reshape(NOPS, 1, groups, SUB, blk)
    return (corr, returned)


def shards(intensities, observed, qweights, ops, pick):
    if lax.axis_size("dp") == PLANES * PLANE and lax.axis_size("refl") == 1:
        return shards_by_plane(intensities, observed, qweights, ops, pick)
    return shards_direct(intensities, observed, qweights, ops, pick)


def shards_direct(intensities, observed, qweights, ops, pick):
    blk, width = intensities.shape
    groups = lax.axis_size("dp")
    shares = lax.axis_size("refl")
    local_ops = ops - lax.axis_index("refl") * width
    send, own_w = pack(pick[:, 0], intensities, observed, qweights)
    got = lax.all_to_all(send, "dp", split_axis=0, concat_axis=0, tiled=True)
    moved = move(local_ops, intensities, own_w)
    stats = sums(got.reshape(groups * SLAB, width), moved)
    if shares > 1:
        stats = lax.psum(stats, "refl")
    stats = stats.reshape(2, groups, SLAB, NOPS, LANES)
    full = pearson(stats, blk)
    rows = blk // shares
    if shares > 1:
        full = lax.dynamic_slice_in_dim(full, lax.axis_index("refl") * rows, rows, 3)
    corr = jnp.transpose(full, (2, 3, 0, 1)).reshape(NOPS, rows, groups * SUB)
    back = lax.all_to_all(full, "dp", split_axis=0, concat_axis=0, tiled=True)
    returned = jnp.transpose(back, (2, 0, 1, 3))[:, None]
    return (corr, returned)


def solution(mesh):
    return jax.shard_map(
        shards,
        mesh=mesh,
        in_specs=(
            P("dp", "refl"),
            P("dp", "refl"),
            P("dp", "refl"),
            P(None, "refl"),
            P(None, "dp"),
        ),
        out_specs=(P(None, ("dp", "refl"), None), P(None, "dp", None, None, "refl")),
        check_vma=False,
    )
```

```python
import functools

import jax
import jax.numpy as jnp
from jax import lax
from jax.experimental import pallas as pl
from jax.experimental.pallas import tpu as pltpu
from jax.sharding import PartitionSpec as P

SUB = 4
NOPS = 4
LANES = 128
SLAB = 2 * SUB
VMEM_LIMIT = 56 * 1024 * 1024
PLANES = 4
PLANE = 8
UNROLL = 128
PARTS = 4


def params():
    return pltpu.CompilerParams(vmem_limit_bytes=VMEM_LIMIT)


def pack_kernel(pick_ref, x_ref, obs_ref, qw_ref, send_ref, w_ref, slabs, sems):
    blk, width = x_ref.shape
    step = min(512, width)

    @pl.loop(0, width // step)
    def _(i):
        cols = pl.ds(pl.multiple_of(i * step, step), step)
        wide_w = obs_ref[:, cols].astype(jnp.float32) * qw_ref[:, cols].astype(jnp.float32)
        wide_x = x_ref[:, cols].astype(jnp.float32)
        w_ref[:, cols] = wide_w.astype(jnp.bfloat16)
        for g in range(blk // SUB):
            rows = slice(g * SUB, (g + 1) * SUB)
            slab = jnp.concatenate([wide_x[rows], wide_w[rows]], 0)
            slabs[g, :, cols] = slab.astype(jnp.bfloat16)

    groups = send_ref.shape[0]

    def copy(d):
        return pltpu.make_async_copy(slabs.at[pick_ref[d]], send_ref.at[d], sems.at[d])

    @pl.loop(0, groups)
    def _(d):
        copy(d).start()

    @pl.loop(0, groups)
    def _(d):
        copy(d).wait()


def pack(pick, intensities, observed, qweights):
    blk, width = intensities.shape
    groups = pick.shape[0]
    whole = pl.BlockSpec(memory_space=pltpu.VMEM)
    return pl.pallas_call(
        pack_kernel,
        out_shape=(
            jax.ShapeDtypeStruct((groups, SLAB, width), jnp.bfloat16),
            jax.ShapeDtypeStruct((blk, width), jnp.bfloat16),
        ),
        in_specs=[pl.BlockSpec(memory_space=pltpu.SMEM), whole, whole, whole],
        out_specs=(pl.BlockSpec(memory_space=pl.ANY), whole),
        scratch_shapes=[
            pltpu.VMEM((blk // SUB, SLAB, width), jnp.bfloat16),
            pltpu.SemaphoreType.DMA((groups,)),
        ],
        compiler_params=params(),
        cost_estimate=pl.CostEstimate(
            flops=blk * width * 4, bytes_accessed=(groups * SLAB * 2 + blk * 10) * width, transcendentals=0
        ),
        name="pack",
    )(pick, intensities, observed, qweights)


def move_kernel(ops_ref, x_ref, w_ref, moved_ref, table, target):
    blk, width = x_ref.shape

    @pl.when(pl.program_id(0) == 0)
    def _():
        @pl.loop(0, width // LANES)
        def _(i):
            cols = pl.ds(pl.multiple_of(i * LANES, LANES), LANES)
            wide_x = x_ref[:, cols].astype(jnp.float32)
            wide_w = w_ref[:, cols].astype(jnp.float32)
            wx = (wide_w * wide_x).astype(jnp.bfloat16).astype(jnp.float32)
            wxx = (wide_w * wide_x * wide_x).astype(jnp.bfloat16).astype(jnp.float32)
            stacked = jnp.concatenate([wide_w, wx, wxx, jnp.zeros((LANES - 3 * blk, LANES), jnp.float32)], 0)
            table[cols, :] = stacked.T

    unroll = 16

    @pl.loop(0, width // unroll)
    def _(i):
        base = pl.multiple_of(i * unroll, unroll)
        for j in range(unroll):
            to = ops_ref[0, 0, base + j]
            target[pl.ds(to, 1), :] = table[pl.ds(base + j, 1), :]

    step = min(512, width)

    @pl.loop(0, width // step)
    def _(i):
        rows = pl.ds(pl.multiple_of(i * step, step), step)
        moved_ref[rows, :] = target[rows, :].astype(jnp.bfloat16)


def move(local_ops, intensities, own_w):
    blk, width = intensities.shape
    whole = pl.BlockSpec(memory_space=pltpu.VMEM)
    return pl.pallas_call(
        move_kernel,
        grid=(NOPS,),
        out_shape=jax.ShapeDtypeStruct((width, NOPS * LANES), jnp.bfloat16),
        in_specs=[
            pl.BlockSpec((1, 1, width), lambda k: (k, 0, 0), memory_space=pltpu.SMEM),
            whole,
            whole,
        ],
        out_specs=pl.BlockSpec((width, LANES), lambda k: (0, k)),
        scratch_shapes=[
            pltpu.VMEM((width, LANES), jnp.float32),
            pltpu.VMEM((width, LANES), jnp.float32),
        ],
        compiler_params=params(),
        cost_estimate=pl.CostEstimate(
            flops=0, bytes_accessed=NOPS * width * LANES * 100, transcendentals=0
        ),
        name="move",
    )(local_ops[:, None, :], intensities, own_w)


def sums_kernel(got_ref, moved_ref, out_ref):
    rows, depth = got_ref.shape
    step = min(512, depth)

    @pl.when(pl.program_id(0) == 0)
    def _():
        out_ref[...] = jnp.zeros_like(out_ref)

    is_x = lax.broadcasted_iota(jnp.int32, (rows // SLAB, SLAB, step), 1) < SUB

    @pl.loop(0, depth // step)
    def _(i):
        cols = pl.ds(pl.multiple_of(i * step, step), step)
        raw = got_ref[:, cols]
        wide = raw.astype(jnp.float32).reshape(rows // SLAB, SLAB, step)
        product = wide * pltpu.roll(wide, SUB, 1)
        second = jnp.where(is_x, product * wide, product)
        second = second.reshape(rows, step).astype(jnp.bfloat16)
        right = moved_ref[cols, :]
        out_ref[0] += jnp.dot(raw, right, preferred_element_type=jnp.float32)
        out_ref[1] += jnp.dot(second, right, preferred_element_type=jnp.float32)


def sums(got, moved):
    rows, width = got.shape
    depth = min(2048, width)
    return pl.pallas_call(
        sums_kernel,
        grid=(width // depth,),
        out_shape=jax.ShapeDtypeStruct((2, rows, moved.shape[1]), jnp.float32),
        in_specs=[
            pl.BlockSpec((rows, depth), lambda i: (0, i)),
            pl.BlockSpec((depth, moved.shape[1]), lambda i: (i, 0)),
        ],
        out_specs=pl.BlockSpec((2, rows, moved.shape[1]), lambda i: (0, 0, 0)),
        compiler_params=params(),
        cost_estimate=pl.CostEstimate(
            flops=4 * rows * width * moved.shape[1],
            bytes_accessed=2 * width * (rows + moved.shape[1]),
            transcendentals=0,
        ),
        name="sums",
    )(got, moved)


def pearson(share, blk):
    first, second = share[0], share[1]
    total_w = first[:, SUB:, :, :blk]
    sum_x = first[:, SUB:, :, blk : 2 * blk]
    sum_xx = first[:, SUB:, :, 2 * blk : 3 * blk]
    sum_y = second[:, SUB:, :, :blk]
    sum_xy = second[:, SUB:, :, blk : 2 * blk]
    sum_yy = second[:, :SUB, :, :blk]
    numer = total_w * sum_xy - sum_x * sum_y
    var_x = jnp.maximum(total_w * sum_xx - sum_x * sum_x, 0.05 * total_w * sum_xx)
    var_y = jnp.maximum(total_w * sum_yy - sum_y * sum_y, 0.05 * total_w * sum_yy)
    return numer / jnp.sqrt(var_x * var_y)


def fill_slabs(slabs, xw_ref, offset, width):
    blk = xw_ref.shape[0] // 2
    step = min(512, width)

    @pl.loop(0, width // step)
    def _(i):
        cols = pl.ds(pl.multiple_of(offset + i * step, step), step)
        wide = xw_ref[:, cols].astype(jnp.float32)
        for g in range(blk // SUB):
            rows = slice(g * SUB, (g + 1) * SUB)
            slab = jnp.concatenate([wide[:blk][rows], wide[blk:][rows]], 0)
            slabs[g, :, cols] = slab.astype(jnp.bfloat16)


def send_slabs(xw_ref, pick_ref, send_ref, slabs, sems, ready):
    mine = lax.div(lax.axis_index("dp"), PLANE)
    partner = mine + 1 - 2 * lax.rem(mine, 2)
    span = xw_ref.shape[1] // PARTS
    copies = []
    for part in range(PARTS):
        ready(part)
        fill_slabs(slabs, xw_ref, part * span, span)
        cols = pl.ds(part * span, span)
        for c in range(PLANE):
            for t, plane in enumerate((mine, partner)):
                group = pick_ref[plane * PLANE + c]
                copy = pltpu.make_async_copy(
                    slabs.at[group, :, cols], send_ref.at[c, t, :, cols], sems.at[c, t, part]
                )
                copy.start()
                copies.append(copy)
    for copy in copies:
        copy.wait()


def own_pack_kernel(pick_ref, xw_ref, send_ref, slabs, sems):
    send_slabs(xw_ref, pick_ref, send_ref, slabs, sems, lambda part: None)


def far_pack_kernel(pick_ref, outer_ref, inner_ref, after_ref, send_ref, buf, in_sems, slabs, sems):
    plane = lax.div(lax.axis_index("dp"), PLANE)
    is_inner = (plane == 1) | (plane == 2)
    span = buf.shape[1] // PARTS

    def forward(ref):
        fetches = []
        for part in range(PARTS):
            cols = pl.ds(part * span, span)
            fetches.append(pltpu.make_async_copy(ref.at[:, cols], buf.at[:, cols], in_sems.at[part]))
        for fetch in fetches:
            fetch.start()
        send_slabs(buf, pick_ref, send_ref, slabs, sems, lambda part: fetches[part].wait())

    @pl.when(is_inner)
    def _():
        forward(inner_ref)

    @pl.when(jnp.logical_not(is_inner))
    def _():
        forward(outer_ref)


def pack_call(kernel, name, specs, scratch, blk, width, *operands):
    return pl.pallas_call(
        kernel,
        out_shape=jax.ShapeDtypeStruct((PLANE, 2, SLAB, width), jnp.bfloat16),
        in_specs=[pl.BlockSpec(memory_space=pltpu.SMEM)] + specs,
        out_specs=pl.BlockSpec(memory_space=pl.ANY),
        scratch_shapes=scratch
        + [pltpu.VMEM((blk // SUB, SLAB, width), jnp.bfloat16), pltpu.SemaphoreType.DMA((PLANE, 2, PARTS))],
        compiler_params=params(),
        cost_estimate=pl.CostEstimate(
            flops=blk * width * 4, bytes_accessed=(PLANE * 2 * SLAB * 2 + blk * 4) * width, transcendentals=0
        ),
        name=name,
    )(*operands)


def own_pack(pick, xw):
    rows, width = xw.shape
    specs = [pl.BlockSpec(memory_space=pltpu.VMEM)]
    return pack_call(own_pack_kernel, "own_pack", specs, [], rows // 2, width, pick, xw)


def far_pack(pick, outer, inner, after):
    rows, width = outer.shape
    scratch = [pltpu.VMEM((rows, width), jnp.bfloat16), pltpu.SemaphoreType.DMA((PARTS,))]
    specs = [pl.BlockSpec(memory_space=pl.ANY)] * 3
    return pack_call(far_pack_kernel, "far_pack", specs, scratch, rows // 2, width, pick, outer, inner, after)


def place_kernel(ops_ref, mine_ref, near_ref, after_ref, moved_ref, table, target):
    blk, depth = mine_ref.shape[0] // 2, mine_ref.shape[1]
    width = target.shape[0]
    part = pl.multiple_of(pl.program_id(1) * depth, depth)

    @pl.when(pl.program_id(0) == 0)
    def _():
        step = min(256, depth)
        diagonal = lax.broadcasted_iota(jnp.int32, (step, step), 0) == lax.broadcasted_iota(
            jnp.int32, (step, step), 1
        )
        identity = jnp.where(diagonal, 1.0, 0.0).astype(jnp.bfloat16)
        for i in range(depth // step):
            cols = slice(i * step, (i + 1) * step)
            pair = (mine_ref, near_ref)
            rows = jnp.concatenate([ref[:blk, cols] for ref in pair] + [ref[blk:, cols] for ref in pair], 0)
            table[pl.ds(part + i * step, step), :] = lax.dot_general(
                identity, rows, (((1,), (1,)), ((), ())), preferred_element_type=jnp.float32
            )

    @pl.loop(0, depth // UNROLL)
    def _(i):
        base = pl.multiple_of(i * UNROLL, UNROLL)
        row = pl.multiple_of(part + base, UNROLL)
        for j in range(UNROLL):
            to = ops_ref[0, 0, base + j]
            target[pl.ds(to, 1), :] = table[pl.ds(row + j, 1), :]

    @pl.when(pl.program_id(1) == pl.num_programs(1) - 1)
    def _():
        step = min(512, width)

        @pl.loop(0, width // step)
        def _(i):
            rows = pl.ds(pl.multiple_of(i * step, step), step)
            moved_ref[rows, :] = target[rows, :].astype(jnp.bfloat16)


def place(ops, mine, near, after):
    count = ops.shape[0]
    rows, width = mine.shape
    depth = min(8192, width)
    last = width // depth - 1
    part = pl.BlockSpec((rows, depth), lambda k, i: (0, jnp.where(k == 0, i, last)))
    return pl.pallas_call(
        place_kernel,
        grid=(count, width // depth),
        out_shape=jax.ShapeDtypeStruct((width, count * LANES), jnp.bfloat16),
        in_specs=[
            pl.BlockSpec((1, 1, depth), lambda k, i: (k, 0, i), memory_space=pltpu.SMEM),
            part,
            part,
            pl.BlockSpec(memory_space=pl.ANY),
        ],
        out_specs=pl.BlockSpec((width, LANES), lambda k, i: (0, k)),
        scratch_shapes=[pltpu.VMEM((width, LANES), jnp.float32)] * 2,
        compiler_params=params(),
        cost_estimate=pl.CostEstimate(
            flops=0, bytes_accessed=count * width * LANES * 64, transcendentals=0
        ),
        name="place",
    )(ops[:, None, :], mine, near, after)


def ratio(total_w, sum_x, sum_xx, sum_y, sum_xy, sum_yy):
    numer = total_w * sum_xy - sum_x * sum_y
    var_x = jnp.maximum(total_w * sum_xx - sum_x * sum_x, 0.05 * total_w * sum_xx)
    var_y = jnp.maximum(total_w * sum_yy - sum_y * sum_y, 0.05 * total_w * sum_yy)
    return numer / jnp.sqrt(var_x * var_y)


def add_sums(acc, got_ref, cols, right):
    rows = got_ref.shape[0]
    slabs = rows // SLAB
    wide = got_ref[:, cols].astype(jnp.float32).reshape(slabs, SLAB, -1)
    is_x = lax.broadcasted_iota(jnp.int32, wide.shape, 1) < SUB
    rolled = pltpu.roll(wide, SUB, 1)
    product = wide * rolled
    products = jnp.where(is_x, product * wide, product).reshape(rows, -1)
    mine = rolled.reshape(slabs // 2, 2, SLAB, -1)[:, 0]
    partner = wide.reshape(slabs // 2, 2, SLAB, -1)[:, 1]
    weights = jnp.where(is_x[: slabs // 2], mine, partner).reshape(rows // 2, -1)
    left = jnp.concatenate([weights, products], 0).astype(jnp.bfloat16)
    acc[...] += jnp.dot(left, right, preferred_element_type=jnp.float32)


def correlations(acc):
    rows = acc.shape[0] // 3
    half = LANES // 2
    blk = half // 2
    tiles = rows // SLAB
    top = lax.broadcasted_iota(jnp.int32, (tiles, SLAB, LANES), 1) < SUB
    lane = lax.broadcasted_iota(jnp.int32, (rows, LANES), 1)
    result = jnp.zeros((rows, LANES), jnp.float32)
    count = acc.shape[1] * 2 // 3 // LANES
    for k in range(count):
        lanes = slice(k * LANES, (k + 1) * LANES)
        squares = slice((count + k // 2) * LANES, (count + k // 2 + 1) * LANES)
        with_w = acc[:rows, lanes]
        with_y = acc[rows:, lanes].reshape(tiles, 2, SLAB, LANES)
        mine, partner = with_y[:, 0], with_y[:, 1]
        y = jnp.where(top, pltpu.roll(mine, SUB, 1), partner).reshape(rows, LANES)
        yy = jnp.where(top, mine, pltpu.roll(partner, SUB, 1)).reshape(rows, LANES)
        sum_xx = acc[:rows, squares]
        if k % 2 == 1:
            sum_xx = pltpu.roll(sum_xx, half, 1)
        both = ratio(
            pltpu.roll(with_w, half, 1), with_w, sum_xx, pltpu.roll(y, half, 1), y, pltpu.roll(yy, half, 1)
        )
        both = jnp.where(top.reshape(rows, LANES), both, pltpu.roll(both, LANES - blk, 1))
        moved = both if k == 0 else pltpu.roll(both, k * blk, 1)
        result = jnp.where((lane >= k * blk) & (lane < (k + 1) * blk), moved, result)
    return result


def plane_sums_kernel(pairs, got_ref, *refs):
    moved_refs, refs, acc = refs[:pairs], refs[pairs:-1], refs[-1]
    depth = got_ref.shape[1]
    step = min(2048, depth)
    half = LANES // 2

    @pl.when(pl.program_id(0) == 0)
    def _():
        acc[...] = jnp.zeros_like(acc)

    low = lax.broadcasted_iota(jnp.int32, (step, LANES), 1) < half
    for i in range(depth // step):
        cols = slice(i * step, (i + 1) * step)
        linear, square = [], []
        for ref in moved_refs:
            even, odd = None, None
            for k in range(2):
                values = ref[cols, k * LANES : (k + 1) * LANES].astype(jnp.float32)
                swapped = pltpu.roll(values, half, 1)
                product = values * swapped
                linear.append(jnp.where(low, product, values).astype(jnp.bfloat16))
                if k == 0:
                    even = product * values
                else:
                    odd = product * swapped
            square.append(jnp.where(low, even, odd).astype(jnp.bfloat16))
        add_sums(acc, got_ref, cols, jnp.concatenate(linear + square, 1))

    @pl.when(pl.program_id(0) == pl.num_programs(0) - 1)
    def _():
        if len(refs) == 1:
            refs[0][...] = correlations(acc)
            return
        first_ref, second_ref, mine_ref, other_ref, back_ref = refs
        upper = lax.div(lax.axis_index("dp"), 2 * PLANE)
        count = first_ref.shape[0] // 2
        low = lax.broadcasted_iota(jnp.int32, first_ref.shape, 1) < half
        own = jnp.where(low, first_ref[...], pltpu.roll(second_ref[...], half, 1))
        for part, result in enumerate((own, correlations(acc))):
            slot = part + upper - 2 * part * upper
            back_ref[slot] = result.reshape(PLANE, SLAB, LANES)
            pairs = result.reshape(PLANE // 2, 2, SLAB, LANES)
            even, odd = pairs[:, 0], pairs[:, 1]
            top = lax.broadcasted_iota(jnp.int32, even.shape, 1) < SUB
            here = slice(part * count, (part + 1) * count)
            mine_ref[here, :] = jnp.where(top, even, pltpu.roll(odd, SUB, 1)).reshape(count, LANES)
            other_ref[here, :] = jnp.where(top, pltpu.roll(even, SUB, 1), odd).reshape(count, LANES)


def plane_sums(got, moved, own):
    rows, width = got.shape
    depth = min(4096, width)
    lanes = 3 * len(moved) * LANES
    ended = len(own) > 0
    placed = pl.BlockSpec((depth, 2 * LANES), lambda i: (i, 0))
    result = (rows // 2, LANES)
    shapes = (result, result, (2, PLANE, SLAB, LANES)) if ended else (result,)
    entire = [pl.BlockSpec(shape, lambda i, shape=shape: (0,) * len(shape)) for shape in shapes]
    outs = pl.pallas_call(
        functools.partial(plane_sums_kernel, len(moved)),
        grid=(width // depth,),
        out_shape=tuple(jax.ShapeDtypeStruct(shape, jnp.float32) for shape in shapes),
        in_specs=[pl.BlockSpec((rows, depth), lambda i: (0, i))] + [placed] * len(moved) + [entire[0]] * len(own),
        out_specs=tuple(entire),
        scratch_shapes=[pltpu.VMEM((rows * 3 // 2, lanes), jnp.float32)],
        compiler_params=params(),
        cost_estimate=pl.CostEstimate(
            flops=3 * rows * width * lanes, bytes_accessed=2 * width * (rows + 2 * len(moved) * LANES), transcendentals=0
        ),
        name="plane_sums",
    )(got, *moved, *own)
    return outs if ended else outs[0]


def shards_by_plane(intensities, observed, qweights, ops, pick):
    blk, width = intensities.shape
    groups = PLANES * PLANE
    near = [(i, i ^ PLANE) for i in range(groups)]
    far = [(i, i ^ (2 * PLANE)) for i in range(groups)]
    middle = [(i, 3 * PLANE + 2 * (i % PLANE) - i) for i in range(PLANE, 3 * PLANE)]
    outward = [(i, i - PLANE if i < 2 * PLANE else i + PLANE) for i in range(PLANE, 3 * PLANE)]
    rings = [[z * PLANE + c for c in range(PLANE)] for z in range(PLANES)]
    couples = [[z * PLANE + c for z in (odd, odd + 2) for c in range(PLANE)] for odd in range(2)]
    plane = lax.axis_index("dp") // PLANE
    odd, upper = plane % 2 == 1, plane >= 2

    def spread(send):
        got = lax.all_to_all(send, "dp", split_axis=0, concat_axis=0, axis_index_groups=rings, tiled=True)
        return got.reshape(PLANE * 2 * SLAB, width)

    own_pick = pick[:, 0]
    own_w = (observed.astype(jnp.float32) * qweights.astype(jnp.float32)).astype(jnp.bfloat16)
    mine_xw = jnp.concatenate([intensities, own_w], 0)
    near_xw = lax.ppermute(mine_xw, "dp", near)
    mid_xw = lax.ppermute(mine_xw, "dp", middle)
    far_pick = lax.ppermute(own_pick, "dp", far)
    own_got = spread(own_pack(own_pick, mine_xw))
    near_xw, mid_xw, far_pick = lax.optimization_barrier((near_xw, mid_xw, far_pick))
    outer_xw = lax.ppermute(mid_xw, "dp", outward)
    inner_xw = lax.ppermute(near_xw, "dp", middle)
    first = place(ops[:2], mine_xw, near_xw, own_pick)
    own_first = plane_sums(own_got, (first,), ())
    far_send = far_pack(far_pick, outer_xw, inner_xw, own_first)
    far_got = spread(far_send)
    second = place(ops[2:], mine_xw, near_xw, far_send)
    own_second = plane_sums(own_got, (second,), ())
    mine, other, back = plane_sums(far_got, (first, second), (own_first, own_second))

    from_near = lax.ppermute(other, "dp", near)
    pair = [each.reshape(2, PLANE, SUB, NOPS * blk) for each in (mine, from_near)]
    pair = jnp.stack(pair, 1)
    pair = jnp.where(odd, pair[:, ::-1], pair)
    pair = jnp.where(upper, pair[::-1], pair)
    corr = pair.reshape(groups * SUB, NOPS * blk).T.reshape(NOPS, blk, groups * SUB)

    back = back.reshape(2 * PLANE, 2 * SUB, NOPS * blk)
    back = lax.all_to_all(back, "dp", split_axis=0, concat_axis=0, axis_index_groups=couples, tiled=True)
    back = back.reshape(2, PLANE, 2, SUB, NOPS, blk)
    back = jnp.where(odd, back[:, :, ::-1], back)
    returned = jnp.transpose(back, (4, 0, 2, 1, 3, 5)).reshape(NOPS, 1, groups, SUB, blk)
    return (corr, returned)


def shards(intensities, observed, qweights, ops, pick):
    if lax.axis_size("dp") == PLANES * PLANE and lax.axis_size("refl") == 1:
        return shards_by_plane(intensities, observed, qweights, ops, pick)
    return shards_direct(intensities, observed, qweights, ops, pick)


def shards_direct(intensities, observed, qweights, ops, pick):
    blk, width = intensities.shape
    groups = lax.axis_size("dp")
    shares = lax.axis_size("refl")
    local_ops = ops - lax.axis_index("refl") * width
    send, own_w = pack(pick[:, 0], intensities, observed, qweights)
    got = lax.all_to_all(send, "dp", split_axis=0, concat_axis=0, tiled=True)
    moved = move(local_ops, intensities, own_w)
    stats = sums(got.reshape(groups * SLAB, width), moved)
    if shares > 1:
        stats = lax.psum(stats, "refl")
    stats = stats.reshape(2, groups, SLAB, NOPS, LANES)
    full = pearson(stats, blk)
    rows = blk // shares
    if shares > 1:
        full = lax.dynamic_slice_in_dim(full, lax.axis_index("refl") * rows, rows, 3)
    corr = jnp.transpose(full, (2, 3, 0, 1)).reshape(NOPS, rows, groups * SUB)
    back = lax.all_to_all(full, "dp", split_axis=0, concat_axis=0, tiled=True)
    returned = jnp.transpose(back, (2, 0, 1, 3))[:, None]
    return (corr, returned)


def solution(mesh):
    return jax.shard_map(
        shards,
        mesh=mesh,
        in_specs=(
            P("dp", "refl"),
            P("dp", "refl"),
            P("dp", "refl"),
            P(None, "refl"),
            P(None, "dp"),
        ),
        out_specs=(P(None, ("dp", "refl"), None), P(None, "dp", None, None, "refl")),
        check_vma=False,
    )
```
